32 devices in a mesh: dp: 8 (over z, core), tensor: 4 (over y, x).
Axes of the slice: x: 2, y: 2, z: 4, core: 2. Of those that a mesh axis runs over, the one named last changes fastest.
Arguments:
- tokens: bfloat16 [8192, 1024], P(('dp', 'tensor')), as said below
- upstream: bfloat16 [8192, 1024], P(('dp', 'tensor')), may hold values from -6 to 6
- segment_ids: int32 [8192], P('dp'), may hold values from 0 to 5, as said below
- query_proj: bfloat16 [2, 1024, 1024], P(None, None, 'tensor'), may hold values from -0.1875 to 0.1875
- key_proj: bfloat16 [2, 1024, 1024], P(None, None, 'tensor'), may hold values from -0.1875 to 0.1875
- value_proj: bfloat16 [2, 1024, 1024], P(None, None, 'tensor'), may hold values from -0.1875 to 0.1875
- gate_proj: bfloat16 [2, 1024, 1024], P(None, None, 'tensor'), may hold values from -0.1875 to 0.1875
- output_proj: bfloat16 [2, 1024, 1024], P(None, 'tensor'), may hold values from -0.1875 to 0.1875
- left_proj: bfloat16 [2, 1024, 2816], P(None, None, 'tensor'), may hold values from -0.1875 to 0.1875
- right_proj: bfloat16 [2, 1024, 2816], P(None, None, 'tensor'), may hold values from -0.1875 to 0.1875
- down_proj: bfloat16 [2, 2816, 1024], P(None, 'tensor'), may hold values from -0.109375 to 0.109375
Outputs:
- block_out: bfloat16 [8192, 1024], P(('dp', 'tensor'))
- input_grad: bfloat16 [8192, 1024], P(('dp', 'tensor'))
- query_grad: float32 [2, 1024, 1024], P(None, None, 'tensor')
- key_grad: float32 [2, 1024, 1024], P(None, None, 'tensor')
- value_grad: float32 [2, 1024, 1024], P(None, None, 'tensor')
- gate_grad: float32 [2, 1024, 1024], P(None, None, 'tensor')
- output_grad: float32 [2, 1024, 1024], P(None, 'tensor')
- left_grad: float32 [2, 1024, 2816], P(None, None, 'tensor')
- right_grad: float32 [2, 1024, 2816], P(None, None, 'tensor')
- down_grad: float32 [2, 2816, 1024], P(None, 'tensor')
- rms_stats: float32 [2, 3], replicated
The draws below stay inside these ranges and needn't reach their ends.
Inputs may be any that keep to these rules, and one draw needn't show every extreme that they name: `tokens`: input activations. `segment_ids`: in each sequence of 1024 tokens the ids start at 0 and rise by one at the first token of each document; every document but the last one of a sequence has 200 to 2000 tokens.
All inputs are finite; a program needn't handle non-finite values.
Results may differ from the reference program's by a relative error of at most 0.034.
Values may be sent and summed in bfloat16 or wider, within the bound.
A program may use at most 256 MiB of HBM per device.

```python
import math
from functools import partial
import jax
import jax.numpy as jnp
from jax import lax

D = 1024
HEADS = 8
HDIM = 128
FF = 2816
LAYERS = 2
LEN = 1024
BLK = 512
DOC_MIN = 200
DOC_MAX = 2000
TOKENS = 8192


def draw_tokens(key, part):
    first_key, second_key, third_key = jax.random.split(key, 3)
    places = jnp.arange(TOKENS, dtype=jnp.float32) / (TOKENS - 1)
    rising = 0.5 + places
    row_scale = jnp.exp(jax.random.uniform(second_key, (TOKENS, 1), minval=math.log(0.5), maxval=math.log(2.0)))
    column_scale = jnp.exp(jax.random.uniform(third_key, (1, D), minval=math.log(0.7), maxval=math.log(1.4)))
    base_values = jax.random.normal(first_key, (TOKENS, D))
    return (base_values * row_scale * column_scale * rising[:, None]).astype(jnp.bfloat16)


def draw_segment_ids(key, part):
    length_key, pick_key = jax.random.split(jax.random.fold_in(key, 11), 2)
    sequences = TOKENS // LEN
    documents = LEN // DOC_MIN + 1
    lengths = jax.random.randint(length_key, (sequences, documents), DOC_MIN, DOC_MAX + 1)
    shortest = jax.random.randint(pick_key, (), 0, sequences)
    chosen = (jnp.arange(sequences, dtype=jnp.int32) == shortest)[:, None]
    lengths = jnp.where(chosen, jnp.int32(DOC_MIN), lengths)
    ends = jnp.cumsum(lengths, axis=1)
    positions = jnp.arange(LEN, dtype=jnp.int32)
    passed = (ends[:, :, None] <= positions[None, None, :]).astype(jnp.int32)
    return jnp.sum(passed, axis=1).reshape(TOKENS).astype(jnp.int32)


def block_levels(key, extent, cuts, low, largest):
    def one(dim, shards_of):
        steps = jax.random.uniform(jax.random.fold_in(jax.random.fold_in(key, 6), dim), (shards_of,), jnp.float32, low / len(cuts), largest / len(cuts))
        return jnp.repeat(jnp.exp(steps), extent[dim] // shards_of).reshape((-1,) + (1,) * (len(extent) - dim - 1))

    gain = one(*cuts[0])
    for cut in cuts[1:]:
        gain = gain * one(*cut)
    return gain


def scatter_about(rng, shape, deviation, most, shards=(), held_as=jnp.bfloat16):
    values = jax.random.normal(rng, shape, jnp.float32) * deviation
    if len(shards) > 0:
        values = block_levels(rng, shape, shards, -0.22, 0.18) * values
    return jnp.clip(values, min=-most, max=most).astype(held_as)


def setup_inputs(seed: int = 0) -> dict:
    streams_of = jax.random.split(jax.random.key(seed), 12)
    return {
        "tokens": draw_tokens(jax.random.fold_in(streams_of[11], 71), 0),
        "upstream": scatter_about(streams_of[1], (TOKENS, D), 1.0, 6.0, ((0, 32),)),
        "segment_ids": draw_segment_ids(jax.random.fold_in(streams_of[11], 71), 0),
        "query_proj": scatter_about(streams_of[3], (LAYERS, D, D), D ** -0.5, 0.1875, ((2, 4),)),
        "key_proj": scatter_about(streams_of[4], (LAYERS, D, D), D ** -0.5, 0.1875, ((2, 4),)),
        "value_proj": scatter_about(streams_of[5], (LAYERS, D, D), D ** -0.5, 0.1875, ((2, 4),)),
        "gate_proj": scatter_about(streams_of[6], (LAYERS, D, D), D ** -0.5, 0.1875, ((2, 4),)),
        "output_proj": scatter_about(streams_of[7], (LAYERS, D, D), D ** -0.5, 0.1875, ((1, 4),)),
        "left_proj": scatter_about(streams_of[8], (LAYERS, D, FF), D ** -0.5, 0.1875, ((2, 4),)),
        "right_proj": scatter_about(streams_of[9], (LAYERS, D, FF), D ** -0.5, 0.1875, ((2, 4),)),
        "down_proj": scatter_about(streams_of[10], (LAYERS, FF, D), FF ** -0.5, 0.109375, ((1, 4),)),
    }


epsilon = 1e-06
depth_start = 0.5
depth_step = 1.0 / 24.0
highest = lax.Precision.HIGHEST

@jax.custom_vjp
def low(v):
    return lax.optimization_barrier(v.astype(jnp.bfloat16)).astype(jnp.float32)

@jax.custom_vjp
def low_back(v):
    return v

def low_keep(v):
    return (low(v), None)

def low_pass(kept, grad):
    return (grad,)

def back_keep(v):
    return (v, None)

def back_low(kept, grad):
    return (low(grad),)
low.defvjp(low_keep, low_pass)
low_back.defvjp(back_keep, back_low)

def simple_rms(values):
    return values * lax.rsqrt(lax.optimization_barrier(jnp.mean(values * values, axis=-1, keepdims=True)) + epsilon)

def log_decay(layer_index):
    slopes = jnp.exp2(-8.0 * (jnp.arange(HEADS, dtype=jnp.float32) + 1.0) / HEADS)
    return -slopes * (1.0 - depth_start - depth_step * layer_index)

def rotate(values, cosine, sine_table):
    return jnp.concatenate([values * cosine[:, None, :], values * sine_table[:, None, :]], axis=2)

def block_attend(decay_log, state_now, block_items):
    query_block, key_block, value_block, seg_block, next_seg = block_items
    block_width = query_block.shape[0]
    places = jnp.arange(block_width, dtype=jnp.float32)
    distance = places[:, None] - places[None, :]
    allowed = (distance >= 0) & (seg_block[:, None] == seg_block[None, :])
    decay_grid = jnp.where(allowed[None], jnp.exp(decay_log[:, None, None] * jnp.maximum(distance, 0.0)[None]), 0.0)
    first_seg = seg_block[0]
    query_gain = jnp.where((seg_block == first_seg)[:, None], jnp.exp(places[:, None] * decay_log[None, :]), 0.0)
    key_gain = jnp.where((seg_block == next_seg)[:, None], jnp.exp((block_width - places)[:, None] * decay_log[None, :]), 0.0)
    carry_gain = jnp.where(first_seg == next_seg, jnp.exp(decay_log * block_width), 0.0)
    scores = jnp.einsum('rhd,shd->hrs', query_block, key_block, precision=highest) * decay_grid
    block_out = jnp.einsum('hrs,she->rhe', scores, value_block, precision=highest)
    block_out = block_out + jnp.einsum('rhd,hde->rhe', query_block, state_now, precision=highest) * query_gain[:, :, None]
    new_state = carry_gain[:, None, None] * state_now + jnp.einsum('shd,she->hde', key_block * key_gain[:, :, None], value_block, precision=highest)
    return (new_state, block_out)

def attend(queries, keys_rot, values, segments, decay_log):
    length = queries.shape[0]
    pair_width = queries.shape[2]
    block_count = length // BLK
    query_blocks = queries.reshape(block_count, BLK, HEADS, pair_width)
    key_blocks = keys_rot.reshape(block_count, BLK, HEADS, pair_width)
    value_blocks = values.reshape(block_count, BLK, HEADS, HDIM)
    seg_blocks = segments.reshape(block_count, BLK)
    next_segs = jnp.concatenate([seg_blocks[1:, 0], jnp.full((1,), -1, jnp.int32)])
    zero_state = jnp.zeros((HEADS, pair_width, HDIM), jnp.float32)
    step_fn = jax.checkpoint(partial(block_attend, decay_log))
    _, block_outs = lax.scan(step_fn, zero_state, (query_blocks, key_blocks, value_blocks, seg_blocks, next_segs))
    return block_outs.reshape(length, HEADS * HDIM)

def layer_forward(inputs, weights, segments, cosine, sine_table, layer_index):
    query_mat, key_mat, value_mat, gate_mat, output_mat, left_mat, right_mat, down_mat = weights
    length = inputs.shape[0]
    normed = low(simple_rms(inputs))
    query_lin = low_back(jnp.dot(normed, query_mat, precision=highest))
    key_lin = low_back(jnp.dot(normed, key_mat, precision=highest))
    value_lin = low(low_back(jnp.dot(normed, value_mat, precision=highest)))
    gate_lin = low_back(jnp.dot(normed, gate_mat, precision=highest))
    queries = low(rotate(jax.nn.silu(query_lin).reshape(length, HEADS, HDIM), cosine, sine_table))
    keys_rot = low(rotate(jax.nn.silu(key_lin).reshape(length, HEADS, HDIM), cosine, sine_table))
    heads_out = attend(queries, keys_rot, value_lin.reshape(length, HEADS, HDIM), segments, log_decay(layer_index))
    branch = low(simple_rms(heads_out) * gate_lin)
    attn_out = low_back(jnp.dot(branch, output_mat, precision=highest))
    middle = inputs + attn_out
    normed_mid = low(simple_rms(middle))
    left_lin = low_back(jnp.dot(normed_mid, left_mat, precision=highest))
    right_lin = low_back(jnp.dot(normed_mid, right_mat, precision=highest))
    hidden = low(left_lin * right_lin)
    glu_out = low_back(jnp.dot(hidden, down_mat, precision=highest))
    after = middle + glu_out
    return (after, jnp.stack([jnp.sum(attn_out * attn_out), jnp.sum(glu_out * glu_out), jnp.sum(after * after)]))

def reference(tokens, upstream, segment_ids, query_proj, key_proj, value_proj, gate_proj, output_proj, left_proj, right_proj, down_proj):
    weights = tuple((matrix.astype(jnp.float32) for matrix in (query_proj, key_proj, value_proj, gate_proj, output_proj, left_proj, right_proj, down_proj)))
    sequences = tokens.shape[0] // LEN
    sequence_rows = tokens.astype(jnp.float32).reshape(sequences, LEN, D)
    cotangent = upstream.astype(jnp.float32).reshape(sequences, LEN, D)
    segment_rows = segment_ids.reshape(sequences, LEN)
    positions = jnp.arange(LEN, dtype=jnp.float32)
    frequency = jnp.exp(-math.log(10000.0) * jnp.arange(HDIM, dtype=jnp.float32) / HDIM)
    angles = positions[:, None] * frequency[None, :]
    cosine = jnp.cos(angles)
    sine_table = jnp.sin(angles)

    def one_sequence(grad_sums, seq_items):
        inputs, seq_cotangent, segments = seq_items

        def forward(layer_input, layer_weights):
            stat_list = []
            current = layer_input
            for layer_index in range(LAYERS):
                chosen = tuple((matrix[layer_index] for matrix in layer_weights))
                current, stat_row = layer_forward(current, chosen, segments, cosine, sine_table, layer_index)
                stat_list.append(stat_row)
            return (current, jnp.stack(stat_list))
        result, pullback, stat_rows = jax.vjp(forward, inputs, weights, has_aux=True)
        input_cot, weight_cots = pullback(seq_cotangent)
        grad_sums = tuple((total + extra for total, extra in zip(grad_sums, weight_cots)))
        return (grad_sums, (result, input_cot, stat_rows))
    zero_grads = tuple((jnp.zeros_like(matrix) for matrix in weights))
    grad_sums, (results, input_cots, stat_rows) = lax.scan(one_sequence, zero_grads, (sequence_rows, cotangent, segment_rows))
    rms_stats = jnp.sqrt(lax.optimization_barrier(jnp.sum(stat_rows, axis=0)) / (TOKENS * D))
    return (results.reshape(TOKENS, D).astype(jnp.bfloat16), input_cots.reshape(TOKENS, D).astype(jnp.bfloat16), grad_sums[0], grad_sums[1], grad_sums[2], grad_sums[3], grad_sums[4], grad_sums[5], grad_sums[6], grad_sums[7], rms_stats)
```

```python
import functools
import math
import types

import jax
import jax.numpy as jnp
from jax import lax
from jax.experimental import pallas as pl
from jax.experimental.pallas import tpu as pltpu
from jax.sharding import PartitionSpec as P

HEADS = 8
HDIM = 128
BLK = 512


epsilon = 1e-06
depth_start = 0.5
depth_step = 1.0 / 24.0
highest = lax.Precision.HIGHEST


def rms_rows(values):
    return values * lax.rsqrt(jnp.mean(values * values, axis=1, keepdims=True) + epsilon)


def rms_back(values, gradient):
    scaling = lax.rsqrt(jnp.mean(values * values, axis=1, keepdims=True) + epsilon)
    normed = values * scaling
    return scaling * (gradient - normed * jnp.mean(gradient * normed, axis=1, keepdims=True))


def contract_last(left_part, right_part):
    return lax.dot_general(
        left_part, right_part, (((1,), (1,)), ((), ())), preferred_element_type=jnp.float32
    )


def contract_first(left_part, right_part):
    return lax.dot_general(
        left_part, right_part, (((0,), (0,)), ((), ())), preferred_element_type=jnp.float32
    )


def rotate(values, cosine, sine_table):
    return jnp.concatenate([values * cosine[:, None, :], values * sine_table[:, None, :]], axis=2)


def unrotate(gradient, cosine, sine_table):
    half_width = gradient.shape[2] // 2
    return (
        gradient[:, :, :half_width] * cosine[:, None, :]
        + gradient[:, :, half_width:] * sine_table[:, None, :]
    )


def split_blocks(array, block_count):
    return array.reshape((block_count, BLK) + array.shape[1:])


def block_weights(seg_block, next_seg, decay_log):
    block_width = seg_block.shape[0]
    places = jnp.arange(block_width, dtype=jnp.float32)
    distance = places[:, None] - places[None, :]
    allowed = (distance >= 0) & (seg_block[:, None] == seg_block[None, :])
    decay_grid = jnp.where(
        allowed[None], jnp.exp(decay_log[:, None, None] * jnp.maximum(distance, 0.0)[None]), 0.0
    )
    first_seg = seg_block[0]
    query_gain = jnp.where(
        (seg_block == first_seg)[:, None], jnp.exp(places[:, None] * decay_log[None, :]), 0.0
    )
    key_gain = jnp.where(
        (seg_block == next_seg)[:, None],
        jnp.exp((block_width - places)[:, None] * decay_log[None, :]),
        0.0,
    )
    carry_gain = jnp.where(first_seg == next_seg, jnp.exp(decay_log * block_width), 0.0)
    return (decay_grid, query_gain, key_gain, carry_gain)


def next_segments(segments, block_count):
    seg_blocks = segments.reshape(block_count, BLK)
    return (seg_blocks, jnp.concatenate([seg_blocks[1:, 0], jnp.full((1,), -1, jnp.int32)]))


def attend_forward(queries, keys_rot, values, segments, decay_log):
    length, heads_here, pair_width = queries.shape
    block_count = length // BLK
    seg_blocks, next_segs = next_segments(segments, block_count)

    def advance(state_now, block_items):
        query_block, key_block, value_block, seg_block, next_seg = block_items
        query_float = query_block.astype(jnp.float32)
        key_float = key_block.astype(jnp.float32)
        value_float = value_block.astype(jnp.float32)
        decay_grid, query_gain, key_gain, carry_gain = block_weights(seg_block, next_seg, decay_log)
        scores = (
            jnp.einsum("rhd,shd->hrs", query_block, key_block, preferred_element_type=jnp.float32)
            * decay_grid
        )
        block_out = jnp.einsum("hrs,she->rhe", scores, value_float, precision=highest)
        block_out = (
            block_out
            + jnp.einsum("rhd,hde->rhe", query_float, state_now, precision=highest)
            * query_gain[:, :, None]
        )
        new_state = carry_gain[:, None, None] * state_now + jnp.einsum(
            "shd,she->hde", key_float * key_gain[:, :, None], value_float, precision=highest
        )
        return (new_state, (block_out, state_now))

    zero_state = jnp.zeros((heads_here, pair_width, pair_width // 2), jnp.float32)
    _, (block_outs, states) = lax.scan(
        advance,
        zero_state,
        (
            split_blocks(queries, block_count),
            split_blocks(keys_rot, block_count),
            split_blocks(values, block_count),
            seg_blocks,
            next_segs,
        ),
    )
    return (block_outs.reshape(length, heads_here * (pair_width // 2)), states)


def attend_backward(queries, keys_rot, values, segments, decay_log, states, grad_heads):
    length, heads_here, pair_width = queries.shape
    block_count = length // BLK
    seg_blocks, next_segs = next_segments(segments, block_count)

    def retreat(later_grad, block_items):
        query_block, key_block, value_block, seg_block, next_seg, state_now, grad_block = (
            block_items
        )
        query_float = query_block.astype(jnp.float32)
        key_float = key_block.astype(jnp.float32)
        value_float = value_block.astype(jnp.float32)
        decay_grid, query_gain, key_gain, carry_gain = block_weights(seg_block, next_seg, decay_log)
        scores = (
            jnp.einsum("rhd,shd->hrs", query_block, key_block, preferred_element_type=jnp.float32)
            * decay_grid
        )
        pulled = jnp.einsum("rhe,she->hrs", grad_block, value_float, precision=highest) * decay_grid
        grad_query = jnp.einsum("hrs,shd->rhd", pulled, key_float, precision=highest)
        grad_query = (
            grad_query
            + jnp.einsum("rhe,hde->rhd", grad_block, state_now, precision=highest)
            * query_gain[:, :, None]
        )
        grad_key = jnp.einsum("hrs,rhd->shd", pulled, query_float, precision=highest)
        grad_key = (
            grad_key
            + jnp.einsum("she,hde->shd", value_float, later_grad, precision=highest)
            * key_gain[:, :, None]
        )
        grad_value = jnp.einsum("hrs,rhe->she", scores, grad_block, precision=highest)
        grad_value = (
            grad_value
            + jnp.einsum("shd,hde->she", key_float, later_grad, precision=highest)
            * key_gain[:, :, None]
        )
        earlier_grad = carry_gain[:, None, None] * later_grad + jnp.einsum(
            "rhd,rhe->hde", query_float * query_gain[:, :, None], grad_block, precision=highest
        )
        return (earlier_grad, (grad_query, grad_key, grad_value))

    zero_state = jnp.zeros((heads_here, pair_width, pair_width // 2), jnp.float32)
    _, (grad_query, grad_key, grad_value) = lax.scan(
        retreat,
        zero_state,
        (
            split_blocks(queries, block_count),
            split_blocks(keys_rot, block_count),
            split_blocks(values, block_count),
            seg_blocks,
            next_segs,
            states,
            split_blocks(grad_heads, block_count),
        ),
        reverse=True,
    )
    return (
        grad_query.reshape(length, heads_here, pair_width),
        grad_key.reshape(length, heads_here, pair_width),
        grad_value.reshape(length, heads_here, pair_width // 2),
    )


def per_device(
    tokens,
    upstream,
    segment_ids,
    query_proj,
    key_proj,
    value_proj,
    gate_proj,
    output_proj,
    left_proj,
    right_proj,
    down_proj,
):
    layers = query_proj.shape[0]
    row_count, model_width = tokens.shape
    length = segment_ids.shape[0]
    local_width = query_proj.shape[2]
    ff_local = left_proj.shape[2]
    heads_here = local_width // HDIM
    positions = jnp.arange(length, dtype=jnp.float32)
    frequency = jnp.exp(-math.log(10000.0) * jnp.arange(HDIM, dtype=jnp.float32) / HDIM)
    angles = positions[:, None] * frequency[None, :]
    cosine = jnp.cos(angles)
    sine_table = jnp.sin(angles)
    head_index = (lax.axis_index("tensor") * heads_here + jnp.arange(heads_here)).astype(
        jnp.float32
    )
    slopes = jnp.exp2(-8.0 * (head_index + 1.0) / HEADS)

    def gather_normed(normed):
        return lax.all_gather(normed, "tensor", axis=0, tiled=True)

    def gather_again(normed):
        return lax.all_gather(normed, "tensor", axis=0, tiled=True)

    def gather_grads(gradient):
        return lax.all_gather(gradient, "tensor", axis=0, tiled=True)

    def branch_sum(operand, matrix):
        return lax.psum_scatter(
            jnp.dot(operand, matrix, preferred_element_type=jnp.float32).astype(jnp.bfloat16),
            "tensor",
            scatter_dimension=0,
            tiled=True,
        ).astype(jnp.float32)

    def input_sum(pieces, matrix):
        operand = jnp.concatenate(pieces, axis=1)
        return lax.psum_scatter(
            contract_last(operand, matrix).astype(jnp.bfloat16),
            "tensor",
            scatter_dimension=0,
            tiled=True,
        ).astype(jnp.float32)

    current = tokens.astype(jnp.float32)
    saved_layers = []
    stat_terms = []
    for layer_index in range(layers):
        residual = current
        normed = rms_rows(residual).astype(jnp.bfloat16)
        full_normed = gather_normed(normed)
        attn_weight = jnp.concatenate(
            [
                query_proj[layer_index],
                key_proj[layer_index],
                value_proj[layer_index],
                gate_proj[layer_index],
            ],
            axis=1,
        )
        projected = jnp.dot(full_normed, attn_weight, preferred_element_type=jnp.float32)
        query_lin = projected[:, :local_width]
        key_lin = projected[:, local_width : 2 * local_width]
        values = (
            projected[:, 2 * local_width : 3 * local_width]
            .astype(jnp.bfloat16)
            .reshape(length, heads_here, HDIM)
        )
        gate_lin = projected[:, 3 * local_width :]
        queries = rotate(
            jax.nn.silu(query_lin).reshape(length, heads_here, HDIM), cosine, sine_table
        ).astype(jnp.bfloat16)
        keys_rot = rotate(
            jax.nn.silu(key_lin).reshape(length, heads_here, HDIM), cosine, sine_table
        ).astype(jnp.bfloat16)
        decay_log = -slopes * (1.0 - depth_start - depth_step * layer_index)
        heads_out, states = attend_forward(queries, keys_rot, values, segment_ids, decay_log)
        squares = lax.psum(jnp.sum(heads_out * heads_out, axis=1), "tensor")
        scaling = lax.rsqrt(squares / model_width + epsilon)[:, None]
        normed_heads = heads_out * scaling
        branch = (normed_heads * gate_lin).astype(jnp.bfloat16)
        attn_rows = branch_sum(branch, output_proj[layer_index])
        middle = residual + attn_rows
        normed_mid = rms_rows(middle).astype(jnp.bfloat16)
        full_mid = gather_normed(normed_mid)
        glu_weight = jnp.concatenate([left_proj[layer_index], right_proj[layer_index]], axis=1)
        gates_both = jnp.dot(full_mid, glu_weight, preferred_element_type=jnp.float32)
        left_lin = gates_both[:, :ff_local]
        right_lin = gates_both[:, ff_local:]
        hidden = (left_lin * right_lin).astype(jnp.bfloat16)
        glu_rows = branch_sum(hidden, down_proj[layer_index])
        current = middle + glu_rows
        stat_terms.append(
            jnp.stack(
                [
                    jnp.sum(attn_rows * attn_rows),
                    jnp.sum(glu_rows * glu_rows),
                    jnp.sum(current * current),
                ]
            )
        )
        saved_layers.append(
            (
                residual,
                middle,
                normed,
                normed_mid,
                full_normed,
                full_mid,
                attn_weight,
                glu_weight,
                query_lin,
                key_lin,
                gate_lin,
                queries,
                keys_rot,
                values,
                decay_log,
                states,
                normed_heads,
                scaling,
                branch,
                left_lin,
                right_lin,
                hidden,
            )
        )
    stat_sums = lax.psum(jnp.stack(stat_terms), ("dp", "tensor"))
    rms_stats = jnp.sqrt(stat_sums / (length * lax.axis_size("dp") * model_width))
    final_rows = current.astype(jnp.bfloat16)
    gradient = upstream.astype(jnp.float32)
    layer_results = [None] * layers
    for layer_index in reversed(range(layers)):
        (
            residual,
            middle,
            normed,
            normed_mid,
            full_normed,
            full_mid,
            attn_weight,
            glu_weight,
            query_lin,
            key_lin,
            gate_lin,
            queries,
            keys_rot,
            values,
            decay_log,
            states,
            normed_heads,
            scaling,
            branch,
            left_lin,
            right_lin,
            hidden,
        ) = saved_layers[layer_index]
        glu_grad = gather_grads(gradient.astype(jnp.bfloat16))
        grad_hidden = contract_last(glu_grad, down_proj[layer_index])
        down_part = contract_first(hidden, glu_grad)
        grad_left = (grad_hidden * right_lin).astype(jnp.bfloat16)
        grad_right = (grad_hidden * left_lin).astype(jnp.bfloat16)
        grad_gates = jnp.concatenate([grad_left, grad_right], axis=1)
        mid_rows = input_sum((grad_left, grad_right), glu_weight)
        source_mid = gather_again(normed_mid)
        glu_part = contract_first(source_mid, grad_gates)
        gradient = gradient + rms_back(middle, mid_rows)
        attn_grad = gather_grads(gradient.astype(jnp.bfloat16))
        output_part = contract_first(branch, attn_grad)
        grad_branch = contract_last(attn_grad, output_proj[layer_index])
        grad_normed = grad_branch * gate_lin
        grad_gate = (grad_branch * normed_heads).astype(jnp.bfloat16)
        inner_sum = lax.psum(jnp.sum(grad_normed * normed_heads, axis=1), "tensor")
        grad_heads = scaling * (grad_normed - normed_heads * (inner_sum / model_width)[:, None])
        grad_query, grad_key, grad_value = attend_backward(
            queries,
            keys_rot,
            values,
            segment_ids,
            decay_log,
            states,
            grad_heads.reshape(length, heads_here, HDIM),
        )
        sigmoid_query = jax.nn.sigmoid(query_lin)
        sigmoid_key = jax.nn.sigmoid(key_lin)
        query_back = unrotate(grad_query, cosine, sine_table).reshape(length, local_width)
        key_back = unrotate(grad_key, cosine, sine_table).reshape(length, local_width)
        grad_query_lin = (
            query_back * (sigmoid_query + query_lin * sigmoid_query * (1.0 - sigmoid_query))
        ).astype(jnp.bfloat16)
        grad_key_lin = (
            key_back * (sigmoid_key + key_lin * sigmoid_key * (1.0 - sigmoid_key))
        ).astype(jnp.bfloat16)
        grad_value_lin = grad_value.reshape(length, local_width).astype(jnp.bfloat16)
        grad_projected = jnp.concatenate(
            [grad_query_lin, grad_key_lin, grad_value_lin, grad_gate], axis=1
        )
        in_rows = input_sum((grad_query_lin, grad_key_lin, grad_value_lin, grad_gate), attn_weight)
        source_normed = gather_again(normed)
        attn_part = contract_first(source_normed, grad_projected)
        gradient = gradient + rms_back(residual, in_rows)
        query_part = attn_part[:, :local_width]
        key_part = attn_part[:, local_width : 2 * local_width]
        value_part = attn_part[:, 2 * local_width : 3 * local_width]
        gate_part = attn_part[:, 3 * local_width :]
        left_part = glu_part[:, :ff_local]
        right_part = glu_part[:, ff_local:]
        layer_results[layer_index] = (
            query_part,
            key_part,
            value_part,
            gate_part,
            output_part,
            left_part,
            right_part,
            down_part,
        )
    stacked = [
        jnp.stack([layer_results[index][member] for index in range(layers)]) for member in range(8)
    ]
    totals = (
        lax.psum(stacked[0].astype(jnp.bfloat16), "dp").astype(jnp.float32),
        lax.psum(stacked[1].astype(jnp.bfloat16), "dp").astype(jnp.float32),
        lax.psum(stacked[2].astype(jnp.bfloat16), "dp").astype(jnp.float32),
        lax.psum(stacked[3].astype(jnp.bfloat16), "dp").astype(jnp.float32),
        lax.psum(stacked[4].astype(jnp.bfloat16), "dp").astype(jnp.float32),
        lax.psum(stacked[5].astype(jnp.bfloat16), "dp").astype(jnp.float32),
        lax.psum(stacked[6].astype(jnp.bfloat16), "dp").astype(jnp.float32),
        lax.psum(stacked[7].astype(jnp.bfloat16), "dp").astype(jnp.float32),
    )
    input_grad = gradient.astype(jnp.bfloat16)
    return (
        final_rows,
        input_grad,
        totals[0],
        totals[1],
        totals[2],
        totals[3],
        totals[4],
        totals[5],
        totals[6],
        totals[7],
        rms_stats,
    )


SQUARE_MESH = {"dp": 8, "tensor": 4}


F32 = jnp.float32
BF16 = jnp.bfloat16
MESH = pl.DeviceIdType.MESH
VMEM_LIMIT = 60 * 2**20
SUPER = 2


def nn(a, b):
    return lax.dot_general(a, b, (((1,), (0,)), ((), ())), preferred_element_type=F32)


def nt(a, b):
    return lax.dot_general(a, b, (((1,), (1,)), ((), ())), preferred_element_type=F32)


def tn(a, b):
    return lax.dot_general(a, b, (((0,), (0,)), ((), ())), preferred_element_type=F32)


def exact(a, b, dims):
    return lax.dot_general(a, b, (dims, ((), ())), precision=highest, preferred_element_type=F32)


def aligned(index, size):
    return pl.ds(pl.multiple_of(index, size), size)


class Place:
    def __init__(self):
        self.dp = lax.axis_index("dp")
        self.me = lax.axis_index("tensor")
        self.low = lax.rem(self.me, 2)
        self.high = self.me // 2

    def member(self, step):
        low = lax.rem(self.low + lax.rem(step, 2), 2)
        high = lax.rem(self.high + step // 2, 2)
        return 2 * high + low

    def device(self, step):
        return (self.dp, self.member(step))

    def greet(self):
        barrier = pltpu.get_barrier_semaphore()
        for step in (1, 2, 3):
            pl.semaphore_signal(barrier, inc=1, device_id=self.device(step), device_id_type=MESH)
        pl.semaphore_wait(barrier, 3)


class Wire:
    def __init__(self, place, step, send_sem, recv_sem, source, target, landing):
        self.source, self.target, self.landing = source, target, landing
        self.common = dict(
            send_sem=send_sem, recv_sem=recv_sem, device_id=place.device(step), device_id_type=MESH
        )

    def out(self):
        return pltpu.make_async_remote_copy(src_ref=self.source, dst_ref=self.target, **self.common)

    def start(self):
        self.out().start()

    def wait_recv(self):
        pltpu.make_async_remote_copy(src_ref=self.landing, dst_ref=self.landing, **self.common).wait_recv()

    def wait_send(self):
        self.out().wait_send()


class Gather:
    def __init__(self, place, buf, send, recv, block):
        self.place, self.buf, self.block = place, buf, block
        self.send, self.recv = send, recv
        self.half = block // (2 * SUPER)

    def rows(self, step, part, half):
        start = self.place.member(step) * self.block + (2 * part + half) * self.half
        return self.buf.at[aligned(start, self.half)]

    def wire(self, part, number):
        step, owner, half = ((1, 0, 0), (2, 0, 1), (1, 0, 1), (2, 0, 0), (2, 1, 0), (1, 2, 1))[number]
        source = self.rows(owner, part, half)
        landing = self.rows((0, 1, 2, 3)[owner ^ step], part, half)
        return Wire(self.place, step, self.send.at[part, number], self.recv.at[part, number], source, source, landing)

    def start(self, part):
        for number in range(4):
            self.wire(part, number).start()

    def forward(self, part):
        self.wire(part, 0).wait_recv()
        self.wire(part, 4).start()
        self.wire(part, 1).wait_recv()
        self.wire(part, 5).start()

    def finish(self, part, step):
        for number in {0: (), 1: (2,), 2: (3,), 3: (4, 5)}[step]:
            self.wire(part, number).wait_recv()

    def drain(self):
        for part in range(SUPER):
            for number in range(6):
                self.wire(part, number).wait_send()


class Scatter:
    def __init__(self, place, buf, land, send, recv, block):
        self.place, self.buf, self.land, self.block = place, buf, land, block
        self.send, self.recv = send, recv
        self.half = block // (2 * SUPER)

    def rows(self, step, part, half):
        start = self.place.member(step) * self.block + (2 * part + half) * self.half
        return aligned(start, self.half)

    def wire(self, part, number):
        step, owner, half = ((1, 3, 0), (1, 1, 0), (2, 3, 1), (2, 2, 1), (2, 2, 0), (1, 1, 1))[number]
        target = self.land.at[part, number]
        return Wire(
            self.place, step, self.send.at[part, number], self.recv.at[part, number],
            self.buf.at[self.rows(owner, part, half)], target, target,
        )

    def send_block(self, part, step):
        for number in {0: (), 1: (1,), 2: (3,), 3: (0, 2)}[step]:
            self.wire(part, number).start()

    def middle(self, part):
        for first, second, owner, half in ((0, 4, 2, 0), (2, 5, 1, 1)):
            self.wire(part, first).wait_recv()
            rows = self.rows(owner, part, half)
            self.buf[rows, :] = (
                self.buf[rows, :].astype(F32) + self.land[part, first].astype(F32)
            ).astype(BF16)
            self.wire(part, second).start()

    def finish(self, part, half):
        first, second = ((1, 4), (3, 5))[half]
        self.wire(part, first).wait_recv()
        self.wire(part, second).wait_recv()

    def total(self, part, half, start, count):
        first, second = ((1, 4), (3, 5))[half]
        own = self.place.me * self.block + (2 * part + half) * self.half + start
        rows = pl.ds(start, count)
        return (
            self.buf[aligned(own, count), :].astype(F32)
            + self.land[part, first, rows, :].astype(F32)
            + self.land[part, second, rows, :].astype(F32)
        )

    def drain(self):
        for part in range(SUPER):
            for number in range(6):
                self.wire(part, number).wait_send()


class Share:
    def __init__(self, place, mine, land, send, recv):
        self.wires = [
            Wire(place, step, send.at[step - 1], recv.at[step - 1], mine, land.at[step - 1], land.at[step - 1])
            for step in (1, 2, 3)
        ]
        self.mine, self.land = mine, land

    def start(self):
        for wire in self.wires:
            wire.start()

    def total(self):
        for wire in self.wires:
            wire.wait_recv()
        return self.mine[...] + self.land[0] + self.land[1] + self.land[2]

    def drain(self):
        for wire in self.wires:
            wire.wait_send()


class Local:
    def __init__(self, sems):
        self.sems, self.used = sems, 0

    def start(self, source, target):
        copy = pltpu.make_async_copy(source, target, self.sems.at[self.used])
        self.used += 1
        copy.start()
        return copy


def row_sums(values, target, chunk):
    sums = exact(jnp.ones((8, values.shape[1]), F32), values, ((1,), (1,)))
    target[pl.ds(chunk, 1), :] = sums[0:1, :]


def spread(sums, chunk):
    picked = (lax.broadcasted_iota(jnp.int32, (8, 128), 0) == chunk).astype(F32)
    return exact(sums, picked, ((0,), (0,)))


def widen(columns, times):
    return jnp.concatenate([columns] * times, axis=1)


def decay_tiles(dec_ref, tiles, heads_here, size):
    rows = lax.broadcasted_iota(jnp.int32, (size, size), 0)
    cols = lax.broadcasted_iota(jnp.int32, (size, size), 1)
    distance = (rows - cols).astype(F32)
    for head in range(heads_here):
        decay = dec_ref[head : head + 1, 0:1]
        tiles[head, 0] = jnp.where(rows >= cols, jnp.exp(decay * jnp.maximum(distance, 0.0)), 0.0)
        tiles[head, 1] = jnp.exp(decay * (distance + float(size)))


def tile_weight(dec_ref, tiles, segc_ref, segr_ref, head, row_tile, col_tile, size):
    gap = row_tile - col_tile
    if gap == 0:
        weight = tiles[head, 0]
    else:
        weight = tiles[head, 1]
        if gap > 1:
            weight = weight * jnp.exp(dec_ref[pl.ds(head, 1), 0:1] * float(size * (gap - 1)))
    row_seg = widen(segc_ref[row_tile * size : (row_tile + 1) * size, :], size // 128)
    col_seg = segr_ref[0:1, col_tile * size : (col_tile + 1) * size]
    return jnp.where(row_seg == col_seg, weight, 0.0)


def namespace(names, refs):
    return types.SimpleNamespace(**dict(zip(names, refs)))


def fwd_kernel(cfg, names, *refs):
    r = namespace(names, refs)
    layer, block, length, width, local = cfg.layer, cfg.block, cfg.length, cfg.width, cfg.local
    heads_here, size = cfg.heads_here, cfg.block
    place = Place()
    copies = Local(r.local_sem)
    w_in = [copies.start(h.at[layer], v) for h, v in (
        (r.wq_h, r.wq), (r.wk_h, r.wk), (r.wv_h, r.wv), (r.wg_h, r.wg))]
    w_out = copies.start(r.wo_h.at[layer], r.wo)
    w_glu = [copies.start(h.at[layer], v) for h, v in ((r.wl_h, r.wl), (r.wr_h, r.wr), (r.wd_h, r.wd))]
    saves = []
    first = Gather(place, r.n1, r.ag1_send, r.ag1_recv, block)
    mid_sum = Scatter(place, r.part1, r.land1, r.rs1_send, r.rs1_recv, block)
    second = Gather(place, r.n2, r.ag2_send, r.ag2_recv, block)
    out_sum = Scatter(place, r.part2, r.land2, r.rs2_send, r.rs2_recv, block)
    share = Share(place, r.ss, r.ss_land, r.ss_send, r.ss_recv)
    half, step_rows = first.half, 32
    own_start = place.me * block

    @pl.loop(0, block // step_rows)
    def _(i):
        rows = aligned(i * step_rows, step_rows)
        v = r.x[rows, :]
        scale = lax.rsqrt(jnp.mean(v * v, axis=1, keepdims=True) + epsilon)
        r.n1[aligned(own_start + i * step_rows, step_rows), :] = (v * scale).astype(BF16)

    place.greet()
    for part in range(SUPER):
        first.start(part)
    decay_tiles(r.dec, r.tiles, heads_here, size)
    for copy in w_in:
        copy.wait()

    @pl.loop(0, 4)
    def _(step):
        @pl.when(step == 1)
        def _():
            for part in range(SUPER):
                first.forward(part)
        for which in (1, 2, 3):
            @pl.when(step == which)
            def _():
                for part in range(SUPER):
                    first.finish(part, which)
        rows = aligned(place.member(step) * block, block)
        a = r.n1[rows, :]
        cosine, sine = r.cos[rows, :], r.sin[rows, :]
        for w, lin, rot in ((r.wq, r.ql, r.q), (r.wk, r.kl, r.k)):
            v = nn(a, w[...])
            lin[rows, :] = v.astype(BF16)
            v = v / (1.0 + jnp.exp(-v))
            for head in range(heads_here):
                one = v[:, head * HDIM : (head + 1) * HDIM]
                rot[rows, 2 * head * HDIM : (2 * head + 1) * HDIM] = (one * cosine).astype(BF16)
                rot[rows, (2 * head + 1) * HDIM : (2 * head + 2) * HDIM] = (one * sine).astype(BF16)
        r.v[rows, :] = nn(a, r.wv[...]).astype(BF16)
        r.gate[rows, :] = nn(a, r.wg[...])

    for v, h in ((r.n1, r.n1_h), (r.ql, r.ql_h), (r.kl, r.kl_h), (r.q, r.q_h), (r.k, r.k_h), (r.v, r.v_h), (r.gate, r.gate_h)):
        saves.append(copies.start(v, h))

    tiles_here = length // size

    @pl.loop(0, heads_here)
    def _(head):
        wide = aligned(head * 2 * HDIM, 2 * HDIM)
        thin = aligned(head * HDIM, HDIM)
        for row_tile in range(tiles_here):
            rows = slice(row_tile * size, (row_tile + 1) * size)
            queries = r.q[rows, wide]
            acc = None
            for col_tile in range(row_tile + 1):
                cols = slice(col_tile * size, (col_tile + 1) * size)
                weight = tile_weight(r.dec, r.tiles, r.segc, r.segr, head, row_tile, col_tile, size)
                scores = (nt(queries, r.k[cols, wide]) * weight).astype(BF16)
                term = nn(scores, r.v[cols, thin])
                acc = term if acc is None else acc + term
            r.heads[rows, thin] = acc
            r.u[rows, thin] = (acc * r.gate[rows, thin]).astype(BF16)

    for chunk in range(length // 128):
        v = r.heads[chunk * 128 : (chunk + 1) * 128, :]
        row_sums(v * v, r.ss, chunk)
    share.start()
    saves.append(copies.start(r.heads, r.heads_h))
    w_out.wait()

    part_rows = 2 * half
    for part in range(SUPER):
        for step in (3, 1, 2, 0):
            rows = aligned(place.member(step) * block + part * part_rows, part_rows)
            r.part1[rows, :] = nn(r.u[rows, :], r.wo[...]).astype(BF16)
            mid_sum.send_block(part, step)
    for part in range(SUPER):
        mid_sum.middle(part)
    r.sstot[...] = share.total()
    saves.append(copies.start(r.sstot, r.ss_h))
    scaling = lax.rsqrt(r.sstot[...] / width + epsilon)
    per_block = block // 128
    for chunk in range(per_block):
        r.scale[chunk * 128 : (chunk + 1) * 128, :] = spread(scaling, place.me * per_block + chunk)
    r.stat[...] = jnp.zeros_like(r.stat)

    def add_stat(row, v):
        sums = jnp.sum(v * v, axis=0, keepdims=True)
        r.stat[row : row + 1, :] += sums

    step_rows = min(32, half)
    for part in range(SUPER):
        for h in range(2):
            mid_sum.finish(part, h)
            for i in range(half // step_rows):
                offset = (2 * part + h) * half + i * step_rows
                scale = widen(r.scale[offset : offset + step_rows, :], width // 128)
                attn = mid_sum.total(part, h, i * step_rows, step_rows) * scale
                middle = r.x[offset : offset + step_rows, :] + attn
                r.mid[offset : offset + step_rows, :] = middle
                add_stat(0, attn)
                norm = lax.rsqrt(jnp.mean(middle * middle, axis=1, keepdims=True) + epsilon)
                r.n2[aligned(own_start + offset, step_rows), :] = (middle * norm).astype(BF16)
        second.start(part)
    saves.append(copies.start(r.mid, r.mid_h))
    for copy in w_glu:
        copy.wait()
    for part in range(SUPER):

        def glu(step):
            rows = aligned(place.member(step) * block + part * part_rows, part_rows)
            a = r.n2[rows, :]
            left = nn(a, r.wl[...])
            right = nn(a, r.wr[...])
            hidden = (left * right).astype(BF16)
            r.left[rows, :] = left.astype(BF16)
            r.right[rows, :] = right.astype(BF16)
            r.hid[rows, :] = hidden
            r.part2[rows, :] = nn(hidden, r.wd[...]).astype(BF16)

        @pl.loop(0, 4)
        def _(step):
            if part == 0:
                @pl.when(step == 1)
                def _():
                    for other in range(SUPER):
                        second.forward(other)
            for which in (1, 2, 3):
                @pl.when(step == which)
                def _():
                    second.finish(part, which)
            glu(step)
            for which in (1, 2, 3):
                @pl.when(step == which)
                def _():
                    out_sum.send_block(part, which)
    for v, h in ((r.n2, r.n2_h), (r.left, r.left_h), (r.right, r.right_h), (r.hid, r.hid_h)):
        saves.append(copies.start(v, h))
    for part in range(SUPER):
        out_sum.middle(part)
    for part in range(SUPER):
        for h in range(2):
            out_sum.finish(part, h)
            for i in range(half // step_rows):
                offset = (2 * part + h) * half + i * step_rows
                glu_rows = out_sum.total(part, h, i * step_rows, step_rows)
                after = r.mid[offset : offset + step_rows, :] + glu_rows
                r.xo[offset : offset + step_rows, :] = after
                add_stat(1, glu_rows)
                add_stat(2, after)
    for copy in saves:
        copy.wait()
    for group in (first, mid_sum, second, out_sum, share):
        group.drain()


def bwd_kernel(cfg, names, *refs):
    r = namespace(names, refs)
    layer, block, length, width, local = cfg.layer, cfg.block, cfg.length, cfg.width, cfg.local
    heads_here, size = cfg.heads_here, cfg.block
    place = Place()
    copies = Local(r.local_sem)
    load_glu = [copies.start(s, v) for s, v in (
        (r.wd_h.at[layer], r.wd), (r.left_h, r.left), (r.right_h, r.right),
        (r.wl_h.at[layer], r.wl), (r.wr_h.at[layer], r.wr))]
    load_glu_grad = [copies.start(r.hid_h, r.hid), copies.start(r.n2_h, r.n2)]
    load_out = [copies.start(s, v) for s, v in (
        (r.ss_h, r.sstot), (r.wo_h.at[layer], r.wo), (r.gate_h, r.gate), (r.heads_h, r.heads))]
    load_attn = [copies.start(s, v) for s, v in (
        (r.q_h, r.q), (r.k_h, r.k), (r.v_h, r.v), (r.ql_h, r.ql), (r.kl_h, r.kl))]
    load_in = [copies.start(s, v) for s, v in (
        (r.wq_h.at[layer], r.wq), (r.wk_h.at[layer], r.wk), (r.wv_h.at[layer], r.wv),
        (r.wg_h.at[layer], r.wg))]
    load_in_grad = [copies.start(r.n1_h, r.n1)]
    saves = []
    first = Gather(place, r.gd, r.ag1_send, r.ag1_recv, block)
    mid_sum = Scatter(place, r.part1, r.land1, r.rs1_send, r.rs1_recv, block)
    second = Gather(place, r.ga, r.ag2_send, r.ag2_recv, block)
    in_sum = Scatter(place, r.part2, r.land2, r.rs2_send, r.rs2_recv, block)
    share = Share(place, r.inner, r.inner_land, r.in_send, r.in_recv)
    half = first.half
    part_rows = 2 * half
    own_start = place.me * block
    step_rows = min(32, half)

    @pl.loop(0, block // 32)
    def _(i):
        rows = aligned(i * 32, 32)
        r.gd[aligned(own_start + i * 32, 32), :] = r.g[rows, :].astype(BF16)

    place.greet()
    for part in range(SUPER):
        first.start(part)
    decay_tiles(r.dec, r.tiles, heads_here, size)
    for copy in load_glu:
        copy.wait()
    for copy in load_out:
        copy.wait()
    scaling = lax.rsqrt(r.sstot[...] / width + epsilon)
    for chunk in range(length // 128):
        r.scale[chunk * 128 : (chunk + 1) * 128, :] = spread(scaling, chunk)

    for part in range(SUPER):
        @pl.loop(0, 4)
        def _(step):
            if part == 0:
                @pl.when(step == 1)
                def _():
                    for other in range(SUPER):
                        first.forward(other)
            for which in (1, 2, 3):
                @pl.when(step == which)
                def _():
                    first.finish(part, which)
            rows = aligned(place.member(step) * block + part * part_rows, part_rows)
            grad_hidden = nt(r.gd[rows, :], r.wd[...])
            grad_left = (grad_hidden * r.right[rows, :].astype(F32)).astype(BF16)
            grad_right = (grad_hidden * r.left[rows, :].astype(F32)).astype(BF16)
            r.dl[rows, :] = grad_left
            r.dr[rows, :] = grad_right
            r.part1[rows, :] = (nt(grad_left, r.wl[...]) + nt(grad_right, r.wr[...])).astype(BF16)
            for which in (1, 2, 3):
                @pl.when(step == which)
                def _():
                    mid_sum.send_block(part, which)

    for copy in load_glu_grad:
        copy.wait()
    for n in range(width // 256):
        cols = slice(n * 256, (n + 1) * 256)
        r.down_g[:, cols] = tn(r.hid[...], r.gd[:, cols]).astype(BF16)
    saves.append(copies.start(r.down_g, r.down_o))
    for part in range(SUPER):
        mid_sum.middle(part)
    for n in range(width // 256):
        cols = slice(n * 256, (n + 1) * 256)
        r.left_g[cols, :] = tn(r.n2[:, cols], r.dl[...]).astype(BF16)
    saves.append(copies.start(r.left_g, r.left_o))

    def back_rows(total, values_ref, grad_ref, offset):
        values = values_ref[offset : offset + step_rows, :]
        norm = lax.rsqrt(jnp.mean(values * values, axis=1, keepdims=True) + epsilon)
        m = values * norm
        inner = jnp.mean(total * m, axis=1, keepdims=True)
        return grad_ref[offset : offset + step_rows, :] + norm * (total - m * inner)

    for part in range(SUPER):
        for h in range(2):
            mid_sum.finish(part, h)
            for i in range(half // step_rows):
                offset = (2 * part + h) * half + i * step_rows
                total = mid_sum.total(part, h, i * step_rows, step_rows)
                new = back_rows(total, r.mid, r.g, offset)
                r.gm[offset : offset + step_rows, :] = new
                r.ga[aligned(own_start + offset, step_rows), :] = new.astype(BF16)
        second.start(part)
    for n in range(width // 256):
        cols = slice(n * 256, (n + 1) * 256)
        r.right_g[cols, :] = tn(r.n2[:, cols], r.dr[...]).astype(BF16)
    saves.append(copies.start(r.right_g, r.right_o))

    per_block = block // 128

    @pl.loop(0, 4)
    def _(step):
        @pl.when(step == 1)
        def _():
            for part in range(SUPER):
                second.forward(part)
        for which in (1, 2, 3):
            @pl.when(step == which)
            def _():
                for part in range(SUPER):
                    second.finish(part, which)
        member = place.member(step)
        for chunk in range(per_block):
            rows = aligned(member * block + chunk * 128, 128)
            grad_branch = nt(r.ga[rows, :], r.wo[...])
            gate = r.gate[rows, :]
            normed = r.heads[rows, :] * widen(r.scale[rows, :], local // 128)
            grad_normed = grad_branch * gate
            r.gn[rows, :] = grad_normed
            r.dx[rows, 3 * local : 4 * local] = (grad_branch * normed).astype(BF16)
            r.branch[rows, :] = (normed * gate).astype(BF16)
            row_sums(grad_normed * normed, r.inner, member * per_block + chunk)
    share.start()
    r.out_g[...] = tn(r.branch[...], r.ga[...]).astype(BF16)
    saves.append(copies.start(r.out_g, r.out_o))
    for copy in load_attn:
        copy.wait()
    r.intot[...] = share.total() / width
    for chunk in range(length // 128):
        rows = slice(chunk * 128, (chunk + 1) * 128)
        scale = widen(r.scale[rows, :], local // 128)
        inner = widen(spread(r.intot[...], chunk), local // 128)
        normed = r.heads[rows, :] * scale
        r.dh[rows, :] = (scale * (r.gn[rows, :] - normed * inner)).astype(BF16)

    tiles_here = length // size

    @pl.loop(0, heads_here)
    def _(head):
        wide = aligned(head * 2 * HDIM, 2 * HDIM)
        thin = aligned(head * HDIM, HDIM)
        for col_tile in range(tiles_here):
            cols = slice(col_tile * size, (col_tile + 1) * size)
            keys = r.k[cols, wide]
            values = r.v[cols, thin]
            acc_key, acc_value = None, None
            for row_tile in range(col_tile, tiles_here):
                rows = slice(row_tile * size, (row_tile + 1) * size)
                queries = r.q[rows, wide]
                grads = r.dh[rows, thin]
                weight = tile_weight(r.dec, r.tiles, r.segc, r.segr, head, row_tile, col_tile, size)
                scores = (nt(queries, keys) * weight).astype(BF16)
                pulled = (nt(grads, values) * weight).astype(BF16)
                term = nn(pulled, keys)
                if col_tile == 0:
                    r.dq[rows, :] = term
                else:
                    r.dq[rows, :] += term
                key_term = tn(pulled, queries)
                value_term = tn(scores, grads)
                acc_key = key_term if acc_key is None else acc_key + key_term
                acc_value = value_term if acc_value is None else acc_value + value_term
            r.dk[cols, :] = acc_key
            r.dx[cols, aligned(2 * local + head * HDIM, HDIM)] = acc_value.astype(BF16)
        for row_tile in range(tiles_here):
            rows = slice(row_tile * size, (row_tile + 1) * size)
            cosine, sine = r.cos[rows, :], r.sin[rows, :]
            for grad, lin, base in ((r.dq, r.ql, 0), (r.dk, r.kl, local)):
                v = lin[rows, thin].astype(F32)
                gate = 1.0 / (1.0 + jnp.exp(-v))
                back = grad[rows, :HDIM] * cosine + grad[rows, HDIM:] * sine
                back = back * (gate + v * gate * (1.0 - gate))
                r.dx[rows, aligned(base + head * HDIM, HDIM)] = back.astype(BF16)

    for copy in load_in:
        copy.wait()
    weights = (r.wq, r.wk, r.wv, r.wg)
    for part in range(SUPER):
        for step in (3, 1, 2, 0):
            rows = aligned(place.member(step) * block + part * part_rows, part_rows)
            total = None
            for n, w in enumerate(weights):
                term = nt(r.dx[rows, n * local : (n + 1) * local], w[...])
                total = term if total is None else total + term
            r.part2[rows, :] = total.astype(BF16)
            in_sum.send_block(part, step)
    for copy in load_in_grad:
        copy.wait()

    def attn_grad(n):
        cols = slice(n * local, (n + 1) * local)
        r.attn_g[n] = tn(r.n1[...], r.dx[:, cols]).astype(BF16)
        saves.append(copies.start(r.attn_g.at[n], r.attn_o.at[n]))

    attn_grad(0)
    attn_grad(1)
    for part in range(SUPER):
        in_sum.middle(part)
    attn_grad(2)
    attn_grad(3)
    for part in range(SUPER):
        for h in range(2):
            in_sum.finish(part, h)
            for i in range(half // step_rows):
                offset = (2 * part + h) * half + i * step_rows
                total = in_sum.total(part, h, i * step_rows, step_rows)
                r.go[offset : offset + step_rows, :] = back_rows(total, r.x, r.gm, offset)
    for copy in saves:
        copy.wait()
    for group in (first, mid_sum, second, in_sum, share):
        group.drain()


def call_kernel(body, cfg, inputs, outputs, scratch, collective_id, name):
    vmem, anywhere = pl.BlockSpec(memory_space=pltpu.VMEM), pl.BlockSpec(memory_space=pl.ANY)
    names = list(inputs) + list(outputs) + list(scratch)
    result = pl.pallas_call(
        functools.partial(body, cfg, names),
        out_shape=[shape for shape, _ in outputs.values()],
        in_specs=[vmem if placed else anywhere for _, placed in inputs.values()],
        out_specs=[vmem if placed else anywhere for _, placed in outputs.values()],
        scratch_shapes=list(scratch.values()),
        compiler_params=pltpu.CompilerParams(
            collective_id=collective_id, has_side_effects=True, vmem_limit_bytes=VMEM_LIMIT
        ),
        name=name,
    )(*[array for array, _ in inputs.values()])
    return dict(zip(outputs, result))


def collective_scratch(cfg):
    dma = pltpu.SemaphoreType.DMA
    half = cfg.block // (2 * SUPER)
    out = {}
    for name in ("ag1", "ag2", "rs1", "rs2"):
        out[name + "_send"] = dma((SUPER, 6))
        out[name + "_recv"] = dma((SUPER, 6))
    out["land1"] = pltpu.VMEM((SUPER, 6, half, cfg.width), BF16)
    out["land2"] = pltpu.VMEM((SUPER, 6, half, cfg.width), BF16)
    out["part1"] = pltpu.VMEM((cfg.length, cfg.width), BF16)
    out["part2"] = pltpu.VMEM((cfg.length, cfg.width), BF16)
    out["local_sem"] = dma((40,))
    return out


def weight_scratch(cfg):
    v = pltpu.VMEM
    return {
        "wq": v((cfg.width, cfg.local), BF16), "wk": v((cfg.width, cfg.local), BF16),
        "wv": v((cfg.width, cfg.local), BF16), "wg": v((cfg.width, cfg.local), BF16),
        "wo": v((cfg.local, cfg.width), BF16), "wl": v((cfg.width, cfg.ff), BF16),
        "wr": v((cfg.width, cfg.ff), BF16), "wd": v((cfg.ff, cfg.width), BF16),
    }


def run_forward(cfg, x, tables, weights):
    v, dma, s = pltpu.VMEM, pltpu.SemaphoreType.DMA, jax.ShapeDtypeStruct
    rows, wide, local, ff, block = cfg.length, cfg.width, cfg.local, cfg.ff, cfg.block
    inputs = {"x": (x, True), **{k: (a, True) for k, a in tables.items()}, **{k + "_h": (a, False) for k, a in weights.items()}}
    kept = {
        "n1": ((rows, wide), BF16), "ql": ((rows, local), BF16), "kl": ((rows, local), BF16),
        "q": ((rows, 2 * local), BF16), "k": ((rows, 2 * local), BF16), "v": ((rows, local), BF16),
        "gate": ((rows, local), F32), "heads": ((rows, local), F32), "mid": ((block, wide), F32),
        "n2": ((rows, wide), BF16), "left": ((rows, ff), BF16), "right": ((rows, ff), BF16), "hid": ((rows, ff), BF16),
    }
    outputs = {
        "xo": (s((block, wide), F32), True), "stat": (s((8, wide), F32), True), "ss_h": (s((8, 128), F32), False),
        **{k + "_h": (s(*a), False) for k, a in kept.items()},
    }
    scratch = {
        **weight_scratch(cfg), **collective_scratch(cfg), **{k: v(*a) for k, a in kept.items()},
        "tiles": v((cfg.heads_here, 2, block, block), F32), "u": v((rows, local), BF16),
        "ss": v((8, 128), F32), "sstot": v((8, 128), F32), "scale": v((block, 128), F32),
        "ss_land": v((3, 8, 128), F32), "ss_send": dma((3,)), "ss_recv": dma((3,)),
    }
    return call_kernel(fwd_kernel, cfg, inputs, outputs, scratch, 2 * cfg.layer, "layer_forward")


def run_backward(cfg, g, x, saved, tables, weights):
    v, dma, s = pltpu.VMEM, pltpu.SemaphoreType.DMA, jax.ShapeDtypeStruct
    rows, wide, local, ff, block = cfg.length, cfg.width, cfg.local, cfg.ff, cfg.block
    inputs = {
        "g": (g, True), "x": (x, True), "mid": (saved["mid_h"], True),
        **{k: (a, True) for k, a in tables.items()}, **{k + "_h": (a, False) for k, a in weights.items()},
        **{k: (saved[k], False) for k in ("ss_h", "n1_h", "ql_h", "kl_h", "q_h", "k_h", "v_h", "gate_h", "heads_h", "n2_h", "left_h", "right_h", "hid_h")},
    }
    outputs = {
        "go": (s((block, wide), F32), True), "attn_o": (s((4, wide, local), BF16), False),
        "out_o": (s((local, wide), BF16), False), "left_o": (s((wide, ff), BF16), False),
        "right_o": (s((wide, ff), BF16), False), "down_o": (s((ff, wide), BF16), False),
    }
    scratch = {
        **weight_scratch(cfg), **collective_scratch(cfg),
        "n1": v((rows, wide), BF16), "ql": v((rows, local), BF16), "kl": v((rows, local), BF16),
        "q": v((rows, 2 * local), BF16), "k": v((rows, 2 * local), BF16), "v": v((rows, local), BF16),
        "gate": v((rows, local), F32), "heads": v((rows, local), F32), "n2": v((rows, wide), BF16),
        "left": v((rows, ff), BF16), "right": v((rows, ff), BF16), "hid": v((rows, ff), BF16),
        "gd": v((rows, wide), BF16), "ga": v((rows, wide), BF16), "gm": v((block, wide), F32),
        "dl": v((rows, ff), BF16), "dr": v((rows, ff), BF16), "gn": v((rows, local), F32),
        "dh": v((rows, local), BF16), "branch": v((rows, local), BF16), "dx": v((rows, 4 * local), BF16),
        "dq": v((rows, 2 * HDIM), F32), "dk": v((rows, 2 * HDIM), F32),
        "attn_g": v((4, wide, local), BF16), "out_g": v((local, wide), BF16), "left_g": v((wide, ff), BF16),
        "right_g": v((wide, ff), BF16), "down_g": v((ff, wide), BF16),
        "tiles": v((cfg.heads_here, 2, block, block), F32), "scale": v((rows, 128), F32),
        "sstot": v((8, 128), F32), "inner": v((8, 128), F32), "intot": v((8, 128), F32),
        "inner_land": v((3, 8, 128), F32), "in_send": dma((3,)), "in_recv": dma((3,)),
    }
    return call_kernel(bwd_kernel, cfg, inputs, outputs, scratch, 2 * cfg.layer + 1, "layer_backward")


def per_device_square(
    tokens, upstream, segment_ids, query_proj, key_proj, value_proj, gate_proj, output_proj, left_proj, right_proj, down_proj
):
    layers = query_proj.shape[0]
    block, width = tokens.shape
    length = segment_ids.shape[0]
    local, ff = query_proj.shape[2], left_proj.shape[2]
    heads_here = local // HDIM
    positions = jnp.arange(length, dtype=F32)
    frequency = jnp.exp(-math.log(10000.0) * jnp.arange(HDIM, dtype=F32) / HDIM)
    angles = positions[:, None] * frequency[None, :]
    head_index = (lax.axis_index("tensor") * heads_here + jnp.arange(heads_here)).astype(F32)
    slopes = jnp.exp2(-8.0 * (head_index + 1.0) / HEADS)
    fixed = {
        "cos": jnp.cos(angles), "sin": jnp.sin(angles),
        "segc": jnp.broadcast_to(segment_ids[:, None], (length, 128)),
        "segr": jnp.broadcast_to(segment_ids[None, :], (8, length)),
    }
    weights = {
        "wq": query_proj, "wk": key_proj, "wv": value_proj, "wg": gate_proj,
        "wo": output_proj, "wl": left_proj, "wr": right_proj, "wd": down_proj,
    }
    current = tokens.astype(F32)
    runs = []
    for layer in range(layers):
        cfg = types.SimpleNamespace(
            layer=layer, block=block, length=length, width=width, local=local, ff=ff, heads_here=heads_here
        )
        decay = -slopes * (1.0 - depth_start - depth_step * layer)
        decay = jnp.concatenate([decay, jnp.zeros((8 - heads_here,), F32)])
        tables = {**fixed, "dec": jnp.broadcast_to(decay[:, None], (8, 128))}
        saved = run_forward(cfg, current, tables, weights)
        runs.append((cfg, current, tables, saved))
        current = saved["xo"]
    stats = jnp.stack([jnp.sum(run[3]["stat"][:3], axis=1) for run in runs])
    stat_sums = lax.psum(stats, ("dp", "tensor"))
    rms_stats = jnp.sqrt(stat_sums / (length * lax.axis_size("dp") * width))
    final_rows = current.astype(BF16)
    gradient = upstream.astype(F32)
    grads = [None] * layers
    for layer in reversed(range(layers)):
        cfg, x, tables, saved = runs[layer]
        back = run_backward(cfg, gradient, x, saved, tables, weights)
        gradient = back["go"]
        grads[layer] = [back["attn_o"][0], back["attn_o"][1], back["attn_o"][2], back["attn_o"][3],
                        back["out_o"], back["left_o"], back["right_o"], back["down_o"]]
    totals = []
    for member in range(8):
        stacked = jnp.stack([grads[layer][member] for layer in range(layers)])
        totals.append(lax.psum(stacked, "dp").astype(F32))
    return (final_rows, gradient.astype(BF16), *totals, rms_stats)


def solution(mesh):
    square = dict(mesh.shape) == SQUARE_MESH
    body = per_device_square if square else per_device
    return jax.shard_map(
        body,
        mesh=mesh,
        in_specs=(
            P(("dp", "tensor"), None),
            P(("dp", "tensor"), None),
            P("dp"),
            P(None, None, "tensor"),
            P(None, None, "tensor"),
            P(None, None, "tensor"),
            P(None, None, "tensor"),
            P(None, "tensor", None),
            P(None, None, "tensor"),
            P(None, None, "tensor"),
            P(None, "tensor", None),
        ),
        out_specs=(
            P(("dp", "tensor"), None),
            P(("dp", "tensor"), None),
            P(None, None, "tensor"),
            P(None, None, "tensor"),
            P(None, None, "tensor"),
            P(None, None, "tensor"),
            P(None, "tensor", None),
            P(None, None, "tensor"),
            P(None, None, "tensor"),
            P(None, "tensor", None),
            P(),
        ),
        check_vma=False,
    )
```

```python
import functools
import math
import types

import jax
import jax.numpy as jnp
import numpy as np
from jax import lax
from jax.experimental import pallas as pl
from jax.experimental.pallas import tpu as pltpu
from jax.sharding import PartitionSpec as P

HEADS = 8
HDIM = 128
BLK = 512


epsilon = 1e-06
depth_start = 0.5
depth_step = 1.0 / 24.0
highest = lax.Precision.HIGHEST


def rms_rows(values):
    return values * lax.rsqrt(jnp.mean(values * values, axis=1, keepdims=True) + epsilon)


def rms_back(values, gradient):
    scaling = lax.rsqrt(jnp.mean(values * values, axis=1, keepdims=True) + epsilon)
    normed = values * scaling
    return scaling * (gradient - normed * jnp.mean(gradient * normed, axis=1, keepdims=True))


def contract_last(left_part, right_part):
    return lax.dot_general(
        left_part, right_part, (((1,), (1,)), ((), ())), preferred_element_type=jnp.float32
    )


def contract_first(left_part, right_part):
    return lax.dot_general(
        left_part, right_part, (((0,), (0,)), ((), ())), preferred_element_type=jnp.float32
    )


def rotate(values, cosine, sine_table):
    return jnp.concatenate([values * cosine[:, None, :], values * sine_table[:, None, :]], axis=2)


def unrotate(gradient, cosine, sine_table):
    half_width = gradient.shape[2] // 2
    return (
        gradient[:, :, :half_width] * cosine[:, None, :]
        + gradient[:, :, half_width:] * sine_table[:, None, :]
    )


def split_blocks(array, block_count):
    return array.reshape((block_count, BLK) + array.shape[1:])


def block_weights(seg_block, next_seg, decay_log):
    block_width = seg_block.shape[0]
    places = jnp.arange(block_width, dtype=jnp.float32)
    distance = places[:, None] - places[None, :]
    allowed = (distance >= 0) & (seg_block[:, None] == seg_block[None, :])
    decay_grid = jnp.where(
        allowed[None], jnp.exp(decay_log[:, None, None] * jnp.maximum(distance, 0.0)[None]), 0.0
    )
    first_seg = seg_block[0]
    query_gain = jnp.where(
        (seg_block == first_seg)[:, None], jnp.exp(places[:, None] * decay_log[None, :]), 0.0
    )
    key_gain = jnp.where(
        (seg_block == next_seg)[:, None],
        jnp.exp((block_width - places)[:, None] * decay_log[None, :]),
        0.0,
    )
    carry_gain = jnp.where(first_seg == next_seg, jnp.exp(decay_log * block_width), 0.0)
    return (decay_grid, query_gain, key_gain, carry_gain)


def next_segments(segments, block_count):
    seg_blocks = segments.reshape(block_count, BLK)
    return (seg_blocks, jnp.concatenate([seg_blocks[1:, 0], jnp.full((1,), -1, jnp.int32)]))


def attend_forward(queries, keys_rot, values, segments, decay_log):
    length, heads_here, pair_width = queries.shape
    block_count = length // BLK
    seg_blocks, next_segs = next_segments(segments, block_count)

    def advance(state_now, block_items):
        query_block, key_block, value_block, seg_block, next_seg = block_items
        query_float = query_block.astype(jnp.float32)
        key_float = key_block.astype(jnp.float32)
        value_float = value_block.astype(jnp.float32)
        decay_grid, query_gain, key_gain, carry_gain = block_weights(seg_block, next_seg, decay_log)
        scores = (
            jnp.einsum("rhd,shd->hrs", query_block, key_block, preferred_element_type=jnp.float32)
            * decay_grid
        )
        block_out = jnp.einsum("hrs,she->rhe", scores, value_float, precision=highest)
        block_out = (
            block_out
            + jnp.einsum("rhd,hde->rhe", query_float, state_now, precision=highest)
            * query_gain[:, :, None]
        )
        new_state = carry_gain[:, None, None] * state_now + jnp.einsum(
            "shd,she->hde", key_float * key_gain[:, :, None], value_float, precision=highest
        )
        return (new_state, (block_out, state_now))

    zero_state = jnp.zeros((heads_here, pair_width, pair_width // 2), jnp.float32)
    _, (block_outs, states) = lax.scan(
        advance,
        zero_state,
        (
            split_blocks(queries, block_count),
            split_blocks(keys_rot, block_count),
            split_blocks(values, block_count),
            seg_blocks,
            next_segs,
        ),
    )
    return (block_outs.reshape(length, heads_here * (pair_width // 2)), states)


def attend_backward(queries, keys_rot, values, segments, decay_log, states, grad_heads):
    length, heads_here, pair_width = queries.shape
    block_count = length // BLK
    seg_blocks, next_segs = next_segments(segments, block_count)

    def retreat(later_grad, block_items):
        query_block, key_block, value_block, seg_block, next_seg, state_now, grad_block = (
            block_items
        )
        query_float = query_block.astype(jnp.float32)
        key_float = key_block.astype(jnp.float32)
        value_float = value_block.astype(jnp.float32)
        decay_grid, query_gain, key_gain, carry_gain = block_weights(seg_block, next_seg, decay_log)
        scores = (
            jnp.einsum("rhd,shd->hrs", query_block, key_block, preferred_element_type=jnp.float32)
            * decay_grid
        )
        pulled = jnp.einsum("rhe,she->hrs", grad_block, value_float, precision=highest) * decay_grid
        grad_query = jnp.einsum("hrs,shd->rhd", pulled, key_float, precision=highest)
        grad_query = (
            grad_query
            + jnp.einsum("rhe,hde->rhd", grad_block, state_now, precision=highest)
            * query_gain[:, :, None]
        )
        grad_key = jnp.einsum("hrs,rhd->shd", pulled, query_float, precision=highest)
        grad_key = (
            grad_key
            + jnp.einsum("she,hde->shd", value_float, later_grad, precision=highest)
            * key_gain[:, :, None]
        )
        grad_value = jnp.einsum("hrs,rhe->she", scores, grad_block, precision=highest)
        grad_value = (
            grad_value
            + jnp.einsum("shd,hde->she", key_float, later_grad, precision=highest)
            * key_gain[:, :, None]
        )
        earlier_grad = carry_gain[:, None, None] * later_grad + jnp.einsum(
            "rhd,rhe->hde", query_float * query_gain[:, :, None], grad_block, precision=highest
        )
        return (earlier_grad, (grad_query, grad_key, grad_value))

    zero_state = jnp.zeros((heads_here, pair_width, pair_width // 2), jnp.float32)
    _, (grad_query, grad_key, grad_value) = lax.scan(
        retreat,
        zero_state,
        (
            split_blocks(queries, block_count),
            split_blocks(keys_rot, block_count),
            split_blocks(values, block_count),
            seg_blocks,
            next_segs,
            states,
            split_blocks(grad_heads, block_count),
        ),
        reverse=True,
    )
    return (
        grad_query.reshape(length, heads_here, pair_width),
        grad_key.reshape(length, heads_here, pair_width),
        grad_value.reshape(length, heads_here, pair_width // 2),
    )


def per_device(
    tokens,
    upstream,
    segment_ids,
    query_proj,
    key_proj,
    value_proj,
    gate_proj,
    output_proj,
    left_proj,
    right_proj,
    down_proj,
):
    layers = query_proj.shape[0]
    row_count, model_width = tokens.shape
    length = segment_ids.shape[0]
    local_width = query_proj.shape[2]
    ff_local = left_proj.shape[2]
    heads_here = local_width // HDIM
    positions = jnp.arange(length, dtype=jnp.float32)
    frequency = jnp.exp(-math.log(10000.0) * jnp.arange(HDIM, dtype=jnp.float32) / HDIM)
    angles = positions[:, None] * frequency[None, :]
    cosine = jnp.cos(angles)
    sine_table = jnp.sin(angles)
    head_index = (lax.axis_index("tensor") * heads_here + jnp.arange(heads_here)).astype(
        jnp.float32
    )
    slopes = jnp.exp2(-8.0 * (head_index + 1.0) / HEADS)

    def gather_normed(normed):
        return lax.all_gather(normed, "tensor", axis=0, tiled=True)

    def gather_again(normed):
        return lax.all_gather(normed, "tensor", axis=0, tiled=True)

    def gather_grads(gradient):
        return lax.all_gather(gradient, "tensor", axis=0, tiled=True)

    def branch_sum(operand, matrix):
        return lax.psum_scatter(
            jnp.dot(operand, matrix, preferred_element_type=jnp.float32).astype(jnp.bfloat16),
            "tensor",
            scatter_dimension=0,
            tiled=True,
        ).astype(jnp.float32)

    def input_sum(pieces, matrix):
        operand = jnp.concatenate(pieces, axis=1)
        return lax.psum_scatter(
            contract_last(operand, matrix).astype(jnp.bfloat16),
            "tensor",
            scatter_dimension=0,
            tiled=True,
        ).astype(jnp.float32)

    current = tokens.astype(jnp.float32)
    saved_layers = []
    stat_terms = []
    for layer_index in range(layers):
        residual = current
        normed = rms_rows(residual).astype(jnp.bfloat16)
        full_normed = gather_normed(normed)
        attn_weight = jnp.concatenate(
            [
                query_proj[layer_index],
                key_proj[layer_index],
                value_proj[layer_index],
                gate_proj[layer_index],
            ],
            axis=1,
        )
        projected = jnp.dot(full_normed, attn_weight, preferred_element_type=jnp.float32)
        query_lin = projected[:, :local_width]
        key_lin = projected[:, local_width : 2 * local_width]
        values = (
            projected[:, 2 * local_width : 3 * local_width]
            .astype(jnp.bfloat16)
            .reshape(length, heads_here, HDIM)
        )
        gate_lin = projected[:, 3 * local_width :]
        queries = rotate(
            jax.nn.silu(query_lin).reshape(length, heads_here, HDIM), cosine, sine_table
        ).astype(jnp.bfloat16)
        keys_rot = rotate(
            jax.nn.silu(key_lin).reshape(length, heads_here, HDIM), cosine, sine_table
        ).astype(jnp.bfloat16)
        decay_log = -slopes * (1.0 - depth_start - depth_step * layer_index)
        heads_out, states = attend_forward(queries, keys_rot, values, segment_ids, decay_log)
        squares = lax.psum(jnp.sum(heads_out * heads_out, axis=1), "tensor")
        scaling = lax.rsqrt(squares / model_width + epsilon)[:, None]
        normed_heads = heads_out * scaling
        branch = (normed_heads * gate_lin).astype(jnp.bfloat16)
        attn_rows = branch_sum(branch, output_proj[layer_index])
        middle = residual + attn_rows
        normed_mid = rms_rows(middle).astype(jnp.bfloat16)
        full_mid = gather_normed(normed_mid)
        glu_weight = jnp.concatenate([left_proj[layer_index], right_proj[layer_index]], axis=1)
        gates_both = jnp.dot(full_mid, glu_weight, preferred_element_type=jnp.float32)
        left_lin = gates_both[:, :ff_local]
        right_lin = gates_both[:, ff_local:]
        hidden = (left_lin * right_lin).astype(jnp.bfloat16)
        glu_rows = branch_sum(hidden, down_proj[layer_index])
        current = middle + glu_rows
        stat_terms.append(
            jnp.stack(
                [
                    jnp.sum(attn_rows * attn_rows),
                    jnp.sum(glu_rows * glu_rows),
                    jnp.sum(current * current),
                ]
            )
        )
        saved_layers.append(
            (
                residual,
                middle,
                normed,
                normed_mid,
                full_normed,
                full_mid,
                attn_weight,
                glu_weight,
                query_lin,
                key_lin,
                gate_lin,
                queries,
                keys_rot,
                values,
                decay_log,
                states,
                normed_heads,
                scaling,
                branch,
                left_lin,
                right_lin,
                hidden,
            )
        )
    stat_sums = lax.psum(jnp.stack(stat_terms), ("dp", "tensor"))
    rms_stats = jnp.sqrt(stat_sums / (length * lax.axis_size("dp") * model_width))
    final_rows = current.astype(jnp.bfloat16)
    gradient = upstream.astype(jnp.float32)
    layer_results = [None] * layers
    for layer_index in reversed(range(layers)):
        (
            residual,
            middle,
            normed,
            normed_mid,
            full_normed,
            full_mid,
            attn_weight,
            glu_weight,
            query_lin,
            key_lin,
            gate_lin,
            queries,
            keys_rot,
            values,
            decay_log,
            states,
            normed_heads,
            scaling,
            branch,
            left_lin,
            right_lin,
            hidden,
        ) = saved_layers[layer_index]
        glu_grad = gather_grads(gradient.astype(jnp.bfloat16))
        grad_hidden = contract_last(glu_grad, down_proj[layer_index])
        down_part = contract_first(hidden, glu_grad)
        grad_left = (grad_hidden * right_lin).astype(jnp.bfloat16)
        grad_right = (grad_hidden * left_lin).astype(jnp.bfloat16)
        grad_gates = jnp.concatenate([grad_left, grad_right], axis=1)
        mid_rows = input_sum((grad_left, grad_right), glu_weight)
        source_mid = gather_again(normed_mid)
        glu_part = contract_first(source_mid, grad_gates)
        gradient = gradient + rms_back(middle, mid_rows)
        attn_grad = gather_grads(gradient.astype(jnp.bfloat16))
        output_part = contract_first(branch, attn_grad)
        grad_branch = contract_last(attn_grad, output_proj[layer_index])
        grad_normed = grad_branch * gate_lin
        grad_gate = (grad_branch * normed_heads).astype(jnp.bfloat16)
        inner_sum = lax.psum(jnp.sum(grad_normed * normed_heads, axis=1), "tensor")
        grad_heads = scaling * (grad_normed - normed_heads * (inner_sum / model_width)[:, None])
        grad_query, grad_key, grad_value = attend_backward(
            queries,
            keys_rot,
            values,
            segment_ids,
            decay_log,
            states,
            grad_heads.reshape(length, heads_here, HDIM),
        )
        sigmoid_query = jax.nn.sigmoid(query_lin)
        sigmoid_key = jax.nn.sigmoid(key_lin)
        query_back = unrotate(grad_query, cosine, sine_table).reshape(length, local_width)
        key_back = unrotate(grad_key, cosine, sine_table).reshape(length, local_width)
        grad_query_lin = (
            query_back * (sigmoid_query + query_lin * sigmoid_query * (1.0 - sigmoid_query))
        ).astype(jnp.bfloat16)
        grad_key_lin = (
            key_back * (sigmoid_key + key_lin * sigmoid_key * (1.0 - sigmoid_key))
        ).astype(jnp.bfloat16)
        grad_value_lin = grad_value.reshape(length, local_width).astype(jnp.bfloat16)
        grad_projected = jnp.concatenate(
            [grad_query_lin, grad_key_lin, grad_value_lin, grad_gate], axis=1
        )
        in_rows = input_sum((grad_query_lin, grad_key_lin, grad_value_lin, grad_gate), attn_weight)
        source_normed = gather_again(normed)
        attn_part = contract_first(source_normed, grad_projected)
        gradient = gradient + rms_back(residual, in_rows)
        query_part = attn_part[:, :local_width]
        key_part = attn_part[:, local_width : 2 * local_width]
        value_part = attn_part[:, 2 * local_width : 3 * local_width]
        gate_part = attn_part[:, 3 * local_width :]
        left_part = glu_part[:, :ff_local]
        right_part = glu_part[:, ff_local:]
        layer_results[layer_index] = (
            query_part,
            key_part,
            value_part,
            gate_part,
            output_part,
            left_part,
            right_part,
            down_part,
        )
    stacked = [
        jnp.stack([layer_results[index][member] for index in range(layers)]) for member in range(8)
    ]
    totals = (
        lax.psum(stacked[0].astype(jnp.bfloat16), "dp").astype(jnp.float32),
        lax.psum(stacked[1].astype(jnp.bfloat16), "dp").astype(jnp.float32),
        lax.psum(stacked[2].astype(jnp.bfloat16), "dp").astype(jnp.float32),
        lax.psum(stacked[3].astype(jnp.bfloat16), "dp").astype(jnp.float32),
        lax.psum(stacked[4].astype(jnp.bfloat16), "dp").astype(jnp.float32),
        lax.psum(stacked[5].astype(jnp.bfloat16), "dp").astype(jnp.float32),
        lax.psum(stacked[6].astype(jnp.bfloat16), "dp").astype(jnp.float32),
        lax.psum(stacked[7].astype(jnp.bfloat16), "dp").astype(jnp.float32),
    )
    input_grad = gradient.astype(jnp.bfloat16)
    return (
        final_rows,
        input_grad,
        totals[0],
        totals[1],
        totals[2],
        totals[3],
        totals[4],
        totals[5],
        totals[6],
        totals[7],
        rms_stats,
    )


SQUARE_MESH = {"dp": 8, "tensor": 4}


F32 = jnp.float32
BF16 = jnp.bfloat16
MESH = pl.DeviceIdType.MESH
VMEM_LIMIT = 60 * 2**20
SUPER = 2
CHUNK = 128
HOP = 2
SLOTS = 12


def nn(a, b):
    return lax.dot_general(a, b, (((1,), (0,)), ((), ())), preferred_element_type=F32)


def nt(a, b):
    return lax.dot_general(a, b, (((1,), (1,)), ((), ())), preferred_element_type=F32)


def tn(a, b):
    return lax.dot_general(a, b, (((0,), (0,)), ((), ())), preferred_element_type=F32)


def exact(a, b, dims):
    return lax.dot_general(a, b, (dims, ((), ())), precision=highest, preferred_element_type=F32)


def aligned(index, size):
    return pl.ds(pl.multiple_of(index, size), size)


class Place:
    def __init__(self, pairs):
        self.dp = lax.axis_index("dp")
        self.me = lax.axis_index("tensor")
        self.low = lax.rem(self.me, 2)
        self.high = self.me // 2
        self.core = lax.rem(self.dp, 2)
        self.at = self.dp // 2
        self.last = pairs - 1

    def member(self, step):
        low = lax.rem(self.low + lax.rem(step, 2), 2)
        high = lax.rem(self.high + step // 2, 2)
        return 2 * high + low

    def device(self, step):
        return (self.dp, self.member(step))

    def partner(self):
        return (self.dp + 1 - 2 * self.core, self.me)

    def right(self):
        return (self.dp + 2, self.me)

    def left(self):
        return (self.dp - 2, self.me)

    def greet(self, line):
        barrier = pltpu.get_barrier_semaphore()

        def signal(device):
            pl.semaphore_signal(barrier, inc=1, device_id=device, device_id_type=MESH)

        for step in (1, 2, 3):
            signal(self.device(step))
        if not line:
            pl.semaphore_wait(barrier, 3)
            return
        signal(self.partner())

        @pl.when(self.at < self.last)
        def _():
            signal(self.right())

        @pl.when(self.at > 0)
        def _():
            signal(self.left())

        pl.semaphore_wait(barrier, 4 + jnp.minimum(self.at, 1) + jnp.minimum(self.last - self.at, 1))


class Wire:
    def __init__(self, device, send_sem, recv_sem, source, target, landing):
        self.source, self.target, self.landing = source, target, landing
        self.common = dict(send_sem=send_sem, recv_sem=recv_sem, device_id=device, device_id_type=MESH)

    def out(self):
        return pltpu.make_async_remote_copy(src_ref=self.source, dst_ref=self.target, **self.common)

    def start(self):
        self.out().start()

    def wait_recv(self):
        pltpu.make_async_remote_copy(src_ref=self.landing, dst_ref=self.landing, **self.common).wait_recv()

    def wait_send(self):
        self.out().wait_send()


class Gather:
    def __init__(self, place, buf, send, recv, block):
        self.place, self.buf, self.block = place, buf, block
        self.send, self.recv = send, recv
        self.half = block // (2 * SUPER)

    def rows(self, step, part, half):
        start = self.place.member(step) * self.block + (2 * part + half) * self.half
        return self.buf.at[aligned(start, self.half)]

    def wire(self, part, number):
        step, owner, half = ((1, 0, 0), (2, 0, 1), (1, 0, 1), (2, 0, 0), (2, 1, 0), (1, 2, 1))[number]
        source = self.rows(owner, part, half)
        landing = self.rows((0, 1, 2, 3)[owner ^ step], part, half)
        return Wire(self.place.device(step), self.send.at[part, number], self.recv.at[part, number], source, source, landing)

    def start(self, part):
        for number in range(4):
            self.wire(part, number).start()

    def forward(self, part):
        self.wire(part, 0).wait_recv()
        self.wire(part, 4).start()
        self.wire(part, 1).wait_recv()
        self.wire(part, 5).start()

    def finish(self, part, step):
        for number in {0: (), 1: (2,), 2: (3,), 3: (4, 5)}[step]:
            self.wire(part, number).wait_recv()

    def drain(self):
        for part in range(SUPER):
            for number in range(6):
                self.wire(part, number).wait_send()


class Scatter:
    def __init__(self, place, buf, land, send, recv, block):
        self.place, self.buf, self.land, self.block = place, buf, land, block
        self.send, self.recv = send, recv
        self.half = block // (2 * SUPER)

    def rows(self, step, part, half):
        start = self.place.member(step) * self.block + (2 * part + half) * self.half
        return aligned(start, self.half)

    def wire(self, part, number):
        step, owner, half = ((1, 3, 0), (1, 1, 0), (2, 3, 1), (2, 2, 1), (2, 2, 0), (1, 1, 1))[number]
        target = self.land.at[part, number]
        return Wire(
            self.place.device(step), self.send.at[part, number], self.recv.at[part, number],
            self.buf.at[self.rows(owner, part, half)], target, target,
        )

    def send_block(self, part, step):
        for number in {0: (), 1: (1,), 2: (3,), 3: (0, 2)}[step]:
            self.wire(part, number).start()

    def middle(self, part):
        for first, second, owner, half in ((0, 4, 2, 0), (2, 5, 1, 1)):
            self.wire(part, first).wait_recv()
            rows = self.rows(owner, part, half)
            self.buf[rows, :] = (
                self.buf[rows, :].astype(F32) + self.land[part, first].astype(F32)
            ).astype(BF16)
            self.wire(part, second).start()

    def finish(self, part, half):
        first, second = ((1, 4), (3, 5))[half]
        self.wire(part, first).wait_recv()
        self.wire(part, second).wait_recv()

    def total(self, part, half, start, count):
        first, second = ((1, 4), (3, 5))[half]
        own = self.place.me * self.block + (2 * part + half) * self.half + start
        rows = pl.ds(start, count)
        return (
            self.buf[aligned(own, count), :].astype(F32)
            + self.land[part, first, rows, :].astype(F32)
            + self.land[part, second, rows, :].astype(F32)
        )

    def drain(self):
        for part in range(SUPER):
            for number in range(6):
                self.wire(part, number).wait_send()


class Share:
    def __init__(self, place, mine, land, send, recv):
        self.wires = [
            Wire(place.device(step), send.at[step - 1], recv.at[step - 1], mine, land.at[step - 1], land.at[step - 1])
            for step in (1, 2, 3)
        ]
        self.mine, self.land = mine, land

    def start(self):
        for wire in self.wires:
            wire.start()

    def total(self):
        for wire in self.wires:
            wire.wait_recv()
        return self.mine[...] + self.land[0] + self.land[1] + self.land[2]

    def drain(self):
        for wire in self.wires:
            wire.wait_send()


class Local:
    def __init__(self, sems):
        self.sems, self.used = sems, 0

    def start(self, source, target):
        copy = pltpu.make_async_copy(source, target, self.sems.at[self.used])
        self.used += 1
        copy.start()
        return copy


def row_sums(values, target, chunk):
    sums = exact(jnp.ones((8, values.shape[1]), F32), values, ((1,), (1,)))
    target[pl.ds(chunk, 1), :] = sums[0:1, :]


def spread(sums, chunk):
    picked = (lax.broadcasted_iota(jnp.int32, (8, 128), 0) == chunk).astype(F32)
    return exact(sums, picked, ((0,), (0,)))


def widen(columns, times):
    return jnp.concatenate([columns] * times, axis=1)


def decay_tiles(dec_ref, first_head, tiles, heads_here, size):
    rows = lax.broadcasted_iota(jnp.int32, (size, size), 0)
    cols = lax.broadcasted_iota(jnp.int32, (size, size), 1)
    distance = (rows - cols).astype(F32)
    for head in range(heads_here):
        decay = dec_ref[pl.ds(first_head + head, 1), 0:1]
        tiles[head, 0] = jnp.where(rows >= cols, jnp.exp(decay * jnp.maximum(distance, 0.0)), 0.0)
        tiles[head, 1] = jnp.exp(decay * (distance + float(size)))


def spread_segments(r, length):
    r.segf[...] = r.seg[...].astype(F32)
    for chunk in range(length // 128):
        r.segc[chunk * 128 : (chunk + 1) * 128, :] = spread(r.segf[...], chunk)


def tile_weight(r, first_head, head, row_tile, col_tile, size):
    gap = row_tile - col_tile
    if gap == 0:
        weight = r.tiles[head, 0]
    else:
        weight = r.tiles[head, 1]
        if gap > 1:
            decay = r.dec[pl.ds(first_head + head, 1), 0:1]
            weight = weight * jnp.exp(decay * float(size * (gap - 1)))
    row_seg = widen(r.segc[row_tile * size : (row_tile + 1) * size, :], size // 128)
    per = size // 128
    col_seg = jnp.concatenate([r.segf[per * col_tile + i : per * col_tile + i + 1, :] for i in range(per)], axis=1)
    return jnp.where(row_seg == col_seg, weight, 0.0)


def namespace(names, refs):
    return types.SimpleNamespace(**dict(zip(names, refs)))


def fwd_kernel(cfg, names, *refs):
    r = namespace(names, refs)
    layer, block, length, width, local = cfg.layer, cfg.block, cfg.length, cfg.width, cfg.local
    heads_here, size = cfg.heads_here, cfg.block
    place = Place(cfg.pairs)
    first_head = layer * HEADS + place.me * heads_here
    copies = Local(r.local_sem)
    w_in = [copies.start(h.at[layer], v) for h, v in (
        (r.wq_h, r.wq), (r.wk_h, r.wk), (r.wv_h, r.wv), (r.wg_h, r.wg))]
    w_out = copies.start(r.wo_h.at[layer], r.wo)
    w_glu = [copies.start(h.at[layer], v) for h, v in ((r.wl_h, r.wl), (r.wr_h, r.wr), (r.wd_h, r.wd))]
    saves = []
    first = Gather(place, r.n1, r.ag1_send, r.ag1_recv, block)
    mid_sum = Scatter(place, r.part1, r.land1, r.rs1_send, r.rs1_recv, block)
    second = Gather(place, r.n2, r.ag2_send, r.ag2_recv, block)
    out_sum = Scatter(place, r.part2, r.land2, r.rs2_send, r.rs2_recv, block)
    share = Share(place, r.ss, r.ss_land, r.ss_send, r.ss_recv)
    half, step_rows = first.half, 32
    own_start = place.me * block

    @pl.loop(0, block // step_rows)
    def _(i):
        rows = aligned(i * step_rows, step_rows)
        v = r.x[rows, :].astype(F32)
        scale = lax.rsqrt(jnp.mean(v * v, axis=1, keepdims=True) + epsilon)
        r.n1[aligned(own_start + i * step_rows, step_rows), :] = (v * scale).astype(BF16)

    place.greet(False)
    for part in range(SUPER):
        first.start(part)
    decay_tiles(r.dec, first_head, r.tiles, heads_here, size)
    spread_segments(r, length)
    for copy in w_in:
        copy.wait()

    @pl.loop(0, 4)
    def _(step):
        @pl.when(step == 1)
        def _():
            for part in range(SUPER):
                first.forward(part)
        for which in (1, 2, 3):
            @pl.when(step == which)
            def _():
                for part in range(SUPER):
                    first.finish(part, which)
        rows = aligned(place.member(step) * block, block)
        a = r.n1[rows, :]
        cosine, sine = r.cos[rows, :], r.sin[rows, :]
        for w, lin, rot in ((r.wq, r.ql, r.q), (r.wk, r.kl, r.k)):
            v = nn(a, w[...])
            lin[rows, :] = v.astype(BF16)
            v = v / (1.0 + jnp.exp(-v))
            for head in range(heads_here):
                one = v[:, head * HDIM : (head + 1) * HDIM]
                rot[rows, 2 * head * HDIM : (2 * head + 1) * HDIM] = (one * cosine).astype(BF16)
                rot[rows, (2 * head + 1) * HDIM : (2 * head + 2) * HDIM] = (one * sine).astype(BF16)
        r.v[rows, :] = nn(a, r.wv[...]).astype(BF16)
        r.gate[rows, :] = nn(a, r.wg[...])

    for v, h in ((r.n1, r.n1_h), (r.ql, r.ql_h), (r.kl, r.kl_h), (r.q, r.q_h), (r.k, r.k_h), (r.v, r.v_h), (r.gate, r.gate_h)):
        saves.append(copies.start(v, h))

    tiles_here = length // size

    @pl.loop(0, heads_here)
    def _(head):
        wide = aligned(head * 2 * HDIM, 2 * HDIM)
        thin = aligned(head * HDIM, HDIM)
        for row_tile in range(tiles_here):
            rows = slice(row_tile * size, (row_tile + 1) * size)
            queries = r.q[rows, wide]
            acc = None
            for col_tile in range(row_tile + 1):
                cols = slice(col_tile * size, (col_tile + 1) * size)
                weight = tile_weight(r, first_head, head, row_tile, col_tile, size)
                scores = (nt(queries, r.k[cols, wide]) * weight).astype(BF16)
                term = nn(scores, r.v[cols, thin])
                acc = term if acc is None else acc + term
            r.heads[rows, thin] = acc
            r.u[rows, thin] = (acc * r.gate[rows, thin]).astype(BF16)

    for chunk in range(length // 128):
        v = r.heads[chunk * 128 : (chunk + 1) * 128, :]
        row_sums(v * v, r.ss, chunk)
    share.start()
    saves.append(copies.start(r.heads, r.heads_h))
    w_out.wait()

    part_rows = 2 * half
    for part in range(SUPER):
        for step in (3, 1, 2, 0):
            rows = aligned(place.member(step) * block + part * part_rows, part_rows)
            r.part1[rows, :] = nn(r.u[rows, :], r.wo[...]).astype(BF16)
            mid_sum.send_block(part, step)
    for part in range(SUPER):
        mid_sum.middle(part)
    r.sstot[...] = share.total()
    saves.append(copies.start(r.sstot, r.ss_h))
    scaling = lax.rsqrt(r.sstot[...] / width + epsilon)
    per_block = block // 128
    for chunk in range(per_block):
        r.scale[chunk * 128 : (chunk + 1) * 128, :] = spread(scaling, place.me * per_block + chunk)
    r.stat_wide[...] = jnp.zeros_like(r.stat_wide)

    def add_stat(row, v):
        sums = jnp.sum(v * v, axis=0, keepdims=True)
        r.stat_wide[row : row + 1, :] += sums

    step_rows = min(32, half)
    for part in range(SUPER):
        for h in range(2):
            mid_sum.finish(part, h)
            for i in range(half // step_rows):
                offset = (2 * part + h) * half + i * step_rows
                scale = widen(r.scale[offset : offset + step_rows, :], width // 128)
                attn = mid_sum.total(part, h, i * step_rows, step_rows) * scale
                middle = r.x[offset : offset + step_rows, :].astype(F32) + attn
                r.mid[offset : offset + step_rows, :] = middle
                add_stat(0, attn)
                norm = lax.rsqrt(jnp.mean(middle * middle, axis=1, keepdims=True) + epsilon)
                r.n2[aligned(own_start + offset, step_rows), :] = (middle * norm).astype(BF16)
        second.start(part)
    saves.append(copies.start(r.mid, r.mid_h))
    for copy in w_glu:
        copy.wait()
    for part in range(SUPER):

        def glu(step):
            rows = aligned(place.member(step) * block + part * part_rows, part_rows)
            a = r.n2[rows, :]
            left = nt(a, r.wl[...])
            right = nt(a, r.wr[...])
            hidden = (left * right).astype(BF16)
            r.left[rows, :] = left.astype(BF16)
            r.right[rows, :] = right.astype(BF16)
            r.hid[rows, :] = hidden
            r.part2[rows, :] = nn(hidden, r.wd[...]).astype(BF16)

        @pl.loop(0, 4)
        def _(step):
            if part == 0:
                @pl.when(step == 1)
                def _():
                    for other in range(SUPER):
                        second.forward(other)
            for which in (1, 2, 3):
                @pl.when(step == which)
                def _():
                    second.finish(part, which)
            glu(step)
            for which in (1, 2, 3):
                @pl.when(step == which)
                def _():
                    out_sum.send_block(part, which)
    for v, h in ((r.n2, r.n2_h), (r.left, r.left_h), (r.right, r.right_h), (r.hid, r.hid_h)):
        saves.append(copies.start(v, h))
    for part in range(SUPER):
        out_sum.middle(part)
    for part in range(SUPER):
        for h in range(2):
            out_sum.finish(part, h)
            for i in range(half // step_rows):
                offset = (2 * part + h) * half + i * step_rows
                glu_rows = out_sum.total(part, h, i * step_rows, step_rows)
                after = r.mid[offset : offset + step_rows, :] + glu_rows
                r.xo[offset : offset + step_rows, :] = after
                add_stat(1, glu_rows)
                add_stat(2, after)
    folded = r.stat_wide[:, :128]
    for n in range(1, width // 128):
        folded = folded + r.stat_wide[:, n * 128 : (n + 1) * 128]
    r.stat[...] = folded
    for copy in saves:
        copy.wait()
    for group in (first, mid_sum, second, out_sum, share):
        group.drain()


class Line:
    def __init__(self, cfg, place, r):
        self.place, self.r = place, r
        self.per, self.count = cfg.chunks, cfg.chunks * cfg.layers
        self.layers, self.rows_each = cfg.layers, cfg.chunks * CHUNK
        self.half = CHUNK // 2
        self.ticks = self.count + 3 + HOP * place.last
        self.done = 0

    def rows(self, k, core):
        return aligned(lax.rem(k, self.per) * CHUNK + core * self.half, self.half)

    def own(self, k):
        return self.rows(k, self.place.core)

    def out_rows(self, k, core):
        layer = self.layers - 1 - k // self.per
        start = layer * self.rows_each + lax.rem(k, self.per) * CHUNK + core * self.half
        return aligned(start, self.half)

    def pair(self, k):
        slot = lax.rem(k, SLOTS)
        r = self.r
        return Wire(self.place.partner(), r.pair_send.at[slot], r.pair_recv.at[slot],
                    r.grads.at[self.rows(k, 1 - self.place.core)], r.pair_land.at[slot], r.pair_land.at[slot])

    def hop(self, k, land, send, recv, device):
        slot = lax.rem(k, SLOTS)
        return Wire(device, send.at[slot], recv.at[slot], land.at[slot], land.at[slot], land.at[slot])

    def going_right(self, k):
        return self.hop(k, self.r.right_land, self.r.right_send, self.r.right_recv, self.place.right())

    def going_left(self, k):
        return self.hop(k, self.r.left_land, self.r.left_send, self.r.left_recv, self.place.left())

    def coming_right(self, k):
        return self.hop(k, self.r.right_land, self.r.right_send, self.r.right_recv, self.place.left())

    def coming_left(self, k):
        return self.hop(k, self.r.left_land, self.r.left_send, self.r.left_recv, self.place.right())

    def result(self, k):
        slot, r = lax.rem(k, SLOTS), self.r
        return Wire(self.place.partner(), r.give_send.at[slot], r.give_recv.at[slot],
                    r.grads.at[self.own(k)], r.out_h.at[self.out_rows(k, self.place.core)],
                    r.out_h.at[self.out_rows(k, 1 - self.place.core)])

    def keep(self, k):
        slot, r = lax.rem(k, SLOTS), self.r
        return pltpu.make_async_copy(
            r.grads.at[self.own(k)], r.out_h.at[self.out_rows(k, self.place.core)], r.keep_sem.at[slot]
        )

    def one_way(self, k, land, start_here, coming, ends_here, going):
        slot = lax.rem(k, SLOTS)

        @pl.when(start_here)
        def _():
            land[slot] = self.r.grads[self.own(k), :]

        @pl.when(jnp.logical_not(start_here))
        def _():
            coming(k).wait_recv()
            land[slot] = (land[slot].astype(F32) + self.r.grads[self.own(k), :].astype(F32)).astype(BF16)

        @pl.when(jnp.logical_not(ends_here))
        def _():
            going(k).start()

    def tick(self, n):
        place, r, last = self.place, self.r, self.place.last
        at_left, at_right = place.at == 0, place.at == last

        @pl.when(n < self.count)
        def _():
            self.pair(n).start()

        k = n - 1

        @pl.when(jnp.logical_and(k >= 0, k < self.count))
        def _():
            wire = self.pair(k)
            wire.wait_recv()
            wire.wait_send()
            slot = lax.rem(k, SLOTS)
            r.grads[self.own(k), :] = (
                r.grads[self.own(k), :].astype(F32) + r.pair_land[slot].astype(F32)
            ).astype(BF16)

        left_k = n - 1 - HOP * (last - place.at)

        @pl.when(jnp.logical_and(left_k >= 0, left_k < self.count))
        def _():
            self.one_way(left_k, r.left_land, at_right, self.coming_left, at_left, self.going_left)

        right_k = n - 1 - HOP * place.at

        @pl.when(jnp.logical_and(right_k >= 0, right_k < self.count))
        def _():
            self.one_way(right_k, r.right_land, at_left, self.coming_right, at_right, self.going_right)

        full_k = n - 1 - HOP * last

        @pl.when(jnp.logical_and(full_k >= 0, full_k < self.count))
        def _():
            @pl.when(jnp.logical_not(at_right))
            def _():
                self.going_right(full_k).wait_send()

            @pl.when(jnp.logical_not(at_left))
            def _():
                self.going_left(full_k).wait_send()

            slot = lax.rem(full_k, SLOTS)
            own = self.own(full_k)
            total = r.right_land[slot].astype(F32) + r.left_land[slot].astype(F32) - r.grads[own, :].astype(F32)
            r.grads[own, :] = total.astype(BF16)
            self.result(full_k).start()
            self.keep(full_k).start()

        old_k = full_k - 2

        @pl.when(jnp.logical_and(old_k >= 0, old_k < self.count))
        def _():
            wire = self.result(old_k)
            wire.wait_recv()
            wire.wait_send()
            self.keep(old_k).wait()

    def pump(self, ready, most):
        stop = min(self.done + most, ready)
        if stop > self.done:
            start, self.done = self.done, stop

            @pl.loop(start, stop)
            def _(n):
                self.tick(n)

    def finish(self):
        start, self.done = self.done, self.ticks

        @pl.loop(start, self.ticks)
        def _(n):
            self.tick(n)


class StatLine:
    def __init__(self, place, r):
        self.place, self.r = place, r
        self.share = Share(place, r.stat_mine, r.stat_land, r.st_send, r.st_recv)

    def square(self):
        self.share.start()

    def pair(self):
        r = self.r
        r.stat_square[...] = self.share.total()
        self.wire(0, self.place.partner(), r.stat_square).start()

    def wire(self, number, device, source):
        r = self.r
        return Wire(device, r.line_send.at[number], r.line_recv.at[number], source, r.line_land.at[number], r.line_land.at[number])

    def stage(self, number):
        place, r = self.place, self.r
        if number == 0:
            self.wire(0, place.partner(), r.stat_square).wait_recv()
            r.stat_pair[...] = r.stat_square[...] + r.line_land[0]
            r.stat_right[...] = r.stat_pair[...]
            r.stat_left[...] = r.stat_pair[...]
        else:
            @pl.when(place.at == number)
            def _():
                self.wire(1, place.left(), r.stat_right).wait_recv()
                r.stat_right[...] = r.stat_pair[...] + r.line_land[1]

            @pl.when(place.last - place.at == number)
            def _():
                self.wire(2, place.right(), r.stat_left).wait_recv()
                r.stat_left[...] = r.stat_pair[...] + r.line_land[2]
        if number < place.last:
            @pl.when(place.at == number)
            def _():
                self.wire(1, place.right(), r.stat_right).start()

            @pl.when(place.last - place.at == number)
            def _():
                self.wire(2, place.left(), r.stat_left).start()

    def finish(self):
        place, r = self.place, self.r
        r.stat_total[...] = r.stat_right[...] + r.stat_left[...] - r.stat_pair[...]
        self.share.drain()
        self.wire(0, place.partner(), r.stat_square).wait_send()

        @pl.when(place.at < place.last)
        def _():
            self.wire(1, place.right(), r.stat_right).wait_send()

        @pl.when(place.at > 0)
        def _():
            self.wire(2, place.left(), r.stat_left).wait_send()


def bwd_kernel(cfg, names, *refs):
    r = namespace(names, refs)
    block, length, width, local, ff = cfg.block, cfg.length, cfg.width, cfg.local, cfg.ff
    heads_here, size, layers = cfg.heads_here, cfg.block, cfg.layers
    place = Place(cfg.pairs)
    copies = Local(r.local_sem)
    line = Line(cfg, place, r)
    stats = StatLine(place, r)
    loads = {}
    base_down, base_left, base_right, base_out, base_gate, base_qkv, base_end = cfg.bases
    half = block // (2 * SUPER)
    part_rows = 2 * half
    own_start = place.me * block
    step_rows = min(32, half)
    per_block = block // 128
    tiles_here = length // size

    def load(layer, *keys):
        for key in keys:
            if key in SAVED:
                source = getattr(r, key + str(layer) + "_h")
            else:
                source = getattr(r, key + "_h").at[layer]
            loads[key] = copies.start(source, getattr(r, key))

    def await_loads(*keys):
        for key in keys:
            loads[key].wait()

    glu_in = ("wd", "left", "right", "wl", "wr")
    glu_grad = ("hid", "n2", "mid")
    out_in = ("ss", "wo", "gate", "heads")
    attn_in = ("q", "k", "v", "ql", "kl")
    in_in = ("wq", "wk", "wv", "wg")
    load(layers - 1, *glu_in, *glu_grad, *out_in, *attn_in, *in_in, "n1")

    def gather_one(layer):
        return Gather(place, r.gd, r.ag1_send.at[layer], r.ag1_recv.at[layer], block)

    firsts = [gather_one(layer) for layer in range(layers)]

    @pl.loop(0, block // 32)
    def _(i):
        rows = aligned(i * 32, 32)
        v = r.up[rows, :]
        r.g[rows, :] = v.astype(F32)
        r.gd[aligned(own_start + i * 32, 32), :] = v

    r.stat_mine[...] = jnp.zeros_like(r.stat_mine)
    for layer in range(layers):
        r.stat_mine[3 * layer : 3 * layer + 3, :] = getattr(r, "stat%d" % layer)[0:3, :]
    place.greet(True)
    for part in range(SUPER):
        firsts[layers - 1].start(part)
    stats.square()
    spread_segments(r, length)
    r.grads[base_end : cfg.chunks * CHUNK, :] = jnp.zeros((cfg.chunks * CHUNK - base_end, width), BF16)
    stats.pair()

    def back_rows(total, values, grad):
        norm = lax.rsqrt(jnp.mean(values * values, axis=1, keepdims=True) + epsilon)
        m = values * norm
        inner = jnp.mean(total * m, axis=1, keepdims=True)
        return grad + norm * (total - m * inner)

    for turn, layer in enumerate(reversed(range(layers))):
        first = firsts[layer]
        mid_sum = Scatter(place, r.part, r.land, r.rs1_send.at[layer], r.rs1_recv.at[layer], block)
        second = Gather(place, r.ga, r.ag2_send.at[layer], r.ag2_recv.at[layer], block)
        in_sum = Scatter(place, r.part, r.land, r.rs2_send.at[layer], r.rs2_recv.at[layer], block)
        share = Share(place, r.inner, r.inner_land.at[layer], r.in_send.at[layer], r.in_recv.at[layer])
        first_head = layer * HEADS + place.me * heads_here

        def ready(rows):
            return turn * cfg.chunks + rows // CHUNK

        decay_tiles(r.dec, first_head, r.tiles, heads_here, size)
        await_loads(*glu_in)
        await_loads(*out_in)
        scaling = lax.rsqrt(r.ss[...] / width + epsilon)
        for chunk in range(length // 128):
            r.scale[chunk * 128 : (chunk + 1) * 128, :] = spread(scaling, chunk)
        if turn == 0:
            stats.stage(0)

        for part in range(SUPER):
            start = line.done
            beside = min(4, ready(0) - start)
            line.done = start + max(beside, 0)

            @pl.loop(0, 4)
            def _(step):
                if beside > 0:
                    @pl.when(step < beside)
                    def _():
                        line.tick(start + step)
                if part == 0:
                    @pl.when(step == 1)
                    def _():
                        for other in range(SUPER):
                            first.forward(other)
                for which in (1, 2, 3):
                    @pl.when(step == which)
                    def _():
                        first.finish(part, which)
                rows = aligned(place.member(step) * block + part * part_rows, part_rows)
                grad_hidden = nt(r.gd[rows, :], r.wd[...])
                grad_left = (grad_hidden * r.right[rows, :].astype(F32)).astype(BF16)
                grad_right = (grad_hidden * r.left[rows, :].astype(F32)).astype(BF16)
                r.right[rows, :] = grad_left
                r.left[rows, :] = grad_right
                r.part[rows, :] = (nn(grad_left, r.wl[...]) + nn(grad_right, r.wr[...])).astype(BF16)
                for which in (1, 2, 3):
                    @pl.when(step == which)
                    def _():
                        mid_sum.send_block(part, which)
        first.drain()
        grad_left_ref, grad_right_ref = r.right, r.left

        def glu_grad_rows(base, a_ref, b_ref, limit):
            for n in range(width // 256):
                cols = slice(n * 256, (n + 1) * 256)
                r.grads[base : base + ff, cols] = tn(a_ref[...], b_ref[:, cols]).astype(BF16)
                if n % 2 == 1:
                    line.pump(ready(limit), 1)

        await_loads(*glu_grad)
        glu_grad_rows(base_down, r.hid, r.gd, 0)
        if turn == 0:
            stats.stage(1)
        for part in range(SUPER):
            line.pump(ready(base_left), 1)
            mid_sum.middle(part)
        glu_grad_rows(base_left, grad_left_ref, r.n2, base_left)
        for part in range(SUPER):
            for h in range(2):
                line.pump(ready(base_right), 1)
                mid_sum.finish(part, h)
                for i in range(half // step_rows):
                    offset = (2 * part + h) * half + i * step_rows
                    rows = slice(offset, offset + step_rows)
                    total = mid_sum.total(part, h, i * step_rows, step_rows)
                    new = back_rows(total, r.mid[rows, :], r.g[rows, :])
                    r.gm[rows, :] = new
                    r.ga[aligned(own_start + offset, step_rows), :] = new.astype(BF16)
            second.start(part)
        mid_sum.drain()
        if turn == 0:
            stats.stage(2)
        glu_grad_rows(base_right, grad_right_ref, r.n2, base_right)
        if turn + 1 < layers:
            load(layer - 1, *glu_in, *glu_grad)
        if turn == 0:
            stats.stage(3)
        start = line.done
        beside = max(min(4, ready(base_out) - start), 0)
        line.done = start + beside

        @pl.loop(0, 4)
        def _(step):
            if beside > 0:
                @pl.when(step < beside)
                def _():
                    line.tick(start + step)
            @pl.when(step == 1)
            def _():
                for part in range(SUPER):
                    second.forward(part)
            for which in (1, 2, 3):
                @pl.when(step == which)
                def _():
                    for part in range(SUPER):
                        second.finish(part, which)
            member = place.member(step)
            for chunk in range(per_block):
                rows = aligned(member * block + chunk * 128, 128)
                grad_branch = nt(r.ga[rows, :], r.wo[...])
                gate = r.gate[rows, :]
                normed = r.heads[rows, :] * widen(r.scale[rows, :], local // 128)
                grad_normed = grad_branch * gate
                r.dx[rows, 3 * local : 4 * local] = (grad_branch * normed).astype(BF16)
                r.branch[rows, :] = (normed * gate).astype(BF16)
                r.gate[rows, :] = grad_normed
                row_sums(grad_normed * normed, r.inner, member * per_block + chunk)
        share.start()
        r.grads[base_out : base_out + local, :] = tn(r.branch[...], r.ga[...]).astype(BF16)
        line.pump(ready(base_gate), 1)

        def in_grad_rows(number, base):
            cols = slice(number * local, (number + 1) * local)
            for n in range(width // local):
                part_grad = tn(r.n1[:, n * local : (n + 1) * local], r.dx[:, cols])
                r.grads[base : base + local, n * local : (n + 1) * local] = part_grad.astype(BF16)

        await_loads("n1")
        in_grad_rows(3, base_gate)
        line.pump(ready(base_qkv), 1)
        await_loads(*attn_in)
        r.intot[...] = share.total() / width
        for chunk in range(length // 128):
            rows = slice(chunk * 128, (chunk + 1) * 128)
            scale = widen(r.scale[rows, :], local // 128)
            inner = widen(spread(r.intot[...], chunk), local // 128)
            normed = r.heads[rows, :] * scale
            r.dh[rows, :] = (scale * (r.gate[rows, :] - normed * inner)).astype(BF16)
        share.drain()
        second.drain()
        if turn + 1 < layers:
            load(layer - 1, *out_in)
        start = line.done
        beside = max(min(heads_here, ready(base_qkv) - start), 0)
        line.done = start + beside

        @pl.loop(0, heads_here)
        def _(head):
            if beside > 0:
                @pl.when(head < beside)
                def _():
                    line.tick(start + head)
            wide = aligned(head * 2 * HDIM, 2 * HDIM)
            thin = aligned(head * HDIM, HDIM)
            for col_tile in range(tiles_here):
                cols = slice(col_tile * size, (col_tile + 1) * size)
                keys = r.k[cols, wide]
                values = r.v[cols, thin]
                acc_key, acc_value = None, None
                for row_tile in range(col_tile, tiles_here):
                    rows = slice(row_tile * size, (row_tile + 1) * size)
                    queries = r.q[rows, wide]
                    grads = r.dh[rows, thin]
                    weight = tile_weight(r, first_head, head, row_tile, col_tile, size)
                    scores = (nt(queries, keys) * weight).astype(BF16)
                    pulled = (nt(grads, values) * weight).astype(BF16)
                    term = nn(pulled, keys)
                    if col_tile == 0:
                        r.dq[rows, :] = term
                    else:
                        r.dq[rows, :] += term
                    key_term = tn(pulled, queries)
                    value_term = tn(scores, grads)
                    acc_key = key_term if acc_key is None else acc_key + key_term
                    acc_value = value_term if acc_value is None else acc_value + value_term
                r.dk[cols, :] = acc_key
                r.dx[cols, aligned(2 * local + head * HDIM, HDIM)] = acc_value.astype(BF16)
            for row_tile in range(tiles_here):
                rows = slice(row_tile * size, (row_tile + 1) * size)
                cosine, sine = r.cos[rows, :], r.sin[rows, :]
                for grad, lin, base in ((r.dq, r.ql, 0), (r.dk, r.kl, local)):
                    v = lin[rows, thin].astype(F32)
                    gate = 1.0 / (1.0 + jnp.exp(-v))
                    back = grad[rows, :HDIM] * cosine + grad[rows, HDIM:] * sine
                    back = back * (gate + v * gate * (1.0 - gate))
                    r.dx[rows, aligned(base + head * HDIM, HDIM)] = back.astype(BF16)

        if turn + 1 < layers:
            load(layer - 1, *attn_in)
        await_loads(*in_in)
        for part in range(SUPER):
            for step in (3, 1, 2, 0):
                rows = aligned(place.member(step) * block + part * part_rows, part_rows)
                total = None
                for n, w in enumerate((r.wq, r.wk, r.wv, r.wg)):
                    term = nt(r.dx[rows, n * local : (n + 1) * local], w[...])
                    total = term if total is None else total + term
                r.part[rows, :] = total.astype(BF16)
                in_sum.send_block(part, step)
            line.pump(ready(base_qkv), 1)
        for number in range(3):
            in_grad_rows(number, base_qkv + number * local)
            if number < SUPER:
                in_sum.middle(number)
            line.pump(ready(base_qkv + (number + 1) * local), 1)
        if turn + 1 < layers:
            load(layer - 1, *in_in, "n1")
        for part in range(SUPER):
            for h in range(2):
                line.pump(ready(cfg.chunks * CHUNK), 1)
                in_sum.finish(part, h)
                for i in range(half // step_rows):
                    offset = (2 * part + h) * half + i * step_rows
                    rows = slice(offset, offset + step_rows)
                    total = in_sum.total(part, h, i * step_rows, step_rows)
                    values = getattr(r, "x%d" % layer)[rows, :].astype(F32)
                    new = back_rows(total, values, r.gm[rows, :])
                    if layer > 0:
                        r.g[rows, :] = new
                        r.gd[aligned(own_start + offset, step_rows), :] = new.astype(BF16)
                    else:
                        r.go[rows, :] = new.astype(BF16)
            if layer > 0:
                firsts[layer - 1].start(part)
        in_sum.drain()
    stats.finish()
    line.finish()


def call_kernel(body, cfg, inputs, outputs, scratch, collective_id, name):
    vmem, anywhere = pl.BlockSpec(memory_space=pltpu.VMEM), pl.BlockSpec(memory_space=pl.ANY)
    names = list(inputs) + list(outputs) + list(scratch)
    result = pl.pallas_call(
        functools.partial(body, cfg, names),
        out_shape=[shape for shape, _ in outputs.values()],
        in_specs=[vmem if placed else anywhere for _, placed in inputs.values()],
        out_specs=[vmem if placed else anywhere for _, placed in outputs.values()],
        scratch_shapes=list(scratch.values()),
        compiler_params=pltpu.CompilerParams(
            collective_id=collective_id, has_side_effects=True, vmem_limit_bytes=VMEM_LIMIT
        ),
        name=name,
    )(*[array for array, _ in inputs.values()])
    return dict(zip(outputs, result))


def collective_scratch(cfg, copies, lead):
    dma = pltpu.SemaphoreType.DMA
    half = cfg.block // (2 * SUPER)
    out = {}
    for name in ("ag1", "ag2", "rs1", "rs2"):
        out[name + "_send"] = dma((*lead, SUPER, 6))
        out[name + "_recv"] = dma((*lead, SUPER, 6))
    for name in copies:
        out["land" + name] = pltpu.VMEM((SUPER, 6, half, cfg.width), BF16)
        out["part" + name] = pltpu.VMEM((cfg.length, cfg.width), BF16)
    out["local_sem"] = dma((64,))
    return out


def weight_scratch(cfg):
    v = pltpu.VMEM
    return dict(
        wq=v((cfg.width, cfg.local), BF16), wk=v((cfg.width, cfg.local), BF16),
        wv=v((cfg.width, cfg.local), BF16), wg=v((cfg.width, cfg.local), BF16),
        wo=v((cfg.local, cfg.width), BF16), wl=v((cfg.ff, cfg.width), BF16),
        wr=v((cfg.ff, cfg.width), BF16), wd=v((cfg.ff, cfg.width), BF16),
    )


def table_scratch(cfg):
    v = pltpu.VMEM
    return dict(
        segc=v((cfg.length, 128), F32), segf=v((8, 128), F32),
        tiles=v((cfg.heads_here, 2, cfg.block, cfg.block), F32),
    )


def run_forward(cfg, x, tables, weights):
    v, dma, s = pltpu.VMEM, pltpu.SemaphoreType.DMA, jax.ShapeDtypeStruct
    rows, wide, local, ff, block = cfg.length, cfg.width, cfg.local, cfg.ff, cfg.block
    inputs = dict(x=(x, True), **{k: (a, True) for k, a in tables.items()}, **{k + "_h": (a, False) for k, a in weights.items()})
    kept = dict(
        n1=((rows, wide), BF16), ql=((rows, local), BF16), kl=((rows, local), BF16),
        q=((rows, 2 * local), BF16), k=((rows, 2 * local), BF16), v=((rows, local), BF16),
        gate=((rows, local), F32), heads=((rows, local), F32), mid=((block, wide), F32),
        n2=((rows, wide), BF16), left=((rows, ff), BF16), right=((rows, ff), BF16), hid=((rows, ff), BF16),
    )
    outputs = dict(
        xo=(s((block, wide), F32), True), stat=(s((8, 128), F32), True), ss_h=(s((8, 128), F32), False),
        **{k + "_h": (s(*a), False) for k, a in kept.items()},
    )
    scratch = dict(
        **weight_scratch(cfg), **collective_scratch(cfg, ("1", "2"), ()), **table_scratch(cfg),
        **{k: v(*a) for k, a in kept.items()}, u=v((rows, local), BF16), stat_wide=v((8, wide), F32),
        ss=v((8, 128), F32), sstot=v((8, 128), F32), scale=v((block, 128), F32),
        ss_land=v((3, 8, 128), F32), ss_send=dma((3,)), ss_recv=dma((3,)),
    )
    return call_kernel(fwd_kernel, cfg, inputs, outputs, scratch, cfg.layer, "layer_forward")


SAVED = ("ss", "mid", "n1", "ql", "kl", "q", "k", "v", "gate", "heads", "n2", "left", "right", "hid")


def run_backward(cfg, upstream, xs, saved, tables, weights):
    v, dma, s = pltpu.VMEM, pltpu.SemaphoreType.DMA, jax.ShapeDtypeStruct
    rows, wide, local, ff, block = cfg.length, cfg.width, cfg.local, cfg.ff, cfg.block
    inputs = dict(up=(upstream, True), **{k: (a, True) for k, a in tables.items()}, **{k + "_h": (a, False) for k, a in weights.items()})
    for layer in range(cfg.layers):
        inputs["x%d" % layer] = (xs[layer], True)
        inputs["stat%d" % layer] = (saved[layer]["stat"], True)
        for key in SAVED:
            inputs["%s%d_h" % (key, layer)] = (saved[layer][key + "_h"], False)
    total_rows = cfg.chunks * CHUNK
    outputs = dict(
        go=(s((block, wide), BF16), True), stat_total=(s((8, 128), F32), True),
        out_h=(s((cfg.layers * total_rows, wide), BF16), False),
    )
    small, ring, ring_sem = v((8, 128), F32), v((SLOTS, CHUNK // 2, wide), BF16), dma((SLOTS,))
    scratch = dict(
        **weight_scratch(cfg), **collective_scratch(cfg, ("",), (cfg.layers,)), **table_scratch(cfg),
        n1=v((rows, wide), BF16), ql=v((rows, local), BF16), kl=v((rows, local), BF16),
        q=v((rows, 2 * local), BF16), k=v((rows, 2 * local), BF16), v=v((rows, local), BF16),
        gate=v((rows, local), F32), heads=v((rows, local), F32), n2=v((rows, wide), BF16),
        left=v((rows, ff), BF16), right=v((rows, ff), BF16), hid=v((rows, ff), BF16),
        gd=v((rows, wide), BF16), ga=v((rows, wide), BF16),
        g=v((block, wide), F32), gm=v((block, wide), F32), mid=v((block, wide), F32),
        dh=v((rows, local), BF16), branch=v((rows, local), BF16), dx=v((rows, 4 * local), BF16),
        dq=v((rows, 2 * HDIM), F32), dk=v((rows, 2 * HDIM), F32),
        grads=v((total_rows, wide), BF16), scale=v((rows, 128), F32),
        ss=small, inner=small, intot=small,
        inner_land=v((cfg.layers, 3, 8, 128), F32), in_send=dma((cfg.layers, 3)), in_recv=dma((cfg.layers, 3)),
        pair_land=ring, right_land=ring, left_land=ring,
        pair_send=ring_sem, pair_recv=ring_sem, right_send=ring_sem, right_recv=ring_sem, left_send=ring_sem,
        left_recv=ring_sem, give_send=ring_sem, give_recv=ring_sem, keep_sem=ring_sem,
        stat_mine=small, stat_square=small, stat_pair=small, stat_right=small, stat_left=small,
        stat_land=v((3, 8, 128), F32), st_send=dma((3,)), st_recv=dma((3,)),
        line_land=v((3, 8, 128), F32), line_send=dma((3,)), line_recv=dma((3,)),
    )
    return call_kernel(bwd_kernel, cfg, inputs, outputs, scratch, cfg.layers, "layers_backward")


def per_device_square(
    tokens, upstream, segment_ids, query_proj, key_proj, value_proj, gate_proj, output_proj, left_proj, right_proj, down_proj
):
    layers = query_proj.shape[0]
    block, width = tokens.shape
    length = segment_ids.shape[0]
    local, ff = query_proj.shape[2], left_proj.shape[2]
    heads_here = local // HDIM
    positions = np.arange(length, dtype=np.float32)
    frequency = np.exp(np.float32(-math.log(10000.0)) * np.arange(HDIM, dtype=np.float32) / np.float32(HDIM))
    angles = positions[:, None] * frequency[None, :]
    slopes = np.exp2(-8.0 * (np.arange(HEADS) + 1.0) / HEADS)
    decays = np.concatenate([-slopes * (1.0 - depth_start - depth_step * layer) for layer in range(layers)])
    tables = dict(
        cos=jnp.asarray(np.cos(angles)), sin=jnp.asarray(np.sin(angles)),
        dec=jnp.asarray(np.broadcast_to(decays[:, None], (layers * HEADS, 128)).astype(np.float32)),
        seg=segment_ids.reshape(8, length // 8),
    )
    weights = dict(
        wq=query_proj, wk=key_proj, wv=value_proj, wg=gate_proj, wo=output_proj,
        wl=jnp.swapaxes(left_proj, 1, 2), wr=jnp.swapaxes(right_proj, 1, 2), wd=down_proj,
    )
    ends = np.cumsum([0, ff, ff, ff, local, local, 3 * local]).tolist()
    common = dict(
        layers=layers, block=block, length=length, width=width, local=local, ff=ff, heads_here=heads_here,
        pairs=lax.axis_size("dp") // 2, bases=ends, chunks=-(-ends[-1] // CHUNK),
    )
    current, xs, saved = tokens, [], []
    for layer in range(layers):
        xs.append(current)
        saved.append(run_forward(types.SimpleNamespace(layer=layer, **common), current, tables, weights))
        current = saved[-1]["xo"]
    final_rows = current.astype(BF16)
    back = run_backward(types.SimpleNamespace(**common), upstream, xs, saved, tables, weights)
    stats = jnp.sum(back["stat_total"][: 3 * layers], axis=1).reshape(layers, 3)
    rms_stats = jnp.sqrt(stats / (length * lax.axis_size("dp") * width))
    grads = back["out_h"].reshape(layers, -1, width)

    def rows(number):
        return grads[:, ends[number] : ends[number + 1]]

    def unfold(start):
        piece = grads[:, start : start + local].reshape(layers, local, width // local, local)
        return piece.transpose(0, 2, 1, 3).reshape(layers, width, local).astype(F32)

    return (
        final_rows,
        back["go"],
        *[unfold(ends[5] + number * local) for number in range(3)],
        unfold(ends[4]),
        rows(3).astype(F32),
        jnp.swapaxes(rows(1).astype(F32), 1, 2),
        jnp.swapaxes(rows(2).astype(F32), 1, 2),
        rows(0).astype(F32),
        rms_stats,
    )


def solution(mesh):
    square = dict(mesh.shape) == SQUARE_MESH
    body = per_device_square if square else per_device
    return jax.shard_map(
        body,
        mesh=mesh,
        in_specs=(
            P(("dp", "tensor"), None),
            P(("dp", "tensor"), None),
            P("dp"),
            P(None, None, "tensor"),
            P(None, None, "tensor"),
            P(None, None, "tensor"),
            P(None, None, "tensor"),
            P(None, "tensor", None),
            P(None, None, "tensor"),
            P(None, None, "tensor"),
            P(None, "tensor", None),
        ),
        out_specs=(
            P(("dp", "tensor"), None),
            P(("dp", "tensor"), None),
            P(None, None, "tensor"),
            P(None, None, "tensor"),
            P(None, None, "tensor"),
            P(None, None, "tensor"),
            P(None, "tensor", None),
            P(None, None, "tensor"),
            P(None, None, "tensor"),
            P(None, "tensor", None),
            P(),
        ),
        check_vma=False,
    )
```

```python
import functools
import math
import types

import jax
import jax.numpy as jnp
import numpy as np
from jax import lax
from jax.experimental import pallas as pl
from jax.experimental.pallas import tpu as pltpu
from jax.sharding import PartitionSpec as P

HEADS = 8
HDIM = 128
BLK = 512


epsilon = 1e-06
depth_start = 0.5
depth_step = 1.0 / 24.0
highest = lax.Precision.HIGHEST


def rms_rows(values):
    return values * lax.rsqrt(jnp.mean(values * values, axis=1, keepdims=True) + epsilon)


def rms_back(values, gradient):
    scaling = lax.rsqrt(jnp.mean(values * values, axis=1, keepdims=True) + epsilon)
    normed = values * scaling
    return scaling * (gradient - normed * jnp.mean(gradient * normed, axis=1, keepdims=True))


def contract_last(left_part, right_part):
    return lax.dot_general(
        left_part, right_part, (((1,), (1,)), ((), ())), preferred_element_type=jnp.float32
    )


def contract_first(left_part, right_part):
    return lax.dot_general(
        left_part, right_part, (((0,), (0,)), ((), ())), preferred_element_type=jnp.float32
    )


def rotate(values, cosine, sine_table):
    return jnp.concatenate([values * cosine[:, None, :], values * sine_table[:, None, :]], axis=2)


def unrotate(gradient, cosine, sine_table):
    half_width = gradient.shape[2] // 2
    return (
        gradient[:, :, :half_width] * cosine[:, None, :]
        + gradient[:, :, half_width:] * sine_table[:, None, :]
    )


def split_blocks(array, block_count):
    return array.reshape((block_count, BLK) + array.shape[1:])


def block_weights(seg_block, next_seg, decay_log):
    block_width = seg_block.shape[0]
    places = jnp.arange(block_width, dtype=jnp.float32)
    distance = places[:, None] - places[None, :]
    allowed = (distance >= 0) & (seg_block[:, None] == seg_block[None, :])
    decay_grid = jnp.where(
        allowed[None], jnp.exp(decay_log[:, None, None] * jnp.maximum(distance, 0.0)[None]), 0.0
    )
    first_seg = seg_block[0]
    query_gain = jnp.where(
        (seg_block == first_seg)[:, None], jnp.exp(places[:, None] * decay_log[None, :]), 0.0
    )
    key_gain = jnp.where(
        (seg_block == next_seg)[:, None],
        jnp.exp((block_width - places)[:, None] * decay_log[None, :]),
        0.0,
    )
    carry_gain = jnp.where(first_seg == next_seg, jnp.exp(decay_log * block_width), 0.0)
    return (decay_grid, query_gain, key_gain, carry_gain)


def next_segments(segments, block_count):
    seg_blocks = segments.reshape(block_count, BLK)
    return (seg_blocks, jnp.concatenate([seg_blocks[1:, 0], jnp.full((1,), -1, jnp.int32)]))


def attend_forward(queries, keys_rot, values, segments, decay_log):
    length, heads_here, pair_width = queries.shape
    block_count = length // BLK
    seg_blocks, next_segs = next_segments(segments, block_count)

    def advance(state_now, block_items):
        query_block, key_block, value_block, seg_block, next_seg = block_items
        query_float = query_block.astype(jnp.float32)
        key_float = key_block.astype(jnp.float32)
        value_float = value_block.astype(jnp.float32)
        decay_grid, query_gain, key_gain, carry_gain = block_weights(seg_block, next_seg, decay_log)
        scores = (
            jnp.einsum("rhd,shd->hrs", query_block, key_block, preferred_element_type=jnp.float32)
            * decay_grid
        )
        block_out = jnp.einsum("hrs,she->rhe", scores, value_float, precision=highest)
        block_out = (
            block_out
            + jnp.einsum("rhd,hde->rhe", query_float, state_now, precision=highest)
            * query_gain[:, :, None]
        )
        new_state = carry_gain[:, None, None] * state_now + jnp.einsum(
            "shd,she->hde", key_float * key_gain[:, :, None], value_float, precision=highest
        )
        return (new_state, (block_out, state_now))

    zero_state = jnp.zeros((heads_here, pair_width, pair_width // 2), jnp.float32)
    _, (block_outs, states) = lax.scan(
        advance,
        zero_state,
        (
            split_blocks(queries, block_count),
            split_blocks(keys_rot, block_count),
            split_blocks(values, block_count),
            seg_blocks,
            next_segs,
        ),
    )
    return (block_outs.reshape(length, heads_here * (pair_width // 2)), states)


def attend_backward(queries, keys_rot, values, segments, decay_log, states, grad_heads):
    length, heads_here, pair_width = queries.shape
    block_count = length // BLK
    seg_blocks, next_segs = next_segments(segments, block_count)

    def retreat(later_grad, block_items):
        query_block, key_block, value_block, seg_block, next_seg, state_now, grad_block = (
            block_items
        )
        query_float = query_block.astype(jnp.float32)
        key_float = key_block.astype(jnp.float32)
        value_float = value_block.astype(jnp.float32)
        decay_grid, query_gain, key_gain, carry_gain = block_weights(seg_block, next_seg, decay_log)
        scores = (
            jnp.einsum("rhd,shd->hrs", query_block, key_block, preferred_element_type=jnp.float32)
            * decay_grid
        )
        pulled = jnp.einsum("rhe,she->hrs", grad_block, value_float, precision=highest) * decay_grid
        grad_query = jnp.einsum("hrs,shd->rhd", pulled, key_float, precision=highest)
        grad_query = (
            grad_query
            + jnp.einsum("rhe,hde->rhd", grad_block, state_now, precision=highest)
            * query_gain[:, :, None]
        )
        grad_key = jnp.einsum("hrs,rhd->shd", pulled, query_float, precision=highest)
        grad_key = (
            grad_key
            + jnp.einsum("she,hde->shd", value_float, later_grad, precision=highest)
            * key_gain[:, :, None]
        )
        grad_value = jnp.einsum("hrs,rhe->she", scores, grad_block, precision=highest)
        grad_value = (
            grad_value
            + jnp.einsum("shd,hde->she", key_float, later_grad, precision=highest)
            * key_gain[:, :, None]
        )
        earlier_grad = carry_gain[:, None, None] * later_grad + jnp.einsum(
            "rhd,rhe->hde", query_float * query_gain[:, :, None], grad_block, precision=highest
        )
        return (earlier_grad, (grad_query, grad_key, grad_value))

    zero_state = jnp.zeros((heads_here, pair_width, pair_width // 2), jnp.float32)
    _, (grad_query, grad_key, grad_value) = lax.scan(
        retreat,
        zero_state,
        (
            split_blocks(queries, block_count),
            split_blocks(keys_rot, block_count),
            split_blocks(values, block_count),
            seg_blocks,
            next_segs,
            states,
            split_blocks(grad_heads, block_count),
        ),
        reverse=True,
    )
    return (
        grad_query.reshape(length, heads_here, pair_width),
        grad_key.reshape(length, heads_here, pair_width),
        grad_value.reshape(length, heads_here, pair_width // 2),
    )


def per_device(
    tokens,
    upstream,
    segment_ids,
    query_proj,
    key_proj,
    value_proj,
    gate_proj,
    output_proj,
    left_proj,
    right_proj,
    down_proj,
):
    layers = query_proj.shape[0]
    row_count, model_width = tokens.shape
    length = segment_ids.shape[0]
    local_width = query_proj.shape[2]
    ff_local = left_proj.shape[2]
    heads_here = local_width // HDIM
    positions = jnp.arange(length, dtype=jnp.float32)
    frequency = jnp.exp(-math.log(10000.0) * jnp.arange(HDIM, dtype=jnp.float32) / HDIM)
    angles = positions[:, None] * frequency[None, :]
    cosine = jnp.cos(angles)
    sine_table = jnp.sin(angles)
    head_index = (lax.axis_index("tensor") * heads_here + jnp.arange(heads_here)).astype(
        jnp.float32
    )
    slopes = jnp.exp2(-8.0 * (head_index + 1.0) / HEADS)

    def gather_normed(normed):
        return lax.all_gather(normed, "tensor", axis=0, tiled=True)

    def gather_again(normed):
        return lax.all_gather(normed, "tensor", axis=0, tiled=True)

    def gather_grads(gradient):
        return lax.all_gather(gradient, "tensor", axis=0, tiled=True)

    def branch_sum(operand, matrix):
        return lax.psum_scatter(
            jnp.dot(operand, matrix, preferred_element_type=jnp.float32).astype(jnp.bfloat16),
            "tensor",
            scatter_dimension=0,
            tiled=True,
        ).astype(jnp.float32)

    def input_sum(pieces, matrix):
        operand = jnp.concatenate(pieces, axis=1)
        return lax.psum_scatter(
            contract_last(operand, matrix).astype(jnp.bfloat16),
            "tensor",
            scatter_dimension=0,
            tiled=True,
        ).astype(jnp.float32)

    current = tokens.astype(jnp.float32)
    saved_layers = []
    stat_terms = []
    for layer_index in range(layers):
        residual = current
        normed = rms_rows(residual).astype(jnp.bfloat16)
        full_normed = gather_normed(normed)
        attn_weight = jnp.concatenate(
            [
                query_proj[layer_index],
                key_proj[layer_index],
                value_proj[layer_index],
                gate_proj[layer_index],
            ],
            axis=1,
        )
        projected = jnp.dot(full_normed, attn_weight, preferred_element_type=jnp.float32)
        query_lin = projected[:, :local_width]
        key_lin = projected[:, local_width : 2 * local_width]
        values = (
            projected[:, 2 * local_width : 3 * local_width]
            .astype(jnp.bfloat16)
            .reshape(length, heads_here, HDIM)
        )
        gate_lin = projected[:, 3 * local_width :]
        queries = rotate(
            jax.nn.silu(query_lin).reshape(length, heads_here, HDIM), cosine, sine_table
        ).astype(jnp.bfloat16)
        keys_rot = rotate(
            jax.nn.silu(key_lin).reshape(length, heads_here, HDIM), cosine, sine_table
        ).astype(jnp.bfloat16)
        decay_log = -slopes * (1.0 - depth_start - depth_step * layer_index)
        heads_out, states = attend_forward(queries, keys_rot, values, segment_ids, decay_log)
        squares = lax.psum(jnp.sum(heads_out * heads_out, axis=1), "tensor")
        scaling = lax.rsqrt(squares / model_width + epsilon)[:, None]
        normed_heads = heads_out * scaling
        branch = (normed_heads * gate_lin).astype(jnp.bfloat16)
        attn_rows = branch_sum(branch, output_proj[layer_index])
        middle = residual + attn_rows
        normed_mid = rms_rows(middle).astype(jnp.bfloat16)
        full_mid = gather_normed(normed_mid)
        glu_weight = jnp.concatenate([left_proj[layer_index], right_proj[layer_index]], axis=1)
        gates_both = jnp.dot(full_mid, glu_weight, preferred_element_type=jnp.float32)
        left_lin = gates_both[:, :ff_local]
        right_lin = gates_both[:, ff_local:]
        hidden = (left_lin * right_lin).astype(jnp.bfloat16)
        glu_rows = branch_sum(hidden, down_proj[layer_index])
        current = middle + glu_rows
        stat_terms.append(
            jnp.stack(
                [
                    jnp.sum(attn_rows * attn_rows),
                    jnp.sum(glu_rows * glu_rows),
                    jnp.sum(current * current),
                ]
            )
        )
        saved_layers.append(
            (
                residual,
                middle,
                normed,
                normed_mid,
                full_normed,
                full_mid,
                attn_weight,
                glu_weight,
                query_lin,
                key_lin,
                gate_lin,
                queries,
                keys_rot,
                values,
                decay_log,
                states,
                normed_heads,
                scaling,
                branch,
                left_lin,
                right_lin,
                hidden,
            )
        )
    stat_sums = lax.psum(jnp.stack(stat_terms), ("dp", "tensor"))
    rms_stats = jnp.sqrt(stat_sums / (length * lax.axis_size("dp") * model_width))
    final_rows = current.astype(jnp.bfloat16)
    gradient = upstream.astype(jnp.float32)
    layer_results = [None] * layers
    for layer_index in reversed(range(layers)):
        (
            residual,
            middle,
            normed,
            normed_mid,
            full_normed,
            full_mid,
            attn_weight,
            glu_weight,
            query_lin,
            key_lin,
            gate_lin,
            queries,
            keys_rot,
            values,
            decay_log,
            states,
            normed_heads,
            scaling,
            branch,
            left_lin,
            right_lin,
            hidden,
        ) = saved_layers[layer_index]
        glu_grad = gather_grads(gradient.astype(jnp.bfloat16))
        grad_hidden = contract_last(glu_grad, down_proj[layer_index])
        down_part = contract_first(hidden, glu_grad)
        grad_left = (grad_hidden * right_lin).astype(jnp.bfloat16)
        grad_right = (grad_hidden * left_lin).astype(jnp.bfloat16)
        grad_gates = jnp.concatenate([grad_left, grad_right], axis=1)
        mid_rows = input_sum((grad_left, grad_right), glu_weight)
        source_mid = gather_again(normed_mid)
        glu_part = contract_first(source_mid, grad_gates)
        gradient = gradient + rms_back(middle, mid_rows)
        attn_grad = gather_grads(gradient.astype(jnp.bfloat16))
        output_part = contract_first(branch, attn_grad)
        grad_branch = contract_last(attn_grad, output_proj[layer_index])
        grad_normed = grad_branch * gate_lin
        grad_gate = (grad_branch * normed_heads).astype(jnp.bfloat16)
        inner_sum = lax.psum(jnp.sum(grad_normed * normed_heads, axis=1), "tensor")
        grad_heads = scaling * (grad_normed - normed_heads * (inner_sum / model_width)[:, None])
        grad_query, grad_key, grad_value = attend_backward(
            queries,
            keys_rot,
            values,
            segment_ids,
            decay_log,
            states,
            grad_heads.reshape(length, heads_here, HDIM),
        )
        sigmoid_query = jax.nn.sigmoid(query_lin)
        sigmoid_key = jax.nn.sigmoid(key_lin)
        query_back = unrotate(grad_query, cosine, sine_table).reshape(length, local_width)
        key_back = unrotate(grad_key, cosine, sine_table).reshape(length, local_width)
        grad_query_lin = (
            query_back * (sigmoid_query + query_lin * sigmoid_query * (1.0 - sigmoid_query))
        ).astype(jnp.bfloat16)
        grad_key_lin = (
            key_back * (sigmoid_key + key_lin * sigmoid_key * (1.0 - sigmoid_key))
        ).astype(jnp.bfloat16)
        grad_value_lin = grad_value.reshape(length, local_width).astype(jnp.bfloat16)
        grad_projected = jnp.concatenate(
            [grad_query_lin, grad_key_lin, grad_value_lin, grad_gate], axis=1
        )
        in_rows = input_sum((grad_query_lin, grad_key_lin, grad_value_lin, grad_gate), attn_weight)
        source_normed = gather_again(normed)
        attn_part = contract_first(source_normed, grad_projected)
        gradient = gradient + rms_back(residual, in_rows)
        query_part = attn_part[:, :local_width]
        key_part = attn_part[:, local_width : 2 * local_width]
        value_part = attn_part[:, 2 * local_width : 3 * local_width]
        gate_part = attn_part[:, 3 * local_width :]
        left_part = glu_part[:, :ff_local]
        right_part = glu_part[:, ff_local:]
        layer_results[layer_index] = (
            query_part,
            key_part,
            value_part,
            gate_part,
            output_part,
            left_part,
            right_part,
            down_part,
        )
    stacked = [
        jnp.stack([layer_results[index][member] for index in range(layers)]) for member in range(8)
    ]
    totals = (
        lax.psum(stacked[0].astype(jnp.bfloat16), "dp").astype(jnp.float32),
        lax.psum(stacked[1].astype(jnp.bfloat16), "dp").astype(jnp.float32),
        lax.psum(stacked[2].astype(jnp.bfloat16), "dp").astype(jnp.float32),
        lax.psum(stacked[3].astype(jnp.bfloat16), "dp").astype(jnp.float32),
        lax.psum(stacked[4].astype(jnp.bfloat16), "dp").astype(jnp.float32),
        lax.psum(stacked[5].astype(jnp.bfloat16), "dp").astype(jnp.float32),
        lax.psum(stacked[6].astype(jnp.bfloat16), "dp").astype(jnp.float32),
        lax.psum(stacked[7].astype(jnp.bfloat16), "dp").astype(jnp.float32),
    )
    input_grad = gradient.astype(jnp.bfloat16)
    return (
        final_rows,
        input_grad,
        totals[0],
        totals[1],
        totals[2],
        totals[3],
        totals[4],
        totals[5],
        totals[6],
        totals[7],
        rms_stats,
    )


SQUARE_MESH = {"dp": 8, "tensor": 4}


F32 = jnp.float32
BF16 = jnp.bfloat16
MESH = pl.DeviceIdType.MESH
VMEM_LIMIT = 60 * 2**20
SUPER = 2
CHUNK = 128
HOP = 4
SLOTS = 20


def nn(a, b):
    return lax.dot_general(a, b, (((1,), (0,)), ((), ())), preferred_element_type=F32)


def nt(a, b):
    return lax.dot_general(a, b, (((1,), (1,)), ((), ())), preferred_element_type=F32)


def tn(a, b):
    return lax.dot_general(a, b, (((0,), (0,)), ((), ())), preferred_element_type=F32)


def exact(a, b, dims):
    return lax.dot_general(a, b, (dims, ((), ())), precision=highest, preferred_element_type=F32)


def aligned(index, size):
    return pl.ds(pl.multiple_of(index, size), size)


class Place:
    def __init__(self, pairs):
        self.dp = lax.axis_index("dp")
        self.me = lax.axis_index("tensor")
        self.low = lax.rem(self.me, 2)
        self.high = self.me // 2
        self.core = lax.rem(self.dp, 2)
        self.at = self.dp // 2
        self.last = pairs - 1

    def member(self, step):
        low = lax.rem(self.low + lax.rem(step, 2), 2)
        high = lax.rem(self.high + step // 2, 2)
        return 2 * high + low

    def device(self, step):
        return (self.dp, self.member(step))

    def partner(self):
        return (self.dp + 1 - 2 * self.core, self.me)

    def right(self):
        return (self.dp + 2, self.me)

    def left(self):
        return (self.dp - 2, self.me)

    def greet(self, line):
        barrier = pltpu.get_barrier_semaphore()

        def signal(device):
            pl.semaphore_signal(barrier, inc=1, device_id=device, device_id_type=MESH)

        for step in (1, 2, 3):
            signal(self.device(step))
        if not line:
            pl.semaphore_wait(barrier, 3)
            return
        signal(self.partner())

        @pl.when(self.at < self.last)
        def _():
            signal(self.right())

        @pl.when(self.at > 0)
        def _():
            signal(self.left())

        pl.semaphore_wait(barrier, 4 + jnp.minimum(self.at, 1) + jnp.minimum(self.last - self.at, 1))


class Wire:
    def __init__(self, device, send_sem, recv_sem, source, target, landing):
        self.source, self.target, self.landing = source, target, landing
        self.common = dict(send_sem=send_sem, recv_sem=recv_sem, device_id=device, device_id_type=MESH)

    def out(self):
        return pltpu.make_async_remote_copy(src_ref=self.source, dst_ref=self.target, **self.common)

    def start(self):
        self.out().start()

    def wait_recv(self):
        pltpu.make_async_remote_copy(src_ref=self.landing, dst_ref=self.landing, **self.common).wait_recv()

    def wait_send(self):
        self.out().wait_send()


class Gather:
    def __init__(self, place, buf, send, recv, block):
        self.place, self.buf, self.block = place, buf, block
        self.send, self.recv = send, recv
        self.half = block // (2 * SUPER)

    def rows(self, step, part, half):
        start = self.place.member(step) * self.block + (2 * part + half) * self.half
        return self.buf.at[aligned(start, self.half)]

    def wire(self, part, number):
        step, owner, half = ((1, 0, 0), (2, 0, 1), (1, 0, 1), (2, 0, 0), (2, 1, 0), (1, 2, 1))[number]
        source = self.rows(owner, part, half)
        landing = self.rows((0, 1, 2, 3)[owner ^ step], part, half)
        return Wire(self.place.device(step), self.send.at[part, number], self.recv.at[part, number], source, source, landing)

    def start(self, part):
        for number in range(4):
            self.wire(part, number).start()

    def forward(self, part):
        self.wire(part, 0).wait_recv()
        self.wire(part, 4).start()
        self.wire(part, 1).wait_recv()
        self.wire(part, 5).start()

    def finish(self, part, step):
        for number in {0: (), 1: (2,), 2: (3,), 3: (4, 5)}[step]:
            self.wire(part, number).wait_recv()

    def drain(self):
        for part in range(SUPER):
            for number in range(6):
                self.wire(part, number).wait_send()


def gather_stage(gather, block_fn, beside):
    @pl.loop(0, 4 * SUPER)
    def _(i):
        mixed = i - SUPER
        part = jnp.where(i < SUPER, i, jnp.where(i < 3 * SUPER, mixed // 2, i - 3 * SUPER))
        step = jnp.where(i < SUPER, 0, jnp.where(i < 3 * SUPER, 1 + lax.rem(mixed, 2), 3))

        @pl.when(i == SUPER)
        def _():
            for one in range(SUPER):
                beside(one)
                gather.forward(one)

        @pl.when(i == 3 * SUPER)
        def _():
            beside(SUPER)

        for which in (1, 2, 3):
            @pl.when(step == which)
            def _():
                gather.finish(part, which)
        block_fn(part, step)


class Scatter:
    def __init__(self, place, buf, land, send, recv, block):
        self.place, self.buf, self.land, self.block = place, buf, land, block
        self.send, self.recv = send, recv
        self.half = block // (2 * SUPER)

    def rows(self, step, part, half):
        start = self.place.member(step) * self.block + (2 * part + half) * self.half
        return aligned(start, self.half)

    def wire(self, part, number):
        step, owner, half = ((1, 3, 0), (1, 1, 0), (2, 3, 1), (2, 2, 1), (2, 2, 0), (1, 1, 1))[number]
        target = self.land.at[part, number]
        return Wire(
            self.place.device(step), self.send.at[part, number], self.recv.at[part, number],
            self.buf.at[self.rows(owner, part, half)], target, target,
        )

    def send_block(self, part, step):
        for number in {0: (), 1: (1,), 2: (3,), 3: (0, 2)}[step]:
            self.wire(part, number).start()

    def middle(self, part):
        for first, second, owner, half in ((0, 4, 2, 0), (2, 5, 1, 1)):
            self.wire(part, first).wait_recv()
            rows = self.rows(owner, part, half)
            self.buf[rows, :] = self.buf[rows, :] + self.land[part, first]
            self.wire(part, second).start()

    def finish(self, part, half):
        first, second = ((1, 4), (3, 5))[half]
        self.wire(part, first).wait_recv()
        self.wire(part, second).wait_recv()

    def total(self, part, half, start, count):
        first, second = ((1, 4), (3, 5))[half]
        own = self.place.me * self.block + (2 * part + half) * self.half + start
        rows = pl.ds(start, count)
        return (
            self.buf[aligned(own, count), :].astype(F32)
            + self.land[part, first, rows, :].astype(F32)
            + self.land[part, second, rows, :].astype(F32)
        )

    def drain(self):
        for part in range(SUPER):
            for number in range(6):
                self.wire(part, number).wait_send()


class Share:
    def __init__(self, place, mine, land, send, recv):
        self.wires = [
            Wire(place.device(step), send.at[step - 1], recv.at[step - 1], mine, land.at[step - 1], land.at[step - 1])
            for step in (1, 2, 3)
        ]
        self.mine, self.land = mine, land

    def start(self):
        for wire in self.wires:
            wire.start()

    def total(self):
        for wire in self.wires:
            wire.wait_recv()
        return self.mine[...] + self.land[0] + self.land[1] + self.land[2]

    def drain(self):
        for wire in self.wires:
            wire.wait_send()


class Local:
    def __init__(self, sems):
        self.sems, self.used = sems, 0

    def start(self, source, target):
        copy = pltpu.make_async_copy(source, target, self.sems.at[self.used])
        self.used += 1
        copy.start()
        return copy


def row_sums(values, target, chunk):
    sums = exact(jnp.ones((8, values.shape[1]), F32), values, ((1,), (1,)))
    target[pl.ds(chunk, 1), :] = sums[0:1, :]


def spread(sums, chunk):
    picked = (lax.broadcasted_iota(jnp.int32, (8, 128), 0) == chunk).astype(F32)
    return exact(sums, picked, ((0,), (0,)))


def widen(columns, times):
    return jnp.concatenate([columns] * times, axis=1)


def decay_tiles(dec_ref, first_head, tiles, heads_here, size):
    rows = lax.broadcasted_iota(jnp.int32, (size, size), 0)
    cols = lax.broadcasted_iota(jnp.int32, (size, size), 1)
    distance = (rows - cols).astype(F32)
    for head in range(heads_here):
        decay = dec_ref[pl.ds(first_head + head, 1), 0:1]
        tiles[head, 0] = jnp.where(rows >= cols, jnp.exp(decay * jnp.maximum(distance, 0.0)), 0.0)
        tiles[head, 1] = jnp.exp(decay * (distance + float(size)))


def spread_segments(r, length):
    r.segf[...] = r.seg[...].astype(F32)
    for chunk in range(length // 128):
        r.segc[chunk * 128 : (chunk + 1) * 128, :] = spread(r.segf[...], chunk)


def tile_weight(r, first_head, head, row_tile, col_tile, size):
    gap = row_tile - col_tile
    if gap == 0:
        weight = r.tiles[head, 0]
    else:
        weight = r.tiles[head, 1]
        if gap > 1:
            decay = r.dec[pl.ds(first_head + head, 1), 0:1]
            weight = weight * jnp.exp(decay * float(size * (gap - 1)))
    row_seg = widen(r.segc[row_tile * size : (row_tile + 1) * size, :], size // 128)
    per = size // 128
    col_seg = jnp.concatenate([r.segf[per * col_tile + i : per * col_tile + i + 1, :] for i in range(per)], axis=1)
    return jnp.where(row_seg == col_seg, weight, 0.0)


def namespace(names, refs):
    return types.SimpleNamespace(**dict(zip(names, refs)))


def fwd_kernel(cfg, names, *refs):
    r = namespace(names, refs)
    layer, block, length, width, local = cfg.layer, cfg.block, cfg.length, cfg.width, cfg.local
    heads_here, size = cfg.heads_here, cfg.block
    place = Place(cfg.pairs)
    first_head = layer * HEADS + place.me * heads_here
    copies = Local(r.local_sem)
    w_in = [copies.start(h.at[layer], v) for h, v in (
        (r.wq_h, r.wq), (r.wk_h, r.wk), (r.wv_h, r.wv), (r.wg_h, r.wg))]
    w_out = copies.start(r.wo_h.at[layer], r.wo)
    w_glu = [copies.start(h.at[layer], v) for h, v in ((r.wl_h, r.wl), (r.wr_h, r.wr), (r.wd_h, r.wd))]
    saves = []
    first = Gather(place, r.n1, r.ag1_send, r.ag1_recv, block)
    mid_sum = Scatter(place, r.part1, r.land1, r.rs1_send, r.rs1_recv, block)
    second = Gather(place, r.n2, r.ag2_send, r.ag2_recv, block)
    out_sum = Scatter(place, r.part2, r.land2, r.rs2_send, r.rs2_recv, block)
    share = Share(place, r.ss, r.ss_land, r.ss_send, r.ss_recv)
    third = Gather(place, r.gd, r.ag3_send, r.ag3_recv, block) if cfg.last else None
    if cfg.last:
        load_up = copies.start(r.up_h, r.gd.at[aligned(place.me * block, block), :])
    half, step_rows = first.half, 32
    own_start = place.me * block

    @pl.loop(0, block // step_rows)
    def _(i):
        rows = aligned(i * step_rows, step_rows)
        v = r.x[rows, :].astype(F32)
        scale = lax.rsqrt(jnp.mean(v * v, axis=1, keepdims=True) + epsilon)
        r.n1[aligned(own_start + i * step_rows, step_rows), :] = (v * scale).astype(BF16)

    place.greet(False)
    for part in range(SUPER):
        first.start(part)
    decay_tiles(r.dec, first_head, r.tiles, heads_here, size)
    spread_segments(r, length)
    for copy in w_in:
        copy.wait()

    @pl.loop(0, 4)
    def _(step):
        @pl.when(step == 1)
        def _():
            for part in range(SUPER):
                first.forward(part)
        for which in (1, 2, 3):
            @pl.when(step == which)
            def _():
                for part in range(SUPER):
                    first.finish(part, which)
        rows = aligned(place.member(step) * block, block)
        a = r.n1[rows, :]
        cosine, sine = r.cos[rows, :], r.sin[rows, :]
        for w, lin, rot in ((r.wq, r.ql, r.q), (r.wk, r.kl, r.k)):
            v = nn(a, w[...])
            lin[rows, :] = v.astype(BF16)
            v = v / (1.0 + jnp.exp(-v))
            for head in range(heads_here):
                one = v[:, head * HDIM : (head + 1) * HDIM]
                rot[rows, 2 * head * HDIM : (2 * head + 1) * HDIM] = (one * cosine).astype(BF16)
                rot[rows, (2 * head + 1) * HDIM : (2 * head + 2) * HDIM] = (one * sine).astype(BF16)
        r.v[rows, :] = nn(a, r.wv[...]).astype(BF16)
        r.gate[rows, :] = nn(a, r.wg[...])

    for v, h in ((r.n1, r.n1_h), (r.ql, r.ql_h), (r.kl, r.kl_h), (r.q, r.q_h), (r.k, r.k_h), (r.v, r.v_h), (r.gate, r.gate_h)):
        saves.append(copies.start(v, h))

    if cfg.last:
        load_up.wait()
        for part in range(SUPER):
            third.start(part)
    tiles_here = length // size

    @pl.loop(0, heads_here)
    def _(head):
        wide = aligned(head * 2 * HDIM, 2 * HDIM)
        thin = aligned(head * HDIM, HDIM)
        for row_tile in range(tiles_here):
            rows = slice(row_tile * size, (row_tile + 1) * size)
            queries = r.q[rows, wide]
            acc = None
            for col_tile in range(row_tile + 1):
                cols = slice(col_tile * size, (col_tile + 1) * size)
                weight = tile_weight(r, first_head, head, row_tile, col_tile, size)
                scores = (nt(queries, r.k[cols, wide]) * weight).astype(BF16)
                term = nn(scores, r.v[cols, thin])
                acc = term if acc is None else acc + term
            r.heads[rows, thin] = acc
            r.u[rows, thin] = (acc * r.gate[rows, thin]).astype(BF16)

    for chunk in range(length // 128):
        v = r.heads[chunk * 128 : (chunk + 1) * 128, :]
        row_sums(v * v, r.ss, chunk)
    share.start()
    saves.append(copies.start(r.heads, r.heads_h))
    if cfg.last:
        for part in range(SUPER):
            third.forward(part)
    w_out.wait()

    part_rows = 2 * half
    for part in range(SUPER):
        for step in (3, 1, 2, 0):
            rows = aligned(place.member(step) * block + part * part_rows, part_rows)
            r.part1[rows, :] = nn(r.u[rows, :], r.wo[...]).astype(BF16)
            mid_sum.send_block(part, step)
    for part in range(SUPER):
        mid_sum.middle(part)
    r.sstot[...] = share.total()
    saves.append(copies.start(r.sstot, r.ss_h))
    scaling = lax.rsqrt(r.sstot[...] / width + epsilon)
    per_block = block // 128
    for chunk in range(per_block):
        r.scale[chunk * 128 : (chunk + 1) * 128, :] = spread(scaling, place.me * per_block + chunk)
    r.stat_wide[...] = jnp.zeros_like(r.stat_wide)

    def add_stat(row, v):
        sums = jnp.sum(v * v, axis=0, keepdims=True)
        r.stat_wide[row : row + 1, :] += sums

    step_rows = min(32, half)
    for part in range(SUPER):
        for h in range(2):
            mid_sum.finish(part, h)
            for i in range(half // step_rows):
                offset = (2 * part + h) * half + i * step_rows
                scale = widen(r.scale[offset : offset + step_rows, :], width // 128)
                attn = mid_sum.total(part, h, i * step_rows, step_rows) * scale
                middle = r.x[offset : offset + step_rows, :].astype(F32) + attn
                r.mid[offset : offset + step_rows, :] = middle
                add_stat(0, attn)
                norm = lax.rsqrt(jnp.mean(middle * middle, axis=1, keepdims=True) + epsilon)
                r.n2[aligned(own_start + offset, step_rows), :] = (middle * norm).astype(BF16)
        second.start(part)
    saves.append(copies.start(r.mid, r.mid_h))
    for copy in w_glu:
        copy.wait()
    def glu(part, step):
        rows = aligned(place.member(step) * block + part * part_rows, part_rows)
        a = r.n2[rows, :]
        left = nt(a, r.wl[...])
        right = nt(a, r.wr[...])
        hidden = (left * right).astype(BF16)
        r.left[rows, :] = left.astype(BF16)
        r.right[rows, :] = right.astype(BF16)
        r.hid[rows, :] = hidden
        r.part2[rows, :] = nn(hidden, r.wd[...]).astype(BF16)
        for which in (1, 2, 3):
            @pl.when(step == which)
            def _():
                out_sum.send_block(part, which)

    gather_stage(second, glu, lambda i: None)
    for v, h in ((r.n2, r.n2_h), (r.left, r.left_h), (r.right, r.right_h), (r.hid, r.hid_h)):
        saves.append(copies.start(v, h))
    for part in range(SUPER):
        out_sum.middle(part)
    if cfg.last:
        for part in range(SUPER):
            for which in (1, 2, 3):
                third.finish(part, which)
        saves.append(copies.start(r.gd, r.gd_h))
    for part in range(SUPER):
        for h in range(2):
            out_sum.finish(part, h)
            for i in range(half // step_rows):
                offset = (2 * part + h) * half + i * step_rows
                glu_rows = out_sum.total(part, h, i * step_rows, step_rows)
                after = r.mid[offset : offset + step_rows, :] + glu_rows
                r.xo[offset : offset + step_rows, :] = after
                add_stat(1, glu_rows)
                add_stat(2, after)
    folded = r.stat_wide[:, :128]
    for n in range(1, width // 128):
        folded = folded + r.stat_wide[:, n * 128 : (n + 1) * 128]
    r.stat[...] = folded
    for copy in saves:
        copy.wait()
    for group in (first, mid_sum, second, out_sum, share) + ((third,) if cfg.last else ()):
        group.drain()


class Line:
    def __init__(self, cfg, place, r):
        self.place, self.r = place, r
        self.per, self.count = cfg.chunks, cfg.chunks * cfg.layers
        self.layers, self.rows_each = cfg.layers, cfg.chunks * CHUNK
        self.half = CHUNK // 2
        self.ticks = self.count + 3 + HOP * place.last
        self.done = 0

    def rows(self, k, core):
        return aligned(lax.rem(k, self.per) * CHUNK + core * self.half, self.half)

    def own(self, k):
        return self.rows(k, self.place.core)

    def out_rows(self, k, core):
        layer = self.layers - 1 - k // self.per
        start = layer * self.rows_each + lax.rem(k, self.per) * CHUNK + core * self.half
        return aligned(start, self.half)

    def pair(self, k):
        slot = lax.rem(k, SLOTS)
        r = self.r
        return Wire(self.place.partner(), r.pair_send.at[slot], r.pair_recv.at[slot],
                    r.grads.at[self.rows(k, 1 - self.place.core)], r.pair_land.at[slot], r.pair_land.at[slot])

    def hop(self, k, land, send, recv, device):
        slot = lax.rem(k, SLOTS)
        return Wire(device, send.at[slot], recv.at[slot], land.at[slot], land.at[slot], land.at[slot])

    def going_right(self, k):
        return self.hop(k, self.r.right_land, self.r.right_send, self.r.right_recv, self.place.right())

    def going_left(self, k):
        return self.hop(k, self.r.left_land, self.r.left_send, self.r.left_recv, self.place.left())

    def coming_right(self, k):
        return self.hop(k, self.r.right_land, self.r.right_send, self.r.right_recv, self.place.left())

    def coming_left(self, k):
        return self.hop(k, self.r.left_land, self.r.left_send, self.r.left_recv, self.place.right())

    def result(self, k):
        slot, r = lax.rem(k, SLOTS), self.r
        return Wire(self.place.partner(), r.give_send.at[slot], r.give_recv.at[slot],
                    r.grads.at[self.own(k)], r.out_h.at[self.out_rows(k, self.place.core)],
                    r.out_h.at[self.out_rows(k, 1 - self.place.core)])

    def keep(self, k):
        slot, r = lax.rem(k, SLOTS), self.r
        return pltpu.make_async_copy(
            r.grads.at[self.own(k)], r.out_h.at[self.out_rows(k, self.place.core)], r.keep_sem.at[slot]
        )

    def one_way(self, k, land, start_here, coming, ends_here, going):
        slot = lax.rem(k, SLOTS)

        @pl.when(start_here)
        def _():
            land[slot] = self.r.grads[self.own(k), :]

        @pl.when(jnp.logical_not(start_here))
        def _():
            coming(k).wait_recv()
            land[slot] = land[slot] + self.r.grads[self.own(k), :]

        @pl.when(jnp.logical_not(ends_here))
        def _():
            going(k).start()

    def tick(self, n):
        place, r, last = self.place, self.r, self.place.last
        at_left, at_right = place.at == 0, place.at == last

        @pl.when(n < self.count)
        def _():
            self.pair(n).start()

        k = n - 1

        @pl.when(jnp.logical_and(k >= 0, k < self.count))
        def _():
            wire = self.pair(k)
            wire.wait_recv()
            wire.wait_send()
            slot = lax.rem(k, SLOTS)
            r.grads[self.own(k), :] = r.grads[self.own(k), :] + r.pair_land[slot]

        left_k = n - 1 - HOP * (last - place.at)

        @pl.when(jnp.logical_and(left_k >= 0, left_k < self.count))
        def _():
            self.one_way(left_k, r.left_land, at_right, self.coming_left, at_left, self.going_left)

        right_k = n - 1 - HOP * place.at

        @pl.when(jnp.logical_and(right_k >= 0, right_k < self.count))
        def _():
            self.one_way(right_k, r.right_land, at_left, self.coming_right, at_right, self.going_right)

        full_k = n - 1 - HOP * last

        @pl.when(jnp.logical_and(full_k >= 0, full_k < self.count))
        def _():
            @pl.when(jnp.logical_not(at_right))
            def _():
                self.going_right(full_k).wait_send()

            @pl.when(jnp.logical_not(at_left))
            def _():
                self.going_left(full_k).wait_send()

            slot = lax.rem(full_k, SLOTS)
            own = self.own(full_k)
            total = r.right_land[slot].astype(F32) + r.left_land[slot].astype(F32) - r.grads[own, :].astype(F32)
            r.grads[own, :] = total.astype(BF16)
            self.result(full_k).start()
            self.keep(full_k).start()

        old_k = full_k - 2

        @pl.when(jnp.logical_and(old_k >= 0, old_k < self.count))
        def _():
            wire = self.result(old_k)
            wire.wait_recv()
            wire.wait_send()
            self.keep(old_k).wait()

    def pump(self, ready, most):
        stop = min(self.done + most, ready)
        if stop > self.done:
            start, self.done = self.done, stop

            @pl.loop(start, stop)
            def _(n):
                self.tick(n)

    def release(self, turn, rows):
        needed = (turn - 1) * self.per + -(-rows // CHUNK) + 3 + HOP * self.place.last
        if turn > 0 and needed > self.done:
            self.pump(turn * self.per, needed - self.done)
            assert self.done >= needed

    def finish(self):
        start, self.done = self.done, self.ticks

        @pl.loop(start, self.ticks)
        def _(n):
            self.tick(n)


class StatLine:
    def __init__(self, place, r):
        self.place, self.r = place, r
        self.share = Share(place, r.stat_mine, r.stat_land, r.st_send, r.st_recv)

    def square(self):
        self.share.start()

    def pair(self):
        r = self.r
        r.stat_square[...] = self.share.total()
        self.wire(0, self.place.partner(), r.stat_square).start()

    def wire(self, number, device, source):
        r = self.r
        return Wire(device, r.line_send.at[number], r.line_recv.at[number], source, r.line_land.at[number], r.line_land.at[number])

    def stage(self, number):
        place, r = self.place, self.r
        if number == 0:
            self.wire(0, place.partner(), r.stat_square).wait_recv()
            r.stat_pair[...] = r.stat_square[...] + r.line_land[0]
            r.stat_right[...] = r.stat_pair[...]
            r.stat_left[...] = r.stat_pair[...]
        else:
            @pl.when(place.at == number)
            def _():
                self.wire(1, place.left(), r.stat_right).wait_recv()
                r.stat_right[...] = r.stat_pair[...] + r.line_land[1]

            @pl.when(place.last - place.at == number)
            def _():
                self.wire(2, place.right(), r.stat_left).wait_recv()
                r.stat_left[...] = r.stat_pair[...] + r.line_land[2]
        if number < place.last:
            @pl.when(place.at == number)
            def _():
                self.wire(1, place.right(), r.stat_right).start()

            @pl.when(place.last - place.at == number)
            def _():
                self.wire(2, place.left(), r.stat_left).start()

    def finish(self):
        place, r = self.place, self.r
        r.stat_total[...] = r.stat_right[...] + r.stat_left[...] - r.stat_pair[...]
        self.share.drain()
        self.wire(0, place.partner(), r.stat_square).wait_send()

        @pl.when(place.at < place.last)
        def _():
            self.wire(1, place.right(), r.stat_right).wait_send()

        @pl.when(place.at > 0)
        def _():
            self.wire(2, place.left(), r.stat_left).wait_send()


def bwd_kernel(cfg, names, *refs):
    r = namespace(names, refs)
    block, length, width, local, ff = cfg.block, cfg.length, cfg.width, cfg.local, cfg.ff
    heads_here, size, layers = cfg.heads_here, cfg.block, cfg.layers
    place = Place(cfg.pairs)
    copies = Local(r.local_sem)
    line = Line(cfg, place, r)
    stats = StatLine(place, r)
    loads = {}
    base_down, base_left, base_right, base_out, base_gate, base_qkv, base_end = cfg.bases
    half = block // (2 * SUPER)
    part_rows = 2 * half
    own_start = place.me * block
    step_rows = min(32, half)
    per_block = block // 128
    tiles_here = length // size

    def load(layer, *keys):
        for key in keys:
            if key in SAVED:
                source = getattr(r, key + str(layer) + "_h")
            else:
                source = getattr(r, key + "_h").at[layer]
            loads[key] = copies.start(source, getattr(r, key))

    def await_loads(*keys):
        for key in keys:
            loads[key].wait()

    loads["gd"] = copies.start(r.gd_h, r.gd)
    glu_in = ("wd", "left", "right", "wl", "wr")
    glu_grad = ("hid", "n2", "mid")
    out_in = ("ss", "wo", "gate", "heads")
    attn_in = ("q", "k", "v", "ql", "kl")
    in_in = ("wq", "wk", "wv", "wg")
    load(layers - 1, *glu_in, *glu_grad, *out_in, *attn_in, *in_in, "n1")

    def gather_one(layer):
        return Gather(place, r.gd, r.ag1_send.at[layer], r.ag1_recv.at[layer], block)

    firsts = [gather_one(layer) for layer in range(layers)]

    @pl.loop(0, block // 32)
    def _(i):
        rows = aligned(i * 32, 32)
        r.g[rows, :] = r.up[rows, :].astype(F32)

    r.stat_mine[...] = jnp.zeros_like(r.stat_mine)
    for layer in range(layers):
        r.stat_mine[3 * layer : 3 * layer + 3, :] = getattr(r, "stat%d" % layer)[0:3, :]
    place.greet(True)
    stats.square()
    spread_segments(r, length)
    r.grads[base_end : cfg.chunks * CHUNK, :] = jnp.zeros((cfg.chunks * CHUNK - base_end, width), BF16)
    stats.pair()

    def back_rows(total, values, grad):
        norm = lax.rsqrt(jnp.mean(values * values, axis=1, keepdims=True) + epsilon)
        m = values * norm
        inner = jnp.mean(total * m, axis=1, keepdims=True)
        return grad + norm * (total - m * inner)

    for turn, layer in enumerate(reversed(range(layers))):
        first = firsts[layer]
        mid_sum = Scatter(place, r.part, r.land, r.rs1_send.at[layer], r.rs1_recv.at[layer], block)
        second = Gather(place, r.ga, r.ag2_send.at[layer], r.ag2_recv.at[layer], block)
        in_sum = Scatter(place, r.part, r.land, r.rs2_send.at[layer], r.rs2_recv.at[layer], block)
        share = Share(place, r.inner, r.inner_land.at[layer], r.in_send.at[layer], r.in_recv.at[layer])
        first_head = layer * HEADS + place.me * heads_here

        def ready(rows):
            return turn * cfg.chunks + rows // CHUNK

        decay_tiles(r.dec, first_head, r.tiles, heads_here, size)
        await_loads(*glu_in)
        await_loads(*out_in)
        scaling = lax.rsqrt(r.ss[...] / width + epsilon)
        for chunk in range(length // 128):
            r.scale[chunk * 128 : (chunk + 1) * 128, :] = spread(scaling, chunk)
        if turn == 0:
            stats.stage(0)

        def glu_back(part, step):
            rows = aligned(place.member(step) * block + part * part_rows, part_rows)
            grad_hidden = nt(r.gd[rows, :], r.wd[...])
            grad_left = (grad_hidden * r.right[rows, :].astype(F32)).astype(BF16)
            grad_right = (grad_hidden * r.left[rows, :].astype(F32)).astype(BF16)
            r.right[rows, :] = grad_left
            r.left[rows, :] = grad_right
            r.part[rows, :] = (nn(grad_left, r.wl[...]) + nn(grad_right, r.wr[...])).astype(BF16)
            for which in (1, 2, 3):
                @pl.when(step == which)
                def _():
                    mid_sum.send_block(part, which)

        if turn == 0:
            await_loads("gd")
            for part in range(SUPER):
                @pl.loop(0, 4)
                def _(i):
                    glu_back(part, 3 - i)
        else:
            gather_stage(first, glu_back, lambda i: line.pump(ready(0), 2))
            first.drain()
        grad_left_ref, grad_right_ref = r.right, r.left

        def glu_grad_rows(base, a_ref, b_ref):
            line.release(turn, base + ff)
            for n in range(width // 256):
                cols = slice(n * 256, (n + 1) * 256)
                r.grads[base : base + ff, cols] = tn(a_ref[...], b_ref[:, cols]).astype(BF16)

        await_loads(*glu_grad)
        glu_grad_rows(base_down, r.hid, r.gd)
        if turn == 0:
            stats.stage(1)
        for part in range(SUPER):
            line.pump(ready(base_left), 2)
            mid_sum.middle(part)
        glu_grad_rows(base_left, grad_left_ref, r.n2)
        for part in range(SUPER):
            for h in range(2):
                line.pump(ready(base_right), 1)
                mid_sum.finish(part, h)
                for i in range(half // step_rows):
                    offset = (2 * part + h) * half + i * step_rows
                    rows = slice(offset, offset + step_rows)
                    total = mid_sum.total(part, h, i * step_rows, step_rows)
                    new = back_rows(total, r.mid[rows, :], r.g[rows, :])
                    r.gm[rows, :] = new
                    r.ga[aligned(own_start + offset, step_rows), :] = new.astype(BF16)
            second.start(part)
        mid_sum.drain()
        if turn == 0:
            stats.stage(2)
        glu_grad_rows(base_right, grad_right_ref, r.n2)
        if turn + 1 < layers:
            load(layer - 1, *glu_in, *glu_grad)
        if turn == 0:
            stats.stage(3)
        def out_back(part, step):
            member = place.member(step)
            for chunk in range(part_rows // 128):
                number = part * (part_rows // 128) + chunk
                rows = aligned(member * block + number * 128, 128)
                grad_branch = nt(r.ga[rows, :], r.wo[...])
                gate = r.gate[rows, :]
                normed = r.heads[rows, :] * widen(r.scale[rows, :], local // 128)
                grad_normed = grad_branch * gate
                r.dx[rows, 3 * local : 4 * local] = (grad_branch * normed).astype(BF16)
                r.branch[rows, :] = (normed * gate).astype(BF16)
                r.gate[rows, :] = grad_normed
                row_sums(grad_normed * normed, r.inner, member * per_block + number)

        gather_stage(second, out_back, lambda i: line.pump(ready(base_out), 2))
        share.start()
        line.release(turn, base_gate)
        r.grads[base_out : base_out + local, :] = tn(r.branch[...], r.ga[...]).astype(BF16)
        line.pump(ready(base_gate), 1)

        def in_grad_rows(number, base):
            cols = slice(number * local, (number + 1) * local)
            line.release(turn, base + local)
            for n in range(width // local):
                part_grad = tn(r.n1[:, n * local : (n + 1) * local], r.dx[:, cols])
                r.grads[base : base + local, n * local : (n + 1) * local] = part_grad.astype(BF16)

        await_loads("n1")
        in_grad_rows(3, base_gate)
        line.pump(ready(base_qkv), 1)
        await_loads(*attn_in)
        r.intot[...] = share.total() / width
        for chunk in range(length // 128):
            rows = slice(chunk * 128, (chunk + 1) * 128)
            scale = widen(r.scale[rows, :], local // 128)
            inner = widen(spread(r.intot[...], chunk), local // 128)
            normed = r.heads[rows, :] * scale
            r.dh[rows, :] = (scale * (r.gate[rows, :] - normed * inner)).astype(BF16)
        share.drain()
        second.drain()
        if turn + 1 < layers:
            load(layer - 1, *out_in)
        @pl.loop(0, heads_here)
        def _(head):
            wide = aligned(head * 2 * HDIM, 2 * HDIM)
            thin = aligned(head * HDIM, HDIM)
            for col_tile in range(tiles_here):
                cols = slice(col_tile * size, (col_tile + 1) * size)
                keys = r.k[cols, wide]
                values = r.v[cols, thin]
                acc_key, acc_value = None, None
                for row_tile in range(col_tile, tiles_here):
                    rows = slice(row_tile * size, (row_tile + 1) * size)
                    queries = r.q[rows, wide]
                    grads = r.dh[rows, thin]
                    weight = tile_weight(r, first_head, head, row_tile, col_tile, size)
                    scores = (nt(queries, keys) * weight).astype(BF16)
                    pulled = (nt(grads, values) * weight).astype(BF16)
                    term = nn(pulled, keys)
                    if col_tile == 0:
                        r.dq[rows, :] = term
                    else:
                        r.dq[rows, :] += term
                    key_term = tn(pulled, queries)
                    value_term = tn(scores, grads)
                    acc_key = key_term if acc_key is None else acc_key + key_term
                    acc_value = value_term if acc_value is None else acc_value + value_term
                r.dk[cols, :] = acc_key
                r.dx[cols, aligned(2 * local + head * HDIM, HDIM)] = acc_value.astype(BF16)
            for row_tile in range(tiles_here):
                rows = slice(row_tile * size, (row_tile + 1) * size)
                cosine, sine = r.cos[rows, :], r.sin[rows, :]
                for grad, lin, base in ((r.dq, r.ql, 0), (r.dk, r.kl, local)):
                    v = lin[rows, thin].astype(F32)
                    gate = 1.0 / (1.0 + jnp.exp(-v))
                    back = grad[rows, :HDIM] * cosine + grad[rows, HDIM:] * sine
                    back = back * (gate + v * gate * (1.0 - gate))
                    r.dx[rows, aligned(base + head * HDIM, HDIM)] = back.astype(BF16)

        if turn + 1 < layers:
            load(layer - 1, *attn_in)
        await_loads(*in_in)
        last = turn == layers - 1
        if last:
            for number in range(3):
                in_grad_rows(number, base_qkv + number * local)
        for part in range(SUPER):
            for step in (3, 1, 2, 0):
                rows = aligned(place.member(step) * block + part * part_rows, part_rows)
                total = None
                for n, w in enumerate((r.wq, r.wk, r.wv, r.wg)):
                    term = nt(r.dx[rows, n * local : (n + 1) * local], w[...])
                    total = term if total is None else total + term
                r.part[rows, :] = total.astype(BF16)
                in_sum.send_block(part, step)
            if last:
                line.pump(ready(cfg.chunks * CHUNK), 2)
        for number in range(3):
            if not last:
                in_grad_rows(number, base_qkv + number * local)
            line.pump(ready(base_qkv + (number + 1) * local), 2)
            if number < SUPER:
                in_sum.middle(number)
        if turn + 1 < layers:
            load(layer - 1, *in_in, "n1")
        for part in range(SUPER):
            for h in range(2):
                line.pump(ready(cfg.chunks * CHUNK), 1)
                in_sum.finish(part, h)
                for i in range(half // step_rows):
                    offset = (2 * part + h) * half + i * step_rows
                    rows = slice(offset, offset + step_rows)
                    total = in_sum.total(part, h, i * step_rows, step_rows)
                    values = getattr(r, "x%d" % layer)[rows, :].astype(F32)
                    new = back_rows(total, values, r.gm[rows, :])
                    if layer > 0:
                        r.g[rows, :] = new
                        r.gd[aligned(own_start + offset, step_rows), :] = new.astype(BF16)
                    else:
                        r.go[rows, :] = new.astype(BF16)
            if layer > 0:
                firsts[layer - 1].start(part)
        in_sum.drain()
    stats.finish()
    line.finish()


def call_kernel(body, cfg, inputs, outputs, scratch, collective_id, name):
    vmem, anywhere = pl.BlockSpec(memory_space=pltpu.VMEM), pl.BlockSpec(memory_space=pl.ANY)
    names = list(inputs) + list(outputs) + list(scratch)
    result = pl.pallas_call(
        functools.partial(body, cfg, names),
        out_shape=[shape for shape, _ in outputs.values()],
        in_specs=[vmem if placed else anywhere for _, placed in inputs.values()],
        out_specs=[vmem if placed else anywhere for _, placed in outputs.values()],
        scratch_shapes=list(scratch.values()),
        compiler_params=pltpu.CompilerParams(
            collective_id=collective_id, has_side_effects=collective_id is not None, vmem_limit_bytes=VMEM_LIMIT
        ),
        name=name,
    )(*[array for array, _ in inputs.values()])
    return dict(zip(outputs, result))


def collective_scratch(cfg, copies, lead):
    dma = pltpu.SemaphoreType.DMA
    half = cfg.block // (2 * SUPER)
    out = {}
    for name in ("ag1", "ag2", "rs1", "rs2"):
        out[name + "_send"] = dma((*lead, SUPER, 6))
        out[name + "_recv"] = dma((*lead, SUPER, 6))
    for name in copies:
        out["land" + name] = pltpu.VMEM((SUPER, 6, half, cfg.width), BF16)
        out["part" + name] = pltpu.VMEM((cfg.length, cfg.width), BF16)
    out["local_sem"] = dma((64,))
    return out


def weight_scratch(cfg):
    v = pltpu.VMEM
    return dict(
        wq=v((cfg.width, cfg.local), BF16), wk=v((cfg.width, cfg.local), BF16),
        wv=v((cfg.width, cfg.local), BF16), wg=v((cfg.width, cfg.local), BF16),
        wo=v((cfg.local, cfg.width), BF16), wl=v((cfg.ff, cfg.width), BF16),
        wr=v((cfg.ff, cfg.width), BF16), wd=v((cfg.ff, cfg.width), BF16),
    )


def table_scratch(cfg):
    v = pltpu.VMEM
    return dict(
        segc=v((cfg.length, 128), F32), segf=v((8, 128), F32),
        tiles=v((cfg.heads_here, 2, cfg.block, cfg.block), F32),
    )


def run_forward(cfg, x, upstream, tables, weights):
    v, dma, s = pltpu.VMEM, pltpu.SemaphoreType.DMA, jax.ShapeDtypeStruct
    rows, wide, local, ff, block = cfg.length, cfg.width, cfg.local, cfg.ff, cfg.block
    inputs = dict(x=(x, True), **{k: (a, True) for k, a in tables.items()}, **{k + "_h": (a, False) for k, a in weights.items()})
    kept = dict(
        n1=((rows, wide), BF16), ql=((rows, local), BF16), kl=((rows, local), BF16),
        q=((rows, 2 * local), BF16), k=((rows, 2 * local), BF16), v=((rows, local), BF16),
        gate=((rows, local), F32), heads=((rows, local), F32), mid=((block, wide), F32),
        n2=((rows, wide), BF16), left=((rows, ff), BF16), right=((rows, ff), BF16), hid=((rows, ff), BF16),
    )
    outputs = dict(
        xo=(s((block, wide), F32), True), stat=(s((8, 128), F32), True), ss_h=(s((8, 128), F32), False),
        **{k + "_h": (s(*a), False) for k, a in kept.items()},
    )
    scratch = dict(
        **weight_scratch(cfg), **collective_scratch(cfg, ("1", "2"), ()), **table_scratch(cfg),
        **{k: v(*a) for k, a in kept.items()}, u=v((rows, local), BF16), stat_wide=v((8, wide), F32),
        ss=v((8, 128), F32), sstot=v((8, 128), F32), scale=v((block, 128), F32),
        ss_land=v((3, 8, 128), F32), ss_send=dma((3,)), ss_recv=dma((3,)),
    )
    if cfg.last:
        inputs.update(up_h=(upstream, False))
        outputs.update(gd_h=(s((rows, wide), BF16), False))
        scratch.update(gd=v((rows, wide), BF16), ag3_send=dma((SUPER, 6)), ag3_recv=dma((SUPER, 6)))
    return call_kernel(fwd_kernel, cfg, inputs, outputs, scratch, cfg.layer, "layer_forward")


SAVED = ("ss", "mid", "n1", "ql", "kl", "q", "k", "v", "gate", "heads", "n2", "left", "right", "hid")


def run_backward(cfg, upstream, xs, saved, tables, weights):
    v, dma, s = pltpu.VMEM, pltpu.SemaphoreType.DMA, jax.ShapeDtypeStruct
    rows, wide, local, ff, block = cfg.length, cfg.width, cfg.local, cfg.ff, cfg.block
    inputs = dict(up=(upstream, True), gd_h=(saved[-1]["gd_h"], False), **{k: (a, True) for k, a in tables.items()}, **{k + "_h": (a, False) for k, a in weights.items()})
    for layer in range(cfg.layers):
        inputs["x%d" % layer] = (xs[layer], True)
        inputs["stat%d" % layer] = (saved[layer]["stat"], True)
        for key in SAVED:
            inputs["%s%d_h" % (key, layer)] = (saved[layer][key + "_h"], False)
    total_rows = cfg.chunks * CHUNK
    outputs = dict(
        go=(s((block, wide), BF16), True), stat_total=(s((8, 128), F32), True),
        out_h=(s((cfg.layers * total_rows, wide), BF16), False),
    )
    small, ring, ring_sem = v((8, 128), F32), v((SLOTS, CHUNK // 2, wide), BF16), dma((SLOTS,))
    scratch = dict(
        **weight_scratch(cfg), **collective_scratch(cfg, ("",), (cfg.layers,)), **table_scratch(cfg),
        n1=v((rows, wide), BF16), ql=v((rows, local), BF16), kl=v((rows, local), BF16),
        q=v((rows, 2 * local), BF16), k=v((rows, 2 * local), BF16), v=v((rows, local), BF16),
        gate=v((rows, local), F32), heads=v((rows, local), F32), n2=v((rows, wide), BF16),
        left=v((rows, ff), BF16), right=v((rows, ff), BF16), hid=v((rows, ff), BF16),
        gd=v((rows, wide), BF16), ga=v((rows, wide), BF16),
        g=v((block, wide), F32), gm=v((block, wide), F32), mid=v((block, wide), F32),
        dh=v((rows, local), BF16), branch=v((rows, local), BF16), dx=v((rows, 4 * local), BF16),
        dq=v((rows, 2 * HDIM), F32), dk=v((rows, 2 * HDIM), F32),
        grads=v((total_rows, wide), BF16), scale=v((rows, 128), F32),
        ss=small, inner=small, intot=small,
        inner_land=v((cfg.layers, 3, 8, 128), F32), in_send=dma((cfg.layers, 3)), in_recv=dma((cfg.layers, 3)),
        pair_land=ring, right_land=ring, left_land=ring,
        pair_send=ring_sem, pair_recv=ring_sem, right_send=ring_sem, right_recv=ring_sem, left_send=ring_sem,
        left_recv=ring_sem, give_send=ring_sem, give_recv=ring_sem, keep_sem=ring_sem,
        stat_mine=small, stat_square=small, stat_pair=small, stat_right=small, stat_left=small,
        stat_land=v((3, 8, 128), F32), st_send=dma((3,)), st_recv=dma((3,)),
        line_land=v((3, 8, 128), F32), line_send=dma((3,)), line_recv=dma((3,)),
    )
    return call_kernel(bwd_kernel, cfg, inputs, outputs, scratch, cfg.layers, "layers_backward")


def widen_kernel(cfg, names, *refs):
    r = namespace(names, refs)
    tasks = []
    for layer in range(cfg.layers):
        for number, target in enumerate((r.down, r.left, r.right, r.out)):
            start, stop = cfg.bases[number], cfg.bases[number + 1]
            rows = (stop - start) // 2 if stop - start > 512 else stop - start
            for first in range(start, stop, rows):
                tasks.append((layer, first, rows, [(target.at[layer, pl.ds(first - start, rows), :], slice(None))]))
        for number, target in enumerate((r.gate, r.query, r.key, r.value)):
            pieces = [
                (target.at[layer, pl.ds(n * cfg.local, cfg.local), :], slice(n * cfg.local, (n + 1) * cfg.local))
                for n in range(cfg.width // cfg.local)
            ]
            tasks.append((layer, cfg.bases[4] + number * cfg.local, cfg.local, pieces))
    depth = 3

    def fetch(task):
        layer, first, rows, _ = tasks[task]
        start = layer * cfg.chunks * CHUNK + first
        slot = task % depth
        return pltpu.make_async_copy(r.grads.at[pl.ds(start, rows), :], r.narrow.at[slot, pl.ds(0, rows), :], r.in_sem.at[slot])

    def store(task):
        _, _, rows, pieces = tasks[task]
        slot = task % depth
        return [
            pltpu.make_async_copy(r.wide.at[slot, pl.ds(0, rows), lanes], target, r.out_sem.at[slot, n])
            for n, (target, lanes) in enumerate(pieces)
        ]

    for task in range(min(depth, len(tasks))):
        fetch(task).start()
    for task in range(len(tasks)):
        slot, rows = task % depth, tasks[task][2]
        fetch(task).wait()
        if task >= depth:
            for copy in store(task - depth):
                copy.wait()

        @pl.loop(0, rows // 32)
        def _(i):
            part = aligned(i * 32, 32)
            r.wide[slot, part, :] = r.narrow[slot, part, :].astype(F32)

        for copy in store(task):
            copy.start()
        if task + depth < len(tasks):
            fetch(task + depth).start()
    for task in range(max(len(tasks) - depth, 0), len(tasks)):
        for copy in store(task):
            copy.wait()


def run_widen(cfg, grads):
    v, dma, s = pltpu.VMEM, pltpu.SemaphoreType.DMA, jax.ShapeDtypeStruct
    thin, flat = s((cfg.layers, cfg.width, cfg.local), F32), s((cfg.layers, cfg.ff, cfg.width), F32)
    outputs = dict(
        down=(flat, False), left=(flat, False), right=(flat, False), out=(s((cfg.layers, cfg.local, cfg.width), F32), False),
        gate=(thin, False), query=(thin, False), key=(thin, False), value=(thin, False),
    )
    rows = max(cfg.ff // 2, cfg.local, 512)
    scratch = dict(
        narrow=v((3, rows, cfg.width), BF16), wide=v((3, rows, cfg.width), F32),
        in_sem=dma((3,)), out_sem=dma((3, cfg.width // cfg.local)),
    )
    return call_kernel(widen_kernel, cfg, dict(grads=(grads, False)), outputs, scratch, None, "widen_gradients")


def per_device_square(
    tokens, upstream, segment_ids, query_proj, key_proj, value_proj, gate_proj, output_proj, left_proj, right_proj, down_proj
):
    layers = query_proj.shape[0]
    block, width = tokens.shape
    length = segment_ids.shape[0]
    local, ff = query_proj.shape[2], left_proj.shape[2]
    heads_here = local // HDIM
    positions = np.arange(length, dtype=np.float32)
    frequency = np.exp(np.float32(-math.log(10000.0)) * np.arange(HDIM, dtype=np.float32) / np.float32(HDIM))
    angles = positions[:, None] * frequency[None, :]
    slopes = np.exp2(-8.0 * (np.arange(HEADS) + 1.0) / HEADS)
    decays = np.concatenate([-slopes * (1.0 - depth_start - depth_step * layer) for layer in range(layers)])
    tables = dict(
        cos=jnp.asarray(np.cos(angles)), sin=jnp.asarray(np.sin(angles)),
        dec=jnp.asarray(np.broadcast_to(decays[:, None], (layers * HEADS, 128)).astype(np.float32)),
        seg=segment_ids.reshape(8, length // 8),
    )
    weights = dict(
        wq=query_proj, wk=key_proj, wv=value_proj, wg=gate_proj, wo=output_proj,
        wl=jnp.swapaxes(left_proj, 1, 2), wr=jnp.swapaxes(right_proj, 1, 2), wd=down_proj,
    )
    ends = np.cumsum([0, ff, ff, ff, local, local, 3 * local]).tolist()
    common = dict(
        layers=layers, block=block, length=length, width=width, local=local, ff=ff, heads_here=heads_here,
        pairs=lax.axis_size("dp") // 2, bases=ends, chunks=-(-ends[-1] // CHUNK),
    )
    current, xs, saved = tokens, [], []
    for layer in range(layers):
        xs.append(current)
        cfg = types.SimpleNamespace(layer=layer, last=layer == layers - 1, **common)
        saved.append(run_forward(cfg, current, upstream, tables, weights))
        current = saved[-1]["xo"]
    final_rows = current.astype(BF16)
    back = run_backward(types.SimpleNamespace(**common), upstream, xs, saved, tables, weights)
    stats = jnp.sum(back["stat_total"][: 3 * layers], axis=1).reshape(layers, 3)
    rms_stats = jnp.sqrt(stats / (length * lax.axis_size("dp") * width))
    wide = run_widen(types.SimpleNamespace(**common), back["out_h"])
    return (
        final_rows, back["go"], wide["query"], wide["key"], wide["value"], wide["gate"], wide["out"],
        jnp.swapaxes(wide["left"], 1, 2), jnp.swapaxes(wide["right"], 1, 2), wide["down"], rms_stats,
    )


def solution(mesh):
    square = dict(mesh.shape) == SQUARE_MESH
    body = per_device_square if square else per_device
    return jax.shard_map(
        body,
        mesh=mesh,
        in_specs=(
            P(("dp", "tensor"), None),
            P(("dp", "tensor"), None),
            P("dp"),
            P(None, None, "tensor"),
            P(None, None, "tensor"),
            P(None, None, "tensor"),
            P(None, None, "tensor"),
            P(None, "tensor", None),
            P(None, None, "tensor"),
            P(None, None, "tensor"),
            P(None, "tensor", None),
        ),
        out_specs=(
            P(("dp", "tensor"), None),
            P(("dp", "tensor"), None),
            P(None, None, "tensor"),
            P(None, None, "tensor"),
            P(None, None, "tensor"),
            P(None, None, "tensor"),
            P(None, "tensor", None),
            P(None, None, "tensor"),
            P(None, None, "tensor"),
            P(None, "tensor", None),
            P(),
        ),
        check_vma=False,
    )
```

```python
import functools
import math
import types

import jax
import jax.numpy as jnp
import numpy as np
from jax import lax
from jax.experimental import pallas as pl
from jax.experimental.pallas import tpu as pltpu
from jax.sharding import PartitionSpec as P

HEADS = 8
HDIM = 128
BLK = 512


epsilon = 1e-06
depth_start = 0.5
depth_step = 1.0 / 24.0
highest = lax.Precision.HIGHEST


def rms_rows(values):
    return values * lax.rsqrt(jnp.mean(values * values, axis=1, keepdims=True) + epsilon)


def rms_back(values, gradient):
    scaling = lax.rsqrt(jnp.mean(values * values, axis=1, keepdims=True) + epsilon)
    normed = values * scaling
    return scaling * (gradient - normed * jnp.mean(gradient * normed, axis=1, keepdims=True))


def contract_last(left_part, right_part):
    return lax.dot_general(
        left_part, right_part, (((1,), (1,)), ((), ())), preferred_element_type=jnp.float32
    )


def contract_first(left_part, right_part):
    return lax.dot_general(
        left_part, right_part, (((0,), (0,)), ((), ())), preferred_element_type=jnp.float32
    )


def rotate(values, cosine, sine_table):
    return jnp.concatenate([values * cosine[:, None, :], values * sine_table[:, None, :]], axis=2)


def unrotate(gradient, cosine, sine_table):
    half_width = gradient.shape[2] // 2
    return (
        gradient[:, :, :half_width] * cosine[:, None, :]
        + gradient[:, :, half_width:] * sine_table[:, None, :]
    )


def split_blocks(array, block_count):
    return array.reshape((block_count, BLK) + array.shape[1:])


def block_weights(seg_block, next_seg, decay_log):
    block_width = seg_block.shape[0]
    places = jnp.arange(block_width, dtype=jnp.float32)
    distance = places[:, None] - places[None, :]
    allowed = (distance >= 0) & (seg_block[:, None] == seg_block[None, :])
    decay_grid = jnp.where(
        allowed[None], jnp.exp(decay_log[:, None, None] * jnp.maximum(distance, 0.0)[None]), 0.0
    )
    first_seg = seg_block[0]
    query_gain = jnp.where(
        (seg_block == first_seg)[:, None], jnp.exp(places[:, None] * decay_log[None, :]), 0.0
    )
    key_gain = jnp.where(
        (seg_block == next_seg)[:, None],
        jnp.exp((block_width - places)[:, None] * decay_log[None, :]),
        0.0,
    )
    carry_gain = jnp.where(first_seg == next_seg, jnp.exp(decay_log * block_width), 0.0)
    return (decay_grid, query_gain, key_gain, carry_gain)


def next_segments(segments, block_count):
    seg_blocks = segments.reshape(block_count, BLK)
    return (seg_blocks, jnp.concatenate([seg_blocks[1:, 0], jnp.full((1,), -1, jnp.int32)]))


def attend_forward(queries, keys_rot, values, segments, decay_log):
    length, heads_here, pair_width = queries.shape
    block_count = length // BLK
    seg_blocks, next_segs = next_segments(segments, block_count)

    def advance(state_now, block_items):
        query_block, key_block, value_block, seg_block, next_seg = block_items
        query_float = query_block.astype(jnp.float32)
        key_float = key_block.astype(jnp.float32)
        value_float = value_block.astype(jnp.float32)
        decay_grid, query_gain, key_gain, carry_gain = block_weights(seg_block, next_seg, decay_log)
        scores = (
            jnp.einsum("rhd,shd->hrs", query_block, key_block, preferred_element_type=jnp.float32)
            * decay_grid
        )
        block_out = jnp.einsum("hrs,she->rhe", scores, value_float, precision=highest)
        block_out = (
            block_out
            + jnp.einsum("rhd,hde->rhe", query_float, state_now, precision=highest)
            * query_gain[:, :, None]
        )
        new_state = carry_gain[:, None, None] * state_now + jnp.einsum(
            "shd,she->hde", key_float * key_gain[:, :, None], value_float, precision=highest
        )
        return (new_state, (block_out, state_now))

    zero_state = jnp.zeros((heads_here, pair_width, pair_width // 2), jnp.float32)
    _, (block_outs, states) = lax.scan(
        advance,
        zero_state,
        (
            split_blocks(queries, block_count),
            split_blocks(keys_rot, block_count),
            split_blocks(values, block_count),
            seg_blocks,
            next_segs,
        ),
    )
    return (block_outs.reshape(length, heads_here * (pair_width // 2)), states)


def attend_backward(queries, keys_rot, values, segments, decay_log, states, grad_heads):
    length, heads_here, pair_width = queries.shape
    block_count = length // BLK
    seg_blocks, next_segs = next_segments(segments, block_count)

    def retreat(later_grad, block_items):
        query_block, key_block, value_block, seg_block, next_seg, state_now, grad_block = (
            block_items
        )
        query_float = query_block.astype(jnp.float32)
        key_float = key_block.astype(jnp.float32)
        value_float = value_block.astype(jnp.float32)
        decay_grid, query_gain, key_gain, carry_gain = block_weights(seg_block, next_seg, decay_log)
        scores = (
            jnp.einsum("rhd,shd->hrs", query_block, key_block, preferred_element_type=jnp.float32)
            * decay_grid
        )
        pulled = jnp.einsum("rhe,she->hrs", grad_block, value_float, precision=highest) * decay_grid
        grad_query = jnp.einsum("hrs,shd->rhd", pulled, key_float, precision=highest)
        grad_query = (
            grad_query
            + jnp.einsum("rhe,hde->rhd", grad_block, state_now, precision=highest)
            * query_gain[:, :, None]
        )
        grad_key = jnp.einsum("hrs,rhd->shd", pulled, query_float, precision=highest)
        grad_key = (
            grad_key
            + jnp.einsum("she,hde->shd", value_float, later_grad, precision=highest)
            * key_gain[:, :, None]
        )
        grad_value = jnp.einsum("hrs,rhe->she", scores, grad_block, precision=highest)
        grad_value = (
            grad_value
            + jnp.einsum("shd,hde->she", key_float, later_grad, precision=highest)
            * key_gain[:, :, None]
        )
        earlier_grad = carry_gain[:, None, None] * later_grad + jnp.einsum(
            "rhd,rhe->hde", query_float * query_gain[:, :, None], grad_block, precision=highest
        )
        return (earlier_grad, (grad_query, grad_key, grad_value))

    zero_state = jnp.zeros((heads_here, pair_width, pair_width // 2), jnp.float32)
    _, (grad_query, grad_key, grad_value) = lax.scan(
        retreat,
        zero_state,
        (
            split_blocks(queries, block_count),
            split_blocks(keys_rot, block_count),
            split_blocks(values, block_count),
            seg_blocks,
            next_segs,
            states,
            split_blocks(grad_heads, block_count),
        ),
        reverse=True,
    )
    return (
        grad_query.reshape(length, heads_here, pair_width),
        grad_key.reshape(length, heads_here, pair_width),
        grad_value.reshape(length, heads_here, pair_width // 2),
    )


def per_device(
    tokens,
    upstream,
    segment_ids,
    query_proj,
    key_proj,
    value_proj,
    gate_proj,
    output_proj,
    left_proj,
    right_proj,
    down_proj,
):
    layers = query_proj.shape[0]
    row_count, model_width = tokens.shape
    length = segment_ids.shape[0]
    local_width = query_proj.shape[2]
    ff_local = left_proj.shape[2]
    heads_here = local_width // HDIM
    positions = jnp.arange(length, dtype=jnp.float32)
    frequency = jnp.exp(-math.log(10000.0) * jnp.arange(HDIM, dtype=jnp.float32) / HDIM)
    angles = positions[:, None] * frequency[None, :]
    cosine = jnp.cos(angles)
    sine_table = jnp.sin(angles)
    head_index = (lax.axis_index("tensor") * heads_here + jnp.arange(heads_here)).astype(
        jnp.float32
    )
    slopes = jnp.exp2(-8.0 * (head_index + 1.0) / HEADS)

    def gather_normed(normed):
        return lax.all_gather(normed, "tensor", axis=0, tiled=True)

    def gather_again(normed):
        return lax.all_gather(normed, "tensor", axis=0, tiled=True)

    def gather_grads(gradient):
        return lax.all_gather(gradient, "tensor", axis=0, tiled=True)

    def branch_sum(operand, matrix):
        return lax.psum_scatter(
            jnp.dot(operand, matrix, preferred_element_type=jnp.float32).astype(jnp.bfloat16),
            "tensor",
            scatter_dimension=0,
            tiled=True,
        ).astype(jnp.float32)

    def input_sum(pieces, matrix):
        operand = jnp.concatenate(pieces, axis=1)
        return lax.psum_scatter(
            contract_last(operand, matrix).astype(jnp.bfloat16),
            "tensor",
            scatter_dimension=0,
            tiled=True,
        ).astype(jnp.float32)

    current = tokens.astype(jnp.float32)
    saved_layers = []
    stat_terms = []
    for layer_index in range(layers):
        residual = current
        normed = rms_rows(residual).astype(jnp.bfloat16)
        full_normed = gather_normed(normed)
        attn_weight = jnp.concatenate(
            [
                query_proj[layer_index],
                key_proj[layer_index],
                value_proj[layer_index],
                gate_proj[layer_index],
            ],
            axis=1,
        )
        projected = jnp.dot(full_normed, attn_weight, preferred_element_type=jnp.float32)
        query_lin = projected[:, :local_width]
        key_lin = projected[:, local_width : 2 * local_width]
        values = (
            projected[:, 2 * local_width : 3 * local_width]
            .astype(jnp.bfloat16)
            .reshape(length, heads_here, HDIM)
        )
        gate_lin = projected[:, 3 * local_width :]
        queries = rotate(
            jax.nn.silu(query_lin).reshape(length, heads_here, HDIM), cosine, sine_table
        ).astype(jnp.bfloat16)
        keys_rot = rotate(
            jax.nn.silu(key_lin).reshape(length, heads_here, HDIM), cosine, sine_table
        ).astype(jnp.bfloat16)
        decay_log = -slopes * (1.0 - depth_start - depth_step * layer_index)
        heads_out, states = attend_forward(queries, keys_rot, values, segment_ids, decay_log)
        squares = lax.psum(jnp.sum(heads_out * heads_out, axis=1), "tensor")
        scaling = lax.rsqrt(squares / model_width + epsilon)[:, None]
        normed_heads = heads_out * scaling
        branch = (normed_heads * gate_lin).astype(jnp.bfloat16)
        attn_rows = branch_sum(branch, output_proj[layer_index])
        middle = residual + attn_rows
        normed_mid = rms_rows(middle).astype(jnp.bfloat16)
        full_mid = gather_normed(normed_mid)
        glu_weight = jnp.concatenate([left_proj[layer_index], right_proj[layer_index]], axis=1)
        gates_both = jnp.dot(full_mid, glu_weight, preferred_element_type=jnp.float32)
        left_lin = gates_both[:, :ff_local]
        right_lin = gates_both[:, ff_local:]
        hidden = (left_lin * right_lin).astype(jnp.bfloat16)
        glu_rows = branch_sum(hidden, down_proj[layer_index])
        current = middle + glu_rows
        stat_terms.append(
            jnp.stack(
                [
                    jnp.sum(attn_rows * attn_rows),
                    jnp.sum(glu_rows * glu_rows),
                    jnp.sum(current * current),
                ]
            )
        )
        saved_layers.append(
            (
                residual,
                middle,
                normed,
                normed_mid,
                full_normed,
                full_mid,
                attn_weight,
                glu_weight,
                query_lin,
                key_lin,
                gate_lin,
                queries,
                keys_rot,
                values,
                decay_log,
                states,
                normed_heads,
                scaling,
                branch,
                left_lin,
                right_lin,
                hidden,
            )
        )
    stat_sums = lax.psum(jnp.stack(stat_terms), ("dp", "tensor"))
    rms_stats = jnp.sqrt(stat_sums / (length * lax.axis_size("dp") * model_width))
    final_rows = current.astype(jnp.bfloat16)
    gradient = upstream.astype(jnp.float32)
    layer_results = [None] * layers
    for layer_index in reversed(range(layers)):
        (
            residual,
            middle,
            normed,
            normed_mid,
            full_normed,
            full_mid,
            attn_weight,
            glu_weight,
            query_lin,
            key_lin,
            gate_lin,
            queries,
            keys_rot,
            values,
            decay_log,
            states,
            normed_heads,
            scaling,
            branch,
            left_lin,
            right_lin,
            hidden,
        ) = saved_layers[layer_index]
        glu_grad = gather_grads(gradient.astype(jnp.bfloat16))
        grad_hidden = contract_last(glu_grad, down_proj[layer_index])
        down_part = contract_first(hidden, glu_grad)
        grad_left = (grad_hidden * right_lin).astype(jnp.bfloat16)
        grad_right = (grad_hidden * left_lin).astype(jnp.bfloat16)
        grad_gates = jnp.concatenate([grad_left, grad_right], axis=1)
        mid_rows = input_sum((grad_left, grad_right), glu_weight)
        source_mid = gather_again(normed_mid)
        glu_part = contract_first(source_mid, grad_gates)
        gradient = gradient + rms_back(middle, mid_rows)
        attn_grad = gather_grads(gradient.astype(jnp.bfloat16))
        output_part = contract_first(branch, attn_grad)
        grad_branch = contract_last(attn_grad, output_proj[layer_index])
        grad_normed = grad_branch * gate_lin
        grad_gate = (grad_branch * normed_heads).astype(jnp.bfloat16)
        inner_sum = lax.psum(jnp.sum(grad_normed * normed_heads, axis=1), "tensor")
        grad_heads = scaling * (grad_normed - normed_heads * (inner_sum / model_width)[:, None])
        grad_query, grad_key, grad_value = attend_backward(
            queries,
            keys_rot,
            values,
            segment_ids,
            decay_log,
            states,
            grad_heads.reshape(length, heads_here, HDIM),
        )
        sigmoid_query = jax.nn.sigmoid(query_lin)
        sigmoid_key = jax.nn.sigmoid(key_lin)
        query_back = unrotate(grad_query, cosine, sine_table).reshape(length, local_width)
        key_back = unrotate(grad_key, cosine, sine_table).reshape(length, local_width)
        grad_query_lin = (
            query_back * (sigmoid_query + query_lin * sigmoid_query * (1.0 - sigmoid_query))
        ).astype(jnp.bfloat16)
        grad_key_lin = (
            key_back * (sigmoid_key + key_lin * sigmoid_key * (1.0 - sigmoid_key))
        ).astype(jnp.bfloat16)
        grad_value_lin = grad_value.reshape(length, local_width).astype(jnp.bfloat16)
        grad_projected = jnp.concatenate(
            [grad_query_lin, grad_key_lin, grad_value_lin, grad_gate], axis=1
        )
        in_rows = input_sum((grad_query_lin, grad_key_lin, grad_value_lin, grad_gate), attn_weight)
        source_normed = gather_again(normed)
        attn_part = contract_first(source_normed, grad_projected)
        gradient = gradient + rms_back(residual, in_rows)
        query_part = attn_part[:, :local_width]
        key_part = attn_part[:, local_width : 2 * local_width]
        value_part = attn_part[:, 2 * local_width : 3 * local_width]
        gate_part = attn_part[:, 3 * local_width :]
        left_part = glu_part[:, :ff_local]
        right_part = glu_part[:, ff_local:]
        layer_results[layer_index] = (
            query_part,
            key_part,
            value_part,
            gate_part,
            output_part,
            left_part,
            right_part,
            down_part,
        )
    stacked = [
        jnp.stack([layer_results[index][member] for index in range(layers)]) for member in range(8)
    ]
    totals = (
        lax.psum(stacked[0].astype(jnp.bfloat16), "dp").astype(jnp.float32),
        lax.psum(stacked[1].astype(jnp.bfloat16), "dp").astype(jnp.float32),
        lax.psum(stacked[2].astype(jnp.bfloat16), "dp").astype(jnp.float32),
        lax.psum(stacked[3].astype(jnp.bfloat16), "dp").astype(jnp.float32),
        lax.psum(stacked[4].astype(jnp.bfloat16), "dp").astype(jnp.float32),
        lax.psum(stacked[5].astype(jnp.bfloat16), "dp").astype(jnp.float32),
        lax.psum(stacked[6].astype(jnp.bfloat16), "dp").astype(jnp.float32),
        lax.psum(stacked[7].astype(jnp.bfloat16), "dp").astype(jnp.float32),
    )
    input_grad = gradient.astype(jnp.bfloat16)
    return (
        final_rows,
        input_grad,
        totals[0],
        totals[1],
        totals[2],
        totals[3],
        totals[4],
        totals[5],
        totals[6],
        totals[7],
        rms_stats,
    )


SQUARE_MESH = {"dp": 8, "tensor": 4}


F32 = jnp.float32
BF16 = jnp.bfloat16
MESH = pl.DeviceIdType.MESH
VMEM_LIMIT = 60 * 2**20
SUPER = 2
CHUNK = 128
HOP = 3
SLOTS = 16


def nn(a, b):
    return lax.dot_general(a, b, (((1,), (0,)), ((), ())), preferred_element_type=F32)


def nt(a, b):
    return lax.dot_general(a, b, (((1,), (1,)), ((), ())), preferred_element_type=F32)


def tn(a, b):
    return lax.dot_general(a, b, (((0,), (0,)), ((), ())), preferred_element_type=F32)


def exact(a, b, dims):
    return lax.dot_general(a, b, (dims, ((), ())), precision=highest, preferred_element_type=F32)


def aligned(index, size):
    return pl.ds(pl.multiple_of(index, size), size)


class Place:
    def __init__(self, pairs):
        self.dp = lax.axis_index("dp")
        self.me = lax.axis_index("tensor")
        self.low = lax.rem(self.me, 2)
        self.high = self.me // 2
        self.core = lax.rem(self.dp, 2)
        self.at = self.dp // 2
        self.last = pairs - 1

    def member(self, step):
        low = lax.rem(self.low + lax.rem(step, 2), 2)
        high = lax.rem(self.high + step // 2, 2)
        return 2 * high + low

    def device(self, step):
        return (self.dp, self.member(step))

    def partner(self):
        return (self.dp + 1 - 2 * self.core, self.me)

    def right(self):
        return (self.dp + 2, self.me)

    def left(self):
        return (self.dp - 2, self.me)

    def greet(self, line):
        barrier = pltpu.get_barrier_semaphore()

        def signal(device):
            pl.semaphore_signal(barrier, inc=1, device_id=device, device_id_type=MESH)

        for step in (1, 2, 3):
            signal(self.device(step))
        if not line:
            pl.semaphore_wait(barrier, 3)
            return
        signal(self.partner())

        @pl.when(self.at < self.last)
        def _():
            signal(self.right())

        @pl.when(self.at > 0)
        def _():
            signal(self.left())

        pl.semaphore_wait(barrier, 4 + jnp.minimum(self.at, 1) + jnp.minimum(self.last - self.at, 1))


class Wire:
    def __init__(self, device, send_sem, recv_sem, source, target, landing):
        self.source, self.target, self.landing = source, target, landing
        self.common = dict(send_sem=send_sem, recv_sem=recv_sem, device_id=device, device_id_type=MESH)

    def out(self):
        return pltpu.make_async_remote_copy(src_ref=self.source, dst_ref=self.target, **self.common)

    def start(self):
        self.out().start()

    def wait_recv(self):
        pltpu.make_async_remote_copy(src_ref=self.landing, dst_ref=self.landing, **self.common).wait_recv()

    def wait_send(self):
        self.out().wait_send()


class Gather:
    def __init__(self, place, buf, send, recv, block):
        self.place, self.buf, self.block = place, buf, block
        self.send, self.recv = send, recv
        self.half = block // (2 * SUPER)

    def rows(self, step, part, half):
        start = self.place.member(step) * self.block + (2 * part + half) * self.half
        return self.buf.at[aligned(start, self.half)]

    def wire(self, part, number):
        step, owner, half = ((1, 0, 0), (2, 0, 1), (1, 0, 1), (2, 0, 0), (2, 1, 0), (1, 2, 1))[number]
        source = self.rows(owner, part, half)
        landing = self.rows((0, 1, 2, 3)[owner ^ step], part, half)
        return Wire(self.place.device(step), self.send.at[part, number], self.recv.at[part, number], source, source, landing)

    def start(self, part):
        for number in range(4):
            self.wire(part, number).start()

    def forward(self, part):
        self.wire(part, 0).wait_recv()
        self.wire(part, 4).start()
        self.wire(part, 1).wait_recv()
        self.wire(part, 5).start()

    def finish(self, part, step):
        for number in {0: (), 1: (2,), 2: (3,), 3: (4, 5)}[step]:
            self.wire(part, number).wait_recv()

    def drain(self):
        for part in range(SUPER):
            for number in range(6):
                self.wire(part, number).wait_send()


def gather_stage(gather, block_fn, beside):
    @pl.loop(0, 4 * SUPER)
    def _(i):
        mixed = i - SUPER
        part = jnp.where(i < SUPER, i, jnp.where(i < 3 * SUPER, mixed // 2, i - 3 * SUPER))
        step = jnp.where(i < SUPER, 0, jnp.where(i < 3 * SUPER, 1 + lax.rem(mixed, 2), 3))

        @pl.when(i == SUPER)
        def _():
            for one in range(SUPER):
                beside(one)
                gather.forward(one)

        @pl.when(i == 3 * SUPER)
        def _():
            beside(SUPER)

        for which in (1, 2, 3):
            @pl.when(step == which)
            def _():
                gather.finish(part, which)
        block_fn(part, step)


class Scatter:
    def __init__(self, place, buf, land, send, recv, block):
        self.place, self.buf, self.land, self.block = place, buf, land, block
        self.send, self.recv = send, recv
        self.half = block // (2 * SUPER)

    def rows(self, step, part, half):
        start = self.place.member(step) * self.block + (2 * part + half) * self.half
        return aligned(start, self.half)

    def wire(self, part, number):
        step, owner, half = ((1, 3, 0), (1, 1, 0), (2, 3, 1), (2, 2, 1), (2, 2, 0), (1, 1, 1))[number]
        target = self.land.at[part, number]
        return Wire(
            self.place.device(step), self.send.at[part, number], self.recv.at[part, number],
            self.buf.at[self.rows(owner, part, half)], target, target,
        )

    def send_block(self, part, step):
        for number in {0: (), 1: (1,), 2: (3,), 3: (0, 2)}[step]:
            self.wire(part, number).start()

    def middle(self, part):
        for first, second, owner, half in ((0, 4, 2, 0), (2, 5, 1, 1)):
            self.wire(part, first).wait_recv()
            rows = self.rows(owner, part, half)
            self.buf[rows, :] = self.buf[rows, :] + self.land[part, first]
            self.wire(part, second).start()

    def finish(self, part, half):
        first, second = ((1, 4), (3, 5))[half]
        self.wire(part, first).wait_recv()
        self.wire(part, second).wait_recv()

    def total(self, part, half, start, count):
        first, second = ((1, 4), (3, 5))[half]
        own = self.place.me * self.block + (2 * part + half) * self.half + start
        rows = pl.ds(start, count)
        return (
            self.buf[aligned(own, count), :].astype(F32)
            + self.land[part, first, rows, :].astype(F32)
            + self.land[part, second, rows, :].astype(F32)
        )

    def drain(self):
        for part in range(SUPER):
            for number in range(6):
                self.wire(part, number).wait_send()


class Share:
    def __init__(self, place, mine, land, send, recv):
        self.wires = [
            Wire(place.device(step), send.at[step - 1], recv.at[step - 1], mine, land.at[step - 1], land.at[step - 1])
            for step in (1, 2, 3)
        ]
        self.mine, self.land = mine, land

    def start(self):
        for wire in self.wires:
            wire.start()

    def total(self):
        for wire in self.wires:
            wire.wait_recv()
        return self.mine[...] + self.land[0] + self.land[1] + self.land[2]

    def drain(self):
        for wire in self.wires:
            wire.wait_send()


class Local:
    def __init__(self, sems):
        self.sems, self.used = sems, 0

    def start(self, source, target):
        copy = pltpu.make_async_copy(source, target, self.sems.at[self.used])
        self.used += 1
        copy.start()
        return copy


def row_sums(values, target, chunk):
    sums = exact(jnp.ones((8, values.shape[1]), F32), values, ((1,), (1,)))
    target[pl.ds(chunk, 1), :] = sums[0:1, :]


def spread(sums, chunk):
    picked = (lax.broadcasted_iota(jnp.int32, (8, 128), 0) == chunk).astype(F32)
    return exact(sums, picked, ((0,), (0,)))


def widen(columns, times):
    return jnp.concatenate([columns] * times, axis=1)


def decay_tiles(dec_ref, first_head, tiles, heads_here, size):
    rows = lax.broadcasted_iota(jnp.int32, (size, size), 0)
    cols = lax.broadcasted_iota(jnp.int32, (size, size), 1)
    distance = (rows - cols).astype(F32)
    for head in range(heads_here):
        decay = dec_ref[pl.ds(first_head + head, 1), 0:1]
        tiles[head, 0] = jnp.where(rows >= cols, jnp.exp(decay * jnp.maximum(distance, 0.0)), 0.0)
        tiles[head, 1] = jnp.exp(decay * (distance + float(size)))


def spread_segments(r, length):
    r.segf[...] = r.seg[...].astype(F32)
    for chunk in range(length // 128):
        r.segc[chunk * 128 : (chunk + 1) * 128, :] = spread(r.segf[...], chunk)


def tile_weight(r, first_head, head, row_tile, col_tile, size):
    gap = row_tile - col_tile
    if gap == 0:
        weight = r.tiles[head, 0]
    else:
        weight = r.tiles[head, 1]
        if gap > 1:
            decay = r.dec[pl.ds(first_head + head, 1), 0:1]
            weight = weight * jnp.exp(decay * float(size * (gap - 1)))
    row_seg = widen(r.segc[row_tile * size : (row_tile + 1) * size, :], size // 128)
    per = size // 128
    col_seg = jnp.concatenate([r.segf[per * col_tile + i : per * col_tile + i + 1, :] for i in range(per)], axis=1)
    return jnp.where(row_seg == col_seg, weight, 0.0)


def namespace(names, refs):
    return types.SimpleNamespace(**dict(zip(names, refs)))


def fwd_kernel(cfg, names, *refs):
    r = namespace(names, refs)
    layer, block, length, width, local = cfg.layer, cfg.block, cfg.length, cfg.width, cfg.local
    heads_here, size = cfg.heads_here, cfg.block
    place = Place(cfg.pairs)
    first_head = layer * HEADS + place.me * heads_here
    copies = Local(r.local_sem)
    w_in = [copies.start(h.at[layer], v) for h, v in (
        (r.wq_h, r.wq), (r.wk_h, r.wk), (r.wv_h, r.wv), (r.wg_h, r.wg))]
    w_out = copies.start(r.wo_h.at[layer], r.wo)
    w_glu = [copies.start(h.at[layer], v) for h, v in ((r.wl_h, r.wl), (r.wr_h, r.wr), (r.wd_h, r.wd))]
    saves = []
    first = Gather(place, r.n1, r.ag1_send, r.ag1_recv, block)
    mid_sum = Scatter(place, r.part1, r.land1, r.rs1_send, r.rs1_recv, block)
    second = Gather(place, r.n2, r.ag2_send, r.ag2_recv, block)
    out_sum = Scatter(place, r.part2, r.land2, r.rs2_send, r.rs2_recv, block)
    share = Share(place, r.ss, r.ss_land, r.ss_send, r.ss_recv)
    third = Gather(place, r.gd, r.ag3_send, r.ag3_recv, block) if cfg.last else None
    if cfg.last:
        load_up = copies.start(r.up_h, r.gd.at[aligned(place.me * block, block), :])
    half, step_rows = first.half, 32
    own_start = place.me * block

    @pl.loop(0, block // step_rows)
    def _(i):
        rows = aligned(i * step_rows, step_rows)
        v = r.x[rows, :].astype(F32)
        scale = lax.rsqrt(jnp.mean(v * v, axis=1, keepdims=True) + epsilon)
        r.n1[aligned(own_start + i * step_rows, step_rows), :] = (v * scale).astype(BF16)

    place.greet(False)
    for part in range(SUPER):
        first.start(part)
    decay_tiles(r.dec, first_head, r.tiles, heads_here, size)
    spread_segments(r, length)
    for copy in w_in:
        copy.wait()

    @pl.loop(0, 4)
    def _(step):
        @pl.when(step == 1)
        def _():
            for part in range(SUPER):
                first.forward(part)
        for which in (1, 2, 3):
            @pl.when(step == which)
            def _():
                for part in range(SUPER):
                    first.finish(part, which)
        rows = aligned(place.member(step) * block, block)
        a = r.n1[rows, :]
        cosine, sine = r.cos[rows, :], r.sin[rows, :]
        for w, lin, rot in ((r.wq, r.ql, r.q), (r.wk, r.kl, r.k)):
            v = nn(a, w[...])
            lin[rows, :] = v.astype(BF16)
            v = v / (1.0 + jnp.exp(-v))
            for head in range(heads_here):
                one = v[:, head * HDIM : (head + 1) * HDIM]
                rot[rows, 2 * head * HDIM : (2 * head + 1) * HDIM] = (one * cosine).astype(BF16)
                rot[rows, (2 * head + 1) * HDIM : (2 * head + 2) * HDIM] = (one * sine).astype(BF16)
        r.v[rows, :] = nn(a, r.wv[...]).astype(BF16)
        r.gate[rows, :] = nn(a, r.wg[...])

    for v, h in ((r.n1, r.n1_h), (r.ql, r.ql_h), (r.kl, r.kl_h), (r.q, r.q_h), (r.k, r.k_h), (r.v, r.v_h), (r.gate, r.gate_h)):
        saves.append(copies.start(v, h))

    if cfg.last:
        load_up.wait()
        for part in range(SUPER):
            third.start(part)
    tiles_here = length // size

    @pl.loop(0, heads_here)
    def _(head):
        wide = aligned(head * 2 * HDIM, 2 * HDIM)
        thin = aligned(head * HDIM, HDIM)
        for row_tile in range(tiles_here):
            rows = slice(row_tile * size, (row_tile + 1) * size)
            queries = r.q[rows, wide]
            acc = None
            for col_tile in range(row_tile + 1):
                cols = slice(col_tile * size, (col_tile + 1) * size)
                weight = tile_weight(r, first_head, head, row_tile, col_tile, size)
                scores = (nt(queries, r.k[cols, wide]) * weight).astype(BF16)
                term = nn(scores, r.v[cols, thin])
                acc = term if acc is None else acc + term
            r.heads[rows, thin] = acc
            r.u[rows, thin] = (acc * r.gate[rows, thin]).astype(BF16)

    for chunk in range(length // 128):
        v = r.heads[chunk * 128 : (chunk + 1) * 128, :]
        row_sums(v * v, r.ss, chunk)
    share.start()
    saves.append(copies.start(r.heads, r.heads_h))
    if cfg.last:
        for part in range(SUPER):
            third.forward(part)
    w_out.wait()

    part_rows = 2 * half
    for part in range(SUPER):
        for step in (3, 1, 2, 0):
            rows = aligned(place.member(step) * block + part * part_rows, part_rows)
            r.part1[rows, :] = nn(r.u[rows, :], r.wo[...]).astype(BF16)
            mid_sum.send_block(part, step)
    for part in range(SUPER):
        mid_sum.middle(part)
    r.sstot[...] = share.total()
    saves.append(copies.start(r.sstot, r.ss_h))
    scaling = lax.rsqrt(r.sstot[...] / width + epsilon)
    per_block = block // 128
    for chunk in range(per_block):
        r.scale[chunk * 128 : (chunk + 1) * 128, :] = spread(scaling, place.me * per_block + chunk)
    r.stat_wide[...] = jnp.zeros_like(r.stat_wide)

    def add_stat(row, v):
        sums = jnp.sum(v * v, axis=0, keepdims=True)
        r.stat_wide[row : row + 1, :] += sums

    step_rows = min(32, half)
    for part in range(SUPER):
        for h in range(2):
            mid_sum.finish(part, h)
            for i in range(half // step_rows):
                offset = (2 * part + h) * half + i * step_rows
                scale = widen(r.scale[offset : offset + step_rows, :], width // 128)
                attn = mid_sum.total(part, h, i * step_rows, step_rows) * scale
                middle = r.x[offset : offset + step_rows, :].astype(F32) + attn
                r.mid[offset : offset + step_rows, :] = middle
                add_stat(0, attn)
                norm = lax.rsqrt(jnp.mean(middle * middle, axis=1, keepdims=True) + epsilon)
                r.n2[aligned(own_start + offset, step_rows), :] = (middle * norm).astype(BF16)
        second.start(part)
    saves.append(copies.start(r.mid, r.mid_h))
    for copy in w_glu:
        copy.wait()
    def glu(part, step):
        rows = aligned(place.member(step) * block + part * part_rows, part_rows)
        a = r.n2[rows, :]
        left = nt(a, r.wl[...])
        right = nt(a, r.wr[...])
        hidden = (left * right).astype(BF16)
        r.left[rows, :] = left.astype(BF16)
        r.right[rows, :] = right.astype(BF16)
        r.hid[rows, :] = hidden
        r.part2[rows, :] = nn(hidden, r.wd[...]).astype(BF16)
        for which in (1, 2, 3):
            @pl.when(step == which)
            def _():
                out_sum.send_block(part, which)

    gather_stage(second, glu, lambda i: None)
    for v, h in ((r.n2, r.n2_h), (r.left, r.left_h), (r.right, r.right_h), (r.hid, r.hid_h)):
        saves.append(copies.start(v, h))
    for part in range(SUPER):
        out_sum.middle(part)
    if cfg.last:
        for part in range(SUPER):
            for which in (1, 2, 3):
                third.finish(part, which)
        saves.append(copies.start(r.gd, r.gd_h))
    for part in range(SUPER):
        for h in range(2):
            out_sum.finish(part, h)
            for i in range(half // step_rows):
                offset = (2 * part + h) * half + i * step_rows
                glu_rows = out_sum.total(part, h, i * step_rows, step_rows)
                after = r.mid[offset : offset + step_rows, :] + glu_rows
                r.xo[offset : offset + step_rows, :] = after.astype(r.xo.dtype)
                add_stat(1, glu_rows)
                add_stat(2, after)
    folded = r.stat_wide[:, :128]
    for n in range(1, width // 128):
        folded = folded + r.stat_wide[:, n * 128 : (n + 1) * 128]
    r.stat[...] = folded
    for copy in saves:
        copy.wait()
    for group in (first, mid_sum, second, out_sum, share) + ((third,) if cfg.last else ()):
        group.drain()


def turns_of(k, size, count):
    return sum(((k >= size * n).astype(jnp.int32) for n in range(1, -(-count // size))), jnp.int32(0))


class Line:
    def __init__(self, cfg, place, r):
        self.place, self.r = place, r
        self.per, self.count = cfg.chunks, cfg.chunks * cfg.layers
        self.layers, self.rows_each = cfg.layers, cfg.chunks * CHUNK
        self.half = CHUNK // 2
        self.ticks = self.count + 3 + HOP * place.last
        self.done = 0

    def slot(self, k):
        return k - SLOTS * turns_of(k, SLOTS, self.count)

    def rows(self, k, core):
        place = k - self.per * turns_of(k, self.per, self.count)
        return aligned(place * CHUNK + core * self.half, self.half)

    def own(self, k):
        return self.rows(k, self.place.core)

    def out_rows(self, k, core):
        turn = turns_of(k, self.per, self.count)
        place = (self.layers - 1 - turn) * self.per + k - turn * self.per
        start = place * CHUNK + core * self.half
        return aligned(start, self.half)

    def pair(self, k):
        slot = self.slot(k)
        r = self.r
        return Wire(self.place.partner(), r.pair_send.at[slot], r.pair_recv.at[slot],
                    r.grads.at[self.rows(k, 1 - self.place.core)], r.pair_land.at[slot], r.pair_land.at[slot])

    def hop(self, k, land, send, recv, device):
        slot = self.slot(k)
        return Wire(device, send.at[slot], recv.at[slot], land.at[slot], land.at[slot], land.at[slot])

    def going_right(self, k):
        return self.hop(k, self.r.right_land, self.r.right_send, self.r.right_recv, self.place.right())

    def going_left(self, k):
        return self.hop(k, self.r.left_land, self.r.left_send, self.r.left_recv, self.place.left())

    def coming_right(self, k):
        return self.hop(k, self.r.right_land, self.r.right_send, self.r.right_recv, self.place.left())

    def coming_left(self, k):
        return self.hop(k, self.r.left_land, self.r.left_send, self.r.left_recv, self.place.right())

    def result(self, k):
        slot, r = self.slot(k), self.r
        return Wire(self.place.partner(), r.give_send.at[slot], r.give_recv.at[slot],
                    r.grads.at[self.own(k)], r.out_h.at[self.out_rows(k, self.place.core)],
                    r.out_h.at[self.out_rows(k, 1 - self.place.core)])

    def keep(self, k):
        slot, r = self.slot(k), self.r
        return pltpu.make_async_copy(
            r.grads.at[self.own(k)], r.out_h.at[self.out_rows(k, self.place.core)], r.keep_sem.at[slot]
        )

    def one_way(self, k, land, start_here, coming, ends_here, going):
        slot = self.slot(k)

        @pl.when(start_here)
        def _():
            land[slot] = self.r.grads[self.own(k), :]

        @pl.when(jnp.logical_not(start_here))
        def _():
            coming(k).wait_recv()
            land[slot] = land[slot] + self.r.grads[self.own(k), :]

        @pl.when(jnp.logical_not(ends_here))
        def _():
            going(k).start()

    def tick(self, n):
        place, r, last = self.place, self.r, self.place.last
        at_left, at_right = place.at == 0, place.at == last

        @pl.when(n < self.count)
        def _():
            self.pair(n).start()

        k = n - 1

        @pl.when(jnp.logical_and(k >= 0, k < self.count))
        def _():
            wire = self.pair(k)
            wire.wait_recv()
            wire.wait_send()
            slot = self.slot(k)
            r.grads[self.own(k), :] = r.grads[self.own(k), :] + r.pair_land[slot]

        left_k = n - 1 - HOP * (last - place.at)

        @pl.when(jnp.logical_and(left_k >= 0, left_k < self.count))
        def _():
            self.one_way(left_k, r.left_land, at_right, self.coming_left, at_left, self.going_left)

        right_k = n - 1 - HOP * place.at

        @pl.when(jnp.logical_and(right_k >= 0, right_k < self.count))
        def _():
            self.one_way(right_k, r.right_land, at_left, self.coming_right, at_right, self.going_right)

        full_k = n - 1 - HOP * last

        @pl.when(jnp.logical_and(full_k >= 0, full_k < self.count))
        def _():
            @pl.when(jnp.logical_not(at_right))
            def _():
                self.going_right(full_k).wait_send()

            @pl.when(jnp.logical_not(at_left))
            def _():
                self.going_left(full_k).wait_send()

            slot = self.slot(full_k)
            own = self.own(full_k)
            total = r.right_land[slot].astype(F32) + r.left_land[slot].astype(F32) - r.grads[own, :].astype(F32)
            r.grads[own, :] = total.astype(BF16)
            self.result(full_k).start()
            self.keep(full_k).start()

        old_k = full_k - 2

        @pl.when(jnp.logical_and(old_k >= 0, old_k < self.count))
        def _():
            wire = self.result(old_k)
            wire.wait_recv()
            wire.wait_send()
            self.keep(old_k).wait()

    def pump(self, ready, most):
        stop = min(self.done + most, ready)
        if stop > self.done:
            start, self.done = self.done, stop

            @pl.loop(start, stop)
            def _(n):
                self.tick(n)

    def release(self, turn, rows):
        needed = (turn - 1) * self.per + -(-rows // CHUNK) + 3 + HOP * self.place.last
        if turn > 0 and needed > self.done:
            self.pump(turn * self.per, needed - self.done)
            assert self.done >= needed

    def finish(self):
        start, self.done = self.done, self.ticks

        @pl.loop(start, self.ticks)
        def _(n):
            self.tick(n)


class StatLine:
    def __init__(self, place, r):
        self.place, self.r = place, r
        self.share = Share(place, r.stat_mine, r.stat_land, r.st_send, r.st_recv)

    def square(self):
        self.share.start()

    def pair(self):
        r = self.r
        r.stat_square[...] = self.share.total()
        self.wire(0, self.place.partner(), r.stat_square).start()

    def wire(self, number, device, source):
        r = self.r
        return Wire(device, r.line_send.at[number], r.line_recv.at[number], source, r.line_land.at[number], r.line_land.at[number])

    def stage(self, number):
        place, r = self.place, self.r
        if number == 0:
            self.wire(0, place.partner(), r.stat_square).wait_recv()
            r.stat_pair[...] = r.stat_square[...] + r.line_land[0]
            r.stat_right[...] = r.stat_pair[...]
            r.stat_left[...] = r.stat_pair[...]
        else:
            @pl.when(place.at == number)
            def _():
                self.wire(1, place.left(), r.stat_right).wait_recv()
                r.stat_right[...] = r.stat_pair[...] + r.line_land[1]

            @pl.when(place.last - place.at == number)
            def _():
                self.wire(2, place.right(), r.stat_left).wait_recv()
                r.stat_left[...] = r.stat_pair[...] + r.line_land[2]
        if number < place.last:
            @pl.when(place.at == number)
            def _():
                self.wire(1, place.right(), r.stat_right).start()

            @pl.when(place.last - place.at == number)
            def _():
                self.wire(2, place.left(), r.stat_left).start()

    def finish(self):
        place, r = self.place, self.r
        r.stat_total[...] = r.stat_right[...] + r.stat_left[...] - r.stat_pair[...]
        self.share.drain()
        self.wire(0, place.partner(), r.stat_square).wait_send()

        @pl.when(place.at < place.last)
        def _():
            self.wire(1, place.right(), r.stat_right).wait_send()

        @pl.when(place.at > 0)
        def _():
            self.wire(2, place.left(), r.stat_left).wait_send()


def bwd_kernel(cfg, names, *refs):
    r = namespace(names, refs)
    block, length, width, local, ff = cfg.block, cfg.length, cfg.width, cfg.local, cfg.ff
    heads_here, size, layers = cfg.heads_here, cfg.block, cfg.layers
    place = Place(cfg.pairs)
    copies = Local(r.local_sem)
    line = Line(cfg, place, r)
    stats = StatLine(place, r)
    loads = {}
    base_down, base_left, base_right, base_out, base_gate, base_qkv, base_end = cfg.bases
    half = block // (2 * SUPER)
    part_rows = 2 * half
    own_start = place.me * block
    step_rows = min(32, half)
    per_block = block // 128
    tiles_here = length // size

    def load(layer, *keys):
        for key in keys:
            if key in SAVED:
                source = getattr(r, key + str(layer) + "_h")
            else:
                source = getattr(r, key + "_h").at[layer]
            loads[key] = copies.start(source, getattr(r, key))

    def await_loads(*keys):
        for key in keys:
            loads[key].wait()

    loads["gd"] = copies.start(r.gd_h, r.gd)
    glu_in = ("wd", "left", "right", "wl", "wr")
    glu_grad = ("hid", "n2", "mid")
    out_in = ("ss", "wo", "gate", "heads")
    attn_in = ("q", "k", "v", "ql", "kl")
    in_in = ("wq", "wk", "wv", "wg")
    load(layers - 1, *glu_in, *glu_grad, *out_in, *attn_in, *in_in, "n1")

    def gather_one(layer):
        return Gather(place, r.gd, r.ag1_send.at[layer], r.ag1_recv.at[layer], block)

    firsts = [gather_one(layer) for layer in range(layers)]

    @pl.loop(0, block // 32)
    def _(i):
        rows = aligned(i * 32, 32)
        r.g[rows, :] = r.up[rows, :].astype(F32)

    r.stat_mine[...] = jnp.zeros_like(r.stat_mine)
    for layer in range(layers):
        r.stat_mine[3 * layer : 3 * layer + 3, :] = getattr(r, "stat%d" % layer)[0:3, :]
    place.greet(True)
    stats.square()
    spread_segments(r, length)
    r.grads[base_end : cfg.chunks * CHUNK, :] = jnp.zeros((cfg.chunks * CHUNK - base_end, width), BF16)
    stats.pair()

    def back_rows(total, values, grad):
        norm = lax.rsqrt(jnp.mean(values * values, axis=1, keepdims=True) + epsilon)
        m = values * norm
        inner = jnp.mean(total * m, axis=1, keepdims=True)
        return grad + norm * (total - m * inner)

    for turn, layer in enumerate(reversed(range(layers))):
        first = firsts[layer]
        mid_sum = Scatter(place, r.part, r.land, r.rs1_send.at[layer], r.rs1_recv.at[layer], block)
        second = Gather(place, r.ga, r.ag2_send.at[layer], r.ag2_recv.at[layer], block)
        in_sum = Scatter(place, r.part, r.land, r.rs2_send.at[layer], r.rs2_recv.at[layer], block)
        share = Share(place, r.inner, r.inner_land.at[layer], r.in_send.at[layer], r.in_recv.at[layer])
        first_head = layer * HEADS + place.me * heads_here

        def ready(rows):
            return turn * cfg.chunks + rows // CHUNK

        decay_tiles(r.dec, first_head, r.tiles, heads_here, size)
        await_loads(*glu_in)
        await_loads(*out_in)
        scaling = lax.rsqrt(r.ss[...] / width + epsilon)
        for chunk in range(length // 128):
            r.scale[chunk * 128 : (chunk + 1) * 128, :] = spread(scaling, chunk)
        if turn == 0:
            stats.stage(0)

        def glu_back(part, step):
            rows = aligned(place.member(step) * block + part * part_rows, part_rows)
            grad_hidden = nt(r.gd[rows, :], r.wd[...])
            grad_left = (grad_hidden * r.right[rows, :].astype(F32)).astype(BF16)
            grad_right = (grad_hidden * r.left[rows, :].astype(F32)).astype(BF16)
            r.right[rows, :] = grad_left
            r.left[rows, :] = grad_right
            r.part[rows, :] = (nn(grad_left, r.wl[...]) + nn(grad_right, r.wr[...])).astype(BF16)
            for which in (1, 2, 3):
                @pl.when(step == which)
                def _():
                    mid_sum.send_block(part, which)

        if turn == 0:
            await_loads("gd")
            for part in range(SUPER):
                @pl.loop(0, 4)
                def _(i):
                    glu_back(part, 3 - i)
        else:
            gather_stage(first, glu_back, lambda i: line.pump(ready(0), 2))
            first.drain()
        grad_left_ref, grad_right_ref = r.right, r.left

        def glu_grad_rows(base, a_ref, b_ref):
            line.release(turn, base + ff)
            for n in range(width // 256):
                cols = slice(n * 256, (n + 1) * 256)
                r.grads[base : base + ff, cols] = tn(a_ref[...], b_ref[:, cols]).astype(BF16)

        await_loads(*glu_grad)
        glu_grad_rows(base_down, r.hid, r.gd)
        if turn == 0:
            stats.stage(1)
        line.pump(ready(base_left), 1)
        mid_sum.middle(0)
        glu_grad_rows(base_left, grad_left_ref, r.n2)
        line.pump(ready(base_right), 1)
        for part in range(1, SUPER):
            mid_sum.middle(part)
        glu_grad_rows(base_right, grad_right_ref, r.n2)
        for part in range(SUPER):
            line.pump(ready(base_out), 2 - part)
            for h in range(2):
                mid_sum.finish(part, h)
                for i in range(half // step_rows):
                    offset = (2 * part + h) * half + i * step_rows
                    rows = slice(offset, offset + step_rows)
                    total = mid_sum.total(part, h, i * step_rows, step_rows)
                    new = back_rows(total, r.mid[rows, :], r.g[rows, :])
                    r.gm[rows, :] = new
                    r.ga[aligned(own_start + offset, step_rows), :] = new.astype(BF16)
            second.start(part)
        mid_sum.drain()
        if turn == 0:
            stats.stage(2)
        if turn + 1 < layers:
            load(layer - 1, *glu_in, *glu_grad)
        if turn == 0:
            stats.stage(3)
        def out_back(part, step):
            member = place.member(step)
            for chunk in range(part_rows // 128):
                number = part * (part_rows // 128) + chunk
                rows = aligned(member * block + number * 128, 128)
                grad_branch = nt(r.ga[rows, :], r.wo[...])
                gate = r.gate[rows, :]
                normed = r.heads[rows, :] * widen(r.scale[rows, :], local // 128)
                grad_normed = grad_branch * gate
                r.dx[rows, 3 * local : 4 * local] = (grad_branch * normed).astype(BF16)
                r.branch[rows, :] = (normed * gate).astype(BF16)
                r.gate[rows, :] = grad_normed
                row_sums(grad_normed * normed, r.inner, member * per_block + number)

        gather_stage(second, out_back, lambda i: line.pump(ready(base_out), 2))
        share.start()
        line.release(turn, base_gate)
        r.grads[base_out : base_out + local, :] = tn(r.branch[...], r.ga[...]).astype(BF16)
        line.pump(ready(base_gate), 1)

        def in_grad_rows(number, base):
            cols = slice(number * local, (number + 1) * local)
            line.release(turn, base + local)
            for n in range(width // local):
                part_grad = tn(r.n1[:, n * local : (n + 1) * local], r.dx[:, cols])
                r.grads[base : base + local, n * local : (n + 1) * local] = part_grad.astype(BF16)

        await_loads("n1")
        in_grad_rows(3, base_gate)
        line.pump(ready(base_qkv), 1)
        await_loads(*attn_in)
        r.intot[...] = share.total() / width
        for chunk in range(length // 128):
            rows = slice(chunk * 128, (chunk + 1) * 128)
            scale = widen(r.scale[rows, :], local // 128)
            inner = widen(spread(r.intot[...], chunk), local // 128)
            normed = r.heads[rows, :] * scale
            r.dh[rows, :] = (scale * (r.gate[rows, :] - normed * inner)).astype(BF16)
        share.drain()
        second.drain()
        if turn + 1 < layers:
            load(layer - 1, *out_in)
        line.pump(ready(base_qkv), 1)

        @pl.loop(0, heads_here)
        def _(head):
            wide = aligned(head * 2 * HDIM, 2 * HDIM)
            thin = aligned(head * HDIM, HDIM)
            for col_tile in range(tiles_here):
                cols = slice(col_tile * size, (col_tile + 1) * size)
                keys = r.k[cols, wide]
                values = r.v[cols, thin]
                acc_key, acc_value = None, None
                for row_tile in range(col_tile, tiles_here):
                    rows = slice(row_tile * size, (row_tile + 1) * size)
                    queries = r.q[rows, wide]
                    grads = r.dh[rows, thin]
                    weight = tile_weight(r, first_head, head, row_tile, col_tile, size)
                    scores = (nt(queries, keys) * weight).astype(BF16)
                    pulled = (nt(grads, values) * weight).astype(BF16)
                    term = nn(pulled, keys)
                    if col_tile == 0:
                        r.dq[rows, :] = term
                    else:
                        r.dq[rows, :] += term
                    key_term = tn(pulled, queries)
                    value_term = tn(scores, grads)
                    acc_key = key_term if acc_key is None else acc_key + key_term
                    acc_value = value_term if acc_value is None else acc_value + value_term
                r.dk[cols, :] = acc_key
                r.dx[cols, aligned(2 * local + head * HDIM, HDIM)] = acc_value.astype(BF16)
            for row_tile in range(tiles_here):
                rows = slice(row_tile * size, (row_tile + 1) * size)
                cosine, sine = r.cos[rows, :], r.sin[rows, :]
                for grad, lin, base in ((r.dq, r.ql, 0), (r.dk, r.kl, local)):
                    v = lin[rows, thin].astype(F32)
                    gate = 1.0 / (1.0 + jnp.exp(-v))
                    back = grad[rows, :HDIM] * cosine + grad[rows, HDIM:] * sine
                    back = back * (gate + v * gate * (1.0 - gate))
                    r.dx[rows, aligned(base + head * HDIM, HDIM)] = back.astype(BF16)

        if turn + 1 < layers:
            load(layer - 1, *attn_in)
        await_loads(*in_in)
        last = turn == layers - 1
        if last:
            for number in range(3):
                in_grad_rows(number, base_qkv + number * local)
        for part in range(SUPER):
            for step in (3, 1, 2, 0):
                rows = aligned(place.member(step) * block + part * part_rows, part_rows)
                total = None
                for n, w in enumerate((r.wq, r.wk, r.wv, r.wg)):
                    term = nt(r.dx[rows, n * local : (n + 1) * local], w[...])
                    total = term if total is None else total + term
                r.part[rows, :] = total.astype(BF16)
                in_sum.send_block(part, step)
            line.pump(ready(cfg.chunks * CHUNK if last else base_qkv), 2 if last else 1)
        for number in range(3):
            if not last:
                in_grad_rows(number, base_qkv + number * local)
            line.pump(ready(base_qkv + (number + 1) * local), 2 if last else 1)
            if number < SUPER:
                in_sum.middle(number)
        if turn + 1 < layers:
            load(layer - 1, *in_in, "n1")
        for part in range(SUPER):
            line.pump(ready(cfg.chunks * CHUNK), 2)
            for h in range(2):
                in_sum.finish(part, h)
                for i in range(half // step_rows):
                    offset = (2 * part + h) * half + i * step_rows
                    rows = slice(offset, offset + step_rows)
                    total = in_sum.total(part, h, i * step_rows, step_rows)
                    values = getattr(r, "x%d" % layer)[rows, :].astype(F32)
                    new = back_rows(total, values, r.gm[rows, :])
                    if layer > 0:
                        r.g[rows, :] = new
                        r.gd[aligned(own_start + offset, step_rows), :] = new.astype(BF16)
                    else:
                        r.go[rows, :] = new.astype(BF16)
            if layer > 0:
                firsts[layer - 1].start(part)
        in_sum.drain()
    stats.finish()
    line.finish()


def call_kernel(body, cfg, inputs, outputs, scratch, collective_id, name):
    vmem, anywhere = pl.BlockSpec(memory_space=pltpu.VMEM), pl.BlockSpec(memory_space=pl.ANY)
    names = list(inputs) + list(outputs) + list(scratch)
    result = pl.pallas_call(
        functools.partial(body, cfg, names),
        out_shape=[shape for shape, _ in outputs.values()],
        in_specs=[vmem if placed else anywhere for _, placed in inputs.values()],
        out_specs=[vmem if placed else anywhere for _, placed in outputs.values()],
        scratch_shapes=list(scratch.values()),
        compiler_params=pltpu.CompilerParams(
            collective_id=collective_id, has_side_effects=collective_id is not None, vmem_limit_bytes=VMEM_LIMIT
        ),
        name=name,
    )(*[array for array, _ in inputs.values()])
    return dict(zip(outputs, result))


def collective_scratch(cfg, copies, lead):
    dma = pltpu.SemaphoreType.DMA
    half = cfg.block // (2 * SUPER)
    out = {}
    for name in ("ag1", "ag2", "rs1", "rs2"):
        out[name + "_send"] = dma((*lead, SUPER, 6))
        out[name + "_recv"] = dma((*lead, SUPER, 6))
    for name in copies:
        out["land" + name] = pltpu.VMEM((SUPER, 6, half, cfg.width), BF16)
        out["part" + name] = pltpu.VMEM((cfg.length, cfg.width), BF16)
    out["local_sem"] = dma((64,))
    return out


def weight_scratch(cfg):
    v = pltpu.VMEM
    return dict(
        wq=v((cfg.width, cfg.local), BF16), wk=v((cfg.width, cfg.local), BF16),
        wv=v((cfg.width, cfg.local), BF16), wg=v((cfg.width, cfg.local), BF16),
        wo=v((cfg.local, cfg.width), BF16), wl=v((cfg.ff, cfg.width), BF16),
        wr=v((cfg.ff, cfg.width), BF16), wd=v((cfg.ff, cfg.width), BF16),
    )


def table_scratch(cfg):
    v = pltpu.VMEM
    return dict(
        segc=v((cfg.length, 128), F32), segf=v((8, 128), F32),
        tiles=v((cfg.heads_here, 2, cfg.block, cfg.block), F32),
    )


def run_forward(cfg, x, upstream, tables, weights):
    v, dma, s = pltpu.VMEM, pltpu.SemaphoreType.DMA, jax.ShapeDtypeStruct
    rows, wide, local, ff, block = cfg.length, cfg.width, cfg.local, cfg.ff, cfg.block
    inputs = dict(x=(x, True), **{k: (a, True) for k, a in tables.items()}, **{k + "_h": (a, False) for k, a in weights.items()})
    kept = dict(
        n1=((rows, wide), BF16), ql=((rows, local), BF16), kl=((rows, local), BF16),
        q=((rows, 2 * local), BF16), k=((rows, 2 * local), BF16), v=((rows, local), BF16),
        gate=((rows, local), F32), heads=((rows, local), F32), mid=((block, wide), F32),
        n2=((rows, wide), BF16), left=((rows, ff), BF16), right=((rows, ff), BF16), hid=((rows, ff), BF16),
    )
    outputs = dict(
        xo=(s((block, wide), BF16 if cfg.last else F32), True), stat=(s((8, 128), F32), True), ss_h=(s((8, 128), F32), False),
        **{k + "_h": (s(*a), False) for k, a in kept.items()},
    )
    scratch = dict(
        **weight_scratch(cfg), **collective_scratch(cfg, ("1", "2"), ()), **table_scratch(cfg),
        **{k: v(*a) for k, a in kept.items()}, u=v((rows, local), BF16), stat_wide=v((8, wide), F32),
        ss=v((8, 128), F32), sstot=v((8, 128), F32), scale=v((block, 128), F32),
        ss_land=v((3, 8, 128), F32), ss_send=dma((3,)), ss_recv=dma((3,)),
    )
    if cfg.last:
        inputs.update(up_h=(upstream, False))
        outputs.update(gd_h=(s((rows, wide), BF16), False))
        scratch.update(gd=v((rows, wide), BF16), ag3_send=dma((SUPER, 6)), ag3_recv=dma((SUPER, 6)))
    return call_kernel(fwd_kernel, cfg, inputs, outputs, scratch, cfg.layer, "layer_forward")


SAVED = ("ss", "mid", "n1", "ql", "kl", "q", "k", "v", "gate", "heads", "n2", "left", "right", "hid")


def run_backward(cfg, upstream, xs, saved, tables, weights):
    v, dma, s = pltpu.VMEM, pltpu.SemaphoreType.DMA, jax.ShapeDtypeStruct
    rows, wide, local, ff, block = cfg.length, cfg.width, cfg.local, cfg.ff, cfg.block
    inputs = dict(up=(upstream, True), gd_h=(saved[-1]["gd_h"], False), **{k: (a, True) for k, a in tables.items()}, **{k + "_h": (a, False) for k, a in weights.items()})
    for layer in range(cfg.layers):
        inputs["x%d" % layer] = (xs[layer], True)
        inputs["stat%d" % layer] = (saved[layer]["stat"], True)
        for key in SAVED:
            inputs["%s%d_h" % (key, layer)] = (saved[layer][key + "_h"], False)
    total_rows = cfg.chunks * CHUNK
    outputs = dict(
        go=(s((block, wide), BF16), True), stat_total=(s((8, 128), F32), True),
        out_h=(s((cfg.layers * total_rows, wide), BF16), False),
    )
    small, ring, ring_sem = v((8, 128), F32), v((SLOTS, CHUNK // 2, wide), BF16), dma((SLOTS,))
    scratch = dict(
        **weight_scratch(cfg), **collective_scratch(cfg, ("",), (cfg.layers,)), **table_scratch(cfg),
        n1=v((rows, wide), BF16), ql=v((rows, local), BF16), kl=v((rows, local), BF16),
        q=v((rows, 2 * local), BF16), k=v((rows, 2 * local), BF16), v=v((rows, local), BF16),
        gate=v((rows, local), F32), heads=v((rows, local), F32), n2=v((rows, wide), BF16),
        left=v((rows, ff), BF16), right=v((rows, ff), BF16), hid=v((rows, ff), BF16),
        gd=v((rows, wide), BF16), ga=v((rows, wide), BF16),
        g=v((block, wide), F32), gm=v((block, wide), F32), mid=v((block, wide), F32),
        dh=v((rows, local), BF16), branch=v((rows, local), BF16), dx=v((rows, 4 * local), BF16),
        dq=v((rows, 2 * HDIM), F32), dk=v((rows, 2 * HDIM), F32),
        grads=v((total_rows, wide), BF16), scale=v((rows, 128), F32),
        ss=small, inner=small, intot=small,
        inner_land=v((cfg.layers, 3, 8, 128), F32), in_send=dma((cfg.layers, 3)), in_recv=dma((cfg.layers, 3)),
        pair_land=ring, right_land=ring, left_land=ring,
        pair_send=ring_sem, pair_recv=ring_sem, right_send=ring_sem, right_recv=ring_sem, left_send=ring_sem,
        left_recv=ring_sem, give_send=ring_sem, give_recv=ring_sem, keep_sem=ring_sem,
        stat_mine=small, stat_square=small, stat_pair=small, stat_right=small, stat_left=small,
        stat_land=v((3, 8, 128), F32), st_send=dma((3,)), st_recv=dma((3,)),
        line_land=v((3, 8, 128), F32), line_send=dma((3,)), line_recv=dma((3,)),
    )
    return call_kernel(bwd_kernel, cfg, inputs, outputs, scratch, cfg.layers, "layers_backward")


def widen_kernel(cfg, names, *refs):
    r = namespace(names, refs)
    tasks = []
    for layer in range(cfg.layers):
        for number, target in enumerate((r.down, r.left, r.right, r.out)):
            start, stop = cfg.bases[number], cfg.bases[number + 1]
            rows = (stop - start) // 2 if stop - start > 512 else stop - start
            for first in range(start, stop, rows):
                tasks.append((layer, first, rows, [(target.at[layer, pl.ds(first - start, rows), :], slice(None))]))
        for number, target in enumerate((r.gate, r.query, r.key, r.value)):
            pieces = [
                (target.at[layer, pl.ds(n * cfg.local, cfg.local), :], slice(n * cfg.local, (n + 1) * cfg.local))
                for n in range(cfg.width // cfg.local)
            ]
            tasks.append((layer, cfg.bases[4] + number * cfg.local, cfg.local, pieces))
    depth = 3

    def fetch(task):
        layer, first, rows, _ = tasks[task]
        start = layer * cfg.chunks * CHUNK + first
        slot = task % depth
        return pltpu.make_async_copy(r.grads.at[pl.ds(start, rows), :], r.narrow.at[slot, pl.ds(0, rows), :], r.in_sem.at[slot])

    def store(task):
        _, _, rows, pieces = tasks[task]
        slot = task % depth
        return [
            pltpu.make_async_copy(r.wide.at[slot, pl.ds(0, rows), lanes], target, r.out_sem.at[slot, n])
            for n, (target, lanes) in enumerate(pieces)
        ]

    for task in range(min(depth, len(tasks))):
        fetch(task).start()
    for task in range(len(tasks)):
        slot, rows = task % depth, tasks[task][2]
        fetch(task).wait()
        if task >= depth:
            for copy in store(task - depth):
                copy.wait()

        @pl.loop(0, rows // 32)
        def _(i):
            part = aligned(i * 32, 32)
            r.wide[slot, part, :] = r.narrow[slot, part, :].astype(F32)

        for copy in store(task):
            copy.start()
        if task + depth < len(tasks):
            fetch(task + depth).start()
    for task in range(max(len(tasks) - depth, 0), len(tasks)):
        for copy in store(task):
            copy.wait()


def run_widen(cfg, grads):
    v, dma, s = pltpu.VMEM, pltpu.SemaphoreType.DMA, jax.ShapeDtypeStruct
    thin, flat = s((cfg.layers, cfg.width, cfg.local), F32), s((cfg.layers, cfg.ff, cfg.width), F32)
    outputs = dict(
        down=(flat, False), left=(flat, False), right=(flat, False), out=(s((cfg.layers, cfg.local, cfg.width), F32), False),
        gate=(thin, False), query=(thin, False), key=(thin, False), value=(thin, False),
    )
    rows = max(cfg.ff // 2, cfg.local, 512)
    scratch = dict(
        narrow=v((3, rows, cfg.width), BF16), wide=v((3, rows, cfg.width), F32),
        in_sem=dma((3,)), out_sem=dma((3, cfg.width // cfg.local)),
    )
    return call_kernel(widen_kernel, cfg, dict(grads=(grads, False)), outputs, scratch, None, "widen_gradients")


def per_device_square(
    tokens, upstream, segment_ids, query_proj, key_proj, value_proj, gate_proj, output_proj, left_proj, right_proj, down_proj
):
    layers = query_proj.shape[0]
    block, width = tokens.shape
    length = segment_ids.shape[0]
    local, ff = query_proj.shape[2], left_proj.shape[2]
    heads_here = local // HDIM
    positions = np.arange(length, dtype=np.float32)
    frequency = np.exp(np.float32(-math.log(10000.0)) * np.arange(HDIM, dtype=np.float32) / np.float32(HDIM))
    angles = positions[:, None] * frequency[None, :]
    slopes = np.exp2(-8.0 * (np.arange(HEADS) + 1.0) / HEADS)
    decays = np.concatenate([-slopes * (1.0 - depth_start - depth_step * layer) for layer in range(layers)])
    tables = dict(
        cos=jnp.asarray(np.cos(angles)), sin=jnp.asarray(np.sin(angles)),
        dec=jnp.asarray(np.broadcast_to(decays[:, None], (layers * HEADS, 128)).astype(np.float32)),
        seg=segment_ids.reshape(8, length // 8),
    )
    weights = dict(
        wq=query_proj, wk=key_proj, wv=value_proj, wg=gate_proj, wo=output_proj,
        wl=jnp.swapaxes(left_proj, 1, 2), wr=jnp.swapaxes(right_proj, 1, 2), wd=down_proj,
    )
    ends = np.cumsum([0, ff, ff, ff, local, local, 3 * local]).tolist()
    common = dict(
        layers=layers, block=block, length=length, width=width, local=local, ff=ff, heads_here=heads_here,
        pairs=lax.axis_size("dp") // 2, bases=ends, chunks=-(-ends[-1] // CHUNK),
    )
    current, xs, saved = tokens, [], []
    for layer in range(layers):
        xs.append(current)
        cfg = types.SimpleNamespace(layer=layer, last=layer == layers - 1, **common)
        saved.append(run_forward(cfg, current, upstream, tables, weights))
        current = saved[-1]["xo"]
    back = run_backward(types.SimpleNamespace(**common), upstream, xs, saved, tables, weights)
    stats = jnp.sum(back["stat_total"][: 3 * layers], axis=1).reshape(layers, 3)
    rms_stats = jnp.sqrt(stats / (length * lax.axis_size("dp") * width))
    wide = run_widen(types.SimpleNamespace(**common), back["out_h"])
    return (
        current, back["go"], wide["query"], wide["key"], wide["value"], wide["gate"], wide["out"],
        jnp.swapaxes(wide["left"], 1, 2), jnp.swapaxes(wide["right"], 1, 2), wide["down"], rms_stats,
    )


def solution(mesh):
    square = dict(mesh.shape) == SQUARE_MESH
    body = per_device_square if square else per_device
    return jax.shard_map(
        body,
        mesh=mesh,
        in_specs=(
            P(("dp", "tensor"), None),
            P(("dp", "tensor"), None),
            P("dp"),
            P(None, None, "tensor"),
            P(None, None, "tensor"),
            P(None, None, "tensor"),
            P(None, None, "tensor"),
            P(None, "tensor", None),
            P(None, None, "tensor"),
            P(None, None, "tensor"),
            P(None, "tensor", None),
        ),
        out_specs=(
            P(("dp", "tensor"), None),
            P(("dp", "tensor"), None),
            P(None, None, "tensor"),
            P(None, None, "tensor"),
            P(None, None, "tensor"),
            P(None, None, "tensor"),
            P(None, "tensor", None),
            P(None, None, "tensor"),
            P(None, None, "tensor"),
            P(None, "tensor", None),
            P(),
        ),
        check_vma=False,
    )
```

```python
import functools
import math
import types

import jax
import jax.numpy as jnp
import numpy as np
from jax import lax
from jax.experimental import pallas as pl
from jax.experimental.pallas import tpu as pltpu
from jax.sharding import PartitionSpec as P

HEADS = 8
HDIM = 128
BLK = 512


epsilon = 1e-06
depth_start = 0.5
depth_step = 1.0 / 24.0
highest = lax.Precision.HIGHEST


def rms_rows(values):
    return values * lax.rsqrt(jnp.mean(values * values, axis=1, keepdims=True) + epsilon)


def rms_back(values, gradient):
    scaling = lax.rsqrt(jnp.mean(values * values, axis=1, keepdims=True) + epsilon)
    normed = values * scaling
    return scaling * (gradient - normed * jnp.mean(gradient * normed, axis=1, keepdims=True))


def contract_last(left_part, right_part):
    return lax.dot_general(
        left_part, right_part, (((1,), (1,)), ((), ())), preferred_element_type=jnp.float32
    )


def contract_first(left_part, right_part):
    return lax.dot_general(
        left_part, right_part, (((0,), (0,)), ((), ())), preferred_element_type=jnp.float32
    )


def rotate(values, cosine, sine_table):
    return jnp.concatenate([values * cosine[:, None, :], values * sine_table[:, None, :]], axis=2)


def unrotate(gradient, cosine, sine_table):
    half_width = gradient.shape[2] // 2
    return (
        gradient[:, :, :half_width] * cosine[:, None, :]
        + gradient[:, :, half_width:] * sine_table[:, None, :]
    )


def split_blocks(array, block_count):
    return array.reshape((block_count, BLK) + array.shape[1:])


def block_weights(seg_block, next_seg, decay_log):
    block_width = seg_block.shape[0]
    places = jnp.arange(block_width, dtype=jnp.float32)
    distance = places[:, None] - places[None, :]
    allowed = (distance >= 0) & (seg_block[:, None] == seg_block[None, :])
    decay_grid = jnp.where(
        allowed[None], jnp.exp(decay_log[:, None, None] * jnp.maximum(distance, 0.0)[None]), 0.0
    )
    first_seg = seg_block[0]
    query_gain = jnp.where(
        (seg_block == first_seg)[:, None], jnp.exp(places[:, None] * decay_log[None, :]), 0.0
    )
    key_gain = jnp.where(
        (seg_block == next_seg)[:, None],
        jnp.exp((block_width - places)[:, None] * decay_log[None, :]),
        0.0,
    )
    carry_gain = jnp.where(first_seg == next_seg, jnp.exp(decay_log * block_width), 0.0)
    return (decay_grid, query_gain, key_gain, carry_gain)


def next_segments(segments, block_count):
    seg_blocks = segments.reshape(block_count, BLK)
    return (seg_blocks, jnp.concatenate([seg_blocks[1:, 0], jnp.full((1,), -1, jnp.int32)]))


def attend_forward(queries, keys_rot, values, segments, decay_log):
    length, heads_here, pair_width = queries.shape
    block_count = length // BLK
    seg_blocks, next_segs = next_segments(segments, block_count)

    def advance(state_now, block_items):
        query_block, key_block, value_block, seg_block, next_seg = block_items
        query_float = query_block.astype(jnp.float32)
        key_float = key_block.astype(jnp.float32)
        value_float = value_block.astype(jnp.float32)
        decay_grid, query_gain, key_gain, carry_gain = block_weights(seg_block, next_seg, decay_log)
        scores = (
            jnp.einsum("rhd,shd->hrs", query_block, key_block, preferred_element_type=jnp.float32)
            * decay_grid
        )
        block_out = jnp.einsum("hrs,she->rhe", scores, value_float, precision=highest)
        block_out = (
            block_out
            + jnp.einsum("rhd,hde->rhe", query_float, state_now, precision=highest)
            * query_gain[:, :, None]
        )
        new_state = carry_gain[:, None, None] * state_now + jnp.einsum(
            "shd,she->hde", key_float * key_gain[:, :, None], value_float, precision=highest
        )
        return (new_state, (block_out, state_now))

    zero_state = jnp.zeros((heads_here, pair_width, pair_width // 2), jnp.float32)
    _, (block_outs, states) = lax.scan(
        advance,
        zero_state,
        (
            split_blocks(queries, block_count),
            split_blocks(keys_rot, block_count),
            split_blocks(values, block_count),
            seg_blocks,
            next_segs,
        ),
    )
    return (block_outs.reshape(length, heads_here * (pair_width // 2)), states)


def attend_backward(queries, keys_rot, values, segments, decay_log, states, grad_heads):
    length, heads_here, pair_width = queries.shape
    block_count = length // BLK
    seg_blocks, next_segs = next_segments(segments, block_count)

    def retreat(later_grad, block_items):
        query_block, key_block, value_block, seg_block, next_seg, state_now, grad_block = (
            block_items
        )
        query_float = query_block.astype(jnp.float32)
        key_float = key_block.astype(jnp.float32)
        value_float = value_block.astype(jnp.float32)
        decay_grid, query_gain, key_gain, carry_gain = block_weights(seg_block, next_seg, decay_log)
        scores = (
            jnp.einsum("rhd,shd->hrs", query_block, key_block, preferred_element_type=jnp.float32)
            * decay_grid
        )
        pulled = jnp.einsum("rhe,she->hrs", grad_block, value_float, precision=highest) * decay_grid
        grad_query = jnp.einsum("hrs,shd->rhd", pulled, key_float, precision=highest)
        grad_query = (
            grad_query
            + jnp.einsum("rhe,hde->rhd", grad_block, state_now, precision=highest)
            * query_gain[:, :, None]
        )
        grad_key = jnp.einsum("hrs,rhd->shd", pulled, query_float, precision=highest)
        grad_key = (
            grad_key
            + jnp.einsum("she,hde->shd", value_float, later_grad, precision=highest)
            * key_gain[:, :, None]
        )
        grad_value = jnp.einsum("hrs,rhe->she", scores, grad_block, precision=highest)
        grad_value = (
            grad_value
            + jnp.einsum("shd,hde->she", key_float, later_grad, precision=highest)
            * key_gain[:, :, None]
        )
        earlier_grad = carry_gain[:, None, None] * later_grad + jnp.einsum(
            "rhd,rhe->hde", query_float * query_gain[:, :, None], grad_block, precision=highest
        )
        return (earlier_grad, (grad_query, grad_key, grad_value))

    zero_state = jnp.zeros((heads_here, pair_width, pair_width // 2), jnp.float32)
    _, (grad_query, grad_key, grad_value) = lax.scan(
        retreat,
        zero_state,
        (
            split_blocks(queries, block_count),
            split_blocks(keys_rot, block_count),
            split_blocks(values, block_count),
            seg_blocks,
            next_segs,
            states,
            split_blocks(grad_heads, block_count),
        ),
        reverse=True,
    )
    return (
        grad_query.reshape(length, heads_here, pair_width),
        grad_key.reshape(length, heads_here, pair_width),
        grad_value.reshape(length, heads_here, pair_width // 2),
    )


def per_device(
    tokens,
    upstream,
    segment_ids,
    query_proj,
    key_proj,
    value_proj,
    gate_proj,
    output_proj,
    left_proj,
    right_proj,
    down_proj,
):
    layers = query_proj.shape[0]
    row_count, model_width = tokens.shape
    length = segment_ids.shape[0]
    local_width = query_proj.shape[2]
    ff_local = left_proj.shape[2]
    heads_here = local_width // HDIM
    positions = jnp.arange(length, dtype=jnp.float32)
    frequency = jnp.exp(-math.log(10000.0) * jnp.arange(HDIM, dtype=jnp.float32) / HDIM)
    angles = positions[:, None] * frequency[None, :]
    cosine = jnp.cos(angles)
    sine_table = jnp.sin(angles)
    head_index = (lax.axis_index("tensor") * heads_here + jnp.arange(heads_here)).astype(
        jnp.float32
    )
    slopes = jnp.exp2(-8.0 * (head_index + 1.0) / HEADS)

    def gather_normed(normed):
        return lax.all_gather(normed, "tensor", axis=0, tiled=True)

    def gather_again(normed):
        return lax.all_gather(normed, "tensor", axis=0, tiled=True)

    def gather_grads(gradient):
        return lax.all_gather(gradient, "tensor", axis=0, tiled=True)

    def branch_sum(operand, matrix):
        return lax.psum_scatter(
            jnp.dot(operand, matrix, preferred_element_type=jnp.float32).astype(jnp.bfloat16),
            "tensor",
            scatter_dimension=0,
            tiled=True,
        ).astype(jnp.float32)

    def input_sum(pieces, matrix):
        operand = jnp.concatenate(pieces, axis=1)
        return lax.psum_scatter(
            contract_last(operand, matrix).astype(jnp.bfloat16),
            "tensor",
            scatter_dimension=0,
            tiled=True,
        ).astype(jnp.float32)

    current = tokens.astype(jnp.float32)
    saved_layers = []
    stat_terms = []
    for layer_index in range(layers):
        residual = current
        normed = rms_rows(residual).astype(jnp.bfloat16)
        full_normed = gather_normed(normed)
        attn_weight = jnp.concatenate(
            [
                query_proj[layer_index],
                key_proj[layer_index],
                value_proj[layer_index],
                gate_proj[layer_index],
            ],
            axis=1,
        )
        projected = jnp.dot(full_normed, attn_weight, preferred_element_type=jnp.float32)
        query_lin = projected[:, :local_width]
        key_lin = projected[:, local_width : 2 * local_width]
        values = (
            projected[:, 2 * local_width : 3 * local_width]
            .astype(jnp.bfloat16)
            .reshape(length, heads_here, HDIM)
        )
        gate_lin = projected[:, 3 * local_width :]
        queries = rotate(
            jax.nn.silu(query_lin).reshape(length, heads_here, HDIM), cosine, sine_table
        ).astype(jnp.bfloat16)
        keys_rot = rotate(
            jax.nn.silu(key_lin).reshape(length, heads_here, HDIM), cosine, sine_table
        ).astype(jnp.bfloat16)
        decay_log = -slopes * (1.0 - depth_start - depth_step * layer_index)
        heads_out, states = attend_forward(queries, keys_rot, values, segment_ids, decay_log)
        squares = lax.psum(jnp.sum(heads_out * heads_out, axis=1), "tensor")
        scaling = lax.rsqrt(squares / model_width + epsilon)[:, None]
        normed_heads = heads_out * scaling
        branch = (normed_heads * gate_lin).astype(jnp.bfloat16)
        attn_rows = branch_sum(branch, output_proj[layer_index])
        middle = residual + attn_rows
        normed_mid = rms_rows(middle).astype(jnp.bfloat16)
        full_mid = gather_normed(normed_mid)
        glu_weight = jnp.concatenate([left_proj[layer_index], right_proj[layer_index]], axis=1)
        gates_both = jnp.dot(full_mid, glu_weight, preferred_element_type=jnp.float32)
        left_lin = gates_both[:, :ff_local]
        right_lin = gates_both[:, ff_local:]
        hidden = (left_lin * right_lin).astype(jnp.bfloat16)
        glu_rows = branch_sum(hidden, down_proj[layer_index])
        current = middle + glu_rows
        stat_terms.append(
            jnp.stack(
                [
                    jnp.sum(attn_rows * attn_rows),
                    jnp.sum(glu_rows * glu_rows),
                    jnp.sum(current * current),
                ]
            )
        )
        saved_layers.append(
            (
                residual,
                middle,
                normed,
                normed_mid,
                full_normed,
                full_mid,
                attn_weight,
                glu_weight,
                query_lin,
                key_lin,
                gate_lin,
                queries,
                keys_rot,
                values,
                decay_log,
                states,
                normed_heads,
                scaling,
                branch,
                left_lin,
                right_lin,
                hidden,
            )
        )
    stat_sums = lax.psum(jnp.stack(stat_terms), ("dp", "tensor"))
    rms_stats = jnp.sqrt(stat_sums / (length * lax.axis_size("dp") * model_width))
    final_rows = current.astype(jnp.bfloat16)
    gradient = upstream.astype(jnp.float32)
    layer_results = [None] * layers
    for layer_index in reversed(range(layers)):
        (
            residual,
            middle,
            normed,
            normed_mid,
            full_normed,
            full_mid,
            attn_weight,
            glu_weight,
            query_lin,
            key_lin,
            gate_lin,
            queries,
            keys_rot,
            values,
            decay_log,
            states,
            normed_heads,
            scaling,
            branch,
            left_lin,
            right_lin,
            hidden,
        ) = saved_layers[layer_index]
        glu_grad = gather_grads(gradient.astype(jnp.bfloat16))
        grad_hidden = contract_last(glu_grad, down_proj[layer_index])
        down_part = contract_first(hidden, glu_grad)
        grad_left = (grad_hidden * right_lin).astype(jnp.bfloat16)
        grad_right = (grad_hidden * left_lin).astype(jnp.bfloat16)
        grad_gates = jnp.concatenate([grad_left, grad_right], axis=1)
        mid_rows = input_sum((grad_left, grad_right), glu_weight)
        source_mid = gather_again(normed_mid)
        glu_part = contract_first(source_mid, grad_gates)
        gradient = gradient + rms_back(middle, mid_rows)
        attn_grad = gather_grads(gradient.astype(jnp.bfloat16))
        output_part = contract_first(branch, attn_grad)
        grad_branch = contract_last(attn_grad, output_proj[layer_index])
        grad_normed = grad_branch * gate_lin
        grad_gate = (grad_branch * normed_heads).astype(jnp.bfloat16)
        inner_sum = lax.psum(jnp.sum(grad_normed * normed_heads, axis=1), "tensor")
        grad_heads = scaling * (grad_normed - normed_heads * (inner_sum / model_width)[:, None])
        grad_query, grad_key, grad_value = attend_backward(
            queries,
            keys_rot,
            values,
            segment_ids,
            decay_log,
            states,
            grad_heads.reshape(length, heads_here, HDIM),
        )
        sigmoid_query = jax.nn.sigmoid(query_lin)
        sigmoid_key = jax.nn.sigmoid(key_lin)
        query_back = unrotate(grad_query, cosine, sine_table).reshape(length, local_width)
        key_back = unrotate(grad_key, cosine, sine_table).reshape(length, local_width)
        grad_query_lin = (
            query_back * (sigmoid_query + query_lin * sigmoid_query * (1.0 - sigmoid_query))
        ).astype(jnp.bfloat16)
        grad_key_lin = (
            key_back * (sigmoid_key + key_lin * sigmoid_key * (1.0 - sigmoid_key))
        ).astype(jnp.bfloat16)
        grad_value_lin = grad_value.reshape(length, local_width).astype(jnp.bfloat16)
        grad_projected = jnp.concatenate(
            [grad_query_lin, grad_key_lin, grad_value_lin, grad_gate], axis=1
        )
        in_rows = input_sum((grad_query_lin, grad_key_lin, grad_value_lin, grad_gate), attn_weight)
        source_normed = gather_again(normed)
        attn_part = contract_first(source_normed, grad_projected)
        gradient = gradient + rms_back(residual, in_rows)
        query_part = attn_part[:, :local_width]
        key_part = attn_part[:, local_width : 2 * local_width]
        value_part = attn_part[:, 2 * local_width : 3 * local_width]
        gate_part = attn_part[:, 3 * local_width :]
        left_part = glu_part[:, :ff_local]
        right_part = glu_part[:, ff_local:]
        layer_results[layer_index] = (
            query_part,
            key_part,
            value_part,
            gate_part,
            output_part,
            left_part,
            right_part,
            down_part,
        )
    stacked = [
        jnp.stack([layer_results[index][member] for index in range(layers)]) for member in range(8)
    ]
    totals = (
        lax.psum(stacked[0].astype(jnp.bfloat16), "dp").astype(jnp.float32),
        lax.psum(stacked[1].astype(jnp.bfloat16), "dp").astype(jnp.float32),
        lax.psum(stacked[2].astype(jnp.bfloat16), "dp").astype(jnp.float32),
        lax.psum(stacked[3].astype(jnp.bfloat16), "dp").astype(jnp.float32),
        lax.psum(stacked[4].astype(jnp.bfloat16), "dp").astype(jnp.float32),
        lax.psum(stacked[5].astype(jnp.bfloat16), "dp").astype(jnp.float32),
        lax.psum(stacked[6].astype(jnp.bfloat16), "dp").astype(jnp.float32),
        lax.psum(stacked[7].astype(jnp.bfloat16), "dp").astype(jnp.float32),
    )
    input_grad = gradient.astype(jnp.bfloat16)
    return (
        final_rows,
        input_grad,
        totals[0],
        totals[1],
        totals[2],
        totals[3],
        totals[4],
        totals[5],
        totals[6],
        totals[7],
        rms_stats,
    )


SQUARE_MESH = {"dp": 8, "tensor": 4}


F32 = jnp.float32
BF16 = jnp.bfloat16
MESH = pl.DeviceIdType.MESH
VMEM_LIMIT = 60 * 2**20
SUPER = 2
CHUNK = 128
HOP = 3
SLOTS = 16


def nn(a, b):
    return lax.dot_general(a, b, (((1,), (0,)), ((), ())), preferred_element_type=F32)


def nt(a, b):
    return lax.dot_general(a, b, (((1,), (1,)), ((), ())), preferred_element_type=F32)


def tn(a, b):
    return lax.dot_general(a, b, (((0,), (0,)), ((), ())), preferred_element_type=F32)


def exact(a, b, dims):
    return lax.dot_general(a, b, (dims, ((), ())), precision=highest, preferred_element_type=F32)


def aligned(index, size):
    return pl.ds(pl.multiple_of(index, size), size)


class Place:
    def __init__(self, pairs):
        self.dp = lax.axis_index("dp")
        self.me = lax.axis_index("tensor")
        self.low = lax.rem(self.me, 2)
        self.high = self.me // 2
        self.core = lax.rem(self.dp, 2)
        self.at = self.dp // 2
        self.last = pairs - 1

    def member(self, step):
        low = lax.rem(self.low + lax.rem(step, 2), 2)
        high = lax.rem(self.high + step // 2, 2)
        return 2 * high + low

    def device(self, step):
        return (self.dp, self.member(step))

    def partner(self):
        return (self.dp + 1 - 2 * self.core, self.me)

    def right(self):
        return (self.dp + 2, self.me)

    def left(self):
        return (self.dp - 2, self.me)

    def greet(self, line):
        barrier = pltpu.get_barrier_semaphore()

        def signal(device):
            pl.semaphore_signal(barrier, inc=1, device_id=device, device_id_type=MESH)

        for step in (1, 2, 3):
            signal(self.device(step))
        if not line:
            pl.semaphore_wait(barrier, 3)
            return
        signal(self.partner())

        @pl.when(self.at < self.last)
        def _():
            signal(self.right())

        @pl.when(self.at > 0)
        def _():
            signal(self.left())

        pl.semaphore_wait(barrier, 4 + jnp.minimum(self.at, 1) + jnp.minimum(self.last - self.at, 1))


class Wire:
    def __init__(self, device, send_sem, recv_sem, source, target, landing):
        self.source, self.target, self.landing = source, target, landing
        self.common = dict(send_sem=send_sem, recv_sem=recv_sem, device_id=device, device_id_type=MESH)

    def out(self):
        return pltpu.make_async_remote_copy(src_ref=self.source, dst_ref=self.target, **self.common)

    def start(self):
        self.out().start()

    def wait_recv(self):
        pltpu.make_async_remote_copy(src_ref=self.landing, dst_ref=self.landing, **self.common).wait_recv()

    def wait_send(self):
        self.out().wait_send()


class Gather:
    def __init__(self, place, buf, send, recv, block):
        self.place, self.buf, self.block = place, buf, block
        self.send, self.recv = send, recv
        self.half = block // (2 * SUPER)

    def rows(self, step, part, half):
        start = self.place.member(step) * self.block + (2 * part + half) * self.half
        return self.buf.at[aligned(start, self.half)]

    def wire(self, part, number):
        step, owner, half = ((1, 0, 0), (2, 0, 1), (1, 0, 1), (2, 0, 0), (2, 1, 0), (1, 2, 1))[number]
        source = self.rows(owner, part, half)
        landing = self.rows((0, 1, 2, 3)[owner ^ step], part, half)
        return Wire(self.place.device(step), self.send.at[part, number], self.recv.at[part, number], source, source, landing)

    def start(self, part):
        for number in range(4):
            self.wire(part, number).start()

    def forward(self, part):
        self.wire(part, 0).wait_recv()
        self.wire(part, 4).start()
        self.wire(part, 1).wait_recv()
        self.wire(part, 5).start()

    def finish(self, part, step):
        for number in {0: (), 1: (2,), 2: (3,), 3: (4, 5)}[step]:
            self.wire(part, number).wait_recv()

    def drain(self):
        for part in range(SUPER):
            for number in range(6):
                self.wire(part, number).wait_send()


def gather_stage(gather, block_fn, beside):
    @pl.loop(0, 4 * SUPER)
    def _(i):
        mixed = i - SUPER
        part = jnp.where(i < SUPER, i, jnp.where(i < 3 * SUPER, mixed // 2, i - 3 * SUPER))
        step = jnp.where(i < SUPER, 0, jnp.where(i < 3 * SUPER, 1 + lax.rem(mixed, 2), 3))

        @pl.when(i == SUPER)
        def _():
            for one in range(SUPER):
                beside(one)
                gather.forward(one)

        @pl.when(i == 3 * SUPER)
        def _():
            beside(SUPER)

        for which in (1, 2, 3):
            @pl.when(step == which)
            def _():
                gather.finish(part, which)
        block_fn(part, step)


class Scatter:
    def __init__(self, place, buf, land, send, recv, block):
        self.place, self.buf, self.land, self.block = place, buf, land, block
        self.send, self.recv = send, recv
        self.half = block // (2 * SUPER)

    def rows(self, step, part, half):
        start = self.place.member(step) * self.block + (2 * part + half) * self.half
        return aligned(start, self.half)

    def wire(self, part, number):
        step, owner, half = ((1, 3, 0), (1, 1, 0), (2, 3, 1), (2, 2, 1), (2, 2, 0), (1, 1, 1))[number]
        target = self.land.at[part, number]
        return Wire(
            self.place.device(step), self.send.at[part, number], self.recv.at[part, number],
            self.buf.at[self.rows(owner, part, half)], target, target,
        )

    def send_block(self, part, step):
        for number in {0: (), 1: (1,), 2: (3,), 3: (0, 2)}[step]:
            self.wire(part, number).start()

    def middle(self, part):
        for first, second, owner, half in ((0, 4, 2, 0), (2, 5, 1, 1)):
            self.wire(part, first).wait_recv()
            rows = self.rows(owner, part, half)
            self.buf[rows, :] = self.buf[rows, :] + self.land[part, first]
            self.wire(part, second).start()

    def finish(self, part, half):
        first, second = ((1, 4), (3, 5))[half]
        self.wire(part, first).wait_recv()
        self.wire(part, second).wait_recv()

    def total(self, part, half, start, count):
        first, second = ((1, 4), (3, 5))[half]
        own = self.place.me * self.block + (2 * part + half) * self.half + start
        rows = pl.ds(start, count)
        return (
            self.buf[aligned(own, count), :].astype(F32)
            + self.land[part, first, rows, :].astype(F32)
            + self.land[part, second, rows, :].astype(F32)
        )

    def drain(self):
        for part in range(SUPER):
            for number in range(6):
                self.wire(part, number).wait_send()


class Share:
    def __init__(self, place, mine, land, send, recv):
        self.wires = [
            Wire(place.device(step), send.at[step - 1], recv.at[step - 1], mine, land.at[step - 1], land.at[step - 1])
            for step in (1, 2, 3)
        ]
        self.mine, self.land = mine, land

    def start(self):
        for wire in self.wires:
            wire.start()

    def total(self):
        for wire in self.wires:
            wire.wait_recv()
        return self.mine[...] + self.land[0] + self.land[1] + self.land[2]

    def drain(self):
        for wire in self.wires:
            wire.wait_send()


class Local:
    def __init__(self, sems):
        self.sems, self.used = sems, 0

    def start(self, source, target):
        copy = pltpu.make_async_copy(source, target, self.sems.at[self.used])
        self.used += 1
        copy.start()
        return copy


def row_sums(values, target, chunk):
    sums = exact(jnp.ones((8, values.shape[1]), F32), values, ((1,), (1,)))
    target[pl.ds(chunk, 1), :] = sums[0:1, :]


def spread(sums, chunk):
    picked = (lax.broadcasted_iota(jnp.int32, (8, 128), 0) == chunk).astype(F32)
    return exact(sums, picked, ((0,), (0,)))


def widen(columns, times):
    return jnp.concatenate([columns] * times, axis=1)


def decay_tiles(dec_ref, first_head, tiles, heads_here, size):
    rows = lax.broadcasted_iota(jnp.int32, (size, size), 0)
    cols = lax.broadcasted_iota(jnp.int32, (size, size), 1)
    distance = (rows - cols).astype(F32)
    for head in range(heads_here):
        decay = dec_ref[pl.ds(first_head + head, 1), 0:1]
        tiles[head, 0] = jnp.where(rows >= cols, jnp.exp(decay * jnp.maximum(distance, 0.0)), 0.0)
        tiles[head, 1] = jnp.exp(decay * (distance + float(size)))


def spread_segments(r, length):
    r.segf[...] = r.seg[...].astype(F32)
    for chunk in range(length // 128):
        r.segc[chunk * 128 : (chunk + 1) * 128, :] = spread(r.segf[...], chunk)


def tile_weight(r, first_head, head, row_tile, col_tile, size):
    gap = row_tile - col_tile
    if gap == 0:
        weight = r.tiles[head, 0]
    else:
        weight = r.tiles[head, 1]
        if gap > 1:
            decay = r.dec[pl.ds(first_head + head, 1), 0:1]
            weight = weight * jnp.exp(decay * float(size * (gap - 1)))
    row_seg = widen(r.segc[row_tile * size : (row_tile + 1) * size, :], size // 128)
    per = size // 128
    col_seg = jnp.concatenate([r.segf[per * col_tile + i : per * col_tile + i + 1, :] for i in range(per)], axis=1)
    return jnp.where(row_seg == col_seg, weight, 0.0)


def namespace(names, refs):
    return types.SimpleNamespace(**dict(zip(names, refs)))


def fwd_kernel(cfg, names, *refs):
    r = namespace(names, refs)
    layer, block, length, width, local = cfg.layer, cfg.block, cfg.length, cfg.width, cfg.local
    heads_here, size = cfg.heads_here, cfg.block
    place = Place(cfg.pairs)
    first_head = layer * HEADS + place.me * heads_here
    copies = Local(r.local_sem)
    w_in = [copies.start(h.at[layer], v) for h, v in (
        (r.wq_h, r.wq), (r.wk_h, r.wk), (r.wv_h, r.wv), (r.wg_h, r.wg))]
    w_out = copies.start(r.wo_h.at[layer], r.wo)
    w_glu = [copies.start(h.at[layer], v) for h, v in ((r.wl_h, r.wl), (r.wr_h, r.wr), (r.wd_h, r.wd))]
    saves = []
    first = Gather(place, r.n1, r.ag1_send, r.ag1_recv, block)
    mid_sum = Scatter(place, r.part1, r.land1, r.rs1_send, r.rs1_recv, block)
    second = Gather(place, r.n2, r.ag2_send, r.ag2_recv, block)
    out_sum = Scatter(place, r.part2, r.land2, r.rs2_send, r.rs2_recv, block)
    share = Share(place, r.ss, r.ss_land, r.ss_send, r.ss_recv)
    third = Gather(place, r.gd, r.ag3_send, r.ag3_recv, block) if cfg.last else None
    if cfg.last:
        load_up = copies.start(r.up_h, r.gd.at[aligned(place.me * block, block), :])
    half, step_rows = first.half, 32
    own_start = place.me * block

    @pl.loop(0, block // step_rows)
    def _(i):
        rows = aligned(i * step_rows, step_rows)
        v = r.x[rows, :].astype(F32)
        scale = lax.rsqrt(jnp.mean(v * v, axis=1, keepdims=True) + epsilon)
        r.n1[aligned(own_start + i * step_rows, step_rows), :] = (v * scale).astype(BF16)

    place.greet(False)
    for part in range(SUPER):
        first.start(part)
    decay_tiles(r.dec, first_head, r.tiles, heads_here, size)
    spread_segments(r, length)
    for copy in w_in:
        copy.wait()

    @pl.loop(0, 4)
    def _(step):
        @pl.when(step == 1)
        def _():
            for part in range(SUPER):
                first.forward(part)
        for which in (1, 2, 3):
            @pl.when(step == which)
            def _():
                for part in range(SUPER):
                    first.finish(part, which)
        rows = aligned(place.member(step) * block, block)
        a = r.n1[rows, :]
        cosine, sine = r.cos[rows, :], r.sin[rows, :]
        for w, lin, rot in ((r.wq, r.ql, r.q), (r.wk, r.kl, r.k)):
            v = nn(a, w[...])
            lin[rows, :] = v.astype(BF16)
            v = v / (1.0 + jnp.exp(-v))
            for head in range(heads_here):
                one = v[:, head * HDIM : (head + 1) * HDIM]
                rot[rows, 2 * head * HDIM : (2 * head + 1) * HDIM] = (one * cosine).astype(BF16)
                rot[rows, (2 * head + 1) * HDIM : (2 * head + 2) * HDIM] = (one * sine).astype(BF16)
        r.v[rows, :] = nn(a, r.wv[...]).astype(BF16)
        r.gate[rows, :] = nn(a, r.wg[...])

    for v, h in ((r.n1, r.n1_h), (r.ql, r.ql_h), (r.kl, r.kl_h), (r.q, r.q_h), (r.k, r.k_h), (r.v, r.v_h), (r.gate, r.gate_h)):
        saves.append(copies.start(v, h))

    if cfg.last:
        load_up.wait()
        for part in range(SUPER):
            third.start(part)
    tiles_here = length // size

    @pl.loop(0, heads_here)
    def _(head):
        wide = aligned(head * 2 * HDIM, 2 * HDIM)
        thin = aligned(head * HDIM, HDIM)
        for row_tile in range(tiles_here):
            rows = slice(row_tile * size, (row_tile + 1) * size)
            queries = r.q[rows, wide]
            acc = None
            for col_tile in range(row_tile + 1):
                cols = slice(col_tile * size, (col_tile + 1) * size)
                weight = tile_weight(r, first_head, head, row_tile, col_tile, size)
                scores = (nt(queries, r.k[cols, wide]) * weight).astype(BF16)
                term = nn(scores, r.v[cols, thin])
                acc = term if acc is None else acc + term
            r.heads[rows, thin] = acc
            r.u[rows, thin] = (acc * r.gate[rows, thin]).astype(BF16)

    for chunk in range(length // 128):
        v = r.heads[chunk * 128 : (chunk + 1) * 128, :]
        row_sums(v * v, r.ss, chunk)
    share.start()
    saves.append(copies.start(r.heads, r.heads_h))
    if cfg.last:
        for part in range(SUPER):
            third.forward(part)
    w_out.wait()

    part_rows = 2 * half
    for part in range(SUPER):
        for step in (3, 1, 2, 0):
            rows = aligned(place.member(step) * block + part * part_rows, part_rows)
            r.part1[rows, :] = nn(r.u[rows, :], r.wo[...]).astype(BF16)
            mid_sum.send_block(part, step)
    for part in range(SUPER):
        mid_sum.middle(part)
    r.sstot[...] = share.total()
    saves.append(copies.start(r.sstot, r.ss_h))
    scaling = lax.rsqrt(r.sstot[...] / width + epsilon)
    per_block = block // 128
    for chunk in range(per_block):
        r.scale[chunk * 128 : (chunk + 1) * 128, :] = spread(scaling, place.me * per_block + chunk)
    r.stat_wide[...] = jnp.zeros_like(r.stat_wide)

    def add_stat(row, v):
        sums = jnp.sum(v * v, axis=0, keepdims=True)
        r.stat_wide[row : row + 1, :] += sums

    step_rows = min(32, half)
    for part in range(SUPER):
        for h in range(2):
            mid_sum.finish(part, h)
            for i in range(half // step_rows):
                offset = (2 * part + h) * half + i * step_rows
                scale = widen(r.scale[offset : offset + step_rows, :], width // 128)
                attn = mid_sum.total(part, h, i * step_rows, step_rows) * scale
                middle = r.x[offset : offset + step_rows, :].astype(F32) + attn
                r.mid[offset : offset + step_rows, :] = middle
                add_stat(0, attn)
                norm = lax.rsqrt(jnp.mean(middle * middle, axis=1, keepdims=True) + epsilon)
                r.n2[aligned(own_start + offset, step_rows), :] = (middle * norm).astype(BF16)
        second.start(part)
    saves.append(copies.start(r.mid, r.mid_h))
    for copy in w_glu:
        copy.wait()
    def glu(part, step):
        rows = aligned(place.member(step) * block + part * part_rows, part_rows)
        a = r.n2[rows, :]
        left = nt(a, r.wl[...])
        right = nt(a, r.wr[...])
        hidden = (left * right).astype(BF16)
        r.left[rows, :] = left.astype(BF16)
        r.right[rows, :] = right.astype(BF16)
        r.hid[rows, :] = hidden
        r.part2[rows, :] = nn(hidden, r.wd[...]).astype(BF16)
        for which in (1, 2, 3):
            @pl.when(step == which)
            def _():
                out_sum.send_block(part, which)

    gather_stage(second, glu, lambda i: None)
    for v, h in ((r.n2, r.n2_h), (r.left, r.left_h), (r.right, r.right_h), (r.hid, r.hid_h)):
        saves.append(copies.start(v, h))
    for part in range(SUPER):
        out_sum.middle(part)
    if cfg.last:
        for part in range(SUPER):
            for which in (1, 2, 3):
                third.finish(part, which)
        saves.append(copies.start(r.gd, r.gd_h))
    for part in range(SUPER):
        for h in range(2):
            out_sum.finish(part, h)
            for i in range(half // step_rows):
                offset = (2 * part + h) * half + i * step_rows
                glu_rows = out_sum.total(part, h, i * step_rows, step_rows)
                after = r.mid[offset : offset + step_rows, :] + glu_rows
                r.xo[offset : offset + step_rows, :] = after.astype(r.xo.dtype)
                add_stat(1, glu_rows)
                add_stat(2, after)
    folded = r.stat_wide[:, :128]
    for n in range(1, width // 128):
        folded = folded + r.stat_wide[:, n * 128 : (n + 1) * 128]
    r.stat[...] = folded
    for copy in saves:
        copy.wait()
    for group in (first, mid_sum, second, out_sum, share) + ((third,) if cfg.last else ()):
        group.drain()


def turns_of(k, size, count):
    return sum(((k >= size * n).astype(jnp.int32) for n in range(1, -(-count // size))), jnp.int32(0))


class Line:
    def __init__(self, cfg, place, r):
        self.place, self.r = place, r
        self.per, self.count = cfg.chunks, cfg.chunks * cfg.layers
        self.layers, self.rows_each = cfg.layers, cfg.chunks * CHUNK
        self.half = CHUNK // 2
        self.ticks = self.count + 3 + HOP * place.last
        self.done = 0

    def slot(self, k):
        return k - SLOTS * turns_of(k, SLOTS, self.count)

    def rows(self, k, core):
        place = k - self.per * turns_of(k, self.per, self.count)
        return aligned(place * CHUNK + core * self.half, self.half)

    def own(self, k):
        return self.rows(k, self.place.core)

    def out_rows(self, k, core):
        turn = turns_of(k, self.per, self.count)
        place = (self.layers - 1 - turn) * self.per + k - turn * self.per
        start = place * CHUNK + core * self.half
        return aligned(start, self.half)

    def pair(self, k):
        slot = self.slot(k)
        r = self.r
        return Wire(self.place.partner(), r.pair_send.at[slot], r.pair_recv.at[slot],
                    r.grads.at[self.rows(k, 1 - self.place.core)], r.pair_land.at[slot], r.pair_land.at[slot])

    def hop(self, k, land, send, recv, device):
        slot = self.slot(k)
        return Wire(device, send.at[slot], recv.at[slot], land.at[slot], land.at[slot], land.at[slot])

    def going_right(self, k):
        return self.hop(k, self.r.right_land, self.r.right_send, self.r.right_recv, self.place.right())

    def going_left(self, k):
        return self.hop(k, self.r.left_land, self.r.left_send, self.r.left_recv, self.place.left())

    def coming_right(self, k):
        return self.hop(k, self.r.right_land, self.r.right_send, self.r.right_recv, self.place.left())

    def coming_left(self, k):
        return self.hop(k, self.r.left_land, self.r.left_send, self.r.left_recv, self.place.right())

    def result(self, k):
        slot, r = self.slot(k), self.r
        return Wire(self.place.partner(), r.give_send.at[slot], r.give_recv.at[slot],
                    r.grads.at[self.own(k)], r.out_h.at[self.out_rows(k, self.place.core)],
                    r.out_h.at[self.out_rows(k, 1 - self.place.core)])

    def keep(self, k):
        slot, r = self.slot(k), self.r
        return pltpu.make_async_copy(
            r.grads.at[self.own(k)], r.out_h.at[self.out_rows(k, self.place.core)], r.keep_sem.at[slot]
        )

    def one_way(self, k, land, start_here, coming, ends_here, going):
        slot = self.slot(k)

        @pl.when(start_here)
        def _():
            land[slot] = self.r.grads[self.own(k), :]

        @pl.when(jnp.logical_not(start_here))
        def _():
            coming(k).wait_recv()
            land[slot] = land[slot] + self.r.grads[self.own(k), :]

        @pl.when(jnp.logical_not(ends_here))
        def _():
            going(k).start()

    def tick(self, n):
        place, r, last = self.place, self.r, self.place.last
        at_left, at_right = place.at == 0, place.at == last

        @pl.when(n < self.count)
        def _():
            self.pair(n).start()

        k = n - 1

        @pl.when(jnp.logical_and(k >= 0, k < self.count))
        def _():
            wire = self.pair(k)
            wire.wait_recv()
            wire.wait_send()
            slot = self.slot(k)
            r.grads[self.own(k), :] = r.grads[self.own(k), :] + r.pair_land[slot]

        left_k = n - 1 - HOP * (last - place.at)

        @pl.when(jnp.logical_and(left_k >= 0, left_k < self.count))
        def _():
            self.one_way(left_k, r.left_land, at_right, self.coming_left, at_left, self.going_left)

        right_k = n - 1 - HOP * place.at

        @pl.when(jnp.logical_and(right_k >= 0, right_k < self.count))
        def _():
            self.one_way(right_k, r.right_land, at_left, self.coming_right, at_right, self.going_right)

        full_k = n - 1 - HOP * last

        @pl.when(jnp.logical_and(full_k >= 0, full_k < self.count))
        def _():
            @pl.when(jnp.logical_not(at_right))
            def _():
                self.going_right(full_k).wait_send()

            @pl.when(jnp.logical_not(at_left))
            def _():
                self.going_left(full_k).wait_send()

            slot = self.slot(full_k)
            own = self.own(full_k)
            total = r.right_land[slot].astype(F32) + r.left_land[slot].astype(F32) - r.grads[own, :].astype(F32)
            r.grads[own, :] = total.astype(BF16)
            self.result(full_k).start()
            self.keep(full_k).start()

        old_k = full_k - 2

        @pl.when(jnp.logical_and(old_k >= 0, old_k < self.count))
        def _():
            wire = self.result(old_k)
            wire.wait_recv()
            wire.wait_send()
            self.keep(old_k).wait()

    def pump(self, ready, most):
        stop = min(self.done + most, ready)
        if stop > self.done:
            start, self.done = self.done, stop

            @pl.loop(start, stop)
            def _(n):
                self.tick(n)

    def release(self, turn, rows):
        needed = (turn - 1) * self.per + -(-rows // CHUNK) + 3 + HOP * self.place.last
        if turn > 0 and needed > self.done:
            self.pump(turn * self.per, needed - self.done)
            assert self.done >= needed

    def finish(self):
        start, self.done = self.done, self.ticks

        @pl.loop(start, self.ticks)
        def _(n):
            self.tick(n)


class StatLine:
    def __init__(self, place, r):
        self.place, self.r = place, r
        self.share = Share(place, r.stat_mine, r.stat_land, r.st_send, r.st_recv)

    def square(self):
        self.share.start()

    def pair(self):
        r = self.r
        r.stat_square[...] = self.share.total()
        self.wire(0, self.place.partner(), r.stat_square).start()

    def wire(self, number, device, source):
        r = self.r
        return Wire(device, r.line_send.at[number], r.line_recv.at[number], source, r.line_land.at[number], r.line_land.at[number])

    def stage(self, number):
        place, r = self.place, self.r
        if number == 0:
            self.wire(0, place.partner(), r.stat_square).wait_recv()
            r.stat_pair[...] = r.stat_square[...] + r.line_land[0]
            r.stat_right[...] = r.stat_pair[...]
            r.stat_left[...] = r.stat_pair[...]
        else:
            @pl.when(place.at == number)
            def _():
                self.wire(1, place.left(), r.stat_right).wait_recv()
                r.stat_right[...] = r.stat_pair[...] + r.line_land[1]

            @pl.when(place.last - place.at == number)
            def _():
                self.wire(2, place.right(), r.stat_left).wait_recv()
                r.stat_left[...] = r.stat_pair[...] + r.line_land[2]
        if number < place.last:
            @pl.when(place.at == number)
            def _():
                self.wire(1, place.right(), r.stat_right).start()

            @pl.when(place.last - place.at == number)
            def _():
                self.wire(2, place.left(), r.stat_left).start()

    def finish(self):
        place, r = self.place, self.r
        r.stat_total[...] = r.stat_right[...] + r.stat_left[...] - r.stat_pair[...]
        self.share.drain()
        self.wire(0, place.partner(), r.stat_square).wait_send()

        @pl.when(place.at < place.last)
        def _():
            self.wire(1, place.right(), r.stat_right).wait_send()

        @pl.when(place.at > 0)
        def _():
            self.wire(2, place.left(), r.stat_left).wait_send()


def bwd_kernel(cfg, names, *refs):
    r = namespace(names, refs)
    block, length, width, local, ff = cfg.block, cfg.length, cfg.width, cfg.local, cfg.ff
    heads_here, size, layers = cfg.heads_here, cfg.block, cfg.layers
    place = Place(cfg.pairs)
    copies = Local(r.local_sem)
    line = Line(cfg, place, r)
    stats = StatLine(place, r)
    loads = {}
    base_down, base_left, base_right, base_out, base_gate, gate_end, base_qkv, _ = cfg.bases
    half = block // (2 * SUPER)
    part_rows = 2 * half
    own_start = place.me * block
    step_rows = min(32, half)
    per_block = block // 128
    tiles_here = length // size

    def load(layer, *keys):
        for key in keys:
            if key in SAVED:
                source = getattr(r, key + str(layer) + "_h")
            else:
                source = getattr(r, key + "_h").at[layer]
            loads[key] = copies.start(source, getattr(r, key))

    def await_loads(*keys):
        for key in keys:
            loads[key].wait()

    loads["gd"] = copies.start(r.gd_h, r.gd)
    glu_in = ("wd", "left", "right", "wl", "wr")
    glu_grad = ("hid", "n2", "mid")
    out_in = ("ss", "wo", "gate", "heads")
    attn_in = ("q", "k", "v", "ql", "kl")
    in_in = ("wq", "wk", "wv", "wg")
    load(layers - 1, *glu_in, *glu_grad, *out_in, *attn_in, *in_in, "n1")

    def gather_one(layer):
        return Gather(place, r.gd, r.ag1_send.at[layer], r.ag1_recv.at[layer], block)

    firsts = [gather_one(layer) for layer in range(layers)]

    @pl.loop(0, block // 32)
    def _(i):
        rows = aligned(i * 32, 32)
        r.g[rows, :] = r.up[rows, :].astype(F32)

    r.stat_mine[...] = jnp.zeros_like(r.stat_mine)
    for layer in range(layers):
        r.stat_mine[3 * layer : 3 * layer + 3, :] = getattr(r, "stat%d" % layer)[0:3, :]
    place.greet(True)
    stats.square()
    spread_segments(r, length)
    for start, stop in ((gate_end, base_qkv), (base_qkv + 3 * local, cfg.chunks * CHUNK)):
        if stop > start:
            r.grads[start:stop, :] = jnp.zeros((stop - start, width), BF16)
    stats.pair()

    def back_rows(total, values, grad):
        norm = lax.rsqrt(jnp.mean(values * values, axis=1, keepdims=True) + epsilon)
        m = values * norm
        inner = jnp.mean(total * m, axis=1, keepdims=True)
        return grad + norm * (total - m * inner)

    for turn, layer in enumerate(reversed(range(layers))):
        first = firsts[layer]
        mid_sum = Scatter(place, r.part, r.land, r.rs1_send.at[layer], r.rs1_recv.at[layer], block)
        second = Gather(place, r.ga, r.ag2_send.at[layer], r.ag2_recv.at[layer], block)
        in_sum = Scatter(place, r.part, r.land, r.rs2_send.at[layer], r.rs2_recv.at[layer], block)
        share = Share(place, r.inner, r.inner_land.at[layer], r.in_send.at[layer], r.in_recv.at[layer])
        first_head = layer * HEADS + place.me * heads_here

        def ready(rows):
            return turn * cfg.chunks + rows // CHUNK

        decay_tiles(r.dec, first_head, r.tiles, heads_here, size)
        await_loads(*glu_in)
        await_loads(*out_in)
        scaling = lax.rsqrt(r.ss[...] / width + epsilon)
        for chunk in range(length // 128):
            r.scale[chunk * 128 : (chunk + 1) * 128, :] = spread(scaling, chunk)
        if turn == 0:
            stats.stage(0)

        def glu_back(part, step):
            rows = aligned(place.member(step) * block + part * part_rows, part_rows)
            grad_hidden = nt(r.gd[rows, :], r.wd[...])
            grad_left = (grad_hidden * r.right[rows, :].astype(F32)).astype(BF16)
            grad_right = (grad_hidden * r.left[rows, :].astype(F32)).astype(BF16)
            r.right[rows, :] = grad_left
            r.left[rows, :] = grad_right
            r.part[rows, :] = (nn(grad_left, r.wl[...]) + nn(grad_right, r.wr[...])).astype(BF16)
            for which in (1, 2, 3):
                @pl.when(step == which)
                def _():
                    mid_sum.send_block(part, which)

        if turn == 0:
            await_loads("gd")
            for part in range(SUPER):
                @pl.loop(0, 4)
                def _(i):
                    glu_back(part, 3 - i)
        else:
            gather_stage(first, glu_back, lambda i: line.pump(ready(0), 2))
            first.drain()
        grad_left_ref, grad_right_ref = r.right, r.left

        def glu_grad_rows(base, a_ref, b_ref):
            line.release(turn, base + ff)
            for n in range(width // 256):
                cols = slice(n * 256, (n + 1) * 256)
                r.grads[base : base + ff, cols] = tn(a_ref[...], b_ref[:, cols]).astype(BF16)

        await_loads(*glu_grad)
        glu_grad_rows(base_down, r.hid, r.gd)
        if turn == 0:
            stats.stage(1)
        line.pump(ready(base_left), 1 + turn)
        mid_sum.middle(0)
        glu_grad_rows(base_left, grad_left_ref, r.n2)
        line.pump(ready(base_right), 1 + turn)
        for part in range(1, SUPER):
            mid_sum.middle(part)
        glu_grad_rows(base_right, grad_right_ref, r.n2)
        for part in range(SUPER):
            line.pump(ready(base_out), 2 if part == 0 else 1)
            for h in range(2):
                mid_sum.finish(part, h)
                for i in range(half // step_rows):
                    offset = (2 * part + h) * half + i * step_rows
                    rows = slice(offset, offset + step_rows)
                    total = mid_sum.total(part, h, i * step_rows, step_rows)
                    new = back_rows(total, r.mid[rows, :], r.g[rows, :])
                    r.gm[rows, :] = new
                    r.ga[aligned(own_start + offset, step_rows), :] = new.astype(BF16)
            second.start(part)
        mid_sum.drain()
        if turn == 0:
            stats.stage(2)
        if turn + 1 < layers:
            load(layer - 1, *glu_in, *glu_grad)
        if turn == 0:
            stats.stage(3)
        def out_back(part, step):
            member = place.member(step)
            for chunk in range(part_rows // 128):
                number = part * (part_rows // 128) + chunk
                rows = aligned(member * block + number * 128, 128)
                grad_branch = nt(r.ga[rows, :], r.wo[...])
                gate = r.gate[rows, :]
                normed = r.heads[rows, :] * widen(r.scale[rows, :], local // 128)
                grad_normed = grad_branch * gate
                r.dx[rows, 3 * local : 4 * local] = (grad_branch * normed).astype(BF16)
                r.branch[rows, :] = (normed * gate).astype(BF16)
                r.gate[rows, :] = grad_normed
                row_sums(grad_normed * normed, r.inner, member * per_block + number)

        gather_stage(second, out_back, lambda i: line.pump(ready(base_out), 3 if i == SUPER else 2))
        share.start()
        line.release(turn, base_gate)
        r.grads[base_out : base_out + local, :] = tn(r.branch[...], r.ga[...]).astype(BF16)
        line.pump(ready(base_gate), 1)

        def in_grad_rows(number, base):
            cols = slice(number * local, (number + 1) * local)
            line.release(turn, base + local)
            for n in range(width // local):
                part_grad = tn(r.n1[:, n * local : (n + 1) * local], r.dx[:, cols])
                r.grads[base : base + local, n * local : (n + 1) * local] = part_grad.astype(BF16)

        await_loads("n1")
        in_grad_rows(3, base_gate)
        line.pump(ready(base_qkv), 1)
        await_loads(*attn_in)
        r.intot[...] = share.total() / width
        for chunk in range(length // 128):
            rows = slice(chunk * 128, (chunk + 1) * 128)
            scale = widen(r.scale[rows, :], local // 128)
            inner = widen(spread(r.intot[...], chunk), local // 128)
            normed = r.heads[rows, :] * scale
            r.dh[rows, :] = (scale * (r.gate[rows, :] - normed * inner)).astype(BF16)
        share.drain()
        second.drain()
        if turn + 1 < layers:
            load(layer - 1, *out_in)
        line.pump(ready(base_qkv), 1)
        between = line.done
        line.done += 1
        assert line.done <= ready(base_qkv)

        @pl.loop(0, heads_here)
        def _(head):
            @pl.when(head == 1)
            def _():
                line.tick(between + head - 1)

            wide = aligned(head * 2 * HDIM, 2 * HDIM)
            thin = aligned(head * HDIM, HDIM)
            for col_tile in range(tiles_here):
                cols = slice(col_tile * size, (col_tile + 1) * size)
                keys = r.k[cols, wide]
                values = r.v[cols, thin]
                acc_key, acc_value = None, None
                for row_tile in range(col_tile, tiles_here):
                    rows = slice(row_tile * size, (row_tile + 1) * size)
                    queries = r.q[rows, wide]
                    grads = r.dh[rows, thin]
                    weight = tile_weight(r, first_head, head, row_tile, col_tile, size)
                    scores = (nt(queries, keys) * weight).astype(BF16)
                    pulled = (nt(grads, values) * weight).astype(BF16)
                    term = nn(pulled, keys)
                    if col_tile == 0:
                        r.dq[rows, :] = term
                    else:
                        r.dq[rows, :] += term
                    key_term = tn(pulled, queries)
                    value_term = tn(scores, grads)
                    acc_key = key_term if acc_key is None else acc_key + key_term
                    acc_value = value_term if acc_value is None else acc_value + value_term
                r.dk[cols, :] = acc_key
                r.dx[cols, aligned(2 * local + head * HDIM, HDIM)] = acc_value.astype(BF16)
            for row_tile in range(tiles_here):
                rows = slice(row_tile * size, (row_tile + 1) * size)
                cosine, sine = r.cos[rows, :], r.sin[rows, :]
                for grad, lin, base in ((r.dq, r.ql, 0), (r.dk, r.kl, local)):
                    v = lin[rows, thin].astype(F32)
                    gate = 1.0 / (1.0 + jnp.exp(-v))
                    back = grad[rows, :HDIM] * cosine + grad[rows, HDIM:] * sine
                    back = back * (gate + v * gate * (1.0 - gate))
                    r.dx[rows, aligned(base + head * HDIM, HDIM)] = back.astype(BF16)

        if turn + 1 < layers:
            load(layer - 1, *attn_in)
        await_loads(*in_in)
        last = turn == layers - 1
        if last:
            for number in range(3):
                in_grad_rows(number, base_qkv + number * local)
        for part in range(SUPER):
            for step in (3, 1, 2, 0):
                rows = aligned(place.member(step) * block + part * part_rows, part_rows)
                total = None
                for n, w in enumerate((r.wq, r.wk, r.wv, r.wg)):
                    term = nt(r.dx[rows, n * local : (n + 1) * local], w[...])
                    total = term if total is None else total + term
                r.part[rows, :] = total.astype(BF16)
                in_sum.send_block(part, step)
            line.pump(ready(cfg.chunks * CHUNK if last else base_qkv), 2 if last else 1)
        for number in range(3):
            if not last:
                in_grad_rows(number, base_qkv + number * local)
            line.pump(ready(base_qkv + (number + 1) * local), 2 if last else 1)
            if number < SUPER:
                in_sum.middle(number)
        if turn + 1 < layers:
            load(layer - 1, *in_in, "n1")
        for part in range(SUPER):
            line.pump(ready(cfg.chunks * CHUNK), 2)
            for h in range(2):
                in_sum.finish(part, h)
                for i in range(half // step_rows):
                    offset = (2 * part + h) * half + i * step_rows
                    rows = slice(offset, offset + step_rows)
                    total = in_sum.total(part, h, i * step_rows, step_rows)
                    values = getattr(r, "x%d" % layer)[rows, :].astype(F32)
                    new = back_rows(total, values, r.gm[rows, :])
                    if layer > 0:
                        r.g[rows, :] = new
                        r.gd[aligned(own_start + offset, step_rows), :] = new.astype(BF16)
                    else:
                        r.go[rows, :] = new.astype(BF16)
            if layer > 0:
                firsts[layer - 1].start(part)
        in_sum.drain()
    stats.finish()
    line.finish()


def call_kernel(body, cfg, inputs, outputs, scratch, collective_id, name):
    vmem, anywhere = pl.BlockSpec(memory_space=pltpu.VMEM), pl.BlockSpec(memory_space=pl.ANY)
    names = list(inputs) + list(outputs) + list(scratch)
    result = pl.pallas_call(
        functools.partial(body, cfg, names),
        out_shape=[shape for shape, _ in outputs.values()],
        in_specs=[vmem if placed else anywhere for _, placed in inputs.values()],
        out_specs=[vmem if placed else anywhere for _, placed in outputs.values()],
        scratch_shapes=list(scratch.values()),
        compiler_params=pltpu.CompilerParams(
            collective_id=collective_id, has_side_effects=collective_id is not None, vmem_limit_bytes=VMEM_LIMIT
        ),
        name=name,
    )(*[array for array, _ in inputs.values()])
    return dict(zip(outputs, result))


def collective_scratch(cfg, copies, lead):
    dma = pltpu.SemaphoreType.DMA
    half = cfg.block // (2 * SUPER)
    out = {}
    for name in ("ag1", "ag2", "rs1", "rs2"):
        out[name + "_send"] = dma((*lead, SUPER, 6))
        out[name + "_recv"] = dma((*lead, SUPER, 6))
    for name in copies:
        out["land" + name] = pltpu.VMEM((SUPER, 6, half, cfg.width), BF16)
        out["part" + name] = pltpu.VMEM((cfg.length, cfg.width), BF16)
    out["local_sem"] = dma((64,))
    return out


def weight_scratch(cfg):
    v = pltpu.VMEM
    return dict(
        wq=v((cfg.width, cfg.local), BF16), wk=v((cfg.width, cfg.local), BF16),
        wv=v((cfg.width, cfg.local), BF16), wg=v((cfg.width, cfg.local), BF16),
        wo=v((cfg.local, cfg.width), BF16), wl=v((cfg.ff, cfg.width), BF16),
        wr=v((cfg.ff, cfg.width), BF16), wd=v((cfg.ff, cfg.width), BF16),
    )


def table_scratch(cfg):
    v = pltpu.VMEM
    return dict(
        segc=v((cfg.length, 128), F32), segf=v((8, 128), F32),
        tiles=v((cfg.heads_here, 2, cfg.block, cfg.block), F32),
    )


def run_forward(cfg, x, upstream, tables, weights):
    v, dma, s = pltpu.VMEM, pltpu.SemaphoreType.DMA, jax.ShapeDtypeStruct
    rows, wide, local, ff, block = cfg.length, cfg.width, cfg.local, cfg.ff, cfg.block
    inputs = dict(x=(x, True), **{k: (a, True) for k, a in tables.items()}, **{k + "_h": (a, False) for k, a in weights.items()})
    kept = dict(
        n1=((rows, wide), BF16), ql=((rows, local), BF16), kl=((rows, local), BF16),
        q=((rows, 2 * local), BF16), k=((rows, 2 * local), BF16), v=((rows, local), BF16),
        gate=((rows, local), F32), heads=((rows, local), F32), mid=((block, wide), F32),
        n2=((rows, wide), BF16), left=((rows, ff), BF16), right=((rows, ff), BF16), hid=((rows, ff), BF16),
    )
    outputs = dict(
        xo=(s((block, wide), BF16 if cfg.last else F32), True), stat=(s((8, 128), F32), True), ss_h=(s((8, 128), F32), False),
        **{k + "_h": (s(*a), False) for k, a in kept.items()},
    )
    scratch = dict(
        **weight_scratch(cfg), **collective_scratch(cfg, ("1", "2"), ()), **table_scratch(cfg),
        **{k: v(*a) for k, a in kept.items()}, u=v((rows, local), BF16), stat_wide=v((8, wide), F32),
        ss=v((8, 128), F32), sstot=v((8, 128), F32), scale=v((block, 128), F32),
        ss_land=v((3, 8, 128), F32), ss_send=dma((3,)), ss_recv=dma((3,)),
    )
    if cfg.last:
        inputs.update(up_h=(upstream, False))
        outputs.update(gd_h=(s((rows, wide), BF16), False))
        scratch.update(gd=v((rows, wide), BF16), ag3_send=dma((SUPER, 6)), ag3_recv=dma((SUPER, 6)))
    return call_kernel(fwd_kernel, cfg, inputs, outputs, scratch, cfg.layer, "layer_forward")


SAVED = ("ss", "mid", "n1", "ql", "kl", "q", "k", "v", "gate", "heads", "n2", "left", "right", "hid")


def run_backward(cfg, upstream, xs, saved, tables, weights):
    v, dma, s = pltpu.VMEM, pltpu.SemaphoreType.DMA, jax.ShapeDtypeStruct
    rows, wide, local, ff, block = cfg.length, cfg.width, cfg.local, cfg.ff, cfg.block
    inputs = dict(up=(upstream, True), gd_h=(saved[-1]["gd_h"], False), **{k: (a, True) for k, a in tables.items()}, **{k + "_h": (a, False) for k, a in weights.items()})
    for layer in range(cfg.layers):
        inputs["x%d" % layer] = (xs[layer], True)
        inputs["stat%d" % layer] = (saved[layer]["stat"], True)
        for key in SAVED:
            inputs["%s%d_h" % (key, layer)] = (saved[layer][key + "_h"], False)
    total_rows = cfg.chunks * CHUNK
    outputs = dict(
        go=(s((block, wide), BF16), True), stat_total=(s((8, 128), F32), True),
        out_h=(s((cfg.layers * total_rows, wide), BF16), False),
    )
    small, ring, ring_sem = v((8, 128), F32), v((SLOTS, CHUNK // 2, wide), BF16), dma((SLOTS,))
    scratch = dict(
        **weight_scratch(cfg), **collective_scratch(cfg, ("",), (cfg.layers,)), **table_scratch(cfg),
        n1=v((rows, wide), BF16), ql=v((rows, local), BF16), kl=v((rows, local), BF16),
        q=v((rows, 2 * local), BF16), k=v((rows, 2 * local), BF16), v=v((rows, local), BF16),
        gate=v((rows, local), F32), heads=v((rows, local), F32), n2=v((rows, wide), BF16),
        left=v((rows, ff), BF16), right=v((rows, ff), BF16), hid=v((rows, ff), BF16),
        gd=v((rows, wide), BF16), ga=v((rows, wide), BF16),
        g=v((block, wide), F32), gm=v((block, wide), F32), mid=v((block, wide), F32),
        dh=v((rows, local), BF16), branch=v((rows, local), BF16), dx=v((rows, 4 * local), BF16),
        dq=v((rows, 2 * HDIM), F32), dk=v((rows, 2 * HDIM), F32),
        grads=v((total_rows, wide), BF16), scale=v((rows, 128), F32),
        ss=small, inner=small, intot=small,
        inner_land=v((cfg.layers, 3, 8, 128), F32), in_send=dma((cfg.layers, 3)), in_recv=dma((cfg.layers, 3)),
        pair_land=ring, right_land=ring, left_land=ring,
        pair_send=ring_sem, pair_recv=ring_sem, right_send=ring_sem, right_recv=ring_sem, left_send=ring_sem,
        left_recv=ring_sem, give_send=ring_sem, give_recv=ring_sem, keep_sem=ring_sem,
        stat_mine=small, stat_square=small, stat_pair=small, stat_right=small, stat_left=small,
        stat_land=v((3, 8, 128), F32), st_send=dma((3,)), st_recv=dma((3,)),
        line_land=v((3, 8, 128), F32), line_send=dma((3,)), line_recv=dma((3,)),
    )
    return call_kernel(bwd_kernel, cfg, inputs, outputs, scratch, cfg.layers, "layers_backward")


def widen_kernel(cfg, names, *refs):
    r = namespace(names, refs)
    tasks = []
    for layer in range(cfg.layers):
        for number, target in enumerate((r.down, r.left, r.right, r.out)):
            start, stop = cfg.bases[number], cfg.bases[number + 1]
            rows = (stop - start) // 2 if stop - start > 512 else stop - start
            for first in range(start, stop, rows):
                tasks.append((layer, first, rows, [(target.at[layer, pl.ds(first - start, rows), :], slice(None))]))
        for number, target in enumerate((r.gate, r.query, r.key, r.value)):
            pieces = [
                (target.at[layer, pl.ds(n * cfg.local, cfg.local), :], slice(n * cfg.local, (n + 1) * cfg.local))
                for n in range(cfg.width // cfg.local)
            ]
            start = cfg.bases[6] + (number - 1) * cfg.local if number > 0 else cfg.bases[4]
            tasks.append((layer, start, cfg.local, pieces))
    depth = 3

    def fetch(task):
        layer, first, rows, _ = tasks[task]
        start = layer * cfg.chunks * CHUNK + first
        slot = task % depth
        return pltpu.make_async_copy(r.grads.at[pl.ds(start, rows), :], r.narrow.at[slot, pl.ds(0, rows), :], r.in_sem.at[slot])

    def store(task):
        _, _, rows, pieces = tasks[task]
        slot = task % depth
        return [
            pltpu.make_async_copy(r.wide.at[slot, pl.ds(0, rows), lanes], target, r.out_sem.at[slot, n])
            for n, (target, lanes) in enumerate(pieces)
        ]

    for task in range(min(depth, len(tasks))):
        fetch(task).start()
    for task in range(len(tasks)):
        slot, rows = task % depth, tasks[task][2]
        fetch(task).wait()
        if task >= depth:
            for copy in store(task - depth):
                copy.wait()

        @pl.loop(0, rows // 32)
        def _(i):
            part = aligned(i * 32, 32)
            r.wide[slot, part, :] = r.narrow[slot, part, :].astype(F32)

        for copy in store(task):
            copy.start()
        if task + depth < len(tasks):
            fetch(task + depth).start()
    for task in range(max(len(tasks) - depth, 0), len(tasks)):
        for copy in store(task):
            copy.wait()


def run_widen(cfg, grads):
    v, dma, s = pltpu.VMEM, pltpu.SemaphoreType.DMA, jax.ShapeDtypeStruct
    thin, flat = s((cfg.layers, cfg.width, cfg.local), F32), s((cfg.layers, cfg.ff, cfg.width), F32)
    outputs = dict(
        down=(flat, False), left=(flat, False), right=(flat, False), out=(s((cfg.layers, cfg.local, cfg.width), F32), False),
        gate=(thin, False), query=(thin, False), key=(thin, False), value=(thin, False),
    )
    rows = max(cfg.ff // 2, cfg.local, 512)
    scratch = dict(
        narrow=v((3, rows, cfg.width), BF16), wide=v((3, rows, cfg.width), F32),
        in_sem=dma((3,)), out_sem=dma((3, cfg.width // cfg.local)),
    )
    return call_kernel(widen_kernel, cfg, dict(grads=(grads, False)), outputs, scratch, None, "widen_gradients")


def per_device_square(
    tokens, upstream, segment_ids, query_proj, key_proj, value_proj, gate_proj, output_proj, left_proj, right_proj, down_proj
):
    layers = query_proj.shape[0]
    block, width = tokens.shape
    length = segment_ids.shape[0]
    local, ff = query_proj.shape[2], left_proj.shape[2]
    heads_here = local // HDIM
    positions = np.arange(length, dtype=np.float32)
    frequency = np.exp(np.float32(-math.log(10000.0)) * np.arange(HDIM, dtype=np.float32) / np.float32(HDIM))
    angles = positions[:, None] * frequency[None, :]
    slopes = np.exp2(-8.0 * (np.arange(HEADS) + 1.0) / HEADS)
    decays = np.concatenate([-slopes * (1.0 - depth_start - depth_step * layer) for layer in range(layers)])
    tables = dict(
        cos=jnp.asarray(np.cos(angles)), sin=jnp.asarray(np.sin(angles)),
        dec=jnp.asarray(np.broadcast_to(decays[:, None], (layers * HEADS, 128)).astype(np.float32)),
        seg=segment_ids.reshape(8, length // 8),
    )
    weights = dict(
        wq=query_proj, wk=key_proj, wv=value_proj, wg=gate_proj, wo=output_proj,
        wl=jnp.swapaxes(left_proj, 1, 2), wr=jnp.swapaxes(right_proj, 1, 2), wd=down_proj,
    )
    ends = np.cumsum([0, ff, ff, ff, local, local]).tolist()
    ends += [-(-ends[-1] // CHUNK) * CHUNK]
    ends += [-(-(ends[-1] + 3 * local) // CHUNK) * CHUNK]
    common = dict(
        layers=layers, block=block, length=length, width=width, local=local, ff=ff, heads_here=heads_here,
        pairs=lax.axis_size("dp") // 2, bases=ends, chunks=ends[-1] // CHUNK,
    )
    current, xs, saved = tokens, [], []
    for layer in range(layers):
        xs.append(current)
        cfg = types.SimpleNamespace(layer=layer, last=layer == layers - 1, **common)
        saved.append(run_forward(cfg, current, upstream, tables, weights))
        current = saved[-1]["xo"]
    back = run_backward(types.SimpleNamespace(**common), upstream, xs, saved, tables, weights)
    stats = jnp.sum(back["stat_total"][: 3 * layers], axis=1).reshape(layers, 3)
    rms_stats = jnp.sqrt(stats / (length * lax.axis_size("dp") * width))
    wide = run_widen(types.SimpleNamespace(**common), back["out_h"])
    return (
        current, back["go"], wide["query"], wide["key"], wide["value"], wide["gate"], wide["out"],
        jnp.swapaxes(wide["left"], 1, 2), jnp.swapaxes(wide["right"], 1, 2), wide["down"], rms_stats,
    )


def solution(mesh):
    square = dict(mesh.shape) == SQUARE_MESH
    body = per_device_square if square else per_device
    return jax.shard_map(
        body,
        mesh=mesh,
        in_specs=(
            P(("dp", "tensor"), None),
            P(("dp", "tensor"), None),
            P("dp"),
            P(None, None, "tensor"),
            P(None, None, "tensor"),
            P(None, None, "tensor"),
            P(None, None, "tensor"),
            P(None, "tensor", None),
            P(None, None, "tensor"),
            P(None, None, "tensor"),
            P(None, "tensor", None),
        ),
        out_specs=(
            P(("dp", "tensor"), None),
            P(("dp", "tensor"), None),
            P(None, None, "tensor"),
            P(None, None, "tensor"),
            P(None, None, "tensor"),
            P(None, None, "tensor"),
            P(None, "tensor", None),
            P(None, None, "tensor"),
            P(None, None, "tensor"),
            P(None, "tensor", None),
            P(),
        ),
        check_vma=False,
    )
```

```python
import functools
import math
import types

import jax
import jax.numpy as jnp
import numpy as np
from jax import lax
from jax.experimental import pallas as pl
from jax.experimental.pallas import tpu as pltpu
from jax.sharding import PartitionSpec as P

HEADS = 8
HDIM = 128
BLK = 512


epsilon = 1e-06
depth_start = 0.5
depth_step = 1.0 / 24.0
highest = lax.Precision.HIGHEST


def rms_rows(values):
    return values * lax.rsqrt(jnp.mean(values * values, axis=1, keepdims=True) + epsilon)


def rms_back(values, gradient):
    scaling = lax.rsqrt(jnp.mean(values * values, axis=1, keepdims=True) + epsilon)
    normed = values * scaling
    return scaling * (gradient - normed * jnp.mean(gradient * normed, axis=1, keepdims=True))


def contract_last(left_part, right_part):
    return lax.dot_general(
        left_part, right_part, (((1,), (1,)), ((), ())), preferred_element_type=jnp.float32
    )


def contract_first(left_part, right_part):
    return lax.dot_general(
        left_part, right_part, (((0,), (0,)), ((), ())), preferred_element_type=jnp.float32
    )


def rotate(values, cosine, sine_table):
    return jnp.concatenate([values * cosine[:, None, :], values * sine_table[:, None, :]], axis=2)


def unrotate(gradient, cosine, sine_table):
    half_width = gradient.shape[2] // 2
    return (
        gradient[:, :, :half_width] * cosine[:, None, :]
        + gradient[:, :, half_width:] * sine_table[:, None, :]
    )


def split_blocks(array, block_count):
    return array.reshape((block_count, BLK) + array.shape[1:])


def block_weights(seg_block, next_seg, decay_log):
    block_width = seg_block.shape[0]
    places = jnp.arange(block_width, dtype=jnp.float32)
    distance = places[:, None] - places[None, :]
    allowed = (distance >= 0) & (seg_block[:, None] == seg_block[None, :])
    decay_grid = jnp.where(
        allowed[None], jnp.exp(decay_log[:, None, None] * jnp.maximum(distance, 0.0)[None]), 0.0
    )
    first_seg = seg_block[0]
    query_gain = jnp.where(
        (seg_block == first_seg)[:, None], jnp.exp(places[:, None] * decay_log[None, :]), 0.0
    )
    key_gain = jnp.where(
        (seg_block == next_seg)[:, None],
        jnp.exp((block_width - places)[:, None] * decay_log[None, :]),
        0.0,
    )
    carry_gain = jnp.where(first_seg == next_seg, jnp.exp(decay_log * block_width), 0.0)
    return (decay_grid, query_gain, key_gain, carry_gain)


def next_segments(segments, block_count):
    seg_blocks = segments.reshape(block_count, BLK)
    return (seg_blocks, jnp.concatenate([seg_blocks[1:, 0], jnp.full((1,), -1, jnp.int32)]))


def attend_forward(queries, keys_rot, values, segments, decay_log):
    length, heads_here, pair_width = queries.shape
    block_count = length // BLK
    seg_blocks, next_segs = next_segments(segments, block_count)

    def advance(state_now, block_items):
        query_block, key_block, value_block, seg_block, next_seg = block_items
        query_float = query_block.astype(jnp.float32)
        key_float = key_block.astype(jnp.float32)
        value_float = value_block.astype(jnp.float32)
        decay_grid, query_gain, key_gain, carry_gain = block_weights(seg_block, next_seg, decay_log)
        scores = (
            jnp.einsum("rhd,shd->hrs", query_block, key_block, preferred_element_type=jnp.float32)
            * decay_grid
        )
        block_out = jnp.einsum("hrs,she->rhe", scores, value_float, precision=highest)
        block_out = (
            block_out
            + jnp.einsum("rhd,hde->rhe", query_float, state_now, precision=highest)
            * query_gain[:, :, None]
        )
        new_state = carry_gain[:, None, None] * state_now + jnp.einsum(
            "shd,she->hde", key_float * key_gain[:, :, None], value_float, precision=highest
        )
        return (new_state, (block_out, state_now))

    zero_state = jnp.zeros((heads_here, pair_width, pair_width // 2), jnp.float32)
    _, (block_outs, states) = lax.scan(
        advance,
        zero_state,
        (
            split_blocks(queries, block_count),
            split_blocks(keys_rot, block_count),
            split_blocks(values, block_count),
            seg_blocks,
            next_segs,
        ),
    )
    return (block_outs.reshape(length, heads_here * (pair_width // 2)), states)


def attend_backward(queries, keys_rot, values, segments, decay_log, states, grad_heads):
    length, heads_here, pair_width = queries.shape
    block_count = length // BLK
    seg_blocks, next_segs = next_segments(segments, block_count)

    def retreat(later_grad, block_items):
        query_block, key_block, value_block, seg_block, next_seg, state_now, grad_block = (
            block_items
        )
        query_float = query_block.astype(jnp.float32)
        key_float = key_block.astype(jnp.float32)
        value_float = value_block.astype(jnp.float32)
        decay_grid, query_gain, key_gain, carry_gain = block_weights(seg_block, next_seg, decay_log)
        scores = (
            jnp.einsum("rhd,shd->hrs", query_block, key_block, preferred_element_type=jnp.float32)
            * decay_grid
        )
        pulled = jnp.einsum("rhe,she->hrs", grad_block, value_float, precision=highest) * decay_grid
        grad_query = jnp.einsum("hrs,shd->rhd", pulled, key_float, precision=highest)
        grad_query = (
            grad_query
            + jnp.einsum("rhe,hde->rhd", grad_block, state_now, precision=highest)
            * query_gain[:, :, None]
        )
        grad_key = jnp.einsum("hrs,rhd->shd", pulled, query_float, precision=highest)
        grad_key = (
            grad_key
            + jnp.einsum("she,hde->shd", value_float, later_grad, precision=highest)
            * key_gain[:, :, None]
        )
        grad_value = jnp.einsum("hrs,rhe->she", scores, grad_block, precision=highest)
        grad_value = (
            grad_value
            + jnp.einsum("shd,hde->she", key_float, later_grad, precision=highest)
            * key_gain[:, :, None]
        )
        earlier_grad = carry_gain[:, None, None] * later_grad + jnp.einsum(
            "rhd,rhe->hde", query_float * query_gain[:, :, None], grad_block, precision=highest
        )
        return (earlier_grad, (grad_query, grad_key, grad_value))

    zero_state = jnp.zeros((heads_here, pair_width, pair_width // 2), jnp.float32)
    _, (grad_query, grad_key, grad_value) = lax.scan(
        retreat,
        zero_state,
        (
            split_blocks(queries, block_count),
            split_blocks(keys_rot, block_count),
            split_blocks(values, block_count),
            seg_blocks,
            next_segs,
            states,
            split_blocks(grad_heads, block_count),
        ),
        reverse=True,
    )
    return (
        grad_query.reshape(length, heads_here, pair_width),
        grad_key.reshape(length, heads_here, pair_width),
        grad_value.reshape(length, heads_here, pair_width // 2),
    )


def per_device(
    tokens,
    upstream,
    segment_ids,
    query_proj,
    key_proj,
    value_proj,
    gate_proj,
    output_proj,
    left_proj,
    right_proj,
    down_proj,
):
    layers = query_proj.shape[0]
    row_count, model_width = tokens.shape
    length = segment_ids.shape[0]
    local_width = query_proj.shape[2]
    ff_local = left_proj.shape[2]
    heads_here = local_width // HDIM
    positions = jnp.arange(length, dtype=jnp.float32)
    frequency = jnp.exp(-math.log(10000.0) * jnp.arange(HDIM, dtype=jnp.float32) / HDIM)
    angles = positions[:, None] * frequency[None, :]
    cosine = jnp.cos(angles)
    sine_table = jnp.sin(angles)
    head_index = (lax.axis_index("tensor") * heads_here + jnp.arange(heads_here)).astype(
        jnp.float32
    )
    slopes = jnp.exp2(-8.0 * (head_index + 1.0) / HEADS)

    def gather_normed(normed):
        return lax.all_gather(normed, "tensor", axis=0, tiled=True)

    def gather_again(normed):
        return lax.all_gather(normed, "tensor", axis=0, tiled=True)

    def gather_grads(gradient):
        return lax.all_gather(gradient, "tensor", axis=0, tiled=True)

    def branch_sum(operand, matrix):
        return lax.psum_scatter(
            jnp.dot(operand, matrix, preferred_element_type=jnp.float32).astype(jnp.bfloat16),
            "tensor",
            scatter_dimension=0,
            tiled=True,
        ).astype(jnp.float32)

    def input_sum(pieces, matrix):
        operand = jnp.concatenate(pieces, axis=1)
        return lax.psum_scatter(
            contract_last(operand, matrix).astype(jnp.bfloat16),
            "tensor",
            scatter_dimension=0,
            tiled=True,
        ).astype(jnp.float32)

    current = tokens.astype(jnp.float32)
    saved_layers = []
    stat_terms = []
    for layer_index in range(layers):
        residual = current
        normed = rms_rows(residual).astype(jnp.bfloat16)
        full_normed = gather_normed(normed)
        attn_weight = jnp.concatenate(
            [
                query_proj[layer_index],
                key_proj[layer_index],
                value_proj[layer_index],
                gate_proj[layer_index],
            ],
            axis=1,
        )
        projected = jnp.dot(full_normed, attn_weight, preferred_element_type=jnp.float32)
        query_lin = projected[:, :local_width]
        key_lin = projected[:, local_width : 2 * local_width]
        values = (
            projected[:, 2 * local_width : 3 * local_width]
            .astype(jnp.bfloat16)
            .reshape(length, heads_here, HDIM)
        )
        gate_lin = projected[:, 3 * local_width :]
        queries = rotate(
            jax.nn.silu(query_lin).reshape(length, heads_here, HDIM), cosine, sine_table
        ).astype(jnp.bfloat16)
        keys_rot = rotate(
            jax.nn.silu(key_lin).reshape(length, heads_here, HDIM), cosine, sine_table
        ).astype(jnp.bfloat16)
        decay_log = -slopes * (1.0 - depth_start - depth_step * layer_index)
        heads_out, states = attend_forward(queries, keys_rot, values, segment_ids, decay_log)
        squares = lax.psum(jnp.sum(heads_out * heads_out, axis=1), "tensor")
        scaling = lax.rsqrt(squares / model_width + epsilon)[:, None]
        normed_heads = heads_out * scaling
        branch = (normed_heads * gate_lin).astype(jnp.bfloat16)
        attn_rows = branch_sum(branch, output_proj[layer_index])
        middle = residual + attn_rows
        normed_mid = rms_rows(middle).astype(jnp.bfloat16)
        full_mid = gather_normed(normed_mid)
        glu_weight = jnp.concatenate([left_proj[layer_index], right_proj[layer_index]], axis=1)
        gates_both = jnp.dot(full_mid, glu_weight, preferred_element_type=jnp.float32)
        left_lin = gates_both[:, :ff_local]
        right_lin = gates_both[:, ff_local:]
        hidden = (left_lin * right_lin).astype(jnp.bfloat16)
        glu_rows = branch_sum(hidden, down_proj[layer_index])
        current = middle + glu_rows
        stat_terms.append(
            jnp.stack(
                [
                    jnp.sum(attn_rows * attn_rows),
                    jnp.sum(glu_rows * glu_rows),
                    jnp.sum(current * current),
                ]
            )
        )
        saved_layers.append(
            (
                residual,
                middle,
                normed,
                normed_mid,
                full_normed,
                full_mid,
                attn_weight,
                glu_weight,
                query_lin,
                key_lin,
                gate_lin,
                queries,
                keys_rot,
                values,
                decay_log,
                states,
                normed_heads,
                scaling,
                branch,
                left_lin,
                right_lin,
                hidden,
            )
        )
    stat_sums = lax.psum(jnp.stack(stat_terms), ("dp", "tensor"))
    rms_stats = jnp.sqrt(stat_sums / (length * lax.axis_size("dp") * model_width))
    final_rows = current.astype(jnp.bfloat16)
    gradient = upstream.astype(jnp.float32)
    layer_results = [None] * layers
    for layer_index in reversed(range(layers)):
        (
            residual,
            middle,
            normed,
            normed_mid,
            full_normed,
            full_mid,
            attn_weight,
            glu_weight,
            query_lin,
            key_lin,
            gate_lin,
            queries,
            keys_rot,
            values,
            decay_log,
            states,
            normed_heads,
            scaling,
            branch,
            left_lin,
            right_lin,
            hidden,
        ) = saved_layers[layer_index]
        glu_grad = gather_grads(gradient.astype(jnp.bfloat16))
        grad_hidden = contract_last(glu_grad, down_proj[layer_index])
        down_part = contract_first(hidden, glu_grad)
        grad_left = (grad_hidden * right_lin).astype(jnp.bfloat16)
        grad_right = (grad_hidden * left_lin).astype(jnp.bfloat16)
        grad_gates = jnp.concatenate([grad_left, grad_right], axis=1)
        mid_rows = input_sum((grad_left, grad_right), glu_weight)
        source_mid = gather_again(normed_mid)
        glu_part = contract_first(source_mid, grad_gates)
        gradient = gradient + rms_back(middle, mid_rows)
        attn_grad = gather_grads(gradient.astype(jnp.bfloat16))
        output_part = contract_first(branch, attn_grad)
        grad_branch = contract_last(attn_grad, output_proj[layer_index])
        grad_normed = grad_branch * gate_lin
        grad_gate = (grad_branch * normed_heads).astype(jnp.bfloat16)
        inner_sum = lax.psum(jnp.sum(grad_normed * normed_heads, axis=1), "tensor")
        grad_heads = scaling * (grad_normed - normed_heads * (inner_sum / model_width)[:, None])
        grad_query, grad_key, grad_value = attend_backward(
            queries,
            keys_rot,
            values,
            segment_ids,
            decay_log,
            states,
            grad_heads.reshape(length, heads_here, HDIM),
        )
        sigmoid_query = jax.nn.sigmoid(query_lin)
        sigmoid_key = jax.nn.sigmoid(key_lin)
        query_back = unrotate(grad_query, cosine, sine_table).reshape(length, local_width)
        key_back = unrotate(grad_key, cosine, sine_table).reshape(length, local_width)
        grad_query_lin = (
            query_back * (sigmoid_query + query_lin * sigmoid_query * (1.0 - sigmoid_query))
        ).astype(jnp.bfloat16)
        grad_key_lin = (
            key_back * (sigmoid_key + key_lin * sigmoid_key * (1.0 - sigmoid_key))
        ).astype(jnp.bfloat16)
        grad_value_lin = grad_value.reshape(length, local_width).astype(jnp.bfloat16)
        grad_projected = jnp.concatenate(
            [grad_query_lin, grad_key_lin, grad_value_lin, grad_gate], axis=1
        )
        in_rows = input_sum((grad_query_lin, grad_key_lin, grad_value_lin, grad_gate), attn_weight)
        source_normed = gather_again(normed)
        attn_part = contract_first(source_normed, grad_projected)
        gradient = gradient + rms_back(residual, in_rows)
        query_part = attn_part[:, :local_width]
        key_part = attn_part[:, local_width : 2 * local_width]
        value_part = attn_part[:, 2 * local_width : 3 * local_width]
        gate_part = attn_part[:, 3 * local_width :]
        left_part = glu_part[:, :ff_local]
        right_part = glu_part[:, ff_local:]
        layer_results[layer_index] = (
            query_part,
            key_part,
            value_part,
            gate_part,
            output_part,
            left_part,
            right_part,
            down_part,
        )
    stacked = [
        jnp.stack([layer_results[index][member] for index in range(layers)]) for member in range(8)
    ]
    totals = (
        lax.psum(stacked[0].astype(jnp.bfloat16), "dp").astype(jnp.float32),
        lax.psum(stacked[1].astype(jnp.bfloat16), "dp").astype(jnp.float32),
        lax.psum(stacked[2].astype(jnp.bfloat16), "dp").astype(jnp.float32),
        lax.psum(stacked[3].astype(jnp.bfloat16), "dp").astype(jnp.float32),
        lax.psum(stacked[4].astype(jnp.bfloat16), "dp").astype(jnp.float32),
        lax.psum(stacked[5].astype(jnp.bfloat16), "dp").astype(jnp.float32),
        lax.psum(stacked[6].astype(jnp.bfloat16), "dp").astype(jnp.float32),
        lax.psum(stacked[7].astype(jnp.bfloat16), "dp").astype(jnp.float32),
    )
    input_grad = gradient.astype(jnp.bfloat16)
    return (
        final_rows,
        input_grad,
        totals[0],
        totals[1],
        totals[2],
        totals[3],
        totals[4],
        totals[5],
        totals[6],
        totals[7],
        rms_stats,
    )


SQUARE_MESH = {"dp": 8, "tensor": 4}


F32 = jnp.float32
BF16 = jnp.bfloat16
MESH = pl.DeviceIdType.MESH
VMEM_LIMIT = 62 * 2**20
SUPER = 2
CHUNK = 128
HOP = 3
SLOTS = 16


def nn(a, b):
    return lax.dot_general(a, b, (((1,), (0,)), ((), ())), preferred_element_type=F32)


def nt(a, b):
    return lax.dot_general(a, b, (((1,), (1,)), ((), ())), preferred_element_type=F32)


def tn(a, b):
    return lax.dot_general(a, b, (((0,), (0,)), ((), ())), preferred_element_type=F32)


def exact(a, b, dims):
    return lax.dot_general(a, b, (dims, ((), ())), precision=highest, preferred_element_type=F32)


def aligned(index, size):
    return pl.ds(pl.multiple_of(index, size), size)


class Place:
    def __init__(self, pairs):
        self.dp = lax.axis_index("dp")
        self.me = lax.axis_index("tensor")
        self.low = lax.rem(self.me, 2)
        self.high = self.me // 2
        self.core = lax.rem(self.dp, 2)
        self.at = self.dp // 2
        self.last = pairs - 1

    def member(self, step):
        low = lax.rem(self.low + lax.rem(step, 2), 2)
        high = lax.rem(self.high + step // 2, 2)
        return 2 * high + low

    def device(self, step):
        return (self.dp, self.member(step))

    def partner(self):
        return (self.dp + 1 - 2 * self.core, self.me)

    def right(self):
        return (self.dp + 2, self.me)

    def left(self):
        return (self.dp - 2, self.me)

    def greet(self, line):
        barrier = pltpu.get_barrier_semaphore()

        def signal(device):
            pl.semaphore_signal(barrier, inc=1, device_id=device, device_id_type=MESH)

        for step in (1, 2, 3):
            signal(self.device(step))
        if not line:
            pl.semaphore_wait(barrier, 3)
            return
        signal(self.partner())

        @pl.when(self.at < self.last)
        def _():
            signal(self.right())

        @pl.when(self.at > 0)
        def _():
            signal(self.left())

        pl.semaphore_wait(barrier, 4 + jnp.minimum(self.at, 1) + jnp.minimum(self.last - self.at, 1))


class Wire:
    def __init__(self, device, send_sem, recv_sem, source, target, landing):
        self.source, self.target, self.landing = source, target, landing
        self.common = dict(send_sem=send_sem, recv_sem=recv_sem, device_id=device, device_id_type=MESH)

    def out(self):
        return pltpu.make_async_remote_copy(src_ref=self.source, dst_ref=self.target, **self.common)

    def start(self):
        self.out().start()

    def wait_recv(self):
        pltpu.make_async_remote_copy(src_ref=self.landing, dst_ref=self.landing, **self.common).wait_recv()

    def wait_send(self):
        self.out().wait_send()


class Gather:
    def __init__(self, place, buf, send, recv, block):
        self.place, self.buf, self.block = place, buf, block
        self.send, self.recv = send, recv
        self.half = block // (2 * SUPER)

    def rows(self, step, part, half):
        start = self.place.member(step) * self.block + (2 * part + half) * self.half
        return self.buf.at[aligned(start, self.half)]

    def wire(self, part, number):
        step, owner, half = ((1, 0, 0), (2, 0, 1), (1, 0, 1), (2, 0, 0), (2, 1, 0), (1, 2, 1))[number]
        source = self.rows(owner, part, half)
        landing = self.rows((0, 1, 2, 3)[owner ^ step], part, half)
        return Wire(self.place.device(step), self.send.at[part, number], self.recv.at[part, number], source, source, landing)

    def start(self, part):
        for number in range(4):
            self.wire(part, number).start()

    def forward(self, part):
        self.wire(part, 0).wait_recv()
        self.wire(part, 4).start()
        self.wire(part, 1).wait_recv()
        self.wire(part, 5).start()

    def finish(self, part, step):
        for number in {0: (), 1: (2,), 2: (3,), 3: (4, 5)}[step]:
            self.wire(part, number).wait_recv()

    def drain(self):
        for part in range(SUPER):
            for number in range(6):
                self.wire(part, number).wait_send()


def gather_stage(gather, block_fn, beside, behind=None):
    @pl.loop(0, 4 * SUPER)
    def _(i):
        mixed = i - SUPER
        part = jnp.where(i < SUPER, i, jnp.where(i < 3 * SUPER, mixed // 2, i - 3 * SUPER))
        step = jnp.where(i < SUPER, 0, jnp.where(i < 3 * SUPER, 1 + lax.rem(mixed, 2), 3))

        @pl.when(i == SUPER)
        def _():
            for one in range(SUPER):
                beside(one)
                gather.forward(one)
            if behind is not None:
                behind()

        @pl.when(i == 3 * SUPER)
        def _():
            beside(SUPER)

        for which in (1, 2, 3):
            @pl.when(step == which)
            def _():
                gather.finish(part, which)
        block_fn(part, step)


class Scatter:
    def __init__(self, place, buf, land, send, recv, block):
        self.place, self.buf, self.land, self.block = place, buf, land, block
        self.send, self.recv = send, recv
        self.half = block // (2 * SUPER)

    def rows(self, step, part, half):
        start = self.place.member(step) * self.block + (2 * part + half) * self.half
        return aligned(start, self.half)

    def wire(self, part, number):
        step, owner, half = ((1, 3, 0), (1, 1, 0), (2, 3, 1), (2, 2, 1), (2, 2, 0), (1, 1, 1))[number]
        target = self.land.at[part, number]
        return Wire(
            self.place.device(step), self.send.at[part, number], self.recv.at[part, number],
            self.buf.at[self.rows(owner, part, half)], target, target,
        )

    def send_block(self, part, step):
        for number in {0: (), 1: (1,), 2: (3,), 3: (0, 2)}[step]:
            self.wire(part, number).start()

    def middle(self, part):
        for first, second, owner, half in ((0, 4, 2, 0), (2, 5, 1, 1)):
            self.wire(part, first).wait_recv()
            rows = self.rows(owner, part, half)
            self.buf[rows, :] = self.buf[rows, :] + self.land[part, first]
            self.wire(part, second).start()

    def finish(self, part, half):
        first, second = ((1, 4), (3, 5))[half]
        self.wire(part, first).wait_recv()
        self.wire(part, second).wait_recv()

    def total(self, part, half, start, count):
        first, second = ((1, 4), (3, 5))[half]
        own = self.place.me * self.block + (2 * part + half) * self.half + start
        rows = pl.ds(start, count)
        return (
            self.buf[aligned(own, count), :].astype(F32)
            + self.land[part, first, rows, :].astype(F32)
            + self.land[part, second, rows, :].astype(F32)
        )

    def drain(self):
        for part in range(SUPER):
            for number in range(6):
                self.wire(part, number).wait_send()


class Share:
    def __init__(self, place, mine, land, send, recv):
        self.wires = [
            Wire(place.device(step), send.at[step - 1], recv.at[step - 1], mine, land.at[step - 1], land.at[step - 1])
            for step in (1, 2, 3)
        ]
        self.mine, self.land = mine, land

    def start(self):
        for wire in self.wires:
            wire.start()

    def total(self):
        for wire in self.wires:
            wire.wait_recv()
        return self.mine[...] + self.land[0] + self.land[1] + self.land[2]

    def drain(self):
        for wire in self.wires:
            wire.wait_send()


class Local:
    def __init__(self, sems):
        self.sems, self.used = sems, 0

    def start(self, source, target):
        copy = pltpu.make_async_copy(source, target, self.sems.at[self.used])
        self.used += 1
        copy.start()
        return copy


def row_sums(values, target, chunk):
    sums = exact(jnp.ones((8, values.shape[1]), F32), values, ((1,), (1,)))
    target[pl.ds(chunk, 1), :] = sums[0:1, :]


def spread(sums, chunk):
    picked = (lax.broadcasted_iota(jnp.int32, (8, 128), 0) == chunk).astype(F32)
    return exact(sums, picked, ((0,), (0,)))


def widen(columns, times):
    return jnp.concatenate([columns] * times, axis=1)


def decay_tiles(dec_ref, first_head, tiles, heads_here, size):
    rows = lax.broadcasted_iota(jnp.int32, (size, size), 0)
    cols = lax.broadcasted_iota(jnp.int32, (size, size), 1)
    distance = (rows - cols).astype(F32)
    for head in range(heads_here):
        decay = dec_ref[pl.ds(first_head + head, 1), 0:1]
        tiles[head, 0] = jnp.where(rows >= cols, jnp.exp(decay * jnp.maximum(distance, 0.0)), 0.0)
        tiles[head, 1] = jnp.exp(decay * (distance + float(size)))


def spread_segments(r, length):
    r.segf[...] = r.seg[...].astype(F32)
    for chunk in range(length // 128):
        r.segc[chunk * 128 : (chunk + 1) * 128, :] = spread(r.segf[...], chunk)


def tile_weight(r, first_head, head, row_tile, col_tile, size):
    gap = row_tile - col_tile
    if gap == 0:
        weight = r.tiles[head, 0]
    else:
        weight = r.tiles[head, 1]
        if gap > 1:
            decay = r.dec[pl.ds(first_head + head, 1), 0:1]
            weight = weight * jnp.exp(decay * float(size * (gap - 1)))
    row_seg = widen(r.segc[row_tile * size : (row_tile + 1) * size, :], size // 128)
    per = size // 128
    col_seg = jnp.concatenate([r.segf[per * col_tile + i : per * col_tile + i + 1, :] for i in range(per)], axis=1)
    return jnp.where(row_seg == col_seg, weight, 0.0)


def namespace(names, refs):
    return types.SimpleNamespace(**dict(zip(names, refs)))


def forward_front(cfg, r, place, copies, layer, x, save, third, back_block):
    block, length, width = cfg.block, cfg.length, cfg.width
    heads_here, size = cfg.heads_here, cfg.block
    first_head = layer * HEADS + place.me * heads_here
    w_in = [copies.start(h.at[layer], v) for h, v in (
        (r.wq_h, r.wq), (r.wk_h, r.wk), (r.wv_h, r.wv), (r.wg_h, r.wg))]
    w_out = copies.start(r.wo_h.at[layer], r.wo)
    w_glu = [copies.start(h.at[layer], v) for h, v in ((r.wl_h, r.wl), (r.wr_h, r.wr), (r.wd_h, r.wd))]
    first = Gather(place, r.n1, r.fag1_send, r.fag1_recv, block)
    mid_sum = Scatter(place, r.part1, r.land1, r.frs1_send, r.frs1_recv, block)
    second = Gather(place, r.n2, r.fag2_send, r.fag2_recv, block)
    out_sum = Scatter(place, r.part2, r.land2, r.frs2_send, r.frs2_recv, block)
    share = Share(place, r.ss_mine, r.ss_land, r.ss_send, r.ss_recv)
    half, step_rows = first.half, 32
    own_start = place.me * block

    @pl.loop(0, block // step_rows)
    def _(i):
        rows = aligned(i * step_rows, step_rows)
        v = x[rows, :].astype(F32)
        scale = lax.rsqrt(jnp.mean(v * v, axis=1, keepdims=True) + epsilon)
        r.n1[aligned(own_start + i * step_rows, step_rows), :] = (v * scale).astype(BF16)

    place.greet(third is not None)
    for part in range(SUPER):
        first.start(part)
    decay_tiles(r.dec, first_head, r.tiles, heads_here, size)
    spread_segments(r, length)
    for copy in w_in:
        copy.wait()

    @pl.loop(0, 4)
    def _(step):
        @pl.when(step == 1)
        def _():
            for part in range(SUPER):
                first.forward(part)
        for which in (1, 2, 3):
            @pl.when(step == which)
            def _():
                for part in range(SUPER):
                    first.finish(part, which)
        rows = aligned(place.member(step) * block, block)
        a = r.n1[rows, :]
        cosine, sine = r.cos[rows, :], r.sin[rows, :]
        for w, lin, rot in ((r.wq, r.ql, r.q), (r.wk, r.kl, r.k)):
            v = nn(a, w[...])
            lin[rows, :] = v.astype(BF16)
            v = v / (1.0 + jnp.exp(-v))
            for head in range(heads_here):
                one = v[:, head * HDIM : (head + 1) * HDIM]
                rot[rows, 2 * head * HDIM : (2 * head + 1) * HDIM] = (one * cosine).astype(BF16)
                rot[rows, (2 * head + 1) * HDIM : (2 * head + 2) * HDIM] = (one * sine).astype(BF16)
        r.v[rows, :] = nn(a, r.wv[...]).astype(BF16)
        r.gate[rows, :] = nn(a, r.wg[...])

    save("n1", "ql", "kl", "q", "k", "v", "gate")
    if third is not None:
        for part in range(SUPER):
            third.start(part)
    tiles_here = length // size

    @pl.loop(0, heads_here)
    def _(head):
        wide = aligned(head * 2 * HDIM, 2 * HDIM)
        thin = aligned(head * HDIM, HDIM)
        for row_tile in range(tiles_here):
            rows = slice(row_tile * size, (row_tile + 1) * size)
            queries = r.q[rows, wide]
            acc = None
            for col_tile in range(row_tile + 1):
                cols = slice(col_tile * size, (col_tile + 1) * size)
                weight = tile_weight(r, first_head, head, row_tile, col_tile, size)
                scores = (nt(queries, r.k[cols, wide]) * weight).astype(BF16)
                term = nn(scores, r.v[cols, thin])
                acc = term if acc is None else acc + term
            r.heads[rows, thin] = acc
            r.dh[rows, thin] = (acc * r.gate[rows, thin]).astype(BF16)

    for chunk in range(length // 128):
        v = r.heads[chunk * 128 : (chunk + 1) * 128, :]
        row_sums(v * v, r.ss_mine, chunk)
    share.start()
    save("heads")
    if third is not None:
        for part in range(SUPER):
            third.forward(part)
    w_out.wait()

    part_rows = 2 * half
    for part in range(SUPER):
        for step in (3, 1, 2, 0):
            rows = aligned(place.member(step) * block + part * part_rows, part_rows)
            r.part1[rows, :] = nn(r.dh[rows, :], r.wo[...]).astype(BF16)
            mid_sum.send_block(part, step)
    for part in range(SUPER):
        mid_sum.middle(part)
    r.ss[...] = share.total()
    save("ss")
    scaling = lax.rsqrt(r.ss[...] / width + epsilon)
    per_block = block // 128
    for chunk in range(per_block):
        r.scale[aligned(own_start + chunk * 128, 128), :] = spread(scaling, place.me * per_block + chunk)
    r.stat_wide[...] = jnp.zeros_like(r.stat_wide)

    def add_stat(row, v):
        sums = jnp.sum(v * v, axis=0, keepdims=True)
        r.stat_wide[row : row + 1, :] += sums

    step_rows = min(32, half)
    for part in range(SUPER):
        for h in range(2):
            mid_sum.finish(part, h)
            for i in range(half // step_rows):
                offset = (2 * part + h) * half + i * step_rows
                scale = widen(r.scale[aligned(own_start + offset, step_rows), :], width // 128)
                attn = mid_sum.total(part, h, i * step_rows, step_rows) * scale
                middle = x[offset : offset + step_rows, :].astype(F32) + attn
                r.mid[offset : offset + step_rows, :] = middle
                add_stat(0, attn)
                norm = lax.rsqrt(jnp.mean(middle * middle, axis=1, keepdims=True) + epsilon)
                r.n2[aligned(own_start + offset, step_rows), :] = (middle * norm).astype(BF16)
        second.start(part)
    save("mid")
    for copy in w_glu:
        copy.wait()
    if third is not None:
        mid_sum.drain()
        for part in range(SUPER):
            for which in (1, 2, 3):
                third.finish(part, which)

    def glu(part, step):
        rows = aligned(place.member(step) * block + part * part_rows, part_rows)
        a = r.n2[rows, :]
        left = nt(a, r.wl[...])
        right = nt(a, r.wr[...])
        hidden = (left * right).astype(BF16)
        r.hid[rows, :] = hidden
        if back_block is not None:
            back_block(rows, left, right, part, step)
        else:
            r.left[rows, :] = left.astype(BF16)
            r.right[rows, :] = right.astype(BF16)
        r.part2[rows, :] = nn(hidden, r.wd[...]).astype(BF16)
        if back_block is None:
            for which in (1, 2, 3):
                @pl.when(step == which)
                def _():
                    out_sum.send_block(part, which)

    gather_stage(second, glu, lambda i: None)

    def finish():
        for part in range(SUPER):
            for h in range(2):
                out_sum.finish(part, h)
                for i in range(half // step_rows):
                    offset = (2 * part + h) * half + i * step_rows
                    glu_rows = out_sum.total(part, h, i * step_rows, step_rows)
                    after = r.mid[offset : offset + step_rows, :] + glu_rows
                    r.xo[offset : offset + step_rows, :] = after.astype(r.xo.dtype)
                    add_stat(1, glu_rows)
                    add_stat(2, after)
        folded = r.stat_wide[:, :128]
        for n in range(1, width // 128):
            folded = folded + r.stat_wide[:, n * 128 : (n + 1) * 128]
        return folded

    groups = [first, second, share] + ([third] if third is not None else [mid_sum])
    return out_sum, finish, groups


def fwd_kernel(cfg, names, *refs):
    r = namespace(names, refs)
    place = Place(cfg.pairs)
    copies = Local(r.local_sem)
    saves = []

    def save(*keys):
        for key in keys:
            saves.append(copies.start(getattr(r, key), getattr(r, key + "_h")))

    out_sum, finish, groups = forward_front(cfg, r, place, copies, cfg.layer, r.x, save, None, None)
    save("n2", "left", "right", "hid")
    for part in range(SUPER):
        out_sum.middle(part)
    r.stat[...] = finish()
    for copy in saves:
        copy.wait()
    for group in (*groups, out_sum):
        group.drain()


def turns_of(k, size, count):
    return sum(((k >= size * n).astype(jnp.int32) for n in range(1, -(-count // size))), jnp.int32(0))


class Line:
    def __init__(self, cfg, place, r):
        self.place, self.r = place, r
        self.per, self.count = cfg.chunks, cfg.chunks * cfg.layers
        self.layers, self.rows_each = cfg.layers, cfg.chunks * CHUNK
        self.half = CHUNK // 2
        self.ticks = self.count + 3 + HOP * place.last
        self.done = 0

    def slot(self, k):
        return k - SLOTS * turns_of(k, SLOTS, self.count)

    def rows(self, k, core):
        place = k - self.per * turns_of(k, self.per, self.count)
        return aligned(place * CHUNK + core * self.half, self.half)

    def own(self, k):
        return self.rows(k, self.place.core)

    def out_rows(self, k, core):
        turn = turns_of(k, self.per, self.count)
        place = (self.layers - 1 - turn) * self.per + k - turn * self.per
        start = place * CHUNK + core * self.half
        return aligned(start, self.half)

    def pair(self, k):
        slot = self.slot(k)
        r = self.r
        return Wire(self.place.partner(), r.pair_send.at[slot], r.pair_recv.at[slot],
                    r.grads.at[self.rows(k, 1 - self.place.core)], r.pair_land.at[slot], r.pair_land.at[slot])

    def hop(self, k, land, send, recv, device):
        slot = self.slot(k)
        return Wire(device, send.at[slot], recv.at[slot], land.at[slot], land.at[slot], land.at[slot])

    def going_right(self, k):
        return self.hop(k, self.r.right_land, self.r.right_send, self.r.right_recv, self.place.right())

    def going_left(self, k):
        return self.hop(k, self.r.left_land, self.r.left_send, self.r.left_recv, self.place.left())

    def coming_right(self, k):
        return self.hop(k, self.r.right_land, self.r.right_send, self.r.right_recv, self.place.left())

    def coming_left(self, k):
        return self.hop(k, self.r.left_land, self.r.left_send, self.r.left_recv, self.place.right())

    def result(self, k):
        slot, r = self.slot(k), self.r
        return Wire(self.place.partner(), r.give_send.at[slot], r.give_recv.at[slot],
                    r.grads.at[self.own(k)], r.out_h.at[self.out_rows(k, self.place.core)],
                    r.out_h.at[self.out_rows(k, 1 - self.place.core)])

    def keep(self, k):
        slot, r = self.slot(k), self.r
        return pltpu.make_async_copy(
            r.grads.at[self.own(k)], r.out_h.at[self.out_rows(k, self.place.core)], r.keep_sem.at[slot]
        )

    def one_way(self, k, land, start_here, coming, ends_here, going):
        slot = self.slot(k)

        @pl.when(start_here)
        def _():
            land[slot] = self.r.grads[self.own(k), :]

        @pl.when(jnp.logical_not(start_here))
        def _():
            coming(k).wait_recv()
            land[slot] = land[slot] + self.r.grads[self.own(k), :]

        @pl.when(jnp.logical_not(ends_here))
        def _():
            going(k).start()

    def tick(self, n):
        place, r, last = self.place, self.r, self.place.last
        at_left, at_right = place.at == 0, place.at == last

        @pl.when(n < self.count)
        def _():
            self.pair(n).start()

        k = n - 1

        @pl.when(jnp.logical_and(k >= 0, k < self.count))
        def _():
            wire = self.pair(k)
            wire.wait_recv()
            wire.wait_send()
            slot = self.slot(k)
            r.grads[self.own(k), :] = r.grads[self.own(k), :] + r.pair_land[slot]

        left_k = n - 1 - HOP * (last - place.at)

        @pl.when(jnp.logical_and(left_k >= 0, left_k < self.count))
        def _():
            self.one_way(left_k, r.left_land, at_right, self.coming_left, at_left, self.going_left)

        right_k = n - 1 - HOP * place.at

        @pl.when(jnp.logical_and(right_k >= 0, right_k < self.count))
        def _():
            self.one_way(right_k, r.right_land, at_left, self.coming_right, at_right, self.going_right)

        full_k = n - 1 - HOP * last

        @pl.when(jnp.logical_and(full_k >= 0, full_k < self.count))
        def _():
            @pl.when(jnp.logical_not(at_right))
            def _():
                self.going_right(full_k).wait_send()

            @pl.when(jnp.logical_not(at_left))
            def _():
                self.going_left(full_k).wait_send()

            slot = self.slot(full_k)
            own = self.own(full_k)
            total = r.right_land[slot].astype(F32) + r.left_land[slot].astype(F32) - r.grads[own, :].astype(F32)
            r.grads[own, :] = total.astype(BF16)
            self.result(full_k).start()
            self.keep(full_k).start()

        old_k = full_k - 2

        @pl.when(jnp.logical_and(old_k >= 0, old_k < self.count))
        def _():
            wire = self.result(old_k)
            wire.wait_recv()
            wire.wait_send()
            self.keep(old_k).wait()

    def pump(self, ready, most):
        stop = min(self.done + most, ready)
        if stop > self.done:
            start, self.done = self.done, stop

            @pl.loop(start, stop)
            def _(n):
                self.tick(n)

    def release(self, turn, rows):
        needed = (turn - 1) * self.per + -(-rows // CHUNK) + 3 + HOP * self.place.last
        if turn > 0 and needed > self.done:
            self.pump(turn * self.per, needed - self.done)
            assert self.done >= needed

    def finish(self):
        start, self.done = self.done, self.ticks

        @pl.loop(start, self.ticks)
        def _(n):
            self.tick(n)


class StatLine:
    def __init__(self, place, r):
        self.place, self.r = place, r
        self.share = Share(place, r.stat_mine, r.stat_land, r.st_send, r.st_recv)

    def square(self):
        self.share.start()

    def pair(self):
        r = self.r
        r.stat_square[...] = self.share.total()
        self.wire(0, self.place.partner(), r.stat_square).start()

    def wire(self, number, device, source):
        r = self.r
        return Wire(device, r.line_send.at[number], r.line_recv.at[number], source, r.line_land.at[number], r.line_land.at[number])

    def stage(self, number):
        place, r = self.place, self.r
        if number == 0:
            self.wire(0, place.partner(), r.stat_square).wait_recv()
            r.stat_pair[...] = r.stat_square[...] + r.line_land[0]
            r.stat_right[...] = r.stat_pair[...]
            r.stat_left[...] = r.stat_pair[...]
        else:
            @pl.when(place.at == number)
            def _():
                self.wire(1, place.left(), r.stat_right).wait_recv()
                r.stat_right[...] = r.stat_pair[...] + r.line_land[1]

            @pl.when(place.last - place.at == number)
            def _():
                self.wire(2, place.right(), r.stat_left).wait_recv()
                r.stat_left[...] = r.stat_pair[...] + r.line_land[2]
        if number < place.last:
            @pl.when(place.at == number)
            def _():
                self.wire(1, place.right(), r.stat_right).start()

            @pl.when(place.last - place.at == number)
            def _():
                self.wire(2, place.left(), r.stat_left).start()

    def finish(self):
        place, r = self.place, self.r
        r.stat_total[...] = r.stat_right[...] + r.stat_left[...] - r.stat_pair[...]
        self.share.drain()
        self.wire(0, place.partner(), r.stat_square).wait_send()

        @pl.when(place.at < place.last)
        def _():
            self.wire(1, place.right(), r.stat_right).wait_send()

        @pl.when(place.at > 0)
        def _():
            self.wire(2, place.left(), r.stat_left).wait_send()


def bwd_kernel(cfg, names, *refs):
    r = namespace(names, refs)
    block, length, width, local, ff = cfg.block, cfg.length, cfg.width, cfg.local, cfg.ff
    heads_here, size, layers = cfg.heads_here, cfg.block, cfg.layers
    place = Place(cfg.pairs)
    copies = Local(r.local_sem)
    line = Line(cfg, place, r)
    stats = StatLine(place, r)
    loads = {}
    base_down, base_left, base_right, base_out, base_gate, gate_end, base_qkv, _ = cfg.bases
    half = block // (2 * SUPER)
    part_rows = 2 * half
    own_start = place.me * block
    step_rows = min(32, half)
    per_block = block // 128
    tiles_here = length // size

    def load(layer, *keys):
        for key in keys:
            if key in SAVED:
                source = getattr(r, key + str(layer) + "_h")
            else:
                source = getattr(r, key + "_h").at[layer]
            loads[key] = copies.start(source, getattr(r, key))

    def await_loads(*keys):
        for key in keys:
            loads[key].wait()

    glu_in = ("wd", "left", "right", "wl", "wr")
    glu_grad = ("hid", "n2")
    out_in = ("ss", "wo", "gate", "heads")
    attn_in = ("q", "k", "v", "ql", "kl")
    in_in = ("wq", "wk", "wv", "wg")

    def gather_one(layer):
        return Gather(place, r.gd, r.ag1_send.at[layer], r.ag1_recv.at[layer], block)

    firsts = [gather_one(layer) for layer in range(layers)]

    @pl.loop(0, block // 32)
    def _(i):
        rows = aligned(i * 32, 32)
        r.g[rows, :] = r.up[rows, :].astype(F32)

        r.gd[aligned(own_start + i * 32, 32), :] = r.up[rows, :]

    for start, stop in ((gate_end, base_qkv), (base_qkv + 3 * local, cfg.chunks * CHUNK)):
        if stop > start:
            r.grads[start:stop, :] = jnp.zeros((stop - start, width), BF16)
    top = layers - 1
    third = Gather(place, r.gd, r.ag3_send, r.ag3_recv, block)
    top_sum = Scatter(place, r.part1, r.land1, r.rs1_send.at[top], r.rs1_recv.at[top], block)

    def back_block(rows, left, right, part, step):
        grad_hidden = nt(r.gd[rows, :], r.wd[...])
        grad_left = (grad_hidden * right).astype(BF16)
        grad_right = (grad_hidden * left).astype(BF16)
        r.right[rows, :] = grad_left
        r.left[rows, :] = grad_right
        r.part1[rows, :] = (nn(grad_left, r.wl[...]) + nn(grad_right, r.wr[...])).astype(BF16)
        for which in (1, 2, 3):
            @pl.when(step == which)
            def _():
                top_sum.send_block(part, which)

    out_sum, finish_forward, groups = forward_front(
        cfg, r, place, copies, top, getattr(r, "x%d" % top), lambda *keys: None, third, back_block
    )
    for group in groups:
        group.drain()

    def back_rows(total, values, grad):
        norm = lax.rsqrt(jnp.mean(values * values, axis=1, keepdims=True) + epsilon)
        m = values * norm
        inner = jnp.mean(total * m, axis=1, keepdims=True)
        return grad + norm * (total - m * inner)

    for turn, layer in enumerate(reversed(range(layers))):
        first = firsts[layer]
        mid_sum = top_sum if turn == 0 else Scatter(place, r.part1, r.land1, r.rs1_send.at[layer], r.rs1_recv.at[layer], block)
        second = Gather(place, r.ga, r.ag2_send.at[layer], r.ag2_recv.at[layer], block)
        in_sum = Scatter(place, r.part1, r.land1, r.rs2_send.at[layer], r.rs2_recv.at[layer], block)
        share = Share(place, r.inner, r.inner_land.at[layer], r.in_send.at[layer], r.in_recv.at[layer])
        first_head = layer * HEADS + place.me * heads_here

        def ready(rows):
            return turn * cfg.chunks + rows // CHUNK

        if turn > 0:
            decay_tiles(r.dec, first_head, r.tiles, heads_here, size)
            await_loads(*glu_in)
            await_loads(*out_in)
        scaling = lax.rsqrt(r.ss[...] / width + epsilon)
        for chunk in range(length // 128):
            r.scale[chunk * 128 : (chunk + 1) * 128, :] = spread(scaling, chunk)
        def glu_back(part, step):
            rows = aligned(place.member(step) * block + part * part_rows, part_rows)
            grad_hidden = nt(r.gd[rows, :], r.wd[...])
            grad_left = (grad_hidden * r.right[rows, :].astype(F32)).astype(BF16)
            grad_right = (grad_hidden * r.left[rows, :].astype(F32)).astype(BF16)
            r.right[rows, :] = grad_left
            r.left[rows, :] = grad_right
            r.part1[rows, :] = (nn(grad_left, r.wl[...]) + nn(grad_right, r.wr[...])).astype(BF16)
            for which in (1, 2, 3):
                @pl.when(step == which)
                def _():
                    mid_sum.send_block(part, which)

        if turn > 0:
            gather_stage(first, glu_back, lambda i: line.pump(ready(0), 2))
            first.drain()
        grad_left_ref, grad_right_ref = r.right, r.left

        def glu_grad_rows(base, a_ref, b_ref):
            line.release(turn, base + ff)
            for n in range(width // 256):
                cols = slice(n * 256, (n + 1) * 256)
                r.grads[base : base + ff, cols] = tn(a_ref[...], b_ref[:, cols]).astype(BF16)

        if turn > 0:
            await_loads(*glu_grad)
        glu_grad_rows(base_down, r.hid, r.gd)
        if turn == 1:
            folded = finish_forward()
            r.stat_mine[...] = jnp.zeros_like(r.stat_mine)
            for one in range(top):
                r.stat_mine[3 * one : 3 * one + 3, :] = getattr(r, "stat%d" % one)[0:3, :]
            r.stat_mine[3 * top : 3 * top + 3, :] = folded[0:3, :]
            stats.square()
        if turn > 0:
            load(layer, "mid")
        line.pump(ready(base_left), 1 + turn)
        mid_sum.middle(0)
        glu_grad_rows(base_left, grad_left_ref, r.n2)
        line.pump(ready(base_right), 1 + turn)
        for part in range(1, SUPER):
            mid_sum.middle(part)
        glu_grad_rows(base_right, grad_right_ref, r.n2)
        if turn == 1:
            stats.pair()
        if turn > 0:
            await_loads("mid")
        for part in range(SUPER):
            line.pump(ready(base_out), 2 if part == 0 else 1)
            for h in range(2):
                mid_sum.finish(part, h)
                for i in range(half // step_rows):
                    offset = (2 * part + h) * half + i * step_rows
                    rows = slice(offset, offset + step_rows)
                    total = mid_sum.total(part, h, i * step_rows, step_rows)
                    new = back_rows(total, r.mid[rows, :], r.g[rows, :])
                    r.gm[rows, :] = new
                    r.ga[aligned(own_start + offset, step_rows), :] = new.astype(BF16)
            second.start(part)
        mid_sum.drain()
        if turn + 1 < layers:
            load(layer - 1, *glu_in, *glu_grad)

        def send_out():
            for part in range(SUPER):
                for which in (1, 2, 3):
                    out_sum.send_block(part, which)

        def out_back(part, step):
            member = place.member(step)
            for chunk in range(part_rows // 128):
                number = part * (part_rows // 128) + chunk
                rows = aligned(member * block + number * 128, 128)
                grad_branch = nt(r.ga[rows, :], r.wo[...])
                gate = r.gate[rows, :]
                normed = r.heads[rows, :] * widen(r.scale[rows, :], local // 128)
                grad_normed = grad_branch * gate
                r.dx[rows, 3 * local : 4 * local] = (grad_branch * normed).astype(BF16)
                r.branch[rows, :] = (normed * gate).astype(BF16)
                r.gate[rows, :] = grad_normed
                row_sums(grad_normed * normed, r.inner, member * per_block + number)

        gather_stage(second, out_back, lambda i: line.pump(ready(base_out), 3 if i == SUPER else 2),
                     send_out if turn == 0 else None)
        share.start()
        line.release(turn, base_gate)
        r.grads[base_out : base_out + local, :] = tn(r.branch[...], r.ga[...]).astype(BF16)
        line.pump(ready(base_gate), 1)

        def in_grad_rows(number, base):
            cols = slice(number * local, (number + 1) * local)
            line.release(turn, base + local)
            for n in range(width // local):
                part_grad = tn(r.n1[:, n * local : (n + 1) * local], r.dx[:, cols])
                r.grads[base : base + local, n * local : (n + 1) * local] = part_grad.astype(BF16)

        if turn > 0:
            await_loads("n1")
        if turn == 1:
            stats.stage(0)
        in_grad_rows(3, base_gate)
        line.pump(ready(base_qkv), 1)
        if turn > 0:
            await_loads(*attn_in)
        r.intot[...] = share.total() / width
        for chunk in range(length // 128):
            rows = slice(chunk * 128, (chunk + 1) * 128)
            scale = widen(r.scale[rows, :], local // 128)
            inner = widen(spread(r.intot[...], chunk), local // 128)
            normed = r.heads[rows, :] * scale
            r.dh[rows, :] = (scale * (r.gate[rows, :] - normed * inner)).astype(BF16)
        share.drain()
        second.drain()
        if turn + 1 < layers:
            load(layer - 1, *out_in)
        line.pump(ready(base_qkv), 1)
        between = line.done
        line.done += 1
        assert line.done <= ready(base_qkv)

        @pl.loop(0, heads_here)
        def _(head):
            @pl.when(head == 1)
            def _():
                line.tick(between + head - 1)

            wide = aligned(head * 2 * HDIM, 2 * HDIM)
            thin = aligned(head * HDIM, HDIM)
            for col_tile in range(tiles_here):
                cols = slice(col_tile * size, (col_tile + 1) * size)
                keys = r.k[cols, wide]
                values = r.v[cols, thin]
                acc_key, acc_value = None, None
                for row_tile in range(col_tile, tiles_here):
                    rows = slice(row_tile * size, (row_tile + 1) * size)
                    queries = r.q[rows, wide]
                    grads = r.dh[rows, thin]
                    weight = tile_weight(r, first_head, head, row_tile, col_tile, size)
                    scores = (nt(queries, keys) * weight).astype(BF16)
                    pulled = (nt(grads, values) * weight).astype(BF16)
                    term = nn(pulled, keys)
                    if col_tile == 0:
                        r.dq[rows, :] = term
                    else:
                        r.dq[rows, :] += term
                    key_term = tn(pulled, queries)
                    value_term = tn(scores, grads)
                    acc_key = key_term if acc_key is None else acc_key + key_term
                    acc_value = value_term if acc_value is None else acc_value + value_term
                r.dk[cols, :] = acc_key
                r.dx[cols, aligned(2 * local + head * HDIM, HDIM)] = acc_value.astype(BF16)
            for row_tile in range(tiles_here):
                rows = slice(row_tile * size, (row_tile + 1) * size)
                cosine, sine = r.cos[rows, :], r.sin[rows, :]
                for grad, lin, base in ((r.dq, r.ql, 0), (r.dk, r.kl, local)):
                    v = lin[rows, thin].astype(F32)
                    gate = 1.0 / (1.0 + jnp.exp(-v))
                    back = grad[rows, :HDIM] * cosine + grad[rows, HDIM:] * sine
                    back = back * (gate + v * gate * (1.0 - gate))
                    r.dx[rows, aligned(base + head * HDIM, HDIM)] = back.astype(BF16)

        if turn + 1 < layers:
            load(layer - 1, *attn_in)
        if turn > 0:
            await_loads(*in_in)
        if turn == 1:
            stats.stage(1)
        last = turn == layers - 1
        if last:
            for number in range(3):
                in_grad_rows(number, base_qkv + number * local)
        for part in range(SUPER):
            for step in (3, 1, 2, 0):
                rows = aligned(place.member(step) * block + part * part_rows, part_rows)
                total = None
                for n, w in enumerate((r.wq, r.wk, r.wv, r.wg)):
                    term = nt(r.dx[rows, n * local : (n + 1) * local], w[...])
                    total = term if total is None else total + term
                r.part1[rows, :] = total.astype(BF16)
                in_sum.send_block(part, step)
            line.pump(ready(cfg.chunks * CHUNK if last else base_qkv), 2 if last else 1)
        for number in range(3):
            if not last:
                in_grad_rows(number, base_qkv + number * local)
            line.pump(ready(base_qkv + (number + 1) * local), 2 if last else 1)
            if number < SUPER:
                in_sum.middle(number)
        if turn == 0:
            for part in range(SUPER):
                out_sum.middle(part)
        if turn == 1:
            stats.stage(2)
        if turn + 1 < layers:
            load(layer - 1, *in_in, "n1")
        for part in range(SUPER):
            line.pump(ready(cfg.chunks * CHUNK), 2)
            for h in range(2):
                in_sum.finish(part, h)
                for i in range(half // step_rows):
                    offset = (2 * part + h) * half + i * step_rows
                    rows = slice(offset, offset + step_rows)
                    total = in_sum.total(part, h, i * step_rows, step_rows)
                    values = getattr(r, "x%d" % layer)[rows, :].astype(F32)
                    new = back_rows(total, values, r.gm[rows, :])
                    if layer > 0:
                        r.g[rows, :] = new
                        r.gd[aligned(own_start + offset, step_rows), :] = new.astype(BF16)
                    else:
                        r.go[rows, :] = new.astype(BF16)
            if layer > 0:
                firsts[layer - 1].start(part)
        in_sum.drain()
    out_sum.drain()
    for number in range(3, cfg.pairs):
        stats.stage(number)
    stats.finish()
    line.finish()


def call_kernel(body, cfg, inputs, outputs, scratch, collective_id, name):
    vmem, anywhere = pl.BlockSpec(memory_space=pltpu.VMEM), pl.BlockSpec(memory_space=pl.ANY)
    names = list(inputs) + list(outputs) + list(scratch)
    result = pl.pallas_call(
        functools.partial(body, cfg, names),
        out_shape=[shape for shape, _ in outputs.values()],
        in_specs=[vmem if placed else anywhere for _, placed in inputs.values()],
        out_specs=[vmem if placed else anywhere for _, placed in outputs.values()],
        scratch_shapes=list(scratch.values()),
        compiler_params=pltpu.CompilerParams(
            collective_id=collective_id, has_side_effects=collective_id is not None, vmem_limit_bytes=VMEM_LIMIT
        ),
        name=name,
    )(*[array for array, _ in inputs.values()])
    return dict(zip(outputs, result))


def collective_scratch(cfg, copies, lead):
    dma = pltpu.SemaphoreType.DMA
    half = cfg.block // (2 * SUPER)
    out = {}
    for name in ("ag1", "ag2", "rs1", "rs2"):
        out["f" + name + "_send"] = out["f" + name + "_recv"] = dma((SUPER, 6))
        if lead:
            out[name + "_send"] = out[name + "_recv"] = dma((*lead, SUPER, 6))
    for name in copies:
        out["land" + name] = pltpu.VMEM((SUPER, 6, half, cfg.width), BF16)
        out["part" + name] = pltpu.VMEM((cfg.length, cfg.width), BF16)
    out["local_sem"] = dma((64,))
    return out


def weight_scratch(cfg):
    v = pltpu.VMEM
    return dict(
        wq=v((cfg.width, cfg.local), BF16), wk=v((cfg.width, cfg.local), BF16),
        wv=v((cfg.width, cfg.local), BF16), wg=v((cfg.width, cfg.local), BF16),
        wo=v((cfg.local, cfg.width), BF16), wl=v((cfg.ff, cfg.width), BF16),
        wr=v((cfg.ff, cfg.width), BF16), wd=v((cfg.ff, cfg.width), BF16),
    )


def table_scratch(cfg):
    v = pltpu.VMEM
    return dict(
        segc=v((cfg.length, 128), F32), segf=v((8, 128), F32),
        tiles=v((cfg.heads_here, 2, cfg.block, cfg.block), F32),
    )


def forward_scratch(cfg):
    v, dma = pltpu.VMEM, pltpu.SemaphoreType.DMA
    rows, wide, local, ff, block = cfg.length, cfg.width, cfg.local, cfg.ff, cfg.block
    return dict(
        n1=v((rows, wide), BF16), ql=v((rows, local), BF16), kl=v((rows, local), BF16), q=v((rows, 2 * local), BF16),
        k=v((rows, 2 * local), BF16), v=v((rows, local), BF16), gate=v((rows, local), F32), heads=v((rows, local), F32),
        mid=v((block, wide), F32), n2=v((rows, wide), BF16), left=v((rows, ff), BF16), right=v((rows, ff), BF16),
        hid=v((rows, ff), BF16), ss=v((8, 128), F32), ss_mine=v((8, 128), F32), dh=v((rows, local), BF16),
        stat_wide=v((8, wide), F32), scale=v((rows, 128), F32), ss_land=v((3, 8, 128), F32), ss_send=dma((3,)), ss_recv=dma((3,)),
    )


def run_forward(cfg, x, tables, weights):
    s = jax.ShapeDtypeStruct
    inputs = dict(x=(x, True), **{k: (a, True) for k, a in tables.items()}, **{k + "_h": (a, False) for k, a in weights.items()})
    scratch = dict(
        **weight_scratch(cfg), **collective_scratch(cfg, ("1", "2"), ()), **table_scratch(cfg), **forward_scratch(cfg),
    )
    outputs = dict(
        xo=(s((cfg.block, cfg.width), F32), True), stat=(s((8, 128), F32), True),
        **{k + "_h": (s(scratch[k].shape, scratch[k].dtype), False) for k in SAVED},
    )
    return call_kernel(fwd_kernel, cfg, inputs, outputs, scratch, cfg.layer, "layer_forward")


SAVED = ("ss", "mid", "n1", "ql", "kl", "q", "k", "v", "gate", "heads", "n2", "left", "right", "hid")


def run_backward(cfg, upstream, xs, saved, tables, weights):
    v, dma, s = pltpu.VMEM, pltpu.SemaphoreType.DMA, jax.ShapeDtypeStruct
    rows, wide, local, ff, block = cfg.length, cfg.width, cfg.local, cfg.ff, cfg.block
    inputs = dict(up=(upstream, True), **{k: (a, True) for k, a in tables.items()}, **{k + "_h": (a, False) for k, a in weights.items()})
    for layer in range(cfg.layers):
        inputs["x%d" % layer] = (xs[layer], True)
    for layer in range(cfg.layers - 1):
        inputs["stat%d" % layer] = (saved[layer]["stat"], True)
        for key in SAVED:
            inputs["%s%d_h" % (key, layer)] = (saved[layer][key + "_h"], False)
    total_rows = cfg.chunks * CHUNK
    outputs = dict(
        xo=(s((block, wide), BF16), True), go=(s((block, wide), BF16), True), stat_total=(s((8, 128), F32), True),
        out_h=(s((cfg.layers * total_rows, wide), BF16), False),
    )
    small, ring, ring_sem = v((8, 128), F32), v((SLOTS, CHUNK // 2, wide), BF16), dma((SLOTS,))
    scratch = dict(
        **weight_scratch(cfg), **collective_scratch(cfg, ("1", "2"), (cfg.layers,)), **table_scratch(cfg), **forward_scratch(cfg),
        ag3_send=dma((SUPER, 6)), ag3_recv=dma((SUPER, 6)),
        gd=v((rows, wide), BF16), ga=v((rows, wide), BF16),
        g=v((block, wide), F32), gm=v((block, wide), F32),
        branch=v((rows, local), BF16), dx=v((rows, 4 * local), BF16),
        dq=v((rows, 2 * HDIM), F32), dk=v((rows, 2 * HDIM), F32),
        grads=v((total_rows, wide), BF16),
        inner=small, intot=small,
        inner_land=v((cfg.layers, 3, 8, 128), F32), in_send=dma((cfg.layers, 3)), in_recv=dma((cfg.layers, 3)),
        pair_land=ring, right_land=ring, left_land=ring,
        pair_send=ring_sem, pair_recv=ring_sem, right_send=ring_sem, right_recv=ring_sem, left_send=ring_sem,
        left_recv=ring_sem, give_send=ring_sem, give_recv=ring_sem, keep_sem=ring_sem,
        stat_mine=small, stat_square=small, stat_pair=small, stat_right=small, stat_left=small,
        stat_land=v((3, 8, 128), F32), st_send=dma((3,)), st_recv=dma((3,)),
        line_land=v((3, 8, 128), F32), line_send=dma((3,)), line_recv=dma((3,)),
    )
    return call_kernel(bwd_kernel, cfg, inputs, outputs, scratch, cfg.layers, "layers_backward")


def widen_kernel(cfg, names, *refs):
    r = namespace(names, refs)
    tasks = []
    for layer in range(cfg.layers):
        for number, target in enumerate((r.down, r.left, r.right, r.out)):
            start, stop = cfg.bases[number], cfg.bases[number + 1]
            rows = (stop - start) // 2 if stop - start > 512 else stop - start
            for first in range(start, stop, rows):
                tasks.append((layer, first, rows, [(target.at[layer, pl.ds(first - start, rows), :], slice(None))]))
        for number, target in enumerate((r.gate, r.query, r.key, r.value)):
            pieces = [
                (target.at[layer, pl.ds(n * cfg.local, cfg.local), :], slice(n * cfg.local, (n + 1) * cfg.local))
                for n in range(cfg.width // cfg.local)
            ]
            start = cfg.bases[6] + (number - 1) * cfg.local if number > 0 else cfg.bases[4]
            tasks.append((layer, start, cfg.local, pieces))
    depth = 3

    def fetch(task):
        layer, first, rows, _ = tasks[task]
        start = layer * cfg.chunks * CHUNK + first
        slot = task % depth
        return pltpu.make_async_copy(r.grads.at[pl.ds(start, rows), :], r.narrow.at[slot, pl.ds(0, rows), :], r.in_sem.at[slot])

    def store(task):
        _, _, rows, pieces = tasks[task]
        slot = task % depth
        return [
            pltpu.make_async_copy(r.wide.at[slot, pl.ds(0, rows), lanes], target, r.out_sem.at[slot, n])
            for n, (target, lanes) in enumerate(pieces)
        ]

    for task in range(min(depth, len(tasks))):
        fetch(task).start()
    for task in range(len(tasks)):
        slot, rows = task % depth, tasks[task][2]
        fetch(task).wait()
        if task >= depth:
            for copy in store(task - depth):
                copy.wait()

        @pl.loop(0, rows // 32)
        def _(i):
            part = aligned(i * 32, 32)
            r.wide[slot, part, :] = r.narrow[slot, part, :].astype(F32)

        for copy in store(task):
            copy.start()
        if task + depth < len(tasks):
            fetch(task + depth).start()
    for task in range(max(len(tasks) - depth, 0), len(tasks)):
        for copy in store(task):
            copy.wait()


def run_widen(cfg, grads):
    v, dma, s = pltpu.VMEM, pltpu.SemaphoreType.DMA, jax.ShapeDtypeStruct
    thin, flat = s((cfg.layers, cfg.width, cfg.local), F32), s((cfg.layers, cfg.ff, cfg.width), F32)
    outputs = dict(
        down=(flat, False), left=(flat, False), right=(flat, False), out=(s((cfg.layers, cfg.local, cfg.width), F32), False),
        gate=(thin, False), query=(thin, False), key=(thin, False), value=(thin, False),
    )
    rows = max(cfg.ff // 2, cfg.local, 512)
    scratch = dict(
        narrow=v((3, rows, cfg.width), BF16), wide=v((3, rows, cfg.width), F32),
        in_sem=dma((3,)), out_sem=dma((3, cfg.width // cfg.local)),
    )
    return call_kernel(widen_kernel, cfg, dict(grads=(grads, False)), outputs, scratch, None, "widen_gradients")


def per_device_square(
    tokens, upstream, segment_ids, query_proj, key_proj, value_proj, gate_proj, output_proj, left_proj, right_proj, down_proj
):
    layers = query_proj.shape[0]
    block, width = tokens.shape
    length = segment_ids.shape[0]
    local, ff = query_proj.shape[2], left_proj.shape[2]
    heads_here = local // HDIM
    positions = np.arange(length, dtype=np.float32)
    frequency = np.exp(np.float32(-math.log(10000.0)) * np.arange(HDIM, dtype=np.float32) / np.float32(HDIM))
    angles = positions[:, None] * frequency[None, :]
    slopes = np.exp2(-8.0 * (np.arange(HEADS) + 1.0) / HEADS)
    decays = np.concatenate([-slopes * (1.0 - depth_start - depth_step * layer) for layer in range(layers)])
    tables = dict(
        cos=jnp.asarray(np.cos(angles)), sin=jnp.asarray(np.sin(angles)),
        dec=jnp.asarray(np.broadcast_to(decays[:, None], (layers * HEADS, 128)).astype(np.float32)),
        seg=segment_ids.reshape(8, length // 8),
    )
    weights = dict(
        wq=query_proj, wk=key_proj, wv=value_proj, wg=gate_proj, wo=output_proj,
        wl=jnp.swapaxes(left_proj, 1, 2), wr=jnp.swapaxes(right_proj, 1, 2), wd=down_proj,
    )
    ends = np.cumsum([0, ff, ff, ff, local, local]).tolist()
    ends += [-(-ends[-1] // CHUNK) * CHUNK]
    ends += [-(-(ends[-1] + 3 * local) // CHUNK) * CHUNK]
    common = dict(
        layers=layers, block=block, length=length, width=width, local=local, ff=ff, heads_here=heads_here,
        pairs=lax.axis_size("dp") // 2, bases=ends, chunks=ends[-1] // CHUNK,
    )
    current, xs, saved = tokens, [tokens], []
    for layer in range(layers - 1):
        saved.append(run_forward(types.SimpleNamespace(layer=layer, **common), current, tables, weights))
        current = saved[-1]["xo"]
        xs.append(current)
    back = run_backward(types.SimpleNamespace(**common), upstream, xs, saved, tables, weights)
    stats = jnp.sum(back["stat_total"][: 3 * layers], axis=1).reshape(layers, 3)
    rms_stats = jnp.sqrt(stats / (length * lax.axis_size("dp") * width))
    wide = run_widen(types.SimpleNamespace(**common), back["out_h"])
    return (
        back["xo"], back["go"], wide["query"], wide["key"], wide["value"], wide["gate"], wide["out"],
        jnp.swapaxes(wide["left"], 1, 2), jnp.swapaxes(wide["right"], 1, 2), wide["down"], rms_stats,
    )


def solution(mesh):
    square = dict(mesh.shape) == SQUARE_MESH
    body = per_device_square if square else per_device
    return jax.shard_map(
        body,
        mesh=mesh,
        in_specs=(
            P(("dp", "tensor"), None),
            P(("dp", "tensor"), None),
            P("dp"),
            P(None, None, "tensor"),
            P(None, None, "tensor"),
            P(None, None, "tensor"),
            P(None, None, "tensor"),
            P(None, "tensor", None),
            P(None, None, "tensor"),
            P(None, None, "tensor"),
            P(None, "tensor", None),
        ),
        out_specs=(
            P(("dp", "tensor"), None),
            P(("dp", "tensor"), None),
            P(None, None, "tensor"),
            P(None, None, "tensor"),
            P(None, None, "tensor"),
            P(None, None, "tensor"),
            P(None, "tensor", None),
            P(None, None, "tensor"),
            P(None, None, "tensor"),
            P(None, "tensor", None),
            P(),
        ),
        check_vma=False,
    )
```

```python
import functools
import math
import types

import jax
import jax.numpy as jnp
import numpy as np
from jax import lax
from jax.experimental import pallas as pl
from jax.experimental.pallas import tpu as pltpu
from jax.sharding import PartitionSpec as P

HEADS = 8
HDIM = 128
BLK = 512


epsilon = 1e-06
depth_start = 0.5
depth_step = 1.0 / 24.0
highest = lax.Precision.HIGHEST


def rms_rows(values):
    return values * lax.rsqrt(jnp.mean(values * values, axis=1, keepdims=True) + epsilon)


def rms_back(values, gradient):
    scaling = lax.rsqrt(jnp.mean(values * values, axis=1, keepdims=True) + epsilon)
    normed = values * scaling
    return scaling * (gradient - normed * jnp.mean(gradient * normed, axis=1, keepdims=True))


def contract_last(left_part, right_part):
    return lax.dot_general(
        left_part, right_part, (((1,), (1,)), ((), ())), preferred_element_type=jnp.float32
    )


def contract_first(left_part, right_part):
    return lax.dot_general(
        left_part, right_part, (((0,), (0,)), ((), ())), preferred_element_type=jnp.float32
    )


def rotate(values, cosine, sine_table):
    return jnp.concatenate([values * cosine[:, None, :], values * sine_table[:, None, :]], axis=2)


def unrotate(gradient, cosine, sine_table):
    half_width = gradient.shape[2] // 2
    return (
        gradient[:, :, :half_width] * cosine[:, None, :]
        + gradient[:, :, half_width:] * sine_table[:, None, :]
    )


def split_blocks(array, block_count):
    return array.reshape((block_count, BLK) + array.shape[1:])


def block_weights(seg_block, next_seg, decay_log):
    block_width = seg_block.shape[0]
    places = jnp.arange(block_width, dtype=jnp.float32)
    distance = places[:, None] - places[None, :]
    allowed = (distance >= 0) & (seg_block[:, None] == seg_block[None, :])
    decay_grid = jnp.where(
        allowed[None], jnp.exp(decay_log[:, None, None] * jnp.maximum(distance, 0.0)[None]), 0.0
    )
    first_seg = seg_block[0]
    query_gain = jnp.where(
        (seg_block == first_seg)[:, None], jnp.exp(places[:, None] * decay_log[None, :]), 0.0
    )
    key_gain = jnp.where(
        (seg_block == next_seg)[:, None],
        jnp.exp((block_width - places)[:, None] * decay_log[None, :]),
        0.0,
    )
    carry_gain = jnp.where(first_seg == next_seg, jnp.exp(decay_log * block_width), 0.0)
    return (decay_grid, query_gain, key_gain, carry_gain)


def next_segments(segments, block_count):
    seg_blocks = segments.reshape(block_count, BLK)
    return (seg_blocks, jnp.concatenate([seg_blocks[1:, 0], jnp.full((1,), -1, jnp.int32)]))


def attend_forward(queries, keys_rot, values, segments, decay_log):
    length, heads_here, pair_width = queries.shape
    block_count = length // BLK
    seg_blocks, next_segs = next_segments(segments, block_count)

    def advance(state_now, block_items):
        query_block, key_block, value_block, seg_block, next_seg = block_items
        query_float = query_block.astype(jnp.float32)
        key_float = key_block.astype(jnp.float32)
        value_float = value_block.astype(jnp.float32)
        decay_grid, query_gain, key_gain, carry_gain = block_weights(seg_block, next_seg, decay_log)
        scores = (
            jnp.einsum("rhd,shd->hrs", query_block, key_block, preferred_element_type=jnp.float32)
            * decay_grid
        )
        block_out = jnp.einsum("hrs,she->rhe", scores, value_float, precision=highest)
        block_out = (
            block_out
            + jnp.einsum("rhd,hde->rhe", query_float, state_now, precision=highest)
            * query_gain[:, :, None]
        )
        new_state = carry_gain[:, None, None] * state_now + jnp.einsum(
            "shd,she->hde", key_float * key_gain[:, :, None], value_float, precision=highest
        )
        return (new_state, (block_out, state_now))

    zero_state = jnp.zeros((heads_here, pair_width, pair_width // 2), jnp.float32)
    _, (block_outs, states) = lax.scan(
        advance,
        zero_state,
        (
            split_blocks(queries, block_count),
            split_blocks(keys_rot, block_count),
            split_blocks(values, block_count),
            seg_blocks,
            next_segs,
        ),
    )
    return (block_outs.reshape(length, heads_here * (pair_width // 2)), states)


def attend_backward(queries, keys_rot, values, segments, decay_log, states, grad_heads):
    length, heads_here, pair_width = queries.shape
    block_count = length // BLK
    seg_blocks, next_segs = next_segments(segments, block_count)

    def retreat(later_grad, block_items):
        query_block, key_block, value_block, seg_block, next_seg, state_now, grad_block = (
            block_items
        )
        query_float = query_block.astype(jnp.float32)
        key_float = key_block.astype(jnp.float32)
        value_float = value_block.astype(jnp.float32)
        decay_grid, query_gain, key_gain, carry_gain = block_weights(seg_block, next_seg, decay_log)
        scores = (
            jnp.einsum("rhd,shd->hrs", query_block, key_block, preferred_element_type=jnp.float32)
            * decay_grid
        )
        pulled = jnp.einsum("rhe,she->hrs", grad_block, value_float, precision=highest) * decay_grid
        grad_query = jnp.einsum("hrs,shd->rhd", pulled, key_float, precision=highest)
        grad_query = (
            grad_query
            + jnp.einsum("rhe,hde->rhd", grad_block, state_now, precision=highest)
            * query_gain[:, :, None]
        )
        grad_key = jnp.einsum("hrs,rhd->shd", pulled, query_float, precision=highest)
        grad_key = (
            grad_key
            + jnp.einsum("she,hde->shd", value_float, later_grad, precision=highest)
            * key_gain[:, :, None]
        )
        grad_value = jnp.einsum("hrs,rhe->she", scores, grad_block, precision=highest)
        grad_value = (
            grad_value
            + jnp.einsum("shd,hde->she", key_float, later_grad, precision=highest)
            * key_gain[:, :, None]
        )
        earlier_grad = carry_gain[:, None, None] * later_grad + jnp.einsum(
            "rhd,rhe->hde", query_float * query_gain[:, :, None], grad_block, precision=highest
        )
        return (earlier_grad, (grad_query, grad_key, grad_value))

    zero_state = jnp.zeros((heads_here, pair_width, pair_width // 2), jnp.float32)
    _, (grad_query, grad_key, grad_value) = lax.scan(
        retreat,
        zero_state,
        (
            split_blocks(queries, block_count),
            split_blocks(keys_rot, block_count),
            split_blocks(values, block_count),
            seg_blocks,
            next_segs,
            states,
            split_blocks(grad_heads, block_count),
        ),
        reverse=True,
    )
    return (
        grad_query.reshape(length, heads_here, pair_width),
        grad_key.reshape(length, heads_here, pair_width),
        grad_value.reshape(length, heads_here, pair_width // 2),
    )


def per_device(
    tokens,
    upstream,
    segment_ids,
    query_proj,
    key_proj,
    value_proj,
    gate_proj,
    output_proj,
    left_proj,
    right_proj,
    down_proj,
):
    layers = query_proj.shape[0]
    row_count, model_width = tokens.shape
    length = segment_ids.shape[0]
    local_width = query_proj.shape[2]
    ff_local = left_proj.shape[2]
    heads_here = local_width // HDIM
    positions = jnp.arange(length, dtype=jnp.float32)
    frequency = jnp.exp(-math.log(10000.0) * jnp.arange(HDIM, dtype=jnp.float32) / HDIM)
    angles = positions[:, None] * frequency[None, :]
    cosine = jnp.cos(angles)
    sine_table = jnp.sin(angles)
    head_index = (lax.axis_index("tensor") * heads_here + jnp.arange(heads_here)).astype(
        jnp.float32
    )
    slopes = jnp.exp2(-8.0 * (head_index + 1.0) / HEADS)

    def gather_normed(normed):
        return lax.all_gather(normed, "tensor", axis=0, tiled=True)

    def gather_again(normed):
        return lax.all_gather(normed, "tensor", axis=0, tiled=True)

    def gather_grads(gradient):
        return lax.all_gather(gradient, "tensor", axis=0, tiled=True)

    def branch_sum(operand, matrix):
        return lax.psum_scatter(
            jnp.dot(operand, matrix, preferred_element_type=jnp.float32).astype(jnp.bfloat16),
            "tensor",
            scatter_dimension=0,
            tiled=True,
        ).astype(jnp.float32)

    def input_sum(pieces, matrix):
        operand = jnp.concatenate(pieces, axis=1)
        return lax.psum_scatter(
            contract_last(operand, matrix).astype(jnp.bfloat16),
            "tensor",
            scatter_dimension=0,
            tiled=True,
        ).astype(jnp.float32)

    current = tokens.astype(jnp.float32)
    saved_layers = []
    stat_terms = []
    for layer_index in range(layers):
        residual = current
        normed = rms_rows(residual).astype(jnp.bfloat16)
        full_normed = gather_normed(normed)
        attn_weight = jnp.concatenate(
            [
                query_proj[layer_index],
                key_proj[layer_index],
                value_proj[layer_index],
                gate_proj[layer_index],
            ],
            axis=1,
        )
        projected = jnp.dot(full_normed, attn_weight, preferred_element_type=jnp.float32)
        query_lin = projected[:, :local_width]
        key_lin = projected[:, local_width : 2 * local_width]
        values = (
            projected[:, 2 * local_width : 3 * local_width]
            .astype(jnp.bfloat16)
            .reshape(length, heads_here, HDIM)
        )
        gate_lin = projected[:, 3 * local_width :]
        queries = rotate(
            jax.nn.silu(query_lin).reshape(length, heads_here, HDIM), cosine, sine_table
        ).astype(jnp.bfloat16)
        keys_rot = rotate(
            jax.nn.silu(key_lin).reshape(length, heads_here, HDIM), cosine, sine_table
        ).astype(jnp.bfloat16)
        decay_log = -slopes * (1.0 - depth_start - depth_step * layer_index)
        heads_out, states = attend_forward(queries, keys_rot, values, segment_ids, decay_log)
        squares = lax.psum(jnp.sum(heads_out * heads_out, axis=1), "tensor")
        scaling = lax.rsqrt(squares / model_width + epsilon)[:, None]
        normed_heads = heads_out * scaling
        branch = (normed_heads * gate_lin).astype(jnp.bfloat16)
        attn_rows = branch_sum(branch, output_proj[layer_index])
        middle = residual + attn_rows
        normed_mid = rms_rows(middle).astype(jnp.bfloat16)
        full_mid = gather_normed(normed_mid)
        glu_weight = jnp.concatenate([left_proj[layer_index], right_proj[layer_index]], axis=1)
        gates_both = jnp.dot(full_mid, glu_weight, preferred_element_type=jnp.float32)
        left_lin = gates_both[:, :ff_local]
        right_lin = gates_both[:, ff_local:]
        hidden = (left_lin * right_lin).astype(jnp.bfloat16)
        glu_rows = branch_sum(hidden, down_proj[layer_index])
        current = middle + glu_rows
        stat_terms.append(
            jnp.stack(
                [
                    jnp.sum(attn_rows * attn_rows),
                    jnp.sum(glu_rows * glu_rows),
                    jnp.sum(current * current),
                ]
            )
        )
        saved_layers.append(
            (
                residual,
                middle,
                normed,
                normed_mid,
                full_normed,
                full_mid,
                attn_weight,
                glu_weight,
                query_lin,
                key_lin,
                gate_lin,
                queries,
                keys_rot,
                values,
                decay_log,
                states,
                normed_heads,
                scaling,
                branch,
                left_lin,
                right_lin,
                hidden,
            )
        )
    stat_sums = lax.psum(jnp.stack(stat_terms), ("dp", "tensor"))
    rms_stats = jnp.sqrt(stat_sums / (length * lax.axis_size("dp") * model_width))
    final_rows = current.astype(jnp.bfloat16)
    gradient = upstream.astype(jnp.float32)
    layer_results = [None] * layers
    for layer_index in reversed(range(layers)):
        (
            residual,
            middle,
            normed,
            normed_mid,
            full_normed,
            full_mid,
            attn_weight,
            glu_weight,
            query_lin,
            key_lin,
            gate_lin,
            queries,
            keys_rot,
            values,
            decay_log,
            states,
            normed_heads,
            scaling,
            branch,
            left_lin,
            right_lin,
            hidden,
        ) = saved_layers[layer_index]
        glu_grad = gather_grads(gradient.astype(jnp.bfloat16))
        grad_hidden = contract_last(glu_grad, down_proj[layer_index])
        down_part = contract_first(hidden, glu_grad)
        grad_left = (grad_hidden * right_lin).astype(jnp.bfloat16)
        grad_right = (grad_hidden * left_lin).astype(jnp.bfloat16)
        grad_gates = jnp.concatenate([grad_left, grad_right], axis=1)
        mid_rows = input_sum((grad_left, grad_right), glu_weight)
        source_mid = gather_again(normed_mid)
        glu_part = contract_first(source_mid, grad_gates)
        gradient = gradient + rms_back(middle, mid_rows)
        attn_grad = gather_grads(gradient.astype(jnp.bfloat16))
        output_part = contract_first(branch, attn_grad)
        grad_branch = contract_last(attn_grad, output_proj[layer_index])
        grad_normed = grad_branch * gate_lin
        grad_gate = (grad_branch * normed_heads).astype(jnp.bfloat16)
        inner_sum = lax.psum(jnp.sum(grad_normed * normed_heads, axis=1), "tensor")
        grad_heads = scaling * (grad_normed - normed_heads * (inner_sum / model_width)[:, None])
        grad_query, grad_key, grad_value = attend_backward(
            queries,
            keys_rot,
            values,
            segment_ids,
            decay_log,
            states,
            grad_heads.reshape(length, heads_here, HDIM),
        )
        sigmoid_query = jax.nn.sigmoid(query_lin)
        sigmoid_key = jax.nn.sigmoid(key_lin)
        query_back = unrotate(grad_query, cosine, sine_table).reshape(length, local_width)
        key_back = unrotate(grad_key, cosine, sine_table).reshape(length, local_width)
        grad_query_lin = (
            query_back * (sigmoid_query + query_lin * sigmoid_query * (1.0 - sigmoid_query))
        ).astype(jnp.bfloat16)
        grad_key_lin = (
            key_back * (sigmoid_key + key_lin * sigmoid_key * (1.0 - sigmoid_key))
        ).astype(jnp.bfloat16)
        grad_value_lin = grad_value.reshape(length, local_width).astype(jnp.bfloat16)
        grad_projected = jnp.concatenate(
            [grad_query_lin, grad_key_lin, grad_value_lin, grad_gate], axis=1
        )
        in_rows = input_sum((grad_query_lin, grad_key_lin, grad_value_lin, grad_gate), attn_weight)
        source_normed = gather_again(normed)
        attn_part = contract_first(source_normed, grad_projected)
        gradient = gradient + rms_back(residual, in_rows)
        query_part = attn_part[:, :local_width]
        key_part = attn_part[:, local_width : 2 * local_width]
        value_part = attn_part[:, 2 * local_width : 3 * local_width]
        gate_part = attn_part[:, 3 * local_width :]
        left_part = glu_part[:, :ff_local]
        right_part = glu_part[:, ff_local:]
        layer_results[layer_index] = (
            query_part,
            key_part,
            value_part,
            gate_part,
            output_part,
            left_part,
            right_part,
            down_part,
        )
    stacked = [
        jnp.stack([layer_results[index][member] for index in range(layers)]) for member in range(8)
    ]
    totals = (
        lax.psum(stacked[0].astype(jnp.bfloat16), "dp").astype(jnp.float32),
        lax.psum(stacked[1].astype(jnp.bfloat16), "dp").astype(jnp.float32),
        lax.psum(stacked[2].astype(jnp.bfloat16), "dp").astype(jnp.float32),
        lax.psum(stacked[3].astype(jnp.bfloat16), "dp").astype(jnp.float32),
        lax.psum(stacked[4].astype(jnp.bfloat16), "dp").astype(jnp.float32),
        lax.psum(stacked[5].astype(jnp.bfloat16), "dp").astype(jnp.float32),
        lax.psum(stacked[6].astype(jnp.bfloat16), "dp").astype(jnp.float32),
        lax.psum(stacked[7].astype(jnp.bfloat16), "dp").astype(jnp.float32),
    )
    input_grad = gradient.astype(jnp.bfloat16)
    return (
        final_rows,
        input_grad,
        totals[0],
        totals[1],
        totals[2],
        totals[3],
        totals[4],
        totals[5],
        totals[6],
        totals[7],
        rms_stats,
    )


SQUARE_MESH = {"dp": 8, "tensor": 4}


F32 = jnp.float32
BF16 = jnp.bfloat16
MESH = pl.DeviceIdType.MESH
VMEM_LIMIT = 62 * 2**20
SUPER = 2
EARLY = (0,)
CHUNK = 128
HOP = 3
SLOTS = 16


def nn(a, b):
    return lax.dot_general(a, b, (((1,), (0,)), ((), ())), preferred_element_type=F32)


def nt(a, b):
    return lax.dot_general(a, b, (((1,), (1,)), ((), ())), preferred_element_type=F32)


def tn(a, b):
    return lax.dot_general(a, b, (((0,), (0,)), ((), ())), preferred_element_type=F32)


def exact(a, b, dims):
    return lax.dot_general(a, b, (dims, ((), ())), precision=highest, preferred_element_type=F32)


def aligned(index, size):
    return pl.ds(pl.multiple_of(index, size), size)


class Place:
    def __init__(self, pairs):
        self.dp = lax.axis_index("dp")
        self.me = lax.axis_index("tensor")
        self.low = lax.rem(self.me, 2)
        self.high = self.me // 2
        self.core = lax.rem(self.dp, 2)
        self.at = self.dp // 2
        self.last = pairs - 1

    def member(self, step):
        low = lax.rem(self.low + lax.rem(step, 2), 2)
        high = lax.rem(self.high + step // 2, 2)
        return 2 * high + low

    def device(self, step):
        return (self.dp, self.member(step))

    def partner(self):
        return (self.dp + 1 - 2 * self.core, self.me)

    def right(self):
        return (self.dp + 2, self.me)

    def left(self):
        return (self.dp - 2, self.me)

    def greet(self, line):
        barrier = pltpu.get_barrier_semaphore()

        def signal(device):
            pl.semaphore_signal(barrier, inc=1, device_id=device, device_id_type=MESH)

        for step in (1, 2, 3):
            signal(self.device(step))
        if not line:
            pl.semaphore_wait(barrier, 3)
            return
        signal(self.partner())

        @pl.when(self.at < self.last)
        def _():
            signal(self.right())

        @pl.when(self.at > 0)
        def _():
            signal(self.left())

        pl.semaphore_wait(barrier, 4 + jnp.minimum(self.at, 1) + jnp.minimum(self.last - self.at, 1))


class Wire:
    def __init__(self, device, send_sem, recv_sem, source, target, landing):
        self.source, self.target, self.landing = source, target, landing
        self.common = dict(send_sem=send_sem, recv_sem=recv_sem, device_id=device, device_id_type=MESH)

    def out(self):
        return pltpu.make_async_remote_copy(src_ref=self.source, dst_ref=self.target, **self.common)

    def start(self):
        self.out().start()

    def wait_recv(self):
        pltpu.make_async_remote_copy(src_ref=self.landing, dst_ref=self.landing, **self.common).wait_recv()

    def wait_send(self):
        self.out().wait_send()


class Gather:
    def __init__(self, place, buf, send, recv, block):
        self.place, self.buf, self.block = place, buf, block
        self.send, self.recv = send, recv
        self.half = block // (2 * SUPER)

    def rows(self, step, part, half):
        start = self.place.member(step) * self.block + (2 * part + half) * self.half
        return self.buf.at[aligned(start, self.half)]

    def wire(self, part, number):
        step, owner, half = ((1, 0, 0), (2, 0, 1), (1, 0, 1), (2, 0, 0), (2, 1, 0), (1, 2, 1))[number]
        source = self.rows(owner, part, half)
        landing = self.rows((0, 1, 2, 3)[owner ^ step], part, half)
        return Wire(self.place.device(step), self.send.at[part, number], self.recv.at[part, number], source, source, landing)

    def start(self, part):
        for number in range(4):
            self.wire(part, number).start()

    def forward(self, part):
        self.wire(part, 0).wait_recv()
        self.wire(part, 4).start()
        self.wire(part, 1).wait_recv()
        self.wire(part, 5).start()

    def finish(self, part, step):
        for number in {0: (), 1: (2,), 2: (3,), 3: (4, 5)}[step]:
            self.wire(part, number).wait_recv()

    def drain(self, parts=range(SUPER)):
        for part in parts:
            for number in range(6):
                self.wire(part, number).wait_send()


def gather_stage(gather, block_fn, beside):
    @pl.loop(0, 4 * SUPER)
    def _(i):
        mixed = i - SUPER
        part = jnp.where(i < SUPER, i, jnp.where(i < 3 * SUPER, mixed // 2, i - 3 * SUPER))
        step = jnp.where(i < SUPER, 0, jnp.where(i < 3 * SUPER, 1 + lax.rem(mixed, 2), 3))

        @pl.when(i == SUPER)
        def _():
            for one in range(SUPER):
                beside(one)
                gather.forward(one)

        @pl.when(i == 3 * SUPER)
        def _():
            beside(SUPER)

        for which in (1, 2, 3):
            @pl.when(step == which)
            def _():
                gather.finish(part, which)
        block_fn(part, step)


class Scatter:
    def __init__(self, place, buf, land, send, recv, block):
        self.place, self.buf, self.land, self.block = place, buf, land, block
        self.send, self.recv = send, recv
        self.half = block // (2 * SUPER)

    def rows(self, step, part, half):
        start = self.place.member(step) * self.block + (2 * part + half) * self.half
        return aligned(start, self.half)

    def wire(self, part, number):
        step, owner, half = ((1, 3, 0), (1, 1, 0), (2, 3, 1), (2, 2, 1), (2, 2, 0), (1, 1, 1))[number]
        target = self.land.at[part, number]
        return Wire(
            self.place.device(step), self.send.at[part, number], self.recv.at[part, number],
            self.buf.at[self.rows(owner, part, half)], target, target,
        )

    def send_block(self, part, step):
        for number in {0: (), 1: (1,), 2: (3,), 3: (0, 2)}[step]:
            self.wire(part, number).start()

    def middle(self, part):
        for first, second, owner, half in ((0, 4, 2, 0), (2, 5, 1, 1)):
            self.wire(part, first).wait_recv()
            rows = self.rows(owner, part, half)
            self.buf[rows, :] = self.buf[rows, :] + self.land[part, first]
            self.wire(part, second).start()

    def finish(self, part, half):
        first, second = ((1, 4), (3, 5))[half]
        self.wire(part, first).wait_recv()
        self.wire(part, second).wait_recv()

    def total(self, part, half, start, count):
        first, second = ((1, 4), (3, 5))[half]
        own = self.place.me * self.block + (2 * part + half) * self.half + start
        rows = pl.ds(start, count)
        return (
            self.buf[aligned(own, count), :].astype(F32)
            + self.land[part, first, rows, :].astype(F32)
            + self.land[part, second, rows, :].astype(F32)
        )

    def drain(self):
        for part in range(SUPER):
            for number in range(6):
                self.wire(part, number).wait_send()


class Share:
    def __init__(self, place, mine, land, send, recv):
        self.wires = [
            Wire(place.device(step), send.at[step - 1], recv.at[step - 1], mine, land.at[step - 1], land.at[step - 1])
            for step in (1, 2, 3)
        ]
        self.mine, self.land = mine, land

    def start(self):
        for wire in self.wires:
            wire.start()

    def total(self):
        for wire in self.wires:
            wire.wait_recv()
        return self.mine[...] + self.land[0] + self.land[1] + self.land[2]

    def drain(self):
        for wire in self.wires:
            wire.wait_send()


class Local:
    def __init__(self, sems):
        self.sems, self.used = sems, 0

    def start(self, source, target):
        copy = pltpu.make_async_copy(source, target, self.sems.at[self.used])
        self.used += 1
        copy.start()
        return copy


def row_sums(values, target, chunk):
    sums = exact(jnp.ones((8, values.shape[1]), F32), values, ((1,), (1,)))
    target[pl.ds(chunk, 1), :] = sums[0:1, :]


def spread(sums, chunk):
    picked = (lax.broadcasted_iota(jnp.int32, (8, 128), 0) == chunk).astype(F32)
    return exact(sums, picked, ((0,), (0,)))


def widen(columns, times):
    return jnp.concatenate([columns] * times, axis=1)


def decay_tiles(dec_ref, first_head, tiles, heads_here, size):
    rows = lax.broadcasted_iota(jnp.int32, (size, size), 0)
    cols = lax.broadcasted_iota(jnp.int32, (size, size), 1)
    distance = (rows - cols).astype(F32)
    for head in range(heads_here):
        decay = dec_ref[pl.ds(first_head + head, 1), 0:1]
        tiles[head, 0] = jnp.where(rows >= cols, jnp.exp(decay * jnp.maximum(distance, 0.0)), 0.0)
        tiles[head, 1] = jnp.exp(decay * (distance + float(size)))


def spread_segments(r, length):
    r.segf[...] = r.seg[...].astype(F32)
    for chunk in range(length // 128):
        r.segc[chunk * 128 : (chunk + 1) * 128, :] = spread(r.segf[...], chunk)


def tile_weight(r, first_head, head, row_tile, col_tile, size):
    gap = row_tile - col_tile
    if gap == 0:
        weight = r.tiles[head, 0]
    else:
        weight = r.tiles[head, 1]
        if gap > 1:
            decay = r.dec[pl.ds(first_head + head, 1), 0:1]
            weight = weight * jnp.exp(decay * float(size * (gap - 1)))
    row_seg = widen(r.segc[row_tile * size : (row_tile + 1) * size, :], size // 128)
    per = size // 128
    col_seg = jnp.concatenate([r.segf[per * col_tile + i : per * col_tile + i + 1, :] for i in range(per)], axis=1)
    return jnp.where(row_seg == col_seg, weight, 0.0)


def namespace(names, refs):
    return types.SimpleNamespace(**dict(zip(names, refs)))


def forward_front(cfg, r, place, copies, layer, x, save, third, third_parts, back_block):
    block, length, width = cfg.block, cfg.length, cfg.width
    heads_here, size = cfg.heads_here, cfg.block
    first_head = layer * HEADS + place.me * heads_here
    w_in = [copies.start(h.at[layer], v) for h, v in (
        (r.wq_h, r.wq), (r.wk_h, r.wk), (r.wv_h, r.wv), (r.wg_h, r.wg))]
    w_out = copies.start(r.wo_h.at[layer], r.wo)
    w_glu = [copies.start(h.at[layer], v) for h, v in ((r.wl_h, r.wl), (r.wr_h, r.wr), (r.wd_h, r.wd))]
    first = Gather(place, r.n1, r.fag1_send, r.fag1_recv, block)
    mid_sum = Scatter(place, r.part1, r.land1, r.frs1_send, r.frs1_recv, block)
    second = Gather(place, r.n2, r.fag2_send, r.fag2_recv, block)
    out_sum = Scatter(place, r.part2, r.land2, r.frs2_send, r.frs2_recv, block)
    share = Share(place, r.ss_mine, r.ss_land, r.ss_send, r.ss_recv)
    half, step_rows = first.half, 32
    own_start = place.me * block

    @pl.loop(0, block // step_rows)
    def _(i):
        rows = aligned(i * step_rows, step_rows)
        v = x[rows, :].astype(F32)
        scale = lax.rsqrt(jnp.mean(v * v, axis=1, keepdims=True) + epsilon)
        r.n1[aligned(own_start + i * step_rows, step_rows), :] = (v * scale).astype(BF16)

    place.greet(back_block is not None)
    for part in range(SUPER):
        first.start(part)
    decay_tiles(r.dec, first_head, r.tiles, heads_here, size)
    spread_segments(r, length)
    for copy in w_in:
        copy.wait()

    @pl.loop(0, 4)
    def _(step):
        @pl.when(step == 1)
        def _():
            for part in range(SUPER):
                first.forward(part)
        for which in (1, 2, 3):
            @pl.when(step == which)
            def _():
                for part in range(SUPER):
                    first.finish(part, which)
        rows = aligned(place.member(step) * block, block)
        a = r.n1[rows, :]
        cosine, sine = r.cos[rows, :], r.sin[rows, :]
        for w, lin, rot in ((r.wq, r.ql, r.q), (r.wk, r.kl, r.k)):
            v = nn(a, w[...])
            lin[rows, :] = v.astype(BF16)
            v = v / (1.0 + jnp.exp(-v))
            for head in range(heads_here):
                one = v[:, head * HDIM : (head + 1) * HDIM]
                rot[rows, 2 * head * HDIM : (2 * head + 1) * HDIM] = (one * cosine).astype(BF16)
                rot[rows, (2 * head + 1) * HDIM : (2 * head + 2) * HDIM] = (one * sine).astype(BF16)
        r.v[rows, :] = nn(a, r.wv[...]).astype(BF16)
        r.gate[rows, :] = nn(a, r.wg[...])

    save("n1", "ql", "kl", "q", "k", "v", "gate")
    if third is not None:
        for part in third_parts:
            third.start(part)
    tiles_here = length // size

    @pl.loop(0, heads_here)
    def _(head):
        wide = aligned(head * 2 * HDIM, 2 * HDIM)
        thin = aligned(head * HDIM, HDIM)
        for row_tile in range(tiles_here):
            rows = slice(row_tile * size, (row_tile + 1) * size)
            queries = r.q[rows, wide]
            acc = None
            for col_tile in range(row_tile + 1):
                cols = slice(col_tile * size, (col_tile + 1) * size)
                weight = tile_weight(r, first_head, head, row_tile, col_tile, size)
                scores = (nt(queries, r.k[cols, wide]) * weight).astype(BF16)
                term = nn(scores, r.v[cols, thin])
                acc = term if acc is None else acc + term
            r.heads[rows, thin] = acc
            r.dh[rows, thin] = (acc * r.gate[rows, thin]).astype(BF16)

    for chunk in range(length // 128):
        v = r.heads[chunk * 128 : (chunk + 1) * 128, :]
        row_sums(v * v, r.ss_mine, chunk)
    share.start()
    save("heads")
    if third is not None:
        for part in third_parts:
            third.forward(part)
    w_out.wait()

    part_rows = 2 * half
    for part in range(SUPER):
        for step in (3, 1, 2, 0):
            rows = aligned(place.member(step) * block + part * part_rows, part_rows)
            r.part1[rows, :] = nn(r.dh[rows, :], r.wo[...]).astype(BF16)
            mid_sum.send_block(part, step)
    for part in range(SUPER):
        mid_sum.middle(part)
    r.ss[...] = share.total()
    save("ss")
    scaling = lax.rsqrt(r.ss[...] / width + epsilon)
    per_block = block // 128
    for chunk in range(per_block):
        r.scale[aligned(own_start + chunk * 128, 128), :] = spread(scaling, place.me * per_block + chunk)
    r.stat_wide[...] = jnp.zeros_like(r.stat_wide)

    def add_stat(row, v):
        sums = jnp.sum(v * v, axis=0, keepdims=True)
        r.stat_wide[row : row + 1, :] += sums

    step_rows = min(32, half)
    for part in range(SUPER):
        for h in range(2):
            mid_sum.finish(part, h)
            for i in range(half // step_rows):
                offset = (2 * part + h) * half + i * step_rows
                scale = widen(r.scale[aligned(own_start + offset, step_rows), :], width // 128)
                attn = mid_sum.total(part, h, i * step_rows, step_rows) * scale
                middle = x[offset : offset + step_rows, :].astype(F32) + attn
                r.mid[offset : offset + step_rows, :] = middle
                add_stat(0, attn)
                norm = lax.rsqrt(jnp.mean(middle * middle, axis=1, keepdims=True) + epsilon)
                r.n2[aligned(own_start + offset, step_rows), :] = (middle * norm).astype(BF16)
        second.start(part)
    save("mid")
    for copy in w_glu:
        copy.wait()
    if third is not None:
        for part in third_parts:
            for which in (1, 2, 3):
                third.finish(part, which)
    if back_block is not None:
        mid_sum.drain()

    def glu(part, step):
        rows = aligned(place.member(step) * block + part * part_rows, part_rows)
        a = r.n2[rows, :]
        left = nt(a, r.wl[...])
        right = nt(a, r.wr[...])
        hidden = (left * right).astype(BF16)
        r.hid[rows, :] = hidden
        if back_block is not None:
            back_block(rows, left, right, part, step)
        else:
            r.left[rows, :] = left.astype(BF16)
            r.right[rows, :] = right.astype(BF16)
        r.part2[rows, :] = nn(hidden, r.wd[...]).astype(BF16)
        if back_block is None:
            for which in (1, 2, 3):
                @pl.when(step == which)
                def _():
                    out_sum.send_block(part, which)

    gather_stage(second, glu, lambda i: None)

    def finish():
        for part in range(SUPER):
            for h in range(2):
                out_sum.finish(part, h)
                for i in range(half // step_rows):
                    offset = (2 * part + h) * half + i * step_rows
                    glu_rows = out_sum.total(part, h, i * step_rows, step_rows)
                    after = r.mid[offset : offset + step_rows, :] + glu_rows
                    r.xo[offset : offset + step_rows, :] = after.astype(r.xo.dtype)
                    add_stat(1, glu_rows)
                    add_stat(2, after)
        folded = r.stat_wide[:, :128]
        for n in range(1, width // 128):
            folded = folded + r.stat_wide[:, n * 128 : (n + 1) * 128]
        return folded

    groups = [first, second, share] + ([mid_sum] if back_block is None else [])
    return out_sum, finish, groups


def early_rows(cfg):
    part_rows = cfg.block // SUPER
    return [pl.ds(start + part * part_rows, part_rows) for start in range(0, cfg.length, cfg.block) for part in EARLY]


def fwd_kernel(cfg, names, *refs):
    r = namespace(names, refs)
    place = Place(cfg.pairs)
    copies = Local(r.local_sem)
    saves = []

    def save(*keys):
        for key in keys:
            saves.append(copies.start(getattr(r, key), getattr(r, key + "_h")))

    third = None
    if cfg.gathers:
        third = Gather(place, r.gd, r.ag3_send, r.ag3_recv, cfg.block)
        part_rows = cfg.block // SUPER
        for part in EARLY:
            r.gd[aligned(place.me * cfg.block + part * part_rows, part_rows), :] = r.up[part * part_rows : (part + 1) * part_rows, :]
    out_sum, finish, groups = forward_front(cfg, r, place, copies, cfg.layer, r.x, save, third, EARLY, None)
    save("n2", "left", "right", "hid")
    if cfg.gathers:
        for rows in early_rows(cfg):
            saves.append(copies.start(r.gd.at[rows, :], r.gd_h.at[rows, :]))
    for part in range(SUPER):
        out_sum.middle(part)
    r.stat[...] = finish()
    for copy in saves:
        copy.wait()
    for group in (*groups, out_sum):
        group.drain()
    if cfg.gathers:
        third.drain(EARLY)


def turns_of(k, size, count):
    return sum(((k >= size * n).astype(jnp.int32) for n in range(1, -(-count // size))), jnp.int32(0))


class Line:
    def __init__(self, cfg, place, r):
        self.place, self.r = place, r
        self.per, self.count = cfg.chunks, cfg.chunks * cfg.layers
        self.layers, self.rows_each = cfg.layers, cfg.chunks * CHUNK
        self.half = CHUNK // 2
        self.ticks = self.count + 3 + HOP * place.last
        self.done = 0

    def slot(self, k):
        return k - SLOTS * turns_of(k, SLOTS, self.count)

    def rows(self, k, core):
        place = k - self.per * turns_of(k, self.per, self.count)
        return aligned(place * CHUNK + core * self.half, self.half)

    def own(self, k):
        return self.rows(k, self.place.core)

    def out_rows(self, k, core):
        turn = turns_of(k, self.per, self.count)
        place = (self.layers - 1 - turn) * self.per + k - turn * self.per
        start = place * CHUNK + core * self.half
        return aligned(start, self.half)

    def pair(self, k):
        slot = self.slot(k)
        r = self.r
        return Wire(self.place.partner(), r.pair_send.at[slot], r.pair_recv.at[slot],
                    r.grads.at[self.rows(k, 1 - self.place.core)], r.pair_land.at[slot], r.pair_land.at[slot])

    def hop(self, k, land, send, recv, device):
        slot = self.slot(k)
        return Wire(device, send.at[slot], recv.at[slot], land.at[slot], land.at[slot], land.at[slot])

    def going_right(self, k):
        return self.hop(k, self.r.right_land, self.r.right_send, self.r.right_recv, self.place.right())

    def going_left(self, k):
        return self.hop(k, self.r.left_land, self.r.left_send, self.r.left_recv, self.place.left())

    def coming_right(self, k):
        return self.hop(k, self.r.right_land, self.r.right_send, self.r.right_recv, self.place.left())

    def coming_left(self, k):
        return self.hop(k, self.r.left_land, self.r.left_send, self.r.left_recv, self.place.right())

    def result(self, k):
        slot, r = self.slot(k), self.r
        return Wire(self.place.partner(), r.give_send.at[slot], r.give_recv.at[slot],
                    r.grads.at[self.own(k)], r.out_h.at[self.out_rows(k, self.place.core)],
                    r.out_h.at[self.out_rows(k, 1 - self.place.core)])

    def keep(self, k):
        slot, r = self.slot(k), self.r
        return pltpu.make_async_copy(
            r.grads.at[self.own(k)], r.out_h.at[self.out_rows(k, self.place.core)], r.keep_sem.at[slot]
        )

    def one_way(self, k, land, start_here, coming, ends_here, going):
        slot = self.slot(k)

        @pl.when(start_here)
        def _():
            land[slot] = self.r.grads[self.own(k), :]

        @pl.when(jnp.logical_not(start_here))
        def _():
            coming(k).wait_recv()
            land[slot] = land[slot] + self.r.grads[self.own(k), :]

        @pl.when(jnp.logical_not(ends_here))
        def _():
            going(k).start()

    def tick(self, n):
        place, r, last = self.place, self.r, self.place.last
        at_left, at_right = place.at == 0, place.at == last

        @pl.when(n < self.count)
        def _():
            self.pair(n).start()

        k = n - 1

        @pl.when(jnp.logical_and(k >= 0, k < self.count))
        def _():
            wire = self.pair(k)
            wire.wait_recv()
            wire.wait_send()
            slot = self.slot(k)
            r.grads[self.own(k), :] = r.grads[self.own(k), :] + r.pair_land[slot]

        left_k = n - 1 - HOP * (last - place.at)

        @pl.when(jnp.logical_and(left_k >= 0, left_k < self.count))
        def _():
            self.one_way(left_k, r.left_land, at_right, self.coming_left, at_left, self.going_left)

        right_k = n - 1 - HOP * place.at

        @pl.when(jnp.logical_and(right_k >= 0, right_k < self.count))
        def _():
            self.one_way(right_k, r.right_land, at_left, self.coming_right, at_right, self.going_right)

        full_k = n - 1 - HOP * last

        @pl.when(jnp.logical_and(full_k >= 0, full_k < self.count))
        def _():
            @pl.when(jnp.logical_not(at_right))
            def _():
                self.going_right(full_k).wait_send()

            @pl.when(jnp.logical_not(at_left))
            def _():
                self.going_left(full_k).wait_send()

            slot = self.slot(full_k)
            own = self.own(full_k)
            total = r.right_land[slot].astype(F32) + r.left_land[slot].astype(F32) - r.grads[own, :].astype(F32)
            r.grads[own, :] = total.astype(BF16)
            self.result(full_k).start()
            self.keep(full_k).start()

        old_k = full_k - 2

        @pl.when(jnp.logical_and(old_k >= 0, old_k < self.count))
        def _():
            wire = self.result(old_k)
            wire.wait_recv()
            wire.wait_send()
            self.keep(old_k).wait()

    def pump(self, ready, most):
        stop = min(self.done + most, ready)
        if stop > self.done:
            start, self.done = self.done, stop

            @pl.loop(start, stop)
            def _(n):
                self.tick(n)

    def release(self, turn, rows):
        needed = (turn - 1) * self.per + -(-rows // CHUNK) + 3 + HOP * self.place.last
        if turn > 0 and needed > self.done:
            self.pump(turn * self.per, needed - self.done)
            assert self.done >= needed

    def more(self, most):
        self.pump(self.ticks, most)


class StatLine:
    def __init__(self, place, r):
        self.place, self.r = place, r
        self.share = Share(place, r.stat_mine, r.stat_land, r.st_send, r.st_recv)

    def square(self):
        self.share.start()

    def pair(self):
        r = self.r
        r.stat_square[...] = self.share.total()
        self.wire(0, self.place.partner(), r.stat_square).start()

    def wire(self, number, device, source):
        r = self.r
        return Wire(device, r.line_send.at[number], r.line_recv.at[number], source, r.line_land.at[number], r.line_land.at[number])

    def stage(self, number):
        place, r = self.place, self.r
        if number == 0:
            self.wire(0, place.partner(), r.stat_square).wait_recv()
            r.stat_pair[...] = r.stat_square[...] + r.line_land[0]
            r.stat_right[...] = r.stat_pair[...]
            r.stat_left[...] = r.stat_pair[...]
        else:
            @pl.when(place.at == number)
            def _():
                self.wire(1, place.left(), r.stat_right).wait_recv()
                r.stat_right[...] = r.stat_pair[...] + r.line_land[1]

            @pl.when(place.last - place.at == number)
            def _():
                self.wire(2, place.right(), r.stat_left).wait_recv()
                r.stat_left[...] = r.stat_pair[...] + r.line_land[2]
        if number < place.last:
            @pl.when(place.at == number)
            def _():
                self.wire(1, place.right(), r.stat_right).start()

            @pl.when(place.last - place.at == number)
            def _():
                self.wire(2, place.left(), r.stat_left).start()

    def finish(self):
        place, r = self.place, self.r
        r.stat_total[...] = r.stat_right[...] + r.stat_left[...] - r.stat_pair[...]
        self.share.drain()
        self.wire(0, place.partner(), r.stat_square).wait_send()

        @pl.when(place.at < place.last)
        def _():
            self.wire(1, place.right(), r.stat_right).wait_send()

        @pl.when(place.at > 0)
        def _():
            self.wire(2, place.left(), r.stat_left).wait_send()


def bwd_kernel(cfg, names, *refs):
    r = namespace(names, refs)
    block, length, width, local, ff = cfg.block, cfg.length, cfg.width, cfg.local, cfg.ff
    heads_here, size, layers = cfg.heads_here, cfg.block, cfg.layers
    place = Place(cfg.pairs)
    copies = Local(r.local_sem)
    line = Line(cfg, place, r)
    stats = StatLine(place, r)
    loads = {}
    base_down, base_left, base_right, base_out, base_gate, gate_end, base_qkv, _ = cfg.bases
    half = block // (2 * SUPER)
    part_rows = 2 * half
    own_start = place.me * block
    step_rows = min(32, half)
    per_block = block // 128
    tiles_here = length // size

    def load(layer, *keys):
        for key in keys:
            if key in SAVED:
                source = getattr(r, key + str(layer) + "_h")
            else:
                source = getattr(r, key + "_h").at[layer]
            loads[key] = copies.start(source, getattr(r, key))

    def await_loads(*keys):
        for key in keys:
            loads[key].wait()

    glu_in = ("wd", "left", "right", "wl", "wr")
    glu_grad = ("hid", "n2")
    out_in = ("ss", "wo", "gate", "heads")
    attn_in = ("q", "k", "v", "ql", "kl")
    in_in = ("wq", "wk", "wv", "wg")

    def gather_one(layer):
        return Gather(place, r.gd, r.ag1_send.at[layer], r.ag1_recv.at[layer], block)

    firsts = [gather_one(layer) for layer in range(layers)]

    @pl.loop(0, block // 32)
    def _(i):
        rows = aligned(i * 32, 32)
        r.g[rows, :] = r.up[rows, :].astype(F32)


    for part in range(SUPER):
        if part not in EARLY:
            r.gd[aligned(own_start + part * part_rows, part_rows), :] = r.up[part * part_rows : (part + 1) * part_rows, :]
    early = [copies.start(r.gd_h.at[rows, :], r.gd.at[rows, :]) for rows in early_rows(cfg)]
    for start, stop in ((gate_end, base_qkv), (base_qkv + 3 * local, cfg.chunks * CHUNK)):
        if stop > start:
            r.grads[start:stop, :] = jnp.zeros((stop - start, width), BF16)
    top = layers - 1
    third = Gather(place, r.gd, r.ag3_send, r.ag3_recv, block)
    top_sum = Scatter(place, r.part1, r.land1, r.rs1_send.at[top], r.rs1_recv.at[top], block)

    def back_block(rows, left, right, part, step):
        grad_hidden = nt(r.gd[rows, :], r.wd[...])
        grad_left = (grad_hidden * right).astype(BF16)
        grad_right = (grad_hidden * left).astype(BF16)
        r.right[rows, :] = grad_left
        r.left[rows, :] = grad_right
        r.part1[rows, :] = (nn(grad_left, r.wl[...]) + nn(grad_right, r.wr[...])).astype(BF16)
        for which in (1, 2, 3):
            @pl.when(step == which)
            def _():
                top_sum.send_block(part, which)

    def no_save(*keys):
        if "mid" in keys:
            for copy in early:
                copy.wait()

    late = [part for part in range(SUPER) if part not in EARLY]
    out_sum, finish_forward, groups = forward_front(
        cfg, r, place, copies, top, getattr(r, "x%d" % top), no_save, third, late, back_block
    )
    for group in groups:
        group.drain()
    third.drain(late)

    def back_rows(total, values, grad):
        norm = lax.rsqrt(jnp.mean(values * values, axis=1, keepdims=True) + epsilon)
        m = values * norm
        inner = jnp.mean(total * m, axis=1, keepdims=True)
        return grad + norm * (total - m * inner)

    for turn, layer in enumerate(reversed(range(layers))):
        first = firsts[layer]
        mid_sum = top_sum if turn == 0 else Scatter(place, r.part1, r.land1, r.rs1_send.at[layer], r.rs1_recv.at[layer], block)
        second = Gather(place, r.ga, r.ag2_send.at[layer], r.ag2_recv.at[layer], block)
        in_sum = Scatter(place, r.part1, r.land1, r.rs2_send.at[layer], r.rs2_recv.at[layer], block)
        share = Share(place, r.inner, r.inner_land.at[layer], r.in_send.at[layer], r.in_recv.at[layer])
        first_head = layer * HEADS + place.me * heads_here

        def ready(rows):
            return turn * cfg.chunks + rows // CHUNK

        if turn > 0:
            decay_tiles(r.dec, first_head, r.tiles, heads_here, size)
            await_loads(*glu_in)
            await_loads(*out_in)
        scaling = lax.rsqrt(r.ss[...] / width + epsilon)
        for chunk in range(length // 128):
            r.scale[chunk * 128 : (chunk + 1) * 128, :] = spread(scaling, chunk)
        def glu_back(part, step):
            rows = aligned(place.member(step) * block + part * part_rows, part_rows)
            grad_hidden = nt(r.gd[rows, :], r.wd[...])
            grad_left = (grad_hidden * r.right[rows, :].astype(F32)).astype(BF16)
            grad_right = (grad_hidden * r.left[rows, :].astype(F32)).astype(BF16)
            r.right[rows, :] = grad_left
            r.left[rows, :] = grad_right
            r.part1[rows, :] = (nn(grad_left, r.wl[...]) + nn(grad_right, r.wr[...])).astype(BF16)
            for which in (1, 2, 3):
                @pl.when(step == which)
                def _():
                    mid_sum.send_block(part, which)

        if turn > 0:
            gather_stage(first, glu_back, lambda i: line.pump(ready(0), 2))
            first.drain()
        grad_left_ref, grad_right_ref = r.right, r.left

        def glu_grad_rows(base, a_ref, b_ref):
            line.release(turn, base + ff)
            for n in range(width // 256):
                cols = slice(n * 256, (n + 1) * 256)
                r.grads[base : base + ff, cols] = tn(a_ref[...], b_ref[:, cols]).astype(BF16)

        if turn > 0:
            await_loads(*glu_grad)
            for copy in mid_pieces:
                copy.wait()
        glu_grad_rows(base_down, r.hid, r.gd)
        line.pump(ready(base_left), 1 + turn)
        mid_sum.middle(0)
        glu_grad_rows(base_left, grad_left_ref, r.n2)
        line.pump(ready(base_right), 1 + turn)
        for part in range(1, SUPER):
            mid_sum.middle(part)
        glu_grad_rows(base_right, grad_right_ref, r.n2)
        for part in range(SUPER):
            line.pump(ready(base_out), 2 if part == 0 else 1)
            for h in range(2):
                mid_sum.finish(part, h)
                for i in range(half // step_rows):
                    offset = (2 * part + h) * half + i * step_rows
                    rows = slice(offset, offset + step_rows)
                    total = mid_sum.total(part, h, i * step_rows, step_rows)
                    if turn == 0:
                        values = r.mid[rows, :]
                    else:
                        pieces = range(width // (2 * HDIM))
                        values = jnp.concatenate([r.dq[n * block + offset : n * block + offset + step_rows, :] for n in pieces], axis=1)
                    new = back_rows(total, values, r.g[rows, :])
                    r.gm[rows, :] = new
                    r.ga[aligned(own_start + offset, step_rows), :] = new.astype(BF16)
            second.start(part)
        mid_sum.drain()
        if turn + 1 < layers:
            load(layer - 1, *glu_in, *glu_grad)

        def out_back(part, step):
            member = place.member(step)
            for chunk in range(part_rows // 128):
                number = part * (part_rows // 128) + chunk
                rows = aligned(member * block + number * 128, 128)
                grad_branch = nt(r.ga[rows, :], r.wo[...])
                gate = r.gate[rows, :]
                normed = r.heads[rows, :] * widen(r.scale[rows, :], local // 128)
                grad_normed = grad_branch * gate
                r.dx[rows, 3 * local : 4 * local] = (grad_branch * normed).astype(BF16)
                r.branch[rows, :] = (normed * gate).astype(BF16)
                r.gate[rows, :] = grad_normed
                row_sums(grad_normed * normed, r.inner, member * per_block + number)

        gather_stage(second, out_back, lambda i: line.pump(ready(base_out), 3 if i == SUPER else 2))
        share.start()
        line.release(turn, base_gate)
        r.grads[base_out : base_out + local, :] = tn(r.branch[...], r.ga[...]).astype(BF16)
        line.pump(ready(base_gate), 1)

        def in_grad_rows(number, base):
            cols = slice(number * local, (number + 1) * local)
            line.release(turn, base + local)
            for n in range(width // local):
                part_grad = tn(r.n1[:, n * local : (n + 1) * local], r.dx[:, cols])
                r.grads[base : base + local, n * local : (n + 1) * local] = part_grad.astype(BF16)

        if turn > 0:
            await_loads("n1")
        in_grad_rows(3, base_gate)
        line.pump(ready(base_qkv), 1)
        if turn > 0:
            await_loads(*attn_in)
        r.intot[...] = share.total() / width
        for chunk in range(length // 128):
            rows = slice(chunk * 128, (chunk + 1) * 128)
            scale = widen(r.scale[rows, :], local // 128)
            inner = widen(spread(r.intot[...], chunk), local // 128)
            normed = r.heads[rows, :] * scale
            r.dh[rows, :] = (scale * (r.gate[rows, :] - normed * inner)).astype(BF16)
        share.drain()
        second.drain()
        if turn + 1 < layers:
            load(layer - 1, *out_in)
        line.pump(ready(base_qkv), 1)
        between = line.done
        line.done += 1
        assert line.done <= ready(base_qkv)

        @pl.loop(0, heads_here)
        def _(head):
            @pl.when(head == 1)
            def _():
                line.tick(between + head - 1)

            wide = aligned(head * 2 * HDIM, 2 * HDIM)
            thin = aligned(head * HDIM, HDIM)
            for col_tile in range(tiles_here):
                cols = slice(col_tile * size, (col_tile + 1) * size)
                keys = r.k[cols, wide]
                values = r.v[cols, thin]
                acc_key, acc_value = None, None
                for row_tile in range(col_tile, tiles_here):
                    rows = slice(row_tile * size, (row_tile + 1) * size)
                    queries = r.q[rows, wide]
                    grads = r.dh[rows, thin]
                    weight = tile_weight(r, first_head, head, row_tile, col_tile, size)
                    scores = (nt(queries, keys) * weight).astype(BF16)
                    pulled = (nt(grads, values) * weight).astype(BF16)
                    term = nn(pulled, keys)
                    if col_tile == 0:
                        r.dq[rows, :] = term
                    else:
                        r.dq[rows, :] += term
                    key_term = tn(pulled, queries)
                    value_term = tn(scores, grads)
                    acc_key = key_term if acc_key is None else acc_key + key_term
                    acc_value = value_term if acc_value is None else acc_value + value_term
                r.dk[cols, :] = acc_key
                r.dx[cols, aligned(2 * local + head * HDIM, HDIM)] = acc_value.astype(BF16)
            for row_tile in range(tiles_here):
                rows = slice(row_tile * size, (row_tile + 1) * size)
                cosine, sine = r.cos[rows, :], r.sin[rows, :]
                for grad, lin, base in ((r.dq, r.ql, 0), (r.dk, r.kl, local)):
                    v = lin[rows, thin].astype(F32)
                    gate = 1.0 / (1.0 + jnp.exp(-v))
                    back = grad[rows, :HDIM] * cosine + grad[rows, HDIM:] * sine
                    back = back * (gate + v * gate * (1.0 - gate))
                    r.dx[rows, aligned(base + head * HDIM, HDIM)] = back.astype(BF16)

        if turn + 1 < layers:
            load(layer - 1, *attn_in)
            source = getattr(r, "mid%d_h" % (layer - 1))
            mid_pieces = [
                copies.start(source.at[:, pl.ds(n * 2 * HDIM, 2 * HDIM)], r.dq.at[pl.ds(n * block, block), :])
                for n in range(width // (2 * HDIM))
            ]
        if turn > 0:
            await_loads(*in_in)
        last = turn == layers - 1
        if last:
            for number in range(3):
                in_grad_rows(number, base_qkv + number * local)
        for part in range(SUPER):
            for step in (3, 1, 2, 0):
                rows = aligned(place.member(step) * block + part * part_rows, part_rows)
                total = None
                for n, w in enumerate((r.wq, r.wk, r.wv, r.wg)):
                    term = nt(r.dx[rows, n * local : (n + 1) * local], w[...])
                    total = term if total is None else total + term
                r.part1[rows, :] = total.astype(BF16)
                in_sum.send_block(part, step)
            line.pump(ready(cfg.chunks * CHUNK if last else base_qkv), 2 if last else 1)
        for number in range(3):
            if not last:
                in_grad_rows(number, base_qkv + number * local)
            line.pump(ready(base_qkv + (number + 1) * local), 2 if last else 1)
            if number < SUPER:
                in_sum.middle(number)
        if last:
            for part in range(SUPER):
                for which in (1, 2, 3):
                    out_sum.send_block(part, which)
        if turn + 1 < layers:
            load(layer - 1, *in_in, "n1")
        for part in range(SUPER):
            line.pump(ready(cfg.chunks * CHUNK), 2)
            for h in range(2):
                in_sum.finish(part, h)
                for i in range(half // step_rows):
                    offset = (2 * part + h) * half + i * step_rows
                    rows = slice(offset, offset + step_rows)
                    total = in_sum.total(part, h, i * step_rows, step_rows)
                    values = getattr(r, "x%d" % layer)[rows, :].astype(F32)
                    new = back_rows(total, values, r.gm[rows, :])
                    if layer > 0:
                        r.g[rows, :] = new
                        r.gd[aligned(own_start + offset, step_rows), :] = new.astype(BF16)
                    else:
                        r.go[rows, :] = new.astype(BF16)
            if layer > 0:
                firsts[layer - 1].start(part)
        in_sum.drain()
    line.more(2)
    for part in range(SUPER):
        out_sum.middle(part)
        line.more(2)
    folded = finish_forward()
    r.stat_mine[...] = jnp.zeros_like(r.stat_mine)
    for one in range(top):
        r.stat_mine[3 * one : 3 * one + 3, :] = getattr(r, "stat%d" % one)[0:3, :]
    r.stat_mine[3 * top : 3 * top + 3, :] = folded[0:3, :]
    stats.square()
    line.more(1)
    stats.pair()
    for number in range(cfg.pairs):
        line.more(1)
        stats.stage(number)
    out_sum.drain()
    stats.finish()
    line.more(line.ticks)


def call_kernel(body, cfg, inputs, outputs, scratch, collective_id, name):
    vmem, anywhere = pl.BlockSpec(memory_space=pltpu.VMEM), pl.BlockSpec(memory_space=pl.ANY)
    names = list(inputs) + list(outputs) + list(scratch)
    result = pl.pallas_call(
        functools.partial(body, cfg, names),
        out_shape=[shape for shape, _ in outputs.values()],
        in_specs=[vmem if placed else anywhere for _, placed in inputs.values()],
        out_specs=[vmem if placed else anywhere for _, placed in outputs.values()],
        scratch_shapes=list(scratch.values()),
        compiler_params=pltpu.CompilerParams(
            collective_id=collective_id, has_side_effects=collective_id is not None, vmem_limit_bytes=VMEM_LIMIT
        ),
        name=name,
    )(*[array for array, _ in inputs.values()])
    return dict(zip(outputs, result))


def collective_scratch(cfg, copies, lead):
    dma = pltpu.SemaphoreType.DMA
    half = cfg.block // (2 * SUPER)
    out = {}
    for name in ("ag1", "ag2", "rs1", "rs2"):
        out["f" + name + "_send"] = out["f" + name + "_recv"] = dma((SUPER, 6))
        if lead:
            out[name + "_send"] = out[name + "_recv"] = dma((*lead, SUPER, 6))
    for name in copies:
        out["land" + name] = pltpu.VMEM((SUPER, 6, half, cfg.width), BF16)
        out["part" + name] = pltpu.VMEM((cfg.length, cfg.width), BF16)
    out["local_sem"] = dma((64,))
    return out


def weight_scratch(cfg):
    v = pltpu.VMEM
    return dict(
        wq=v((cfg.width, cfg.local), BF16), wk=v((cfg.width, cfg.local), BF16),
        wv=v((cfg.width, cfg.local), BF16), wg=v((cfg.width, cfg.local), BF16),
        wo=v((cfg.local, cfg.width), BF16), wl=v((cfg.ff, cfg.width), BF16),
        wr=v((cfg.ff, cfg.width), BF16), wd=v((cfg.ff, cfg.width), BF16),
    )


def table_scratch(cfg):
    v = pltpu.VMEM
    return dict(
        segc=v((cfg.length, 128), F32), segf=v((8, 128), F32),
        tiles=v((cfg.heads_here, 2, cfg.block, cfg.block), F32),
    )


def forward_scratch(cfg):
    v, dma = pltpu.VMEM, pltpu.SemaphoreType.DMA
    rows, wide, local, ff, block = cfg.length, cfg.width, cfg.local, cfg.ff, cfg.block
    return dict(
        n1=v((rows, wide), BF16), ql=v((rows, local), BF16), kl=v((rows, local), BF16), q=v((rows, 2 * local), BF16),
        k=v((rows, 2 * local), BF16), v=v((rows, local), BF16), gate=v((rows, local), F32), heads=v((rows, local), F32),
        mid=v((block, wide), F32), n2=v((rows, wide), BF16), left=v((rows, ff), BF16), right=v((rows, ff), BF16),
        hid=v((rows, ff), BF16), ss=v((8, 128), F32), ss_mine=v((8, 128), F32), dh=v((rows, local), BF16),
        stat_wide=v((8, wide), F32), scale=v((rows, 128), F32), ss_land=v((3, 8, 128), F32), ss_send=dma((3,)), ss_recv=dma((3,)),
    )


def run_forward(cfg, x, upstream, tables, weights):
    s = jax.ShapeDtypeStruct
    inputs = dict(x=(x, True), **{k: (a, True) for k, a in tables.items()}, **{k + "_h": (a, False) for k, a in weights.items()})
    scratch = dict(
        **weight_scratch(cfg), **collective_scratch(cfg, ("1", "2"), ()), **table_scratch(cfg), **forward_scratch(cfg),
    )
    outputs = dict(
        xo=(s((cfg.block, cfg.width), F32), True), stat=(s((8, 128), F32), True),
        **{k + "_h": (s(scratch[k].shape, scratch[k].dtype), False) for k in SAVED},
    )
    if cfg.gathers:
        gathered = (cfg.length, cfg.width)
        inputs.update(up=(upstream, True))
        outputs.update(gd_h=(s(gathered, BF16), False))
        scratch.update(gd=pltpu.VMEM(gathered, BF16), **gather_sems())
    return call_kernel(fwd_kernel, cfg, inputs, outputs, scratch, cfg.layer, "layer_forward")


def gather_sems():
    sems = pltpu.SemaphoreType.DMA((SUPER, 6))
    return dict(ag3_send=sems, ag3_recv=sems)


SAVED = ("ss", "mid", "n1", "ql", "kl", "q", "k", "v", "gate", "heads", "n2", "left", "right", "hid")


def run_backward(cfg, upstream, xs, saved, tables, weights):
    v, dma, s = pltpu.VMEM, pltpu.SemaphoreType.DMA, jax.ShapeDtypeStruct
    rows, wide, local, ff, block = cfg.length, cfg.width, cfg.local, cfg.ff, cfg.block
    inputs = dict(up=(upstream, True), gd_h=(saved[-1]["gd_h"], False), **{k: (a, True) for k, a in tables.items()}, **{k + "_h": (a, False) for k, a in weights.items()})
    for layer in range(cfg.layers):
        inputs["x%d" % layer] = (xs[layer], True)
    for layer in range(cfg.layers - 1):
        inputs["stat%d" % layer] = (saved[layer]["stat"], True)
        for key in SAVED:
            inputs["%s%d_h" % (key, layer)] = (saved[layer][key + "_h"], False)
    total_rows = cfg.chunks * CHUNK
    outputs = dict(
        xo=(s((block, wide), BF16), True), go=(s((block, wide), BF16), True), stat_total=(s((8, 128), F32), True),
        out_h=(s((cfg.layers * total_rows, wide), BF16), False),
    )
    small, ring, ring_sem = v((8, 128), F32), v((SLOTS, CHUNK // 2, wide), BF16), dma((SLOTS,))
    scratch = dict(
        **weight_scratch(cfg), **collective_scratch(cfg, ("1", "2"), (cfg.layers,)), **table_scratch(cfg), **forward_scratch(cfg),
        **gather_sems(),
        gd=v((rows, wide), BF16), ga=v((rows, wide), BF16),
        g=v((block, wide), F32), gm=v((block, wide), F32),
        branch=v((rows, local), BF16), dx=v((rows, 4 * local), BF16),
        dq=v((rows, 2 * HDIM), F32), dk=v((rows, 2 * HDIM), F32),
        grads=v((total_rows, wide), BF16),
        inner=small, intot=small,
        inner_land=v((cfg.layers, 3, 8, 128), F32), in_send=dma((cfg.layers, 3)), in_recv=dma((cfg.layers, 3)),
        pair_land=ring, right_land=ring, left_land=ring,
        pair_send=ring_sem, pair_recv=ring_sem, right_send=ring_sem, right_recv=ring_sem, left_send=ring_sem,
        left_recv=ring_sem, give_send=ring_sem, give_recv=ring_sem, keep_sem=ring_sem,
        stat_mine=small, stat_square=small, stat_pair=small, stat_right=small, stat_left=small,
        stat_land=v((3, 8, 128), F32), st_send=dma((3,)), st_recv=dma((3,)),
        line_land=v((3, 8, 128), F32), line_send=dma((3,)), line_recv=dma((3,)),
    )
    return call_kernel(bwd_kernel, cfg, inputs, outputs, scratch, cfg.layers, "layers_backward")


def widen_kernel(cfg, names, *refs):
    r = namespace(names, refs)
    tasks = []
    for layer in range(cfg.layers):
        for number, target in enumerate((r.down, r.left, r.right, r.out)):
            start, stop = cfg.bases[number], cfg.bases[number + 1]
            rows = (stop - start) // 2 if stop - start > 512 else stop - start
            for first in range(start, stop, rows):
                tasks.append((layer, first, rows, [(target.at[layer, pl.ds(first - start, rows), :], slice(None))]))
        for number, target in enumerate((r.gate, r.query, r.key, r.value)):
            pieces = [
                (target.at[layer, pl.ds(n * cfg.local, cfg.local), :], slice(n * cfg.local, (n + 1) * cfg.local))
                for n in range(cfg.width // cfg.local)
            ]
            start = cfg.bases[6] + (number - 1) * cfg.local if number > 0 else cfg.bases[4]
            tasks.append((layer, start, cfg.local, pieces))
    depth = 3

    def fetch(task):
        layer, first, rows, _ = tasks[task]
        start = layer * cfg.chunks * CHUNK + first
        slot = task % depth
        return pltpu.make_async_copy(r.grads.at[pl.ds(start, rows), :], r.narrow.at[slot, pl.ds(0, rows), :], r.in_sem.at[slot])

    def store(task):
        _, _, rows, pieces = tasks[task]
        slot = task % depth
        return [
            pltpu.make_async_copy(r.wide.at[slot, pl.ds(0, rows), lanes], target, r.out_sem.at[slot, n])
            for n, (target, lanes) in enumerate(pieces)
        ]

    for task in range(min(depth, len(tasks))):
        fetch(task).start()
    for task in range(len(tasks)):
        slot, rows = task % depth, tasks[task][2]
        fetch(task).wait()
        if task >= depth:
            for copy in store(task - depth):
                copy.wait()

        @pl.loop(0, rows // 32)
        def _(i):
            part = aligned(i * 32, 32)
            r.wide[slot, part, :] = r.narrow[slot, part, :].astype(F32)

        for copy in store(task):
            copy.start()
        if task + depth < len(tasks):
            fetch(task + depth).start()
    for task in range(max(len(tasks) - depth, 0), len(tasks)):
        for copy in store(task):
            copy.wait()


def run_widen(cfg, grads):
    v, dma, s = pltpu.VMEM, pltpu.SemaphoreType.DMA, jax.ShapeDtypeStruct
    thin, flat = s((cfg.layers, cfg.width, cfg.local), F32), s((cfg.layers, cfg.ff, cfg.width), F32)
    outputs = dict(
        down=(flat, False), left=(flat, False), right=(flat, False), out=(s((cfg.layers, cfg.local, cfg.width), F32), False),
        gate=(thin, False), query=(thin, False), key=(thin, False), value=(thin, False),
    )
    rows = max(cfg.ff // 2, cfg.local, 512)
    scratch = dict(
        narrow=v((3, rows, cfg.width), BF16), wide=v((3, rows, cfg.width), F32),
        in_sem=dma((3,)), out_sem=dma((3, cfg.width // cfg.local)),
    )
    return call_kernel(widen_kernel, cfg, dict(grads=(grads, False)), outputs, scratch, None, "widen_gradients")


def per_device_square(
    tokens, upstream, segment_ids, query_proj, key_proj, value_proj, gate_proj, output_proj, left_proj, right_proj, down_proj
):
    layers = query_proj.shape[0]
    block, width = tokens.shape
    length = segment_ids.shape[0]
    local, ff = query_proj.shape[2], left_proj.shape[2]
    heads_here = local // HDIM
    positions = np.arange(length, dtype=np.float32)
    frequency = np.exp(np.float32(-math.log(10000.0)) * np.arange(HDIM, dtype=np.float32) / np.float32(HDIM))
    angles = positions[:, None] * frequency[None, :]
    slopes = np.exp2(-8.0 * (np.arange(HEADS) + 1.0) / HEADS)
    decays = np.concatenate([-slopes * (1.0 - depth_start - depth_step * layer) for layer in range(layers)])
    tables = dict(
        cos=jnp.asarray(np.cos(angles)), sin=jnp.asarray(np.sin(angles)),
        dec=jnp.asarray(np.broadcast_to(decays[:, None], (layers * HEADS, 128)).astype(np.float32)),
        seg=segment_ids.reshape(8, length // 8),
    )
    weights = dict(
        wq=query_proj, wk=key_proj, wv=value_proj, wg=gate_proj, wo=output_proj,
        wl=jnp.swapaxes(left_proj, 1, 2), wr=jnp.swapaxes(right_proj, 1, 2), wd=down_proj,
    )
    ends = np.cumsum([0, ff, ff, ff, local, local]).tolist()
    ends += [-(-ends[-1] // CHUNK) * CHUNK]
    ends += [-(-(ends[-1] + 3 * local) // CHUNK) * CHUNK]
    common = dict(
        layers=layers, block=block, length=length, width=width, local=local, ff=ff, heads_here=heads_here,
        pairs=lax.axis_size("dp") // 2, bases=ends, chunks=ends[-1] // CHUNK,
    )
    current, xs, saved = tokens, [tokens], []
    for layer in range(layers - 1):
        cfg = types.SimpleNamespace(layer=layer, gathers=layer == layers - 2, **common)
        saved.append(run_forward(cfg, current, upstream, tables, weights))
        current = saved[-1]["xo"]
        xs.append(current)
    back = run_backward(types.SimpleNamespace(**common), upstream, xs, saved, tables, weights)
    stats = jnp.sum(back["stat_total"][: 3 * layers], axis=1).reshape(layers, 3)
    rms_stats = jnp.sqrt(stats / (length * lax.axis_size("dp") * width))
    wide = run_widen(types.SimpleNamespace(**common), back["out_h"])
    return (
        back["xo"], back["go"], wide["query"], wide["key"], wide["value"], wide["gate"], wide["out"],
        jnp.swapaxes(wide["left"], 1, 2), jnp.swapaxes(wide["right"], 1, 2), wide["down"], rms_stats,
    )


def solution(mesh):
    square = dict(mesh.shape) == SQUARE_MESH
    body = per_device_square if square else per_device
    return jax.shard_map(
        body,
        mesh=mesh,
        in_specs=(
            P(("dp", "tensor"), None),
            P(("dp", "tensor"), None),
            P("dp"),
            P(None, None, "tensor"),
            P(None, None, "tensor"),
            P(None, None, "tensor"),
            P(None, None, "tensor"),
            P(None, "tensor", None),
            P(None, None, "tensor"),
            P(None, None, "tensor"),
            P(None, "tensor", None),
        ),
        out_specs=(
            P(("dp", "tensor"), None),
            P(("dp", "tensor"), None),
            P(None, None, "tensor"),
            P(None, None, "tensor"),
            P(None, None, "tensor"),
            P(None, None, "tensor"),
            P(None, "tensor", None),
            P(None, None, "tensor"),
            P(None, None, "tensor"),
            P(None, "tensor", None),
            P(),
        ),
        check_vma=False,
    )
```

```python
import functools
import math
import types

import jax
import jax.numpy as jnp
import numpy as np
from jax import lax
from jax.experimental import pallas as pl
from jax.experimental.pallas import tpu as pltpu
from jax.sharding import PartitionSpec as P

HEADS = 8
HDIM = 128
BLK = 512


epsilon = 1e-06
depth_start = 0.5
depth_step = 1.0 / 24.0
highest = lax.Precision.HIGHEST


def rms_rows(values):
    return values * lax.rsqrt(jnp.mean(values * values, axis=1, keepdims=True) + epsilon)


def rms_back(values, gradient):
    scaling = lax.rsqrt(jnp.mean(values * values, axis=1, keepdims=True) + epsilon)
    normed = values * scaling
    return scaling * (gradient - normed * jnp.mean(gradient * normed, axis=1, keepdims=True))


def contract_last(left_part, right_part):
    return lax.dot_general(
        left_part, right_part, (((1,), (1,)), ((), ())), preferred_element_type=jnp.float32
    )


def contract_first(left_part, right_part):
    return lax.dot_general(
        left_part, right_part, (((0,), (0,)), ((), ())), preferred_element_type=jnp.float32
    )


def rotate(values, cosine, sine_table):
    return jnp.concatenate([values * cosine[:, None, :], values * sine_table[:, None, :]], axis=2)


def unrotate(gradient, cosine, sine_table):
    half_width = gradient.shape[2] // 2
    return (
        gradient[:, :, :half_width] * cosine[:, None, :]
        + gradient[:, :, half_width:] * sine_table[:, None, :]
    )


def split_blocks(array, block_count):
    return array.reshape((block_count, BLK) + array.shape[1:])


def block_weights(seg_block, next_seg, decay_log):
    block_width = seg_block.shape[0]
    places = jnp.arange(block_width, dtype=jnp.float32)
    distance = places[:, None] - places[None, :]
    allowed = (distance >= 0) & (seg_block[:, None] == seg_block[None, :])
    decay_grid = jnp.where(
        allowed[None], jnp.exp(decay_log[:, None, None] * jnp.maximum(distance, 0.0)[None]), 0.0
    )
    first_seg = seg_block[0]
    query_gain = jnp.where(
        (seg_block == first_seg)[:, None], jnp.exp(places[:, None] * decay_log[None, :]), 0.0
    )
    key_gain = jnp.where(
        (seg_block == next_seg)[:, None],
        jnp.exp((block_width - places)[:, None] * decay_log[None, :]),
        0.0,
    )
    carry_gain = jnp.where(first_seg == next_seg, jnp.exp(decay_log * block_width), 0.0)
    return (decay_grid, query_gain, key_gain, carry_gain)


def next_segments(segments, block_count):
    seg_blocks = segments.reshape(block_count, BLK)
    return (seg_blocks, jnp.concatenate([seg_blocks[1:, 0], jnp.full((1,), -1, jnp.int32)]))


def attend_forward(queries, keys_rot, values, segments, decay_log):
    length, heads_here, pair_width = queries.shape
    block_count = length // BLK
    seg_blocks, next_segs = next_segments(segments, block_count)

    def advance(state_now, block_items):
        query_block, key_block, value_block, seg_block, next_seg = block_items
        query_float = query_block.astype(jnp.float32)
        key_float = key_block.astype(jnp.float32)
        value_float = value_block.astype(jnp.float32)
        decay_grid, query_gain, key_gain, carry_gain = block_weights(seg_block, next_seg, decay_log)
        scores = (
            jnp.einsum("rhd,shd->hrs", query_block, key_block, preferred_element_type=jnp.float32)
            * decay_grid
        )
        block_out = jnp.einsum("hrs,she->rhe", scores, value_float, precision=highest)
        block_out = (
            block_out
            + jnp.einsum("rhd,hde->rhe", query_float, state_now, precision=highest)
            * query_gain[:, :, None]
        )
        new_state = carry_gain[:, None, None] * state_now + jnp.einsum(
            "shd,she->hde", key_float * key_gain[:, :, None], value_float, precision=highest
        )
        return (new_state, (block_out, state_now))

    zero_state = jnp.zeros((heads_here, pair_width, pair_width // 2), jnp.float32)
    _, (block_outs, states) = lax.scan(
        advance,
        zero_state,
        (
            split_blocks(queries, block_count),
            split_blocks(keys_rot, block_count),
            split_blocks(values, block_count),
            seg_blocks,
            next_segs,
        ),
    )
    return (block_outs.reshape(length, heads_here * (pair_width // 2)), states)


def attend_backward(queries, keys_rot, values, segments, decay_log, states, grad_heads):
    length, heads_here, pair_width = queries.shape
    block_count = length // BLK
    seg_blocks, next_segs = next_segments(segments, block_count)

    def retreat(later_grad, block_items):
        query_block, key_block, value_block, seg_block, next_seg, state_now, grad_block = (
            block_items
        )
        query_float = query_block.astype(jnp.float32)
        key_float = key_block.astype(jnp.float32)
        value_float = value_block.astype(jnp.float32)
        decay_grid, query_gain, key_gain, carry_gain = block_weights(seg_block, next_seg, decay_log)
        scores = (
            jnp.einsum("rhd,shd->hrs", query_block, key_block, preferred_element_type=jnp.float32)
            * decay_grid
        )
        pulled = jnp.einsum("rhe,she->hrs", grad_block, value_float, precision=highest) * decay_grid
        grad_query = jnp.einsum("hrs,shd->rhd", pulled, key_float, precision=highest)
        grad_query = (
            grad_query
            + jnp.einsum("rhe,hde->rhd", grad_block, state_now, precision=highest)
            * query_gain[:, :, None]
        )
        grad_key = jnp.einsum("hrs,rhd->shd", pulled, query_float, precision=highest)
        grad_key = (
            grad_key
            + jnp.einsum("she,hde->shd", value_float, later_grad, precision=highest)
            * key_gain[:, :, None]
        )
        grad_value = jnp.einsum("hrs,rhe->she", scores, grad_block, precision=highest)
        grad_value = (
            grad_value
            + jnp.einsum("shd,hde->she", key_float, later_grad, precision=highest)
            * key_gain[:, :, None]
        )
        earlier_grad = carry_gain[:, None, None] * later_grad + jnp.einsum(
            "rhd,rhe->hde", query_float * query_gain[:, :, None], grad_block, precision=highest
        )
        return (earlier_grad, (grad_query, grad_key, grad_value))

    zero_state = jnp.zeros((heads_here, pair_width, pair_width // 2), jnp.float32)
    _, (grad_query, grad_key, grad_value) = lax.scan(
        retreat,
        zero_state,
        (
            split_blocks(queries, block_count),
            split_blocks(keys_rot, block_count),
            split_blocks(values, block_count),
            seg_blocks,
            next_segs,
            states,
            split_blocks(grad_heads, block_count),
        ),
        reverse=True,
    )
    return (
        grad_query.reshape(length, heads_here, pair_width),
        grad_key.reshape(length, heads_here, pair_width),
        grad_value.reshape(length, heads_here, pair_width // 2),
    )


def per_device(
    tokens,
    upstream,
    segment_ids,
    query_proj,
    key_proj,
    value_proj,
    gate_proj,
    output_proj,
    left_proj,
    right_proj,
    down_proj,
):
    layers = query_proj.shape[0]
    row_count, model_width = tokens.shape
    length = segment_ids.shape[0]
    local_width = query_proj.shape[2]
    ff_local = left_proj.shape[2]
    heads_here = local_width // HDIM
    positions = jnp.arange(length, dtype=jnp.float32)
    frequency = jnp.exp(-math.log(10000.0) * jnp.arange(HDIM, dtype=jnp.float32) / HDIM)
    angles = positions[:, None] * frequency[None, :]
    cosine = jnp.cos(angles)
    sine_table = jnp.sin(angles)
    head_index = (lax.axis_index("tensor") * heads_here + jnp.arange(heads_here)).astype(
        jnp.float32
    )
    slopes = jnp.exp2(-8.0 * (head_index + 1.0) / HEADS)

    def gather_normed(normed):
        return lax.all_gather(normed, "tensor", axis=0, tiled=True)

    def gather_again(normed):
        return lax.all_gather(normed, "tensor", axis=0, tiled=True)

    def gather_grads(gradient):
        return lax.all_gather(gradient, "tensor", axis=0, tiled=True)

    def branch_sum(operand, matrix):
        return lax.psum_scatter(
            jnp.dot(operand, matrix, preferred_element_type=jnp.float32).astype(jnp.bfloat16),
            "tensor",
            scatter_dimension=0,
            tiled=True,
        ).astype(jnp.float32)

    def input_sum(pieces, matrix):
        operand = jnp.concatenate(pieces, axis=1)
        return lax.psum_scatter(
            contract_last(operand, matrix).astype(jnp.bfloat16),
            "tensor",
            scatter_dimension=0,
            tiled=True,
        ).astype(jnp.float32)

    current = tokens.astype(jnp.float32)
    saved_layers = []
    stat_terms = []
    for layer_index in range(layers):
        residual = current
        normed = rms_rows(residual).astype(jnp.bfloat16)
        full_normed = gather_normed(normed)
        attn_weight = jnp.concatenate(
            [
                query_proj[layer_index],
                key_proj[layer_index],
                value_proj[layer_index],
                gate_proj[layer_index],
            ],
            axis=1,
        )
        projected = jnp.dot(full_normed, attn_weight, preferred_element_type=jnp.float32)
        query_lin = projected[:, :local_width]
        key_lin = projected[:, local_width : 2 * local_width]
        values = (
            projected[:, 2 * local_width : 3 * local_width]
            .astype(jnp.bfloat16)
            .reshape(length, heads_here, HDIM)
        )
        gate_lin = projected[:, 3 * local_width :]
        queries = rotate(
            jax.nn.silu(query_lin).reshape(length, heads_here, HDIM), cosine, sine_table
        ).astype(jnp.bfloat16)
        keys_rot = rotate(
            jax.nn.silu(key_lin).reshape(length, heads_here, HDIM), cosine, sine_table
        ).astype(jnp.bfloat16)
        decay_log = -slopes * (1.0 - depth_start - depth_step * layer_index)
        heads_out, states = attend_forward(queries, keys_rot, values, segment_ids, decay_log)
        squares = lax.psum(jnp.sum(heads_out * heads_out, axis=1), "tensor")
        scaling = lax.rsqrt(squares / model_width + epsilon)[:, None]
        normed_heads = heads_out * scaling
        branch = (normed_heads * gate_lin).astype(jnp.bfloat16)
        attn_rows = branch_sum(branch, output_proj[layer_index])
        middle = residual + attn_rows
        normed_mid = rms_rows(middle).astype(jnp.bfloat16)
        full_mid = gather_normed(normed_mid)
        glu_weight = jnp.concatenate([left_proj[layer_index], right_proj[layer_index]], axis=1)
        gates_both = jnp.dot(full_mid, glu_weight, preferred_element_type=jnp.float32)
        left_lin = gates_both[:, :ff_local]
        right_lin = gates_both[:, ff_local:]
        hidden = (left_lin * right_lin).astype(jnp.bfloat16)
        glu_rows = branch_sum(hidden, down_proj[layer_index])
        current = middle + glu_rows
        stat_terms.append(
            jnp.stack(
                [
                    jnp.sum(attn_rows * attn_rows),
                    jnp.sum(glu_rows * glu_rows),
                    jnp.sum(current * current),
                ]
            )
        )
        saved_layers.append(
            (
                residual,
                middle,
                normed,
                normed_mid,
                full_normed,
                full_mid,
                attn_weight,
                glu_weight,
                query_lin,
                key_lin,
                gate_lin,
                queries,
                keys_rot,
                values,
                decay_log,
                states,
                normed_heads,
                scaling,
                branch,
                left_lin,
                right_lin,
                hidden,
            )
        )
    stat_sums = lax.psum(jnp.stack(stat_terms), ("dp", "tensor"))
    rms_stats = jnp.sqrt(stat_sums / (length * lax.axis_size("dp") * model_width))
    final_rows = current.astype(jnp.bfloat16)
    gradient = upstream.astype(jnp.float32)
    layer_results = [None] * layers
    for layer_index in reversed(range(layers)):
        (
            residual,
            middle,
            normed,
            normed_mid,
            full_normed,
            full_mid,
            attn_weight,
            glu_weight,
            query_lin,
            key_lin,
            gate_lin,
            queries,
            keys_rot,
            values,
            decay_log,
            states,
            normed_heads,
            scaling,
            branch,
            left_lin,
            right_lin,
            hidden,
        ) = saved_layers[layer_index]
        glu_grad = gather_grads(gradient.astype(jnp.bfloat16))
        grad_hidden = contract_last(glu_grad, down_proj[layer_index])
        down_part = contract_first(hidden, glu_grad)
        grad_left = (grad_hidden * right_lin).astype(jnp.bfloat16)
        grad_right = (grad_hidden * left_lin).astype(jnp.bfloat16)
        grad_gates = jnp.concatenate([grad_left, grad_right], axis=1)
        mid_rows = input_sum((grad_left, grad_right), glu_weight)
        source_mid = gather_again(normed_mid)
        glu_part = contract_first(source_mid, grad_gates)
        gradient = gradient + rms_back(middle, mid_rows)
        attn_grad = gather_grads(gradient.astype(jnp.bfloat16))
        output_part = contract_first(branch, attn_grad)
        grad_branch = contract_last(attn_grad, output_proj[layer_index])
        grad_normed = grad_branch * gate_lin
        grad_gate = (grad_branch * normed_heads).astype(jnp.bfloat16)
        inner_sum = lax.psum(jnp.sum(grad_normed * normed_heads, axis=1), "tensor")
        grad_heads = scaling * (grad_normed - normed_heads * (inner_sum / model_width)[:, None])
        grad_query, grad_key, grad_value = attend_backward(
            queries,
            keys_rot,
            values,
            segment_ids,
            decay_log,
            states,
            grad_heads.reshape(length, heads_here, HDIM),
        )
        sigmoid_query = jax.nn.sigmoid(query_lin)
        sigmoid_key = jax.nn.sigmoid(key_lin)
        query_back = unrotate(grad_query, cosine, sine_table).reshape(length, local_width)
        key_back = unrotate(grad_key, cosine, sine_table).reshape(length, local_width)
        grad_query_lin = (
            query_back * (sigmoid_query + query_lin * sigmoid_query * (1.0 - sigmoid_query))
        ).astype(jnp.bfloat16)
        grad_key_lin = (
            key_back * (sigmoid_key + key_lin * sigmoid_key * (1.0 - sigmoid_key))
        ).astype(jnp.bfloat16)
        grad_value_lin = grad_value.reshape(length, local_width).astype(jnp.bfloat16)
        grad_projected = jnp.concatenate(
            [grad_query_lin, grad_key_lin, grad_value_lin, grad_gate], axis=1
        )
        in_rows = input_sum((grad_query_lin, grad_key_lin, grad_value_lin, grad_gate), attn_weight)
        source_normed = gather_again(normed)
        attn_part = contract_first(source_normed, grad_projected)
        gradient = gradient + rms_back(residual, in_rows)
        query_part = attn_part[:, :local_width]
        key_part = attn_part[:, local_width : 2 * local_width]
        value_part = attn_part[:, 2 * local_width : 3 * local_width]
        gate_part = attn_part[:, 3 * local_width :]
        left_part = glu_part[:, :ff_local]
        right_part = glu_part[:, ff_local:]
        layer_results[layer_index] = (
            query_part,
            key_part,
            value_part,
            gate_part,
            output_part,
            left_part,
            right_part,
            down_part,
        )
    stacked = [
        jnp.stack([layer_results[index][member] for index in range(layers)]) for member in range(8)
    ]
    totals = (
        lax.psum(stacked[0].astype(jnp.bfloat16), "dp").astype(jnp.float32),
        lax.psum(stacked[1].astype(jnp.bfloat16), "dp").astype(jnp.float32),
        lax.psum(stacked[2].astype(jnp.bfloat16), "dp").astype(jnp.float32),
        lax.psum(stacked[3].astype(jnp.bfloat16), "dp").astype(jnp.float32),
        lax.psum(stacked[4].astype(jnp.bfloat16), "dp").astype(jnp.float32),
        lax.psum(stacked[5].astype(jnp.bfloat16), "dp").astype(jnp.float32),
        lax.psum(stacked[6].astype(jnp.bfloat16), "dp").astype(jnp.float32),
        lax.psum(stacked[7].astype(jnp.bfloat16), "dp").astype(jnp.float32),
    )
    input_grad = gradient.astype(jnp.bfloat16)
    return (
        final_rows,
        input_grad,
        totals[0],
        totals[1],
        totals[2],
        totals[3],
        totals[4],
        totals[5],
        totals[6],
        totals[7],
        rms_stats,
    )


SQUARE_MESH = {"dp": 8, "tensor": 4}


F32 = jnp.float32
BF16 = jnp.bfloat16
MESH = pl.DeviceIdType.MESH
VMEM_LIMIT = 62 * 2**20
SUPER = 2
EARLY = (0,)
WIDEN_DEPTH = 6
CHUNK = 128
HOP = 3
SLOTS = 16


def nn(a, b):
    return lax.dot_general(a, b, (((1,), (0,)), ((), ())), preferred_element_type=F32)


def nt(a, b):
    return lax.dot_general(a, b, (((1,), (1,)), ((), ())), preferred_element_type=F32)


def tn(a, b):
    return lax.dot_general(a, b, (((0,), (0,)), ((), ())), preferred_element_type=F32)


def exact(a, b, dims):
    return lax.dot_general(a, b, (dims, ((), ())), precision=highest, preferred_element_type=F32)


def aligned(index, size):
    return pl.ds(pl.multiple_of(index, size), size)


class Place:
    def __init__(self, pairs):
        self.dp = lax.axis_index("dp")
        self.me = lax.axis_index("tensor")
        self.low = lax.rem(self.me, 2)
        self.high = self.me // 2
        self.core = lax.rem(self.dp, 2)
        self.at = self.dp // 2
        self.last = pairs - 1

    def member(self, step):
        low = lax.rem(self.low + lax.rem(step, 2), 2)
        high = lax.rem(self.high + step // 2, 2)
        return 2 * high + low

    def device(self, step):
        return (self.dp, self.member(step))

    def partner(self):
        return (self.dp + 1 - 2 * self.core, self.me)

    def right(self):
        return (self.dp + 2, self.me)

    def left(self):
        return (self.dp - 2, self.me)

    def greet(self, line):
        barrier = pltpu.get_barrier_semaphore()

        def signal(device):
            pl.semaphore_signal(barrier, inc=1, device_id=device, device_id_type=MESH)

        for step in (1, 2, 3):
            signal(self.device(step))
        if not line:
            pl.semaphore_wait(barrier, 3)
            return
        signal(self.partner())

        @pl.when(self.at < self.last)
        def _():
            signal(self.right())

        @pl.when(self.at > 0)
        def _():
            signal(self.left())

        pl.semaphore_wait(barrier, 4 + jnp.minimum(self.at, 1) + jnp.minimum(self.last - self.at, 1))


class Wire:
    def __init__(self, device, send_sem, recv_sem, source, target, landing):
        self.source, self.target, self.landing = source, target, landing
        self.common = dict(send_sem=send_sem, recv_sem=recv_sem, device_id=device, device_id_type=MESH)

    def out(self):
        return pltpu.make_async_remote_copy(src_ref=self.source, dst_ref=self.target, **self.common)

    def start(self):
        self.out().start()

    def wait_recv(self):
        pltpu.make_async_remote_copy(src_ref=self.landing, dst_ref=self.landing, **self.common).wait_recv()

    def wait_send(self):
        self.out().wait_send()


class Gather:
    def __init__(self, place, buf, send, recv, block):
        self.place, self.buf, self.block = place, buf, block
        self.send, self.recv = send, recv
        self.half = block // (2 * SUPER)

    def rows(self, step, part, half):
        start = self.place.member(step) * self.block + (2 * part + half) * self.half
        return self.buf.at[aligned(start, self.half)]

    def wire(self, part, number):
        step, owner, half = ((1, 0, 0), (2, 0, 1), (1, 0, 1), (2, 0, 0), (2, 1, 0), (1, 2, 1))[number]
        source = self.rows(owner, part, half)
        landing = self.rows((0, 1, 2, 3)[owner ^ step], part, half)
        return Wire(self.place.device(step), self.send.at[part, number], self.recv.at[part, number], source, source, landing)

    def start(self, part):
        for number in range(4):
            self.wire(part, number).start()

    def forward(self, part):
        self.wire(part, 0).wait_recv()
        self.wire(part, 4).start()
        self.wire(part, 1).wait_recv()
        self.wire(part, 5).start()

    def finish(self, part, step):
        for number in {0: (), 1: (2,), 2: (3,), 3: (4, 5)}[step]:
            self.wire(part, number).wait_recv()

    def drain(self, parts=range(SUPER)):
        for part in parts:
            for number in range(6):
                self.wire(part, number).wait_send()


def gather_stage(gather, block_fn, beside):
    @pl.loop(0, 4 * SUPER)
    def _(i):
        mixed = i - SUPER
        part = jnp.where(i < SUPER, i, jnp.where(i < 3 * SUPER, mixed // 2, i - 3 * SUPER))
        step = jnp.where(i < SUPER, 0, jnp.where(i < 3 * SUPER, 1 + lax.rem(mixed, 2), 3))

        @pl.when(i == SUPER)
        def _():
            for one in range(SUPER):
                beside(one)
                gather.forward(one)

        @pl.when(i == 3 * SUPER)
        def _():
            beside(SUPER)

        for which in (1, 2, 3):
            @pl.when(step == which)
            def _():
                gather.finish(part, which)
        block_fn(part, step)


class Scatter:
    def __init__(self, place, buf, land, send, recv, block):
        self.place, self.buf, self.land, self.block = place, buf, land, block
        self.send, self.recv = send, recv
        self.half = block // (2 * SUPER)

    def rows(self, step, part, half):
        start = self.place.member(step) * self.block + (2 * part + half) * self.half
        return aligned(start, self.half)

    def wire(self, part, number):
        step, owner, half = ((1, 3, 0), (1, 1, 0), (2, 3, 1), (2, 2, 1), (2, 2, 0), (1, 1, 1))[number]
        target = self.land.at[part, number]
        return Wire(
            self.place.device(step), self.send.at[part, number], self.recv.at[part, number],
            self.buf.at[self.rows(owner, part, half)], target, target,
        )

    def send_block(self, part, step):
        for number in {0: (), 1: (1,), 2: (3,), 3: (0, 2)}[step]:
            self.wire(part, number).start()

    def middle(self, part):
        for first, second, owner, half in ((0, 4, 2, 0), (2, 5, 1, 1)):
            self.wire(part, first).wait_recv()
            rows = self.rows(owner, part, half)
            self.buf[rows, :] = self.buf[rows, :] + self.land[part, first]
            self.wire(part, second).start()

    def finish(self, part, half):
        first, second = ((1, 4), (3, 5))[half]
        self.wire(part, first).wait_recv()
        self.wire(part, second).wait_recv()

    def total(self, part, half, start, count):
        first, second = ((1, 4), (3, 5))[half]
        own = self.place.me * self.block + (2 * part + half) * self.half + start
        rows = pl.ds(start, count)
        return (
            self.buf[aligned(own, count), :].astype(F32)
            + self.land[part, first, rows, :].astype(F32)
            + self.land[part, second, rows, :].astype(F32)
        )

    def drain(self):
        for part in range(SUPER):
            for number in range(6):
                self.wire(part, number).wait_send()


class Share:
    def __init__(self, place, mine, land, send, recv):
        self.wires = [
            Wire(place.device(step), send.at[step - 1], recv.at[step - 1], mine, land.at[step - 1], land.at[step - 1])
            for step in (1, 2, 3)
        ]
        self.mine, self.land = mine, land

    def start(self):
        for wire in self.wires:
            wire.start()

    def total(self):
        for wire in self.wires:
            wire.wait_recv()
        return self.mine[...] + self.land[0] + self.land[1] + self.land[2]

    def drain(self):
        for wire in self.wires:
            wire.wait_send()


class Local:
    def __init__(self, sems):
        self.sems, self.used = sems, 0

    def start(self, source, target):
        copy = pltpu.make_async_copy(source, target, self.sems.at[self.used])
        self.used += 1
        copy.start()
        return copy


def row_sums(values, target, chunk):
    sums = exact(jnp.ones((8, values.shape[1]), F32), values, ((1,), (1,)))
    target[pl.ds(chunk, 1), :] = sums[0:1, :]


def spread(sums, chunk):
    picked = (lax.broadcasted_iota(jnp.int32, (8, 128), 0) == chunk).astype(F32)
    return exact(sums, picked, ((0,), (0,)))


def widen(columns, times):
    return jnp.concatenate([columns] * times, axis=1)


def decay_tiles(dec_ref, first_head, tiles, heads_here, size):
    rows = lax.broadcasted_iota(jnp.int32, (size, size), 0)
    cols = lax.broadcasted_iota(jnp.int32, (size, size), 1)
    distance = (rows - cols).astype(F32)
    for head in range(heads_here):
        decay = dec_ref[pl.ds(first_head + head, 1), 0:1]
        tiles[head, 0] = jnp.where(rows >= cols, jnp.exp(decay * jnp.maximum(distance, 0.0)), 0.0)
        tiles[head, 1] = jnp.exp(decay * (distance + float(size)))


def spread_segments(r, length):
    r.segf[...] = r.seg[...].astype(F32)
    for chunk in range(length // 128):
        r.segc[chunk * 128 : (chunk + 1) * 128, :] = spread(r.segf[...], chunk)


def tile_weight(r, first_head, head, row_tile, col_tile, size):
    gap = row_tile - col_tile
    if gap == 0:
        weight = r.tiles[head, 0]
    else:
        weight = r.tiles[head, 1]
        if gap > 1:
            decay = r.dec[pl.ds(first_head + head, 1), 0:1]
            weight = weight * jnp.exp(decay * float(size * (gap - 1)))
    row_seg = widen(r.segc[row_tile * size : (row_tile + 1) * size, :], size // 128)
    per = size // 128
    col_seg = jnp.concatenate([r.segf[per * col_tile + i : per * col_tile + i + 1, :] for i in range(per)], axis=1)
    return jnp.where(row_seg == col_seg, weight, 0.0)


def namespace(names, refs):
    return types.SimpleNamespace(**dict(zip(names, refs)))


def forward_front(cfg, r, place, copies, layer, x, save, third, third_parts, back_block):
    block, length, width = cfg.block, cfg.length, cfg.width
    heads_here, size = cfg.heads_here, cfg.block
    first_head = layer * HEADS + place.me * heads_here
    w_in = [copies.start(h.at[layer], v) for h, v in (
        (r.wq_h, r.wq), (r.wk_h, r.wk), (r.wv_h, r.wv), (r.wg_h, r.wg))]
    w_out = copies.start(r.wo_h.at[layer], r.wo)
    w_glu = [copies.start(h.at[layer], v) for h, v in ((r.wl_h, r.wl), (r.wr_h, r.wr), (r.wd_h, r.wd))]
    first = Gather(place, r.n1, r.fag1_send.at[layer], r.fag1_recv.at[layer], block)
    mid_sum = Scatter(place, r.part1, r.land1, r.frs1_send.at[layer], r.frs1_recv.at[layer], block)
    second = Gather(place, r.n2, r.fag2_send.at[layer], r.fag2_recv.at[layer], block)
    out_sum = Scatter(place, r.part2, r.land2, r.frs2_send.at[layer], r.frs2_recv.at[layer], block)
    share = Share(place, r.ss_mine, r.ss_land.at[layer], r.ss_send.at[layer], r.ss_recv.at[layer])
    half, step_rows = first.half, 32
    own_start = place.me * block

    if layer == 0:
        @pl.loop(0, block // step_rows)
        def _(i):
            rows = aligned(i * step_rows, step_rows)
            v = x[rows, :].astype(F32)
            scale = lax.rsqrt(jnp.mean(v * v, axis=1, keepdims=True) + epsilon)
            r.n1[aligned(own_start + i * step_rows, step_rows), :] = (v * scale).astype(BF16)

        place.greet(True)
        for part in range(SUPER):
            first.start(part)
        spread_segments(r, length)
    decay_tiles(r.dec, first_head, r.tiles, heads_here, size)
    for copy in w_in:
        copy.wait()

    @pl.loop(0, 4)
    def _(step):
        @pl.when(step == 1)
        def _():
            for part in range(SUPER):
                first.forward(part)
        for which in (1, 2, 3):
            @pl.when(step == which)
            def _():
                for part in range(SUPER):
                    first.finish(part, which)
        rows = aligned(place.member(step) * block, block)
        a = r.n1[rows, :]
        cosine, sine = r.cos[rows, :], r.sin[rows, :]
        for w, lin, rot in ((r.wq, r.ql, r.q), (r.wk, r.kl, r.k)):
            v = nn(a, w[...])
            lin[rows, :] = v.astype(BF16)
            v = v / (1.0 + jnp.exp(-v))
            for head in range(heads_here):
                one = v[:, head * HDIM : (head + 1) * HDIM]
                rot[rows, 2 * head * HDIM : (2 * head + 1) * HDIM] = (one * cosine).astype(BF16)
                rot[rows, (2 * head + 1) * HDIM : (2 * head + 2) * HDIM] = (one * sine).astype(BF16)
        r.v[rows, :] = nn(a, r.wv[...]).astype(BF16)
        r.gate[rows, :] = nn(a, r.wg[...])

    save("n1", "ql", "kl", "q", "k", "v", "gate")
    if third_parts:
        for part in third_parts:
            third.start(part)
    tiles_here = length // size

    @pl.loop(0, heads_here)
    def _(head):
        wide = aligned(head * 2 * HDIM, 2 * HDIM)
        thin = aligned(head * HDIM, HDIM)
        for row_tile in range(tiles_here):
            rows = slice(row_tile * size, (row_tile + 1) * size)
            queries = r.q[rows, wide]
            acc = None
            for col_tile in range(row_tile + 1):
                cols = slice(col_tile * size, (col_tile + 1) * size)
                weight = tile_weight(r, first_head, head, row_tile, col_tile, size)
                scores = (nt(queries, r.k[cols, wide]) * weight).astype(BF16)
                term = nn(scores, r.v[cols, thin])
                acc = term if acc is None else acc + term
            r.heads[rows, thin] = acc
            r.dh[rows, thin] = (acc * r.gate[rows, thin]).astype(BF16)

    for chunk in range(length // 128):
        v = r.heads[chunk * 128 : (chunk + 1) * 128, :]
        row_sums(v * v, r.ss_mine, chunk)
    share.start()
    save("heads")
    if third_parts:
        for part in third_parts:
            third.forward(part)
    w_out.wait()

    part_rows = 2 * half
    for part in range(SUPER):
        for step in (3, 1, 2, 0):
            rows = aligned(place.member(step) * block + part * part_rows, part_rows)
            r.part1[rows, :] = nn(r.dh[rows, :], r.wo[...]).astype(BF16)
            mid_sum.send_block(part, step)
    for part in range(SUPER):
        mid_sum.middle(part)
    r.ss[...] = share.total()
    save("ss")
    scaling = lax.rsqrt(r.ss[...] / width + epsilon)
    per_block = block // 128
    for chunk in range(per_block):
        r.scale[aligned(own_start + chunk * 128, 128), :] = spread(scaling, place.me * per_block + chunk)
    r.stat_wide[...] = jnp.zeros_like(r.stat_wide)

    def add_stat(row, v):
        sums = jnp.sum(v * v, axis=0, keepdims=True)
        r.stat_wide[row : row + 1, :] += sums

    step_rows = min(32, half)
    for part in range(SUPER):
        for h in range(2):
            mid_sum.finish(part, h)
            for i in range(half // step_rows):
                offset = (2 * part + h) * half + i * step_rows
                scale = widen(r.scale[aligned(own_start + offset, step_rows), :], width // 128)
                attn = mid_sum.total(part, h, i * step_rows, step_rows) * scale
                middle = x[offset : offset + step_rows, :].astype(F32) + attn
                r.mid[offset : offset + step_rows, :] = middle
                add_stat(0, attn)
                norm = lax.rsqrt(jnp.mean(middle * middle, axis=1, keepdims=True) + epsilon)
                r.n2[aligned(own_start + offset, step_rows), :] = (middle * norm).astype(BF16)
        second.start(part)
    save("mid")
    for copy in w_glu:
        copy.wait()
    if third_parts:
        for part in third_parts:
            for which in (1, 2, 3):
                third.finish(part, which)
    if back_block is not None:
        mid_sum.drain()

    def glu(part, step):
        rows = aligned(place.member(step) * block + part * part_rows, part_rows)
        a = r.n2[rows, :]
        left = nt(a, r.wl[...])
        right = nt(a, r.wr[...])
        hidden = (left * right).astype(BF16)
        r.hid[rows, :] = hidden
        if back_block is not None:
            back_block(rows, left, right, part, step)
        else:
            r.left[rows, :] = left.astype(BF16)
            r.right[rows, :] = right.astype(BF16)
        r.part2[rows, :] = nn(hidden, r.wd[...]).astype(BF16)
        if back_block is None:
            for which in (1, 2, 3):
                @pl.when(step == which)
                def _():
                    out_sum.send_block(part, which)

    gather_stage(second, glu, lambda i: None)

    def finish(target, following):
        for part in range(SUPER):
            for h in range(2):
                out_sum.finish(part, h)
                for i in range(half // step_rows):
                    offset = (2 * part + h) * half + i * step_rows
                    glu_rows = out_sum.total(part, h, i * step_rows, step_rows)
                    after = r.mid[offset : offset + step_rows, :] + glu_rows
                    target[offset : offset + step_rows, :] = after.astype(target.dtype)
                    add_stat(1, glu_rows)
                    add_stat(2, after)
                    if following is not None:
                        norm = lax.rsqrt(jnp.mean(after * after, axis=1, keepdims=True) + epsilon)
                        r.n1[aligned(own_start + offset, step_rows), :] = (after * norm).astype(BF16)
            if following is not None:
                following.start(part)
        folded = r.stat_wide[:, :128]
        for n in range(1, width // 128):
            folded = folded + r.stat_wide[:, n * 128 : (n + 1) * 128]
        return folded

    groups = [first, second, share] + ([mid_sum] if back_block is None else [])
    return out_sum, finish, groups


def turns_of(k, size, count):
    return sum(((k >= size * n).astype(jnp.int32) for n in range(1, -(-count // size))), jnp.int32(0))


class Line:
    def __init__(self, cfg, place, r):
        self.place, self.r = place, r
        self.per, self.count = cfg.chunks, cfg.chunks * cfg.layers
        self.layers, self.rows_each = cfg.layers, cfg.chunks * CHUNK
        self.half = CHUNK // 2
        self.ticks = self.count + 3 + HOP * place.last
        self.done = 0

    def slot(self, k):
        return k - SLOTS * turns_of(k, SLOTS, self.count)

    def rows(self, k, core):
        place = k - self.per * turns_of(k, self.per, self.count)
        return aligned(place * CHUNK + core * self.half, self.half)

    def own(self, k):
        return self.rows(k, self.place.core)

    def out_rows(self, k, core):
        turn = turns_of(k, self.per, self.count)
        place = (self.layers - 1 - turn) * self.per + k - turn * self.per
        start = place * CHUNK + core * self.half
        return aligned(start, self.half)

    def pair(self, k):
        slot = self.slot(k)
        r = self.r
        return Wire(self.place.partner(), r.pair_send.at[slot], r.pair_recv.at[slot],
                    r.grads.at[self.rows(k, 1 - self.place.core)], r.pair_land.at[slot], r.pair_land.at[slot])

    def hop(self, k, land, send, recv, device):
        slot = self.slot(k)
        return Wire(device, send.at[slot], recv.at[slot], land.at[slot], land.at[slot], land.at[slot])

    def going_right(self, k):
        return self.hop(k, self.r.right_land, self.r.right_send, self.r.right_recv, self.place.right())

    def going_left(self, k):
        return self.hop(k, self.r.left_land, self.r.left_send, self.r.left_recv, self.place.left())

    def coming_right(self, k):
        return self.hop(k, self.r.right_land, self.r.right_send, self.r.right_recv, self.place.left())

    def coming_left(self, k):
        return self.hop(k, self.r.left_land, self.r.left_send, self.r.left_recv, self.place.right())

    def result(self, k):
        slot, r = self.slot(k), self.r
        return Wire(self.place.partner(), r.give_send.at[slot], r.give_recv.at[slot],
                    r.grads.at[self.own(k)], r.out_h.at[self.out_rows(k, self.place.core)],
                    r.out_h.at[self.out_rows(k, 1 - self.place.core)])

    def keep(self, k):
        slot, r = self.slot(k), self.r
        return pltpu.make_async_copy(
            r.grads.at[self.own(k)], r.out_h.at[self.out_rows(k, self.place.core)], r.keep_sem.at[slot]
        )

    def one_way(self, k, land, start_here, coming, ends_here, going):
        slot = self.slot(k)

        @pl.when(start_here)
        def _():
            land[slot] = self.r.grads[self.own(k), :]

        @pl.when(jnp.logical_not(start_here))
        def _():
            coming(k).wait_recv()
            land[slot] = land[slot] + self.r.grads[self.own(k), :]

        @pl.when(jnp.logical_not(ends_here))
        def _():
            going(k).start()

    def tick(self, n):
        place, r, last = self.place, self.r, self.place.last
        at_left, at_right = place.at == 0, place.at == last

        @pl.when(n < self.count)
        def _():
            self.pair(n).start()

        k = n - 1

        @pl.when(jnp.logical_and(k >= 0, k < self.count))
        def _():
            wire = self.pair(k)
            wire.wait_recv()
            wire.wait_send()
            slot = self.slot(k)
            r.grads[self.own(k), :] = r.grads[self.own(k), :] + r.pair_land[slot]

        left_k = n - 1 - HOP * (last - place.at)

        @pl.when(jnp.logical_and(left_k >= 0, left_k < self.count))
        def _():
            self.one_way(left_k, r.left_land, at_right, self.coming_left, at_left, self.going_left)

        right_k = n - 1 - HOP * place.at

        @pl.when(jnp.logical_and(right_k >= 0, right_k < self.count))
        def _():
            self.one_way(right_k, r.right_land, at_left, self.coming_right, at_right, self.going_right)

        full_k = n - 1 - HOP * last

        @pl.when(jnp.logical_and(full_k >= 0, full_k < self.count))
        def _():
            @pl.when(jnp.logical_not(at_right))
            def _():
                self.going_right(full_k).wait_send()

            @pl.when(jnp.logical_not(at_left))
            def _():
                self.going_left(full_k).wait_send()

            slot = self.slot(full_k)
            own = self.own(full_k)
            total = r.right_land[slot].astype(F32) + r.left_land[slot].astype(F32) - r.grads[own, :].astype(F32)
            r.grads[own, :] = total.astype(BF16)
            self.result(full_k).start()
            self.keep(full_k).start()

        old_k = full_k - 2

        @pl.when(jnp.logical_and(old_k >= 0, old_k < self.count))
        def _():
            wire = self.result(old_k)
            wire.wait_recv()
            wire.wait_send()
            self.keep(old_k).wait()

    def pump(self, ready, most):
        stop = min(self.done + most, ready)
        if stop > self.done:
            start, self.done = self.done, stop

            @pl.loop(start, stop)
            def _(n):
                self.tick(n)

    def release(self, turn, rows):
        needed = (turn - 1) * self.per + -(-rows // CHUNK) + 3 + HOP * self.place.last
        if turn > 0 and needed > self.done:
            self.pump(turn * self.per, needed - self.done)
            assert self.done >= needed

    def more(self, most):
        self.pump(self.ticks, most)


class StatLine:
    def __init__(self, place, r):
        self.place, self.r = place, r
        self.share = Share(place, r.stat_mine, r.stat_land, r.st_send, r.st_recv)

    def square(self):
        self.share.start()

    def pair(self):
        r = self.r
        r.stat_square[...] = self.share.total()
        self.wire(0, self.place.partner(), r.stat_square).start()

    def wire(self, number, device, source):
        r = self.r
        return Wire(device, r.line_send.at[number], r.line_recv.at[number], source, r.line_land.at[number], r.line_land.at[number])

    def stage(self, number):
        place, r = self.place, self.r
        if number == 0:
            self.wire(0, place.partner(), r.stat_square).wait_recv()
            r.stat_pair[...] = r.stat_square[...] + r.line_land[0]
            r.stat_right[...] = r.stat_pair[...]
            r.stat_left[...] = r.stat_pair[...]
        else:
            @pl.when(place.at == number)
            def _():
                self.wire(1, place.left(), r.stat_right).wait_recv()
                r.stat_right[...] = r.stat_pair[...] + r.line_land[1]

            @pl.when(place.last - place.at == number)
            def _():
                self.wire(2, place.right(), r.stat_left).wait_recv()
                r.stat_left[...] = r.stat_pair[...] + r.line_land[2]
        if number < place.last:
            @pl.when(place.at == number)
            def _():
                self.wire(1, place.right(), r.stat_right).start()

            @pl.when(place.last - place.at == number)
            def _():
                self.wire(2, place.left(), r.stat_left).start()

    def finish(self):
        place, r = self.place, self.r
        r.stat_total[...] = r.stat_right[...] + r.stat_left[...] - r.stat_pair[...]
        self.share.drain()
        self.wire(0, place.partner(), r.stat_square).wait_send()

        @pl.when(place.at < place.last)
        def _():
            self.wire(1, place.right(), r.stat_right).wait_send()

        @pl.when(place.at > 0)
        def _():
            self.wire(2, place.left(), r.stat_left).wait_send()


def layers_kernel(cfg, names, *refs):
    r = namespace(names, refs)
    block, length, width, local, ff = cfg.block, cfg.length, cfg.width, cfg.local, cfg.ff
    heads_here, size, layers = cfg.heads_here, cfg.block, cfg.layers
    place = Place(cfg.pairs)
    copies = Local(r.local_sem)
    line = Line(cfg, place, r)
    stats = StatLine(place, r)
    loads = {}
    base_down, base_left, base_right, base_out, base_gate, gate_end, base_qkv, _ = cfg.bases
    half = block // (2 * SUPER)
    part_rows = 2 * half
    own_start = place.me * block
    step_rows = min(32, half)
    per_block = block // 128
    tiles_here = length // size

    def load(layer, *keys):
        for key in keys:
            if key in SAVED:
                source = getattr(r, key + str(layer) + "_h")
            else:
                source = getattr(r, key + "_h").at[layer]
            loads[key] = copies.start(source, getattr(r, key))

    def await_loads(*keys):
        for key in keys:
            loads[key].wait()

    glu_in = ("wd", "left", "right", "wl", "wr")
    glu_grad = ("hid", "n2")
    out_in = ("ss", "wo", "gate", "heads")
    attn_in = ("q", "k", "v", "ql", "kl")
    in_in = ("wq", "wk", "wv", "wg")

    def gather_one(layer):
        return Gather(place, r.gd, r.ag1_send.at[layer], r.ag1_recv.at[layer], block)

    firsts = [gather_one(layer) for layer in range(layers)]

    @pl.loop(0, block // 32)
    def _(i):
        rows = aligned(i * 32, 32)
        r.g[rows, :] = r.up[rows, :].astype(F32)


        r.gd[aligned(own_start + i * 32, 32), :] = r.up[rows, :]
    for start, stop in ((gate_end, base_qkv), (base_qkv + 3 * local, cfg.chunks * CHUNK)):
        if stop > start:
            r.grads[start:stop, :] = jnp.zeros((stop - start, width), BF16)
    top = layers - 1
    third = Gather(place, r.gd, r.ag3_send, r.ag3_recv, block)
    top_sum = Scatter(place, r.part1, r.land1, r.rs1_send.at[top], r.rs1_recv.at[top], block)

    def back_block(rows, left, right, part, step):
        grad_hidden = nt(r.gd[rows, :], r.wd[...])
        grad_left = (grad_hidden * right).astype(BF16)
        grad_right = (grad_hidden * left).astype(BF16)
        r.right[rows, :] = grad_left
        r.left[rows, :] = grad_right
        r.part1[rows, :] = (nn(grad_left, r.wl[...]) + nn(grad_right, r.wr[...])).astype(BF16)
        for which in (1, 2, 3):
            @pl.when(step == which)
            def _():
                top_sum.send_block(part, which)

    r.stat_mine[...] = jnp.zeros_like(r.stat_mine)
    late = [part for part in range(SUPER) if part not in EARLY]
    for layer in range(top):
        saves = []

        def save(*keys):
            for key in keys:
                saves.append(copies.start(getattr(r, key), getattr(r, key + str(layer) + "_h")))

        out_sum, finish_forward, groups = forward_front(
            cfg, r, place, copies, layer, getattr(r, "x%d" % layer), save, third, EARLY if layer == top - 1 else (), None
        )
        for copy in saves:
            copy.wait()
        saves.clear()
        save("n2", "left", "right", "hid")
        for group in groups:
            group.drain()
        for part in range(SUPER):
            out_sum.middle(part)
        following = Gather(place, r.n1, r.fag1_send.at[layer + 1], r.fag1_recv.at[layer + 1], block)
        folded = finish_forward(getattr(r, "x%d" % (layer + 1)), following)
        r.stat_mine[3 * layer : 3 * layer + 3, :] = folded[0:3, :]
        for copy in saves:
            copy.wait()
        out_sum.drain()
    out_sum, finish_forward, groups = forward_front(
        cfg, r, place, copies, top, getattr(r, "x%d" % top), lambda *keys: None, third, late, back_block
    )
    for group in groups:
        group.drain()
    third.drain()

    def back_rows(total, values, grad):
        norm = lax.rsqrt(jnp.mean(values * values, axis=1, keepdims=True) + epsilon)
        m = values * norm
        inner = jnp.mean(total * m, axis=1, keepdims=True)
        return grad + norm * (total - m * inner)

    for turn, layer in enumerate(reversed(range(layers))):
        first = firsts[layer]
        mid_sum = top_sum if turn == 0 else Scatter(place, r.part1, r.land1, r.rs1_send.at[layer], r.rs1_recv.at[layer], block)
        second = Gather(place, r.ga, r.ag2_send.at[layer], r.ag2_recv.at[layer], block)
        in_sum = Scatter(place, r.part1, r.land1, r.rs2_send.at[layer], r.rs2_recv.at[layer], block)
        share = Share(place, r.inner, r.inner_land.at[layer], r.in_send.at[layer], r.in_recv.at[layer])
        first_head = layer * HEADS + place.me * heads_here

        def ready(rows):
            return turn * cfg.chunks + rows // CHUNK

        if turn > 0:
            decay_tiles(r.dec, first_head, r.tiles, heads_here, size)
            await_loads(*glu_in)
            await_loads(*out_in)
        scaling = lax.rsqrt(r.ss[...] / width + epsilon)
        for chunk in range(length // 128):
            r.scale[chunk * 128 : (chunk + 1) * 128, :] = spread(scaling, chunk)
        def glu_back(part, step):
            rows = aligned(place.member(step) * block + part * part_rows, part_rows)
            grad_hidden = nt(r.gd[rows, :], r.wd[...])
            grad_left = (grad_hidden * r.right[rows, :].astype(F32)).astype(BF16)
            grad_right = (grad_hidden * r.left[rows, :].astype(F32)).astype(BF16)
            r.right[rows, :] = grad_left
            r.left[rows, :] = grad_right
            r.part1[rows, :] = (nn(grad_left, r.wl[...]) + nn(grad_right, r.wr[...])).astype(BF16)
            for which in (1, 2, 3):
                @pl.when(step == which)
                def _():
                    mid_sum.send_block(part, which)

        if turn > 0:
            gather_stage(first, glu_back, lambda i: line.pump(ready(0), 2))
            first.drain()
        grad_left_ref, grad_right_ref = r.right, r.left

        def glu_grad_rows(base, a_ref, b_ref):
            line.release(turn, base + ff)
            for n in range(width // 256):
                cols = slice(n * 256, (n + 1) * 256)
                r.grads[base : base + ff, cols] = tn(a_ref[...], b_ref[:, cols]).astype(BF16)

        if turn > 0:
            await_loads(*glu_grad)
            for copy in mid_pieces:
                copy.wait()
        glu_grad_rows(base_down, r.hid, r.gd)
        line.pump(ready(base_left), 1 + turn)
        mid_sum.middle(0)
        glu_grad_rows(base_left, grad_left_ref, r.n2)
        line.pump(ready(base_right), 1 + turn)
        for part in range(1, SUPER):
            mid_sum.middle(part)
        glu_grad_rows(base_right, grad_right_ref, r.n2)
        for part in range(SUPER):
            line.pump(ready(base_out), 2 if part == 0 else 1)
            for h in range(2):
                mid_sum.finish(part, h)
                for i in range(half // step_rows):
                    offset = (2 * part + h) * half + i * step_rows
                    rows = slice(offset, offset + step_rows)
                    total = mid_sum.total(part, h, i * step_rows, step_rows)
                    if turn == 0:
                        values = r.mid[rows, :]
                    else:
                        pieces = range(width // (2 * HDIM))
                        values = jnp.concatenate([r.dq[n * block + offset : n * block + offset + step_rows, :] for n in pieces], axis=1)
                    new = back_rows(total, values, r.g[rows, :])
                    r.gm[rows, :] = new
                    r.ga[aligned(own_start + offset, step_rows), :] = new.astype(BF16)
            second.start(part)
        mid_sum.drain()
        if turn + 1 < layers:
            load(layer - 1, *glu_in, *glu_grad)

        def out_back(part, step):
            member = place.member(step)
            for chunk in range(part_rows // 128):
                number = part * (part_rows // 128) + chunk
                rows = aligned(member * block + number * 128, 128)
                grad_branch = nt(r.ga[rows, :], r.wo[...])
                gate = r.gate[rows, :]
                normed = r.heads[rows, :] * widen(r.scale[rows, :], local // 128)
                grad_normed = grad_branch * gate
                r.dx[rows, 3 * local : 4 * local] = (grad_branch * normed).astype(BF16)
                r.branch[rows, :] = (normed * gate).astype(BF16)
                r.gate[rows, :] = grad_normed
                row_sums(grad_normed * normed, r.inner, member * per_block + number)

        gather_stage(second, out_back, lambda i: line.pump(ready(base_out), 3 if i == SUPER else 2))
        share.start()
        line.release(turn, base_gate)
        r.grads[base_out : base_out + local, :] = tn(r.branch[...], r.ga[...]).astype(BF16)
        line.pump(ready(base_gate), 1)

        def in_grad_rows(number, base):
            cols = slice(number * local, (number + 1) * local)
            line.release(turn, base + local)
            for n in range(width // local):
                part_grad = tn(r.n1[:, n * local : (n + 1) * local], r.dx[:, cols])
                r.grads[base : base + local, n * local : (n + 1) * local] = part_grad.astype(BF16)

        if turn > 0:
            await_loads("n1")
        in_grad_rows(3, base_gate)
        line.pump(ready(base_qkv), 1)
        if turn > 0:
            await_loads(*attn_in)
        r.intot[...] = share.total() / width
        for chunk in range(length // 128):
            rows = slice(chunk * 128, (chunk + 1) * 128)
            scale = widen(r.scale[rows, :], local // 128)
            inner = widen(spread(r.intot[...], chunk), local // 128)
            normed = r.heads[rows, :] * scale
            r.dh[rows, :] = (scale * (r.gate[rows, :] - normed * inner)).astype(BF16)
        share.drain()
        second.drain()
        if turn + 1 < layers:
            load(layer - 1, *out_in)
        line.pump(ready(base_qkv), 1)
        between = line.done
        line.done += 1
        assert line.done <= ready(base_qkv)

        @pl.loop(0, heads_here)
        def _(head):
            @pl.when(head == 1)
            def _():
                line.tick(between + head - 1)

            wide = aligned(head * 2 * HDIM, 2 * HDIM)
            thin = aligned(head * HDIM, HDIM)
            for col_tile in range(tiles_here):
                cols = slice(col_tile * size, (col_tile + 1) * size)
                keys = r.k[cols, wide]
                values = r.v[cols, thin]
                acc_key, acc_value = None, None
                for row_tile in range(col_tile, tiles_here):
                    rows = slice(row_tile * size, (row_tile + 1) * size)
                    queries = r.q[rows, wide]
                    grads = r.dh[rows, thin]
                    weight = tile_weight(r, first_head, head, row_tile, col_tile, size)
                    scores = (nt(queries, keys) * weight).astype(BF16)
                    pulled = (nt(grads, values) * weight).astype(BF16)
                    term = nn(pulled, keys)
                    if col_tile == 0:
                        r.dq[rows, :] = term
                    else:
                        r.dq[rows, :] += term
                    key_term = tn(pulled, queries)
                    value_term = tn(scores, grads)
                    acc_key = key_term if acc_key is None else acc_key + key_term
                    acc_value = value_term if acc_value is None else acc_value + value_term
                r.dk[cols, :] = acc_key
                r.dx[cols, aligned(2 * local + head * HDIM, HDIM)] = acc_value.astype(BF16)
            for row_tile in range(tiles_here):
                rows = slice(row_tile * size, (row_tile + 1) * size)
                cosine, sine = r.cos[rows, :], r.sin[rows, :]
                for grad, lin, base in ((r.dq, r.ql, 0), (r.dk, r.kl, local)):
                    v = lin[rows, thin].astype(F32)
                    gate = 1.0 / (1.0 + jnp.exp(-v))
                    back = grad[rows, :HDIM] * cosine + grad[rows, HDIM:] * sine
                    back = back * (gate + v * gate * (1.0 - gate))
                    r.dx[rows, aligned(base + head * HDIM, HDIM)] = back.astype(BF16)

        if turn + 1 < layers:
            load(layer - 1, *attn_in)
            source = getattr(r, "mid%d_h" % (layer - 1))
            mid_pieces = [
                copies.start(source.at[:, pl.ds(n * 2 * HDIM, 2 * HDIM)], r.dq.at[pl.ds(n * block, block), :])
                for n in range(width // (2 * HDIM))
            ]
        if turn > 0:
            await_loads(*in_in)
        last = turn == layers - 1
        if last:
            for number in range(3):
                in_grad_rows(number, base_qkv + number * local)
        for part in range(SUPER):
            for step in (3, 1, 2, 0):
                rows = aligned(place.member(step) * block + part * part_rows, part_rows)
                total = None
                for n, w in enumerate((r.wq, r.wk, r.wv, r.wg)):
                    term = nt(r.dx[rows, n * local : (n + 1) * local], w[...])
                    total = term if total is None else total + term
                r.part1[rows, :] = total.astype(BF16)
                in_sum.send_block(part, step)
            line.pump(ready(cfg.chunks * CHUNK if last else base_qkv), 2 if last else 1)
        for number in range(3):
            if not last:
                in_grad_rows(number, base_qkv + number * local)
            line.pump(ready(base_qkv + (number + 1) * local), 2 if last else 1)
            if number < SUPER:
                in_sum.middle(number)
        if last:
            for part in range(SUPER):
                for which in (1, 2, 3):
                    out_sum.send_block(part, which)
        if turn + 1 < layers:
            load(layer - 1, *in_in, "n1")
        for part in range(SUPER):
            line.pump(ready(cfg.chunks * CHUNK), 2)
            for h in range(2):
                in_sum.finish(part, h)
                for i in range(half // step_rows):
                    offset = (2 * part + h) * half + i * step_rows
                    rows = slice(offset, offset + step_rows)
                    total = in_sum.total(part, h, i * step_rows, step_rows)
                    values = getattr(r, "x%d" % layer)[rows, :].astype(F32)
                    new = back_rows(total, values, r.gm[rows, :])
                    if layer > 0:
                        r.g[rows, :] = new
                        r.gd[aligned(own_start + offset, step_rows), :] = new.astype(BF16)
                    else:
                        r.go[rows, :] = new.astype(BF16)
            if layer > 0:
                firsts[layer - 1].start(part)
        in_sum.drain()
    line.more(2)
    for part in range(SUPER):
        out_sum.middle(part)
        line.more(2)
    folded = finish_forward(r.xo, None)
    r.stat_mine[3 * top : 3 * top + 3, :] = folded[0:3, :]
    stats.square()
    line.more(1)
    stats.pair()
    for number in range(cfg.pairs):
        line.more(1)
        stats.stage(number)
    out_sum.drain()
    stats.finish()
    line.more(line.ticks)


def call_kernel(body, cfg, inputs, outputs, scratch, collective_id, name):
    vmem, anywhere = pl.BlockSpec(memory_space=pltpu.VMEM), pl.BlockSpec(memory_space=pl.ANY)
    names = list(inputs) + list(outputs) + list(scratch)
    result = pl.pallas_call(
        functools.partial(body, cfg, names),
        out_shape=[shape for shape, _ in outputs.values()],
        in_specs=[vmem if placed else anywhere for _, placed in inputs.values()],
        out_specs=[vmem if placed else anywhere for _, placed in outputs.values()],
        scratch_shapes=list(scratch.values()),
        compiler_params=pltpu.CompilerParams(
            collective_id=collective_id, has_side_effects=collective_id is not None, vmem_limit_bytes=VMEM_LIMIT
        ),
        name=name,
    )(*[array for array, _ in inputs.values()])
    return dict(zip(outputs, result))


def collective_scratch(cfg, copies, lead):
    dma = pltpu.SemaphoreType.DMA
    half = cfg.block // (2 * SUPER)
    out = {}
    for name in ("ag1", "ag2", "rs1", "rs2"):
        for key in (name, "f" + name):
            out[key + "_send"] = out[key + "_recv"] = dma((*lead, SUPER, 6))
    for name in copies:
        out["land" + name] = pltpu.VMEM((SUPER, 6, half, cfg.width), BF16)
        out["part" + name] = pltpu.VMEM((cfg.length, cfg.width), BF16)
    out["local_sem"] = dma((96,))
    return out


def weight_scratch(cfg):
    v = pltpu.VMEM
    return dict(
        wq=v((cfg.width, cfg.local), BF16), wk=v((cfg.width, cfg.local), BF16),
        wv=v((cfg.width, cfg.local), BF16), wg=v((cfg.width, cfg.local), BF16),
        wo=v((cfg.local, cfg.width), BF16), wl=v((cfg.ff, cfg.width), BF16),
        wr=v((cfg.ff, cfg.width), BF16), wd=v((cfg.ff, cfg.width), BF16),
    )


def table_scratch(cfg):
    v = pltpu.VMEM
    return dict(
        segc=v((cfg.length, 128), F32), segf=v((8, 128), F32),
        tiles=v((cfg.heads_here, 2, cfg.block, cfg.block), F32),
    )


def forward_scratch(cfg):
    v, dma = pltpu.VMEM, pltpu.SemaphoreType.DMA
    rows, wide, local, ff, block = cfg.length, cfg.width, cfg.local, cfg.ff, cfg.block
    return dict(
        n1=v((rows, wide), BF16), ql=v((rows, local), BF16), kl=v((rows, local), BF16), q=v((rows, 2 * local), BF16),
        k=v((rows, 2 * local), BF16), v=v((rows, local), BF16), gate=v((rows, local), F32), heads=v((rows, local), F32),
        mid=v((block, wide), F32), n2=v((rows, wide), BF16), left=v((rows, ff), BF16), right=v((rows, ff), BF16),
        hid=v((rows, ff), BF16), ss=v((8, 128), F32), ss_mine=v((8, 128), F32), dh=v((rows, local), BF16),
        stat_wide=v((8, wide), F32), scale=v((rows, 128), F32), ss_land=v((cfg.layers, 3, 8, 128), F32),
        ss_send=dma((cfg.layers, 3)), ss_recv=dma((cfg.layers, 3)),
    )


def gather_sems():
    sems = pltpu.SemaphoreType.DMA((SUPER, 6))
    return dict(ag3_send=sems, ag3_recv=sems)


SAVED = ("ss", "mid", "n1", "ql", "kl", "q", "k", "v", "gate", "heads", "n2", "left", "right", "hid")


def run_layers(cfg, tokens, upstream, tables, weights):
    v, dma, s = pltpu.VMEM, pltpu.SemaphoreType.DMA, jax.ShapeDtypeStruct
    rows, wide, local, ff, block = cfg.length, cfg.width, cfg.local, cfg.ff, cfg.block
    inputs = dict(
        up=(upstream, True), x0=(tokens, True), **{k: (a, True) for k, a in tables.items()},
        **{k + "_h": (a, False) for k, a in weights.items()},
    )
    total_rows = cfg.chunks * CHUNK
    outputs = dict(
        xo=(s((block, wide), BF16), True), go=(s((block, wide), BF16), True), stat_total=(s((8, 128), F32), True),
        out_h=(s((cfg.layers * total_rows, wide), BF16), False),
    )
    small, ring, ring_sem = v((8, 128), F32), v((SLOTS, CHUNK // 2, wide), BF16), dma((SLOTS,))
    scratch = dict(
        **weight_scratch(cfg), **collective_scratch(cfg, ("1", "2"), (cfg.layers,)), **table_scratch(cfg), **forward_scratch(cfg),
        **gather_sems(),
        gd=v((rows, wide), BF16), ga=v((rows, wide), BF16),
        g=v((block, wide), F32), gm=v((block, wide), F32),
        branch=v((rows, local), BF16), dx=v((rows, 4 * local), BF16),
        dq=v((rows, 2 * HDIM), F32), dk=v((rows, 2 * HDIM), F32),
        grads=v((total_rows, wide), BF16),
        inner=small, intot=small,
        inner_land=v((cfg.layers, 3, 8, 128), F32), in_send=dma((cfg.layers, 3)), in_recv=dma((cfg.layers, 3)),
        pair_land=ring, right_land=ring, left_land=ring,
        pair_send=ring_sem, pair_recv=ring_sem, right_send=ring_sem, right_recv=ring_sem, left_send=ring_sem,
        left_recv=ring_sem, give_send=ring_sem, give_recv=ring_sem, keep_sem=ring_sem,
        stat_mine=small, stat_square=small, stat_pair=small, stat_right=small, stat_left=small,
        stat_land=v((3, 8, 128), F32), st_send=dma((3,)), st_recv=dma((3,)),
        line_land=v((3, 8, 128), F32), line_send=dma((3,)), line_recv=dma((3,)),
    )
    for layer in range(1, cfg.layers):
        scratch["x%d" % layer] = v((block, wide), F32)
    for layer in range(cfg.layers - 1):
        for key in SAVED:
            outputs["%s%d_h" % (key, layer)] = (s(scratch[key].shape, scratch[key].dtype), False)
    return call_kernel(layers_kernel, cfg, inputs, outputs, scratch, 0, "layers")


def widen_kernel(cfg, names, *refs):
    r = namespace(names, refs)
    tasks = []
    for layer in range(cfg.layers):
        for number, target in enumerate((r.down, r.left, r.right, r.out)):
            start, stop = cfg.bases[number], cfg.bases[number + 1]
            rows = (stop - start) // 2 if stop - start > 512 else stop - start
            for first in range(start, stop, rows):
                tasks.append((layer, first, rows, [(target.at[layer, pl.ds(first - start, rows), :], slice(None))]))
        for number, target in enumerate((r.gate, r.query, r.key, r.value)):
            pieces = [
                (target.at[layer, pl.ds(n * cfg.local, cfg.local), :], slice(n * cfg.local, (n + 1) * cfg.local))
                for n in range(cfg.width // cfg.local)
            ]
            start = cfg.bases[6] + (number - 1) * cfg.local if number > 0 else cfg.bases[4]
            tasks.append((layer, start, cfg.local, pieces))
    depth = WIDEN_DEPTH

    def fetch(task):
        layer, first, rows, _ = tasks[task]
        start = layer * cfg.chunks * CHUNK + first
        slot = task % depth
        return pltpu.make_async_copy(r.grads.at[pl.ds(start, rows), :], r.narrow.at[slot, pl.ds(0, rows), :], r.in_sem.at[slot])

    def store(task):
        _, _, rows, pieces = tasks[task]
        slot = task % depth
        return [
            pltpu.make_async_copy(r.wide.at[slot, pl.ds(0, rows), lanes], target, r.out_sem.at[slot, n])
            for n, (target, lanes) in enumerate(pieces)
        ]

    for task in range(min(depth, len(tasks))):
        fetch(task).start()
    for task in range(len(tasks)):
        slot, rows = task % depth, tasks[task][2]
        fetch(task).wait()
        if task >= depth:
            for copy in store(task - depth):
                copy.wait()

        @pl.loop(0, rows // 32)
        def _(i):
            part = aligned(i * 32, 32)
            r.wide[slot, part, :] = r.narrow[slot, part, :].astype(F32)

        for copy in store(task):
            copy.start()
        if task + depth < len(tasks):
            fetch(task + depth).start()
    for task in range(max(len(tasks) - depth, 0), len(tasks)):
        for copy in store(task):
            copy.wait()


def run_widen(cfg, grads):
    v, dma, s = pltpu.VMEM, pltpu.SemaphoreType.DMA, jax.ShapeDtypeStruct
    thin, flat = s((cfg.layers, cfg.width, cfg.local), F32), s((cfg.layers, cfg.ff, cfg.width), F32)
    outputs = dict(
        down=(flat, False), left=(flat, False), right=(flat, False), out=(s((cfg.layers, cfg.local, cfg.width), F32), False),
        gate=(thin, False), query=(thin, False), key=(thin, False), value=(thin, False),
    )
    rows = max(cfg.ff // 2, cfg.local, 512)
    scratch = dict(
        narrow=v((WIDEN_DEPTH, rows, cfg.width), BF16), wide=v((WIDEN_DEPTH, rows, cfg.width), F32),
        in_sem=dma((WIDEN_DEPTH,)), out_sem=dma((WIDEN_DEPTH, cfg.width // cfg.local)),
    )
    return call_kernel(widen_kernel, cfg, dict(grads=(grads, False)), outputs, scratch, None, "widen_gradients")


def per_device_square(
    tokens, upstream, segment_ids, query_proj, key_proj, value_proj, gate_proj, output_proj, left_proj, right_proj, down_proj
):
    layers = query_proj.shape[0]
    block, width = tokens.shape
    length = segment_ids.shape[0]
    local, ff = query_proj.shape[2], left_proj.shape[2]
    heads_here = local // HDIM
    positions = np.arange(length, dtype=np.float32)
    frequency = np.exp(np.float32(-math.log(10000.0)) * np.arange(HDIM, dtype=np.float32) / np.float32(HDIM))
    angles = positions[:, None] * frequency[None, :]
    slopes = np.exp2(-8.0 * (np.arange(HEADS) + 1.0) / HEADS)
    decays = np.concatenate([-slopes * (1.0 - depth_start - depth_step * layer) for layer in range(layers)])
    tables = dict(
        cos=jnp.asarray(np.cos(angles)), sin=jnp.asarray(np.sin(angles)),
        dec=jnp.asarray(np.broadcast_to(decays[:, None], (layers * HEADS, 128)).astype(np.float32)),
        seg=segment_ids.reshape(8, length // 8),
    )
    weights = dict(
        wq=query_proj, wk=key_proj, wv=value_proj, wg=gate_proj, wo=output_proj,
        wl=jnp.swapaxes(left_proj, 1, 2), wr=jnp.swapaxes(right_proj, 1, 2), wd=down_proj,
    )
    ends = np.cumsum([0, ff, ff, ff, local, local]).tolist()
    ends += [-(-ends[-1] // CHUNK) * CHUNK]
    ends += [-(-(ends[-1] + 3 * local) // CHUNK) * CHUNK]
    common = dict(
        layers=layers, block=block, length=length, width=width, local=local, ff=ff, heads_here=heads_here,
        pairs=lax.axis_size("dp") // 2, bases=ends, chunks=ends[-1] // CHUNK,
    )
    back = run_layers(types.SimpleNamespace(**common), tokens, upstream, tables, weights)
    stats = jnp.sum(back["stat_total"][: 3 * layers], axis=1).reshape(layers, 3)
    rms_stats = jnp.sqrt(stats / (length * lax.axis_size("dp") * width))
    wide = run_widen(types.SimpleNamespace(**common), back["out_h"])
    return (
        back["xo"], back["go"], wide["query"], wide["key"], wide["value"], wide["gate"], wide["out"],
        jnp.swapaxes(wide["left"], 1, 2), jnp.swapaxes(wide["right"], 1, 2), wide["down"], rms_stats,
    )


def solution(mesh):
    square = dict(mesh.shape) == SQUARE_MESH
    body = per_device_square if square else per_device
    return jax.shard_map(
        body,
        mesh=mesh,
        in_specs=(
            P(("dp", "tensor"), None),
            P(("dp", "tensor"), None),
            P("dp"),
            P(None, None, "tensor"),
            P(None, None, "tensor"),
            P(None, None, "tensor"),
            P(None, None, "tensor"),
            P(None, "tensor", None),
            P(None, None, "tensor"),
            P(None, None, "tensor"),
            P(None, "tensor", None),
        ),
        out_specs=(
            P(("dp", "tensor"), None),
            P(("dp", "tensor"), None),
            P(None, None, "tensor"),
            P(None, None, "tensor"),
            P(None, None, "tensor"),
            P(None, None, "tensor"),
            P(None, "tensor", None),
            P(None, None, "tensor"),
            P(None, None, "tensor"),
            P(None, "tensor", None),
            P(),
        ),
        check_vma=False,
    )
```

```python
import functools
import math
import types

import jax
import jax.numpy as jnp
import numpy as np
from jax import lax
from jax.experimental import pallas as pl
from jax.experimental.pallas import tpu as pltpu
from jax.sharding import PartitionSpec as P

HEADS = 8
HDIM = 128
BLK = 512


epsilon = 1e-06
depth_start = 0.5
depth_step = 1.0 / 24.0
highest = lax.Precision.HIGHEST


def rms_rows(values):
    return values * lax.rsqrt(jnp.mean(values * values, axis=1, keepdims=True) + epsilon)


def rms_back(values, gradient):
    scaling = lax.rsqrt(jnp.mean(values * values, axis=1, keepdims=True) + epsilon)
    normed = values * scaling
    return scaling * (gradient - normed * jnp.mean(gradient * normed, axis=1, keepdims=True))


def contract_last(left_part, right_part):
    return lax.dot_general(
        left_part, right_part, (((1,), (1,)), ((), ())), preferred_element_type=jnp.float32
    )


def contract_first(left_part, right_part):
    return lax.dot_general(
        left_part, right_part, (((0,), (0,)), ((), ())), preferred_element_type=jnp.float32
    )


def rotate(values, cosine, sine_table):
    return jnp.concatenate([values * cosine[:, None, :], values * sine_table[:, None, :]], axis=2)


def unrotate(gradient, cosine, sine_table):
    half_width = gradient.shape[2] // 2
    return (
        gradient[:, :, :half_width] * cosine[:, None, :]
        + gradient[:, :, half_width:] * sine_table[:, None, :]
    )


def split_blocks(array, block_count):
    return array.reshape((block_count, BLK) + array.shape[1:])


def block_weights(seg_block, next_seg, decay_log):
    block_width = seg_block.shape[0]
    places = jnp.arange(block_width, dtype=jnp.float32)
    distance = places[:, None] - places[None, :]
    allowed = (distance >= 0) & (seg_block[:, None] == seg_block[None, :])
    decay_grid = jnp.where(
        allowed[None], jnp.exp(decay_log[:, None, None] * jnp.maximum(distance, 0.0)[None]), 0.0
    )
    first_seg = seg_block[0]
    query_gain = jnp.where(
        (seg_block == first_seg)[:, None], jnp.exp(places[:, None] * decay_log[None, :]), 0.0
    )
    key_gain = jnp.where(
        (seg_block == next_seg)[:, None],
        jnp.exp((block_width - places)[:, None] * decay_log[None, :]),
        0.0,
    )
    carry_gain = jnp.where(first_seg == next_seg, jnp.exp(decay_log * block_width), 0.0)
    return (decay_grid, query_gain, key_gain, carry_gain)


def next_segments(segments, block_count):
    seg_blocks = segments.reshape(block_count, BLK)
    return (seg_blocks, jnp.concatenate([seg_blocks[1:, 0], jnp.full((1,), -1, jnp.int32)]))


def attend_forward(queries, keys_rot, values, segments, decay_log):
    length, heads_here, pair_width = queries.shape
    block_count = length // BLK
    seg_blocks, next_segs = next_segments(segments, block_count)

    def advance(state_now, block_items):
        query_block, key_block, value_block, seg_block, next_seg = block_items
        query_float = query_block.astype(jnp.float32)
        key_float = key_block.astype(jnp.float32)
        value_float = value_block.astype(jnp.float32)
        decay_grid, query_gain, key_gain, carry_gain = block_weights(seg_block, next_seg, decay_log)
        scores = (
            jnp.einsum("rhd,shd->hrs", query_block, key_block, preferred_element_type=jnp.float32)
            * decay_grid
        )
        block_out = jnp.einsum("hrs,she->rhe", scores, value_float, precision=highest)
        block_out = (
            block_out
            + jnp.einsum("rhd,hde->rhe", query_float, state_now, precision=highest)
            * query_gain[:, :, None]
        )
        new_state = carry_gain[:, None, None] * state_now + jnp.einsum(
            "shd,she->hde", key_float * key_gain[:, :, None], value_float, precision=highest
        )
        return (new_state, (block_out, state_now))

    zero_state = jnp.zeros((heads_here, pair_width, pair_width // 2), jnp.float32)
    _, (block_outs, states) = lax.scan(
        advance,
        zero_state,
        (
            split_blocks(queries, block_count),
            split_blocks(keys_rot, block_count),
            split_blocks(values, block_count),
            seg_blocks,
            next_segs,
        ),
    )
    return (block_outs.reshape(length, heads_here * (pair_width // 2)), states)


def attend_backward(queries, keys_rot, values, segments, decay_log, states, grad_heads):
    length, heads_here, pair_width = queries.shape
    block_count = length // BLK
    seg_blocks, next_segs = next_segments(segments, block_count)

    def retreat(later_grad, block_items):
        query_block, key_block, value_block, seg_block, next_seg, state_now, grad_block = (
            block_items
        )
        query_float = query_block.astype(jnp.float32)
        key_float = key_block.astype(jnp.float32)
        value_float = value_block.astype(jnp.float32)
        decay_grid, query_gain, key_gain, carry_gain = block_weights(seg_block, next_seg, decay_log)
        scores = (
            jnp.einsum("rhd,shd->hrs", query_block, key_block, preferred_element_type=jnp.float32)
            * decay_grid
        )
        pulled = jnp.einsum("rhe,she->hrs", grad_block, value_float, precision=highest) * decay_grid
        grad_query = jnp.einsum("hrs,shd->rhd", pulled, key_float, precision=highest)
        grad_query = (
            grad_query
            + jnp.einsum("rhe,hde->rhd", grad_block, state_now, precision=highest)
            * query_gain[:, :, None]
        )
        grad_key = jnp.einsum("hrs,rhd->shd", pulled, query_float, precision=highest)
        grad_key = (
            grad_key
            + jnp.einsum("she,hde->shd", value_float, later_grad, precision=highest)
            * key_gain[:, :, None]
        )
        grad_value = jnp.einsum("hrs,rhe->she", scores, grad_block, precision=highest)
        grad_value = (
            grad_value
            + jnp.einsum("shd,hde->she", key_float, later_grad, precision=highest)
            * key_gain[:, :, None]
        )
        earlier_grad = carry_gain[:, None, None] * later_grad + jnp.einsum(
            "rhd,rhe->hde", query_float * query_gain[:, :, None], grad_block, precision=highest
        )
        return (earlier_grad, (grad_query, grad_key, grad_value))

    zero_state = jnp.zeros((heads_here, pair_width, pair_width // 2), jnp.float32)
    _, (grad_query, grad_key, grad_value) = lax.scan(
        retreat,
        zero_state,
        (
            split_blocks(queries, block_count),
            split_blocks(keys_rot, block_count),
            split_blocks(values, block_count),
            seg_blocks,
            next_segs,
            states,
            split_blocks(grad_heads, block_count),
        ),
        reverse=True,
    )
    return (
        grad_query.reshape(length, heads_here, pair_width),
        grad_key.reshape(length, heads_here, pair_width),
        grad_value.reshape(length, heads_here, pair_width // 2),
    )


def per_device(
    tokens,
    upstream,
    segment_ids,
    query_proj,
    key_proj,
    value_proj,
    gate_proj,
    output_proj,
    left_proj,
    right_proj,
    down_proj,
):
    layers = query_proj.shape[0]
    row_count, model_width = tokens.shape
    length = segment_ids.shape[0]
    local_width = query_proj.shape[2]
    ff_local = left_proj.shape[2]
    heads_here = local_width // HDIM
    positions = jnp.arange(length, dtype=jnp.float32)
    frequency = jnp.exp(-math.log(10000.0) * jnp.arange(HDIM, dtype=jnp.float32) / HDIM)
    angles = positions[:, None] * frequency[None, :]
    cosine = jnp.cos(angles)
    sine_table = jnp.sin(angles)
    head_index = (lax.axis_index("tensor") * heads_here + jnp.arange(heads_here)).astype(
        jnp.float32
    )
    slopes = jnp.exp2(-8.0 * (head_index + 1.0) / HEADS)

    def gather_normed(normed):
        return lax.all_gather(normed, "tensor", axis=0, tiled=True)

    def gather_again(normed):
        return lax.all_gather(normed, "tensor", axis=0, tiled=True)

    def gather_grads(gradient):
        return lax.all_gather(gradient, "tensor", axis=0, tiled=True)

    def branch_sum(operand, matrix):
        return lax.psum_scatter(
            jnp.dot(operand, matrix, preferred_element_type=jnp.float32).astype(jnp.bfloat16),
            "tensor",
            scatter_dimension=0,
            tiled=True,
        ).astype(jnp.float32)

    def input_sum(pieces, matrix):
        operand = jnp.concatenate(pieces, axis=1)
        return lax.psum_scatter(
            contract_last(operand, matrix).astype(jnp.bfloat16),
            "tensor",
            scatter_dimension=0,
            tiled=True,
        ).astype(jnp.float32)

    current = tokens.astype(jnp.float32)
    saved_layers = []
    stat_terms = []
    for layer_index in range(layers):
        residual = current
        normed = rms_rows(residual).astype(jnp.bfloat16)
        full_normed = gather_normed(normed)
        attn_weight = jnp.concatenate(
            [
                query_proj[layer_index],
                key_proj[layer_index],
                value_proj[layer_index],
                gate_proj[layer_index],
            ],
            axis=1,
        )
        projected = jnp.dot(full_normed, attn_weight, preferred_element_type=jnp.float32)
        query_lin = projected[:, :local_width]
        key_lin = projected[:, local_width : 2 * local_width]
        values = (
            projected[:, 2 * local_width : 3 * local_width]
            .astype(jnp.bfloat16)
            .reshape(length, heads_here, HDIM)
        )
        gate_lin = projected[:, 3 * local_width :]
        queries = rotate(
            jax.nn.silu(query_lin).reshape(length, heads_here, HDIM), cosine, sine_table
        ).astype(jnp.bfloat16)
        keys_rot = rotate(
            jax.nn.silu(key_lin).reshape(length, heads_here, HDIM), cosine, sine_table
        ).astype(jnp.bfloat16)
        decay_log = -slopes * (1.0 - depth_start - depth_step * layer_index)
        heads_out, states = attend_forward(queries, keys_rot, values, segment_ids, decay_log)
        squares = lax.psum(jnp.sum(heads_out * heads_out, axis=1), "tensor")
        scaling = lax.rsqrt(squares / model_width + epsilon)[:, None]
        normed_heads = heads_out * scaling
        branch = (normed_heads * gate_lin).astype(jnp.bfloat16)
        attn_rows = branch_sum(branch, output_proj[layer_index])
        middle = residual + attn_rows
        normed_mid = rms_rows(middle).astype(jnp.bfloat16)
        full_mid = gather_normed(normed_mid)
        glu_weight = jnp.concatenate([left_proj[layer_index], right_proj[layer_index]], axis=1)
        gates_both = jnp.dot(full_mid, glu_weight, preferred_element_type=jnp.float32)
        left_lin = gates_both[:, :ff_local]
        right_lin = gates_both[:, ff_local:]
        hidden = (left_lin * right_lin).astype(jnp.bfloat16)
        glu_rows = branch_sum(hidden, down_proj[layer_index])
        current = middle + glu_rows
        stat_terms.append(
            jnp.stack(
                [
                    jnp.sum(attn_rows * attn_rows),
                    jnp.sum(glu_rows * glu_rows),
                    jnp.sum(current * current),
                ]
            )
        )
        saved_layers.append(
            (
                residual,
                middle,
                normed,
                normed_mid,
                full_normed,
                full_mid,
                attn_weight,
                glu_weight,
                query_lin,
                key_lin,
                gate_lin,
                queries,
                keys_rot,
                values,
                decay_log,
                states,
                normed_heads,
                scaling,
                branch,
                left_lin,
                right_lin,
                hidden,
            )
        )
    stat_sums = lax.psum(jnp.stack(stat_terms), ("dp", "tensor"))
    rms_stats = jnp.sqrt(stat_sums / (length * lax.axis_size("dp") * model_width))
    final_rows = current.astype(jnp.bfloat16)
    gradient = upstream.astype(jnp.float32)
    layer_results = [None] * layers
    for layer_index in reversed(range(layers)):
        (
            residual,
            middle,
            normed,
            normed_mid,
            full_normed,
            full_mid,
            attn_weight,
            glu_weight,
            query_lin,
            key_lin,
            gate_lin,
            queries,
            keys_rot,
            values,
            decay_log,
            states,
            normed_heads,
            scaling,
            branch,
            left_lin,
            right_lin,
            hidden,
        ) = saved_layers[layer_index]
        glu_grad = gather_grads(gradient.astype(jnp.bfloat16))
        grad_hidden = contract_last(glu_grad, down_proj[layer_index])
        down_part = contract_first(hidden, glu_grad)
        grad_left = (grad_hidden * right_lin).astype(jnp.bfloat16)
        grad_right = (grad_hidden * left_lin).astype(jnp.bfloat16)
        grad_gates = jnp.concatenate([grad_left, grad_right], axis=1)
        mid_rows = input_sum((grad_left, grad_right), glu_weight)
        source_mid = gather_again(normed_mid)
        glu_part = contract_first(source_mid, grad_gates)
        gradient = gradient + rms_back(middle, mid_rows)
        attn_grad = gather_grads(gradient.astype(jnp.bfloat16))
        output_part = contract_first(branch, attn_grad)
        grad_branch = contract_last(attn_grad, output_proj[layer_index])
        grad_normed = grad_branch * gate_lin
        grad_gate = (grad_branch * normed_heads).astype(jnp.bfloat16)
        inner_sum = lax.psum(jnp.sum(grad_normed * normed_heads, axis=1), "tensor")
        grad_heads = scaling * (grad_normed - normed_heads * (inner_sum / model_width)[:, None])
        grad_query, grad_key, grad_value = attend_backward(
            queries,
            keys_rot,
            values,
            segment_ids,
            decay_log,
            states,
            grad_heads.reshape(length, heads_here, HDIM),
        )
        sigmoid_query = jax.nn.sigmoid(query_lin)
        sigmoid_key = jax.nn.sigmoid(key_lin)
        query_back = unrotate(grad_query, cosine, sine_table).reshape(length, local_width)
        key_back = unrotate(grad_key, cosine, sine_table).reshape(length, local_width)
        grad_query_lin = (
            query_back * (sigmoid_query + query_lin * sigmoid_query * (1.0 - sigmoid_query))
        ).astype(jnp.bfloat16)
        grad_key_lin = (
            key_back * (sigmoid_key + key_lin * sigmoid_key * (1.0 - sigmoid_key))
        ).astype(jnp.bfloat16)
        grad_value_lin = grad_value.reshape(length, local_width).astype(jnp.bfloat16)
        grad_projected = jnp.concatenate(
            [grad_query_lin, grad_key_lin, grad_value_lin, grad_gate], axis=1
        )
        in_rows = input_sum((grad_query_lin, grad_key_lin, grad_value_lin, grad_gate), attn_weight)
        source_normed = gather_again(normed)
        attn_part = contract_first(source_normed, grad_projected)
        gradient = gradient + rms_back(residual, in_rows)
        query_part = attn_part[:, :local_width]
        key_part = attn_part[:, local_width : 2 * local_width]
        value_part = attn_part[:, 2 * local_width : 3 * local_width]
        gate_part = attn_part[:, 3 * local_width :]
        left_part = glu_part[:, :ff_local]
        right_part = glu_part[:, ff_local:]
        layer_results[layer_index] = (
            query_part,
            key_part,
            value_part,
            gate_part,
            output_part,
            left_part,
            right_part,
            down_part,
        )
    stacked = [
        jnp.stack([layer_results[index][member] for index in range(layers)]) for member in range(8)
    ]
    totals = (
        lax.psum(stacked[0].astype(jnp.bfloat16), "dp").astype(jnp.float32),
        lax.psum(stacked[1].astype(jnp.bfloat16), "dp").astype(jnp.float32),
        lax.psum(stacked[2].astype(jnp.bfloat16), "dp").astype(jnp.float32),
        lax.psum(stacked[3].astype(jnp.bfloat16), "dp").astype(jnp.float32),
        lax.psum(stacked[4].astype(jnp.bfloat16), "dp").astype(jnp.float32),
        lax.psum(stacked[5].astype(jnp.bfloat16), "dp").astype(jnp.float32),
        lax.psum(stacked[6].astype(jnp.bfloat16), "dp").astype(jnp.float32),
        lax.psum(stacked[7].astype(jnp.bfloat16), "dp").astype(jnp.float32),
    )
    input_grad = gradient.astype(jnp.bfloat16)
    return (
        final_rows,
        input_grad,
        totals[0],
        totals[1],
        totals[2],
        totals[3],
        totals[4],
        totals[5],
        totals[6],
        totals[7],
        rms_stats,
    )


SQUARE_MESH = {"dp": 8, "tensor": 4}


F32 = jnp.float32
BF16 = jnp.bfloat16
MESH = pl.DeviceIdType.MESH
VMEM_LIMIT = 62 * 2**20
SUPER = 2
EARLY = (0,)
WIDEN_DEPTH = 6
CHUNK = 128
HOP = 3
SLOTS = 16


def nn(a, b):
    return lax.dot_general(a, b, (((1,), (0,)), ((), ())), preferred_element_type=F32)


def nt(a, b):
    return lax.dot_general(a, b, (((1,), (1,)), ((), ())), preferred_element_type=F32)


def tn(a, b):
    return lax.dot_general(a, b, (((0,), (0,)), ((), ())), preferred_element_type=F32)


def exact(a, b, dims):
    return lax.dot_general(a, b, (dims, ((), ())), precision=highest, preferred_element_type=F32)


def aligned(index, size):
    return pl.ds(pl.multiple_of(index, size), size)


class Place:
    def __init__(self, pairs):
        self.dp = lax.axis_index("dp")
        self.me = lax.axis_index("tensor")
        self.low = lax.rem(self.me, 2)
        self.high = self.me // 2
        self.core = lax.rem(self.dp, 2)
        self.at = self.dp // 2
        self.last = pairs - 1

    def member(self, step):
        low = lax.rem(self.low + lax.rem(step, 2), 2)
        high = lax.rem(self.high + step // 2, 2)
        return 2 * high + low

    def device(self, step):
        return (self.dp, self.member(step))

    def partner(self):
        return (self.dp + 1 - 2 * self.core, self.me)

    def right(self):
        return (self.dp + 2, self.me)

    def left(self):
        return (self.dp - 2, self.me)

    def greet(self, line):
        barrier = pltpu.get_barrier_semaphore()

        def signal(device):
            pl.semaphore_signal(barrier, inc=1, device_id=device, device_id_type=MESH)

        for step in (1, 2, 3):
            signal(self.device(step))
        if not line:
            pl.semaphore_wait(barrier, 3)
            return
        signal(self.partner())

        @pl.when(self.at < self.last)
        def _():
            signal(self.right())

        @pl.when(self.at > 0)
        def _():
            signal(self.left())

        pl.semaphore_wait(barrier, 4 + jnp.minimum(self.at, 1) + jnp.minimum(self.last - self.at, 1))


class Wire:
    def __init__(self, device, send_sem, recv_sem, source, target, landing):
        self.source, self.target, self.landing = source, target, landing
        self.common = dict(send_sem=send_sem, recv_sem=recv_sem, device_id=device, device_id_type=MESH)

    def out(self):
        return pltpu.make_async_remote_copy(src_ref=self.source, dst_ref=self.target, **self.common)

    def start(self):
        self.out().start()

    def wait_recv(self):
        pltpu.make_async_remote_copy(src_ref=self.landing, dst_ref=self.landing, **self.common).wait_recv()

    def wait_send(self):
        self.out().wait_send()


class Gather:
    def __init__(self, place, buf, send, recv, block):
        self.place, self.buf, self.block = place, buf, block
        self.send, self.recv = send, recv
        self.half = block // (2 * SUPER)

    def rows(self, step, part, half):
        start = self.place.member(step) * self.block + (2 * part + half) * self.half
        return self.buf.at[aligned(start, self.half)]

    def wire(self, part, number):
        step, owner, half = ((1, 0, 0), (2, 0, 1), (1, 0, 1), (2, 0, 0), (2, 1, 0), (1, 2, 1))[number]
        source = self.rows(owner, part, half)
        landing = self.rows((0, 1, 2, 3)[owner ^ step], part, half)
        return Wire(self.place.device(step), self.send.at[part, number], self.recv.at[part, number], source, source, landing)

    def start(self, part):
        for number in range(4):
            self.wire(part, number).start()

    def forward(self, part):
        self.wire(part, 0).wait_recv()
        self.wire(part, 4).start()
        self.wire(part, 1).wait_recv()
        self.wire(part, 5).start()

    def finish(self, part, step):
        for number in {0: (), 1: (2,), 2: (3,), 3: (4, 5)}[step]:
            self.wire(part, number).wait_recv()

    def drain(self, parts=range(SUPER)):
        for part in parts:
            for number in range(6):
                self.wire(part, number).wait_send()


def gather_stage(gather, block_fn, beside):
    @pl.loop(0, 4 * SUPER)
    def _(i):
        mixed = i - SUPER
        part = jnp.where(i < SUPER, i, jnp.where(i < 3 * SUPER, mixed // 2, i - 3 * SUPER))
        step = jnp.where(i < SUPER, 0, jnp.where(i < 3 * SUPER, 1 + lax.rem(mixed, 2), 3))

        @pl.when(i == SUPER)
        def _():
            for one in range(SUPER):
                beside(one)
                gather.forward(one)

        @pl.when(i == 3 * SUPER)
        def _():
            beside(SUPER)

        for which in (1, 2, 3):
            @pl.when(step == which)
            def _():
                gather.finish(part, which)
        block_fn(part, step)


class Scatter:
    def __init__(self, place, buf, land, send, recv, block):
        self.place, self.buf, self.land, self.block = place, buf, land, block
        self.send, self.recv = send, recv
        self.half = block // (2 * SUPER)

    def rows(self, step, part, half):
        start = self.place.member(step) * self.block + (2 * part + half) * self.half
        return aligned(start, self.half)

    def wire(self, part, number):
        step, owner, half = ((1, 3, 0), (1, 1, 0), (2, 3, 1), (2, 2, 1), (2, 2, 0), (1, 1, 1))[number]
        target = self.land.at[part, number]
        return Wire(
            self.place.device(step), self.send.at[part, number], self.recv.at[part, number],
            self.buf.at[self.rows(owner, part, half)], target, target,
        )

    def send_block(self, part, step):
        for number in {0: (), 1: (1,), 2: (3,), 3: (0, 2)}[step]:
            self.wire(part, number).start()

    def middle(self, part):
        for first, second, owner, half in ((0, 4, 2, 0), (2, 5, 1, 1)):
            self.wire(part, first).wait_recv()
            rows = self.rows(owner, part, half)
            self.buf[rows, :] = self.buf[rows, :] + self.land[part, first]
            self.wire(part, second).start()

    def finish(self, part, half):
        first, second = ((1, 4), (3, 5))[half]
        self.wire(part, first).wait_recv()
        self.wire(part, second).wait_recv()

    def total(self, part, half, start, count):
        first, second = ((1, 4), (3, 5))[half]
        own = self.place.me * self.block + (2 * part + half) * self.half + start
        rows = pl.ds(start, count)
        return (
            self.buf[aligned(own, count), :].astype(F32)
            + self.land[part, first, rows, :].astype(F32)
            + self.land[part, second, rows, :].astype(F32)
        )

    def drain(self):
        for part in range(SUPER):
            for number in range(6):
                self.wire(part, number).wait_send()


class Share:
    def __init__(self, place, mine, land, send, recv):
        self.wires = [
            Wire(place.device(step), send.at[step - 1], recv.at[step - 1], mine, land.at[step - 1], land.at[step - 1])
            for step in (1, 2, 3)
        ]
        self.mine, self.land = mine, land

    def start(self):
        for wire in self.wires:
            wire.start()

    def total(self):
        for wire in self.wires:
            wire.wait_recv()
        return self.mine[...] + self.land[0] + self.land[1] + self.land[2]

    def drain(self):
        for wire in self.wires:
            wire.wait_send()


class Local:
    def __init__(self, sems):
        self.sems, self.used = sems, 0

    def start(self, source, target):
        copy = pltpu.make_async_copy(source, target, self.sems.at[self.used])
        self.used += 1
        copy.start()
        return copy


def row_sums(values, target, chunk):
    sums = exact(jnp.ones((8, values.shape[1]), F32), values, ((1,), (1,)))
    target[pl.ds(chunk, 1), :] = sums[0:1, :]


def spread(sums, chunk):
    picked = (lax.broadcasted_iota(jnp.int32, (8, 128), 0) == chunk).astype(F32)
    return exact(sums, picked, ((0,), (0,)))


def widen(columns, times):
    return jnp.concatenate([columns] * times, axis=1)


def decay_tiles(dec_ref, first_head, tiles, heads_here, size):
    rows = lax.broadcasted_iota(jnp.int32, (size, size), 0)
    cols = lax.broadcasted_iota(jnp.int32, (size, size), 1)
    distance = (rows - cols).astype(F32)
    for head in range(heads_here):
        decay = dec_ref[pl.ds(first_head + head, 1), 0:1]
        tiles[head, 0] = jnp.where(rows >= cols, jnp.exp(decay * jnp.maximum(distance, 0.0)), 0.0)
        tiles[head, 1] = jnp.exp(decay * (distance + float(size)))


def spread_segments(r, length):
    r.segf[...] = r.seg[...].astype(F32)
    for chunk in range(length // 128):
        r.segc[chunk * 128 : (chunk + 1) * 128, :] = spread(r.segf[...], chunk)


def tile_weight(r, first_head, head, row_tile, col_tile, size):
    gap = row_tile - col_tile
    if gap == 0:
        weight = r.tiles[head, 0]
    else:
        weight = r.tiles[head, 1]
        if gap > 1:
            decay = r.dec[pl.ds(first_head + head, 1), 0:1]
            weight = weight * jnp.exp(decay * float(size * (gap - 1)))
    row_seg = widen(r.segc[row_tile * size : (row_tile + 1) * size, :], size // 128)
    per = size // 128
    col_seg = jnp.concatenate([r.segf[per * col_tile + i : per * col_tile + i + 1, :] for i in range(per)], axis=1)
    return jnp.where(row_seg == col_seg, weight, 0.0)


def namespace(names, refs):
    return types.SimpleNamespace(**dict(zip(names, refs)))


def forward_front(cfg, r, place, copies, layer, x, save, third, third_parts, back_block):
    block, length, width = cfg.block, cfg.length, cfg.width
    heads_here, size = cfg.heads_here, cfg.block
    first_head = layer * HEADS + place.me * heads_here
    w_in = [copies.start(h.at[layer], v) for h, v in (
        (r.wq_h, r.wq), (r.wk_h, r.wk), (r.wv_h, r.wv), (r.wg_h, r.wg))]
    w_out = copies.start(r.wo_h.at[layer], r.wo)
    w_glu = [copies.start(h.at[layer], v) for h, v in ((r.wl_h, r.wl), (r.wr_h, r.wr), (r.wd_h, r.wd))]
    first = Gather(place, r.n1, r.fag1_send.at[layer], r.fag1_recv.at[layer], block)
    mid_sum = Scatter(place, r.part1, r.land1, r.frs1_send.at[layer], r.frs1_recv.at[layer], block)
    second = Gather(place, r.n2, r.fag2_send.at[layer], r.fag2_recv.at[layer], block)
    out_sum = Scatter(place, r.part2, r.land2, r.frs2_send.at[layer], r.frs2_recv.at[layer], block)
    share = Share(place, r.ss_mine, r.ss_land.at[layer], r.ss_send.at[layer], r.ss_recv.at[layer])
    half, step_rows = first.half, 32
    own_start = place.me * block

    if layer == 0:
        @pl.loop(0, block // step_rows)
        def _(i):
            rows = aligned(i * step_rows, step_rows)
            v = x[rows, :].astype(F32)
            scale = lax.rsqrt(jnp.mean(v * v, axis=1, keepdims=True) + epsilon)
            r.n1[aligned(own_start + i * step_rows, step_rows), :] = (v * scale).astype(BF16)

        place.greet(True)
        for part in range(SUPER):
            first.start(part)
        spread_segments(r, length)
    decay_tiles(r.dec, first_head, r.tiles, heads_here, size)
    for copy in w_in:
        copy.wait()

    @pl.loop(0, 4)
    def _(step):
        @pl.when(step == 1)
        def _():
            for part in range(SUPER):
                first.forward(part)
        for which in (1, 2, 3):
            @pl.when(step == which)
            def _():
                for part in range(SUPER):
                    first.finish(part, which)
        rows = aligned(place.member(step) * block, block)
        a = r.n1[rows, :]
        cosine, sine = r.cos[rows, :], r.sin[rows, :]
        for w, lin, rot in ((r.wq, r.ql, r.q), (r.wk, r.kl, r.k)):
            v = nn(a, w[...])
            lin[rows, :] = v.astype(BF16)
            v = v / (1.0 + jnp.exp(-v))
            for head in range(heads_here):
                one = v[:, head * HDIM : (head + 1) * HDIM]
                rot[rows, 2 * head * HDIM : (2 * head + 1) * HDIM] = (one * cosine).astype(BF16)
                rot[rows, (2 * head + 1) * HDIM : (2 * head + 2) * HDIM] = (one * sine).astype(BF16)
        r.v[rows, :] = nn(a, r.wv[...]).astype(BF16)
        r.gate[rows, :] = nn(a, r.wg[...])

    save("n1", "ql", "kl", "q", "k", "v", "gate")
    if third_parts:
        for part in third_parts:
            third.start(part)
    w_out.wait()
    part_rows, per = 2 * half, size // 128
    heads = range(heads_here)
    wide = [slice(head * 2 * HDIM, (head + 1) * 2 * HDIM) for head in heads]
    thin = [slice(head * HDIM, (head + 1) * HDIM) for head in heads]
    decay = [r.dec[pl.ds(first_head + head, 1), 0:1] for head in heads]

    @pl.loop(0, 4)
    def _(i):
        step = jnp.where(i == 0, 3, jnp.where(i == 3, 0, i))
        row_tile = place.member(step)
        rows = aligned(row_tile * size, size)
        row_seg = widen(r.segc[rows, :], per)
        queries = [r.q[rows, wide[head]] for head in heads]

        def terms(col_tile, weights):
            cols = aligned(col_tile * size, size)
            col_seg = jnp.concatenate([r.segf[pl.ds(per * col_tile + n, 1), :] for n in range(per)], axis=1)
            same = row_seg == col_seg
            out = []
            for head in heads:
                scores = nt(queries[head], r.k[cols, wide[head]]) * jnp.where(same, weights[head], 0.0)
                out.append(nn(scores.astype(BF16), r.v[cols, thin[head]]))
            return tuple(out)

        def add(col_tile, sums):
            gap = (size * (row_tile - col_tile - 1)).astype(F32)
            more = terms(col_tile, [r.tiles[head, 1] * jnp.exp(decay[head] * gap) for head in heads])
            return tuple(one + other for one, other in zip(sums, more))

        sums = lax.fori_loop(0, row_tile, add, terms(row_tile, [r.tiles[head, 0] for head in heads]))
        for head in heads:
            r.heads[rows, thin[head]] = sums[head]
            r.dh[rows, thin[head]] = (sums[head] * r.gate[rows, thin[head]]).astype(BF16)
        for part in range(SUPER):
            some = aligned(row_tile * block + part * part_rows, part_rows)
            r.part1[some, :] = nn(r.dh[some, :], r.wo[...]).astype(BF16)
            for which in (1, 2, 3):
                @pl.when(step == which)
                def _():
                    mid_sum.send_block(part, which)
        for n in range(per):
            v = r.heads[aligned(row_tile * size + n * 128, 128), :]
            row_sums(v * v, r.ss_mine, row_tile * per + n)

    share.start()
    save("heads")
    if third_parts:
        for part in third_parts:
            third.forward(part)
    for part in range(SUPER):
        mid_sum.middle(part)
    r.ss[...] = share.total()
    save("ss")
    scaling = lax.rsqrt(r.ss[...] / width + epsilon)
    per_block = block // 128
    for chunk in range(per_block):
        r.scale[aligned(own_start + chunk * 128, 128), :] = spread(scaling, place.me * per_block + chunk)
    r.stat_wide[...] = jnp.zeros_like(r.stat_wide)

    def add_stat(row, v):
        sums = jnp.sum(v * v, axis=0, keepdims=True)
        r.stat_wide[row : row + 1, :] += sums

    step_rows = min(32, half)
    for part in range(SUPER):
        for h in range(2):
            mid_sum.finish(part, h)
            for i in range(half // step_rows):
                offset = (2 * part + h) * half + i * step_rows
                scale = widen(r.scale[aligned(own_start + offset, step_rows), :], width // 128)
                attn = mid_sum.total(part, h, i * step_rows, step_rows) * scale
                middle = x[offset : offset + step_rows, :].astype(F32) + attn
                r.mid[offset : offset + step_rows, :] = middle
                add_stat(0, attn)
                norm = lax.rsqrt(jnp.mean(middle * middle, axis=1, keepdims=True) + epsilon)
                r.n2[aligned(own_start + offset, step_rows), :] = (middle * norm).astype(BF16)
        second.start(part)
    save("mid")
    for copy in w_glu:
        copy.wait()
    if third_parts:
        for part in third_parts:
            for which in (1, 2, 3):
                third.finish(part, which)
    if back_block is not None:
        mid_sum.drain()

    def glu(part, step):
        rows = aligned(place.member(step) * block + part * part_rows, part_rows)
        a = r.n2[rows, :]
        left = nt(a, r.wl[...])
        right = nt(a, r.wr[...])
        hidden = (left * right).astype(BF16)
        r.hid[rows, :] = hidden
        if back_block is not None:
            back_block(rows, left, right, part, step)
        else:
            r.left[rows, :] = left.astype(BF16)
            r.right[rows, :] = right.astype(BF16)
        r.part2[rows, :] = nn(hidden, r.wd[...]).astype(BF16)
        if back_block is None:
            for which in (1, 2, 3):
                @pl.when(step == which)
                def _():
                    out_sum.send_block(part, which)

    gather_stage(second, glu, lambda i: None)

    def finish(target, following):
        for part in range(SUPER):
            for h in range(2):
                out_sum.finish(part, h)
                for i in range(half // step_rows):
                    offset = (2 * part + h) * half + i * step_rows
                    glu_rows = out_sum.total(part, h, i * step_rows, step_rows)
                    after = r.mid[offset : offset + step_rows, :] + glu_rows
                    target[offset : offset + step_rows, :] = after.astype(target.dtype)
                    add_stat(1, glu_rows)
                    add_stat(2, after)
                    if following is not None:
                        norm = lax.rsqrt(jnp.mean(after * after, axis=1, keepdims=True) + epsilon)
                        r.n1[aligned(own_start + offset, step_rows), :] = (after * norm).astype(BF16)
            if following is not None:
                following.start(part)
        folded = r.stat_wide[:, :128]
        for n in range(1, width // 128):
            folded = folded + r.stat_wide[:, n * 128 : (n + 1) * 128]
        return folded

    groups = [first, second, share] + ([mid_sum] if back_block is None else [])
    return out_sum, finish, groups


def turns_of(k, size, count):
    return sum(((k >= size * n).astype(jnp.int32) for n in range(1, -(-count // size))), jnp.int32(0))


class Line:
    def __init__(self, cfg, place, r):
        self.place, self.r = place, r
        self.per, self.count = cfg.chunks, cfg.chunks * cfg.layers
        self.layers, self.rows_each = cfg.layers, cfg.chunks * CHUNK
        self.half = CHUNK // 2
        self.ticks = self.count + 3 + HOP * place.last
        self.done = 0

    def slot(self, k):
        return k - SLOTS * turns_of(k, SLOTS, self.count)

    def rows(self, k, core):
        place = k - self.per * turns_of(k, self.per, self.count)
        return aligned(place * CHUNK + core * self.half, self.half)

    def own(self, k):
        return self.rows(k, self.place.core)

    def out_rows(self, k, core):
        turn = turns_of(k, self.per, self.count)
        place = (self.layers - 1 - turn) * self.per + k - turn * self.per
        start = place * CHUNK + core * self.half
        return aligned(start, self.half)

    def pair(self, k):
        slot = self.slot(k)
        r = self.r
        return Wire(self.place.partner(), r.pair_send.at[slot], r.pair_recv.at[slot],
                    r.grads.at[self.rows(k, 1 - self.place.core)], r.pair_land.at[slot], r.pair_land.at[slot])

    def hop(self, k, land, send, recv, device):
        slot = self.slot(k)
        return Wire(device, send.at[slot], recv.at[slot], land.at[slot], land.at[slot], land.at[slot])

    def going_right(self, k):
        return self.hop(k, self.r.right_land, self.r.right_send, self.r.right_recv, self.place.right())

    def going_left(self, k):
        return self.hop(k, self.r.left_land, self.r.left_send, self.r.left_recv, self.place.left())

    def coming_right(self, k):
        return self.hop(k, self.r.right_land, self.r.right_send, self.r.right_recv, self.place.left())

    def coming_left(self, k):
        return self.hop(k, self.r.left_land, self.r.left_send, self.r.left_recv, self.place.right())

    def result(self, k):
        slot, r = self.slot(k), self.r
        return Wire(self.place.partner(), r.give_send.at[slot], r.give_recv.at[slot],
                    r.grads.at[self.own(k)], r.out_h.at[self.out_rows(k, self.place.core)],
                    r.out_h.at[self.out_rows(k, 1 - self.place.core)])

    def keep(self, k):
        slot, r = self.slot(k), self.r
        return pltpu.make_async_copy(
            r.grads.at[self.own(k)], r.out_h.at[self.out_rows(k, self.place.core)], r.keep_sem.at[slot]
        )

    def one_way(self, k, land, start_here, coming, ends_here, going):
        slot = self.slot(k)

        @pl.when(start_here)
        def _():
            land[slot] = self.r.grads[self.own(k), :]

        @pl.when(jnp.logical_not(start_here))
        def _():
            coming(k).wait_recv()
            land[slot] = land[slot] + self.r.grads[self.own(k), :]

        @pl.when(jnp.logical_not(ends_here))
        def _():
            going(k).start()

    def tick(self, n):
        place, r, last = self.place, self.r, self.place.last
        at_left, at_right = place.at == 0, place.at == last

        @pl.when(n < self.count)
        def _():
            self.pair(n).start()

        k = n - 1

        @pl.when(jnp.logical_and(k >= 0, k < self.count))
        def _():
            wire = self.pair(k)
            wire.wait_recv()
            wire.wait_send()
            slot = self.slot(k)
            r.grads[self.own(k), :] = r.grads[self.own(k), :] + r.pair_land[slot]

        left_k = n - 1 - HOP * (last - place.at)

        @pl.when(jnp.logical_and(left_k >= 0, left_k < self.count))
        def _():
            self.one_way(left_k, r.left_land, at_right, self.coming_left, at_left, self.going_left)

        right_k = n - 1 - HOP * place.at

        @pl.when(jnp.logical_and(right_k >= 0, right_k < self.count))
        def _():
            self.one_way(right_k, r.right_land, at_left, self.coming_right, at_right, self.going_right)

        full_k = n - 1 - HOP * last

        @pl.when(jnp.logical_and(full_k >= 0, full_k < self.count))
        def _():
            @pl.when(jnp.logical_not(at_right))
            def _():
                self.going_right(full_k).wait_send()

            @pl.when(jnp.logical_not(at_left))
            def _():
                self.going_left(full_k).wait_send()

            slot = self.slot(full_k)
            own = self.own(full_k)
            total = r.right_land[slot].astype(F32) + r.left_land[slot].astype(F32) - r.grads[own, :].astype(F32)
            r.grads[own, :] = total.astype(BF16)
            self.result(full_k).start()
            self.keep(full_k).start()

        old_k = full_k - 2

        @pl.when(jnp.logical_and(old_k >= 0, old_k < self.count))
        def _():
            wire = self.result(old_k)
            wire.wait_recv()
            wire.wait_send()
            self.keep(old_k).wait()

    def pump(self, ready, most):
        stop = min(self.done + most, ready)
        if stop > self.done:
            start, self.done = self.done, stop

            @pl.loop(start, stop)
            def _(n):
                self.tick(n)

    def release(self, turn, rows):
        needed = (turn - 1) * self.per + -(-rows // CHUNK) + 3 + HOP * self.place.last
        if turn > 0 and needed > self.done:
            self.pump(turn * self.per, needed - self.done)
            assert self.done >= needed

    def more(self, most):
        self.pump(self.ticks, most)


class StatLine:
    def __init__(self, place, r):
        self.place, self.r = place, r
        self.share = Share(place, r.stat_mine, r.stat_land, r.st_send, r.st_recv)

    def square(self):
        self.share.start()

    def pair(self):
        r = self.r
        r.stat_square[...] = self.share.total()
        self.wire(0, self.place.partner(), r.stat_square).start()

    def wire(self, number, device, source):
        r = self.r
        return Wire(device, r.line_send.at[number], r.line_recv.at[number], source, r.line_land.at[number], r.line_land.at[number])

    def stage(self, number):
        place, r = self.place, self.r
        if number == 0:
            self.wire(0, place.partner(), r.stat_square).wait_recv()
            r.stat_pair[...] = r.stat_square[...] + r.line_land[0]
            r.stat_right[...] = r.stat_pair[...]
            r.stat_left[...] = r.stat_pair[...]
        else:
            @pl.when(place.at == number)
            def _():
                self.wire(1, place.left(), r.stat_right).wait_recv()
                r.stat_right[...] = r.stat_pair[...] + r.line_land[1]

            @pl.when(place.last - place.at == number)
            def _():
                self.wire(2, place.right(), r.stat_left).wait_recv()
                r.stat_left[...] = r.stat_pair[...] + r.line_land[2]
        if number < place.last:
            @pl.when(place.at == number)
            def _():
                self.wire(1, place.right(), r.stat_right).start()

            @pl.when(place.last - place.at == number)
            def _():
                self.wire(2, place.left(), r.stat_left).start()

    def finish(self):
        place, r = self.place, self.r
        r.stat_total[...] = r.stat_right[...] + r.stat_left[...] - r.stat_pair[...]
        self.share.drain()
        self.wire(0, place.partner(), r.stat_square).wait_send()

        @pl.when(place.at < place.last)
        def _():
            self.wire(1, place.right(), r.stat_right).wait_send()

        @pl.when(place.at > 0)
        def _():
            self.wire(2, place.left(), r.stat_left).wait_send()


def layers_kernel(cfg, names, *refs):
    r = namespace(names, refs)
    block, length, width, local, ff = cfg.block, cfg.length, cfg.width, cfg.local, cfg.ff
    heads_here, size, layers = cfg.heads_here, cfg.block, cfg.layers
    place = Place(cfg.pairs)
    copies = Local(r.local_sem)
    line = Line(cfg, place, r)
    stats = StatLine(place, r)
    loads = {}
    base_down, base_left, base_right, base_out, base_gate, gate_end, base_qkv, _ = cfg.bases
    half = block // (2 * SUPER)
    part_rows = 2 * half
    own_start = place.me * block
    step_rows = min(32, half)
    per_block = block // 128
    tiles_here = length // size

    def load(layer, *keys):
        for key in keys:
            if key in SAVED:
                source = getattr(r, key + str(layer) + "_h")
            else:
                source = getattr(r, key + "_h").at[layer]
            loads[key] = copies.start(source, getattr(r, key))

    def await_loads(*keys):
        for key in keys:
            loads[key].wait()

    glu_in = ("wd", "left", "right", "wl", "wr")
    glu_grad = ("hid", "n2")
    out_in = ("ss", "wo", "gate", "heads")
    attn_in = ("q", "k", "v", "ql", "kl")
    in_in = ("wq", "wk", "wv", "wg")

    def gather_one(layer):
        return Gather(place, r.gd, r.ag1_send.at[layer], r.ag1_recv.at[layer], block)

    firsts = [gather_one(layer) for layer in range(layers)]

    @pl.loop(0, block // 32)
    def _(i):
        rows = aligned(i * 32, 32)
        r.g[rows, :] = r.up[rows, :].astype(F32)


        r.gd[aligned(own_start + i * 32, 32), :] = r.up[rows, :]
    for start, stop in ((gate_end, base_qkv), (base_qkv + 3 * local, cfg.chunks * CHUNK)):
        if stop > start:
            r.grads[start:stop, :] = jnp.zeros((stop - start, width), BF16)
    top = layers - 1
    third = Gather(place, r.gd, r.ag3_send, r.ag3_recv, block)
    top_sum = Scatter(place, r.part1, r.land1, r.rs1_send.at[top], r.rs1_recv.at[top], block)

    def back_block(rows, left, right, part, step):
        grad_hidden = nt(r.gd[rows, :], r.wd[...])
        grad_left = (grad_hidden * right).astype(BF16)
        grad_right = (grad_hidden * left).astype(BF16)
        r.right[rows, :] = grad_left
        r.left[rows, :] = grad_right
        r.part1[rows, :] = (nn(grad_left, r.wl[...]) + nn(grad_right, r.wr[...])).astype(BF16)
        for which in (1, 2, 3):
            @pl.when(step == which)
            def _():
                top_sum.send_block(part, which)

    r.stat_mine[...] = jnp.zeros_like(r.stat_mine)
    late = [part for part in range(SUPER) if part not in EARLY]
    for layer in range(top):
        saves = []

        def save(*keys):
            for key in keys:
                saves.append(copies.start(getattr(r, key), getattr(r, key + str(layer) + "_h")))

        out_sum, finish_forward, groups = forward_front(
            cfg, r, place, copies, layer, getattr(r, "x%d" % layer), save, third, EARLY if layer == top - 1 else (), None
        )
        for copy in saves:
            copy.wait()
        saves.clear()
        save("n2", "left", "right", "hid")
        for group in groups:
            group.drain()
        for part in range(SUPER):
            out_sum.middle(part)
        following = Gather(place, r.n1, r.fag1_send.at[layer + 1], r.fag1_recv.at[layer + 1], block)
        folded = finish_forward(getattr(r, "x%d" % (layer + 1)), following)
        r.stat_mine[3 * layer : 3 * layer + 3, :] = folded[0:3, :]
        for copy in saves:
            copy.wait()
        out_sum.drain()
    out_sum, finish_forward, groups = forward_front(
        cfg, r, place, copies, top, getattr(r, "x%d" % top), lambda *keys: None, third, late, back_block
    )
    for group in groups:
        group.drain()
    third.drain()

    def back_rows(total, values, grad):
        norm = lax.rsqrt(jnp.mean(values * values, axis=1, keepdims=True) + epsilon)
        m = values * norm
        inner = jnp.mean(total * m, axis=1, keepdims=True)
        return grad + norm * (total - m * inner)

    for turn, layer in enumerate(reversed(range(layers))):
        first = firsts[layer]
        mid_sum = top_sum if turn == 0 else Scatter(place, r.part1, r.land1, r.rs1_send.at[layer], r.rs1_recv.at[layer], block)
        second = Gather(place, r.ga, r.ag2_send.at[layer], r.ag2_recv.at[layer], block)
        in_sum = Scatter(place, r.part1, r.land1, r.rs2_send.at[layer], r.rs2_recv.at[layer], block)
        share = Share(place, r.inner, r.inner_land.at[layer], r.in_send.at[layer], r.in_recv.at[layer])
        first_head = layer * HEADS + place.me * heads_here

        def ready(rows):
            return turn * cfg.chunks + rows // CHUNK

        if turn > 0:
            decay_tiles(r.dec, first_head, r.tiles, heads_here, size)
            await_loads(*glu_in)
            await_loads(*out_in)
        scaling = lax.rsqrt(r.ss[...] / width + epsilon)
        for chunk in range(length // 128):
            r.scale[chunk * 128 : (chunk + 1) * 128, :] = spread(scaling, chunk)
        def glu_back(part, step):
            rows = aligned(place.member(step) * block + part * part_rows, part_rows)
            grad_hidden = nt(r.gd[rows, :], r.wd[...])
            grad_left = (grad_hidden * r.right[rows, :].astype(F32)).astype(BF16)
            grad_right = (grad_hidden * r.left[rows, :].astype(F32)).astype(BF16)
            r.right[rows, :] = grad_left
            r.left[rows, :] = grad_right
            r.part1[rows, :] = (nn(grad_left, r.wl[...]) + nn(grad_right, r.wr[...])).astype(BF16)
            for which in (1, 2, 3):
                @pl.when(step == which)
                def _():
                    mid_sum.send_block(part, which)

        if turn > 0:
            gather_stage(first, glu_back, lambda i: line.pump(ready(0), 2))
            first.drain()
        grad_left_ref, grad_right_ref = r.right, r.left

        def glu_grad_rows(base, a_ref, b_ref):
            line.release(turn, base + ff)
            for n in range(width // 256):
                cols = slice(n * 256, (n + 1) * 256)
                r.grads[base : base + ff, cols] = tn(a_ref[...], b_ref[:, cols]).astype(BF16)

        if turn > 0:
            await_loads(*glu_grad)
            for copy in mid_pieces:
                copy.wait()
        glu_grad_rows(base_down, r.hid, r.gd)
        line.pump(ready(base_left), 1 + turn)
        mid_sum.middle(0)
        glu_grad_rows(base_left, grad_left_ref, r.n2)
        line.pump(ready(base_right), 1 + turn)
        for part in range(1, SUPER):
            mid_sum.middle(part)
        glu_grad_rows(base_right, grad_right_ref, r.n2)
        for part in range(SUPER):
            line.pump(ready(base_out), 2 if part == 0 else 1)
            for h in range(2):
                mid_sum.finish(part, h)
                for i in range(half // step_rows):
                    offset = (2 * part + h) * half + i * step_rows
                    rows = slice(offset, offset + step_rows)
                    total = mid_sum.total(part, h, i * step_rows, step_rows)
                    if turn == 0:
                        values = r.mid[rows, :]
                    else:
                        pieces = range(width // (2 * HDIM))
                        values = jnp.concatenate([r.dq[n * block + offset : n * block + offset + step_rows, :] for n in pieces], axis=1)
                    new = back_rows(total, values, r.g[rows, :])
                    r.gm[rows, :] = new
                    r.ga[aligned(own_start + offset, step_rows), :] = new.astype(BF16)
            second.start(part)
        mid_sum.drain()
        if turn + 1 < layers:
            load(layer - 1, *glu_in, *glu_grad)

        def out_back(part, step):
            member = place.member(step)
            for chunk in range(part_rows // 128):
                number = part * (part_rows // 128) + chunk
                rows = aligned(member * block + number * 128, 128)
                grad_branch = nt(r.ga[rows, :], r.wo[...])
                gate = r.gate[rows, :]
                normed = r.heads[rows, :] * widen(r.scale[rows, :], local // 128)
                grad_normed = grad_branch * gate
                r.dx[rows, 3 * local : 4 * local] = (grad_branch * normed).astype(BF16)
                r.branch[rows, :] = (normed * gate).astype(BF16)
                r.gate[rows, :] = grad_normed
                row_sums(grad_normed * normed, r.inner, member * per_block + number)

        gather_stage(second, out_back, lambda i: line.pump(ready(base_out), 3 if i == SUPER else 2))
        share.start()
        line.release(turn, base_gate)
        r.grads[base_out : base_out + local, :] = tn(r.branch[...], r.ga[...]).astype(BF16)
        line.pump(ready(base_gate), 1)

        def in_grad_rows(number, base):
            cols = slice(number * local, (number + 1) * local)
            line.release(turn, base + local)
            for n in range(width // local):
                part_grad = tn(r.n1[:, n * local : (n + 1) * local], r.dx[:, cols])
                r.grads[base : base + local, n * local : (n + 1) * local] = part_grad.astype(BF16)

        if turn > 0:
            await_loads("n1")
        in_grad_rows(3, base_gate)
        line.pump(ready(base_qkv), 1)
        if turn > 0:
            await_loads(*attn_in)
        r.intot[...] = share.total() / width
        for chunk in range(length // 128):
            rows = slice(chunk * 128, (chunk + 1) * 128)
            scale = widen(r.scale[rows, :], local // 128)
            inner = widen(spread(r.intot[...], chunk), local // 128)
            normed = r.heads[rows, :] * scale
            r.dh[rows, :] = (scale * (r.gate[rows, :] - normed * inner)).astype(BF16)
        share.drain()
        second.drain()
        if turn + 1 < layers:
            load(layer - 1, *out_in)
        line.pump(ready(base_qkv), 1)
        between = line.done
        line.done += 1
        assert line.done <= ready(base_qkv)

        @pl.loop(0, heads_here)
        def _(head):
            @pl.when(head == 1)
            def _():
                line.tick(between + head - 1)

            wide = aligned(head * 2 * HDIM, 2 * HDIM)
            thin = aligned(head * HDIM, HDIM)
            for col_tile in range(tiles_here):
                cols = slice(col_tile * size, (col_tile + 1) * size)
                keys = r.k[cols, wide]
                values = r.v[cols, thin]
                acc_key, acc_value = None, None
                for row_tile in range(col_tile, tiles_here):
                    rows = slice(row_tile * size, (row_tile + 1) * size)
                    queries = r.q[rows, wide]
                    grads = r.dh[rows, thin]
                    weight = tile_weight(r, first_head, head, row_tile, col_tile, size)
                    scores = (nt(queries, keys) * weight).astype(BF16)
                    pulled = (nt(grads, values) * weight).astype(BF16)
                    term = nn(pulled, keys)
                    if col_tile == 0:
                        r.dq[rows, :] = term
                    else:
                        r.dq[rows, :] += term
                    key_term = tn(pulled, queries)
                    value_term = tn(scores, grads)
                    acc_key = key_term if acc_key is None else acc_key + key_term
                    acc_value = value_term if acc_value is None else acc_value + value_term
                r.dk[cols, :] = acc_key
                r.dx[cols, aligned(2 * local + head * HDIM, HDIM)] = acc_value.astype(BF16)
            for row_tile in range(tiles_here):
                rows = slice(row_tile * size, (row_tile + 1) * size)
                cosine, sine = r.cos[rows, :], r.sin[rows, :]
                for grad, lin, base in ((r.dq, r.ql, 0), (r.dk, r.kl, local)):
                    v = lin[rows, thin].astype(F32)
                    gate = 1.0 / (1.0 + jnp.exp(-v))
                    back = grad[rows, :HDIM] * cosine + grad[rows, HDIM:] * sine
                    back = back * (gate + v * gate * (1.0 - gate))
                    r.dx[rows, aligned(base + head * HDIM, HDIM)] = back.astype(BF16)

        if turn + 1 < layers:
            load(layer - 1, *attn_in)
            source = getattr(r, "mid%d_h" % (layer - 1))
            mid_pieces = [
                copies.start(source.at[:, pl.ds(n * 2 * HDIM, 2 * HDIM)], r.dq.at[pl.ds(n * block, block), :])
                for n in range(width // (2 * HDIM))
            ]
        if turn > 0:
            await_loads(*in_in)
        last = turn == layers - 1
        if last:
            for number in range(3):
                in_grad_rows(number, base_qkv + number * local)
        for part in range(SUPER):
            for step in (3, 1, 2, 0):
                rows = aligned(place.member(step) * block + part * part_rows, part_rows)
                total = None
                for n, w in enumerate((r.wq, r.wk, r.wv, r.wg)):
                    term = nt(r.dx[rows, n * local : (n + 1) * local], w[...])
                    total = term if total is None else total + term
                r.part1[rows, :] = total.astype(BF16)
                in_sum.send_block(part, step)
            line.pump(ready(cfg.chunks * CHUNK if last else base_qkv), 2 if last else 1)
        for number in range(3):
            if not last:
                in_grad_rows(number, base_qkv + number * local)
            line.pump(ready(base_qkv + (number + 1) * local), 2 if last else 1)
            if number < SUPER:
                in_sum.middle(number)
        if last:
            for part in range(SUPER):
                for which in (1, 2, 3):
                    out_sum.send_block(part, which)
        if turn + 1 < layers:
            load(layer - 1, *in_in, "n1")
        for part in range(SUPER):
            line.pump(ready(cfg.chunks * CHUNK), 2)
            for h in range(2):
                in_sum.finish(part, h)
                for i in range(half // step_rows):
                    offset = (2 * part + h) * half + i * step_rows
                    rows = slice(offset, offset + step_rows)
                    total = in_sum.total(part, h, i * step_rows, step_rows)
                    values = getattr(r, "x%d" % layer)[rows, :].astype(F32)
                    new = back_rows(total, values, r.gm[rows, :])
                    if layer > 0:
                        r.g[rows, :] = new
                        r.gd[aligned(own_start + offset, step_rows), :] = new.astype(BF16)
                    else:
                        r.go[rows, :] = new.astype(BF16)
            if layer > 0:
                firsts[layer - 1].start(part)
        in_sum.drain()
    line.more(2)
    for part in range(SUPER):
        out_sum.middle(part)
        line.more(2)
    folded = finish_forward(r.xo, None)
    r.stat_mine[3 * top : 3 * top + 3, :] = folded[0:3, :]
    stats.square()
    line.more(1)
    stats.pair()
    for number in range(cfg.pairs):
        line.more(1)
        stats.stage(number)
    out_sum.drain()
    stats.finish()
    line.more(line.ticks)


def call_kernel(body, cfg, inputs, outputs, scratch, collective_id, name):
    vmem, anywhere = pl.BlockSpec(memory_space=pltpu.VMEM), pl.BlockSpec(memory_space=pl.ANY)
    names = list(inputs) + list(outputs) + list(scratch)
    result = pl.pallas_call(
        functools.partial(body, cfg, names),
        out_shape=[shape for shape, _ in outputs.values()],
        in_specs=[vmem if placed else anywhere for _, placed in inputs.values()],
        out_specs=[vmem if placed else anywhere for _, placed in outputs.values()],
        scratch_shapes=list(scratch.values()),
        compiler_params=pltpu.CompilerParams(
            collective_id=collective_id, has_side_effects=collective_id is not None, vmem_limit_bytes=VMEM_LIMIT
        ),
        name=name,
    )(*[array for array, _ in inputs.values()])
    return dict(zip(outputs, result))


def collective_scratch(cfg, copies, lead):
    dma = pltpu.SemaphoreType.DMA
    half = cfg.block // (2 * SUPER)
    out = {}
    for name in ("ag1", "ag2", "rs1", "rs2"):
        for key in (name, "f" + name):
            out[key + "_send"] = out[key + "_recv"] = dma((*lead, SUPER, 6))
    for name in copies:
        out["land" + name] = pltpu.VMEM((SUPER, 6, half, cfg.width), BF16)
        out["part" + name] = pltpu.VMEM((cfg.length, cfg.width), BF16)
    out["local_sem"] = dma((96,))
    return out


def weight_scratch(cfg):
    v = pltpu.VMEM
    return dict(
        wq=v((cfg.width, cfg.local), BF16), wk=v((cfg.width, cfg.local), BF16),
        wv=v((cfg.width, cfg.local), BF16), wg=v((cfg.width, cfg.local), BF16),
        wo=v((cfg.local, cfg.width), BF16), wl=v((cfg.ff, cfg.width), BF16),
        wr=v((cfg.ff, cfg.width), BF16), wd=v((cfg.ff, cfg.width), BF16),
    )


def table_scratch(cfg):
    v = pltpu.VMEM
    return dict(
        segc=v((cfg.length, 128), F32), segf=v((8, 128), F32),
        tiles=v((cfg.heads_here, 2, cfg.block, cfg.block), F32),
    )


def forward_scratch(cfg):
    v, dma = pltpu.VMEM, pltpu.SemaphoreType.DMA
    rows, wide, local, ff, block = cfg.length, cfg.width, cfg.local, cfg.ff, cfg.block
    return dict(
        n1=v((rows, wide), BF16), ql=v((rows, local), BF16), kl=v((rows, local), BF16), q=v((rows, 2 * local), BF16),
        k=v((rows, 2 * local), BF16), v=v((rows, local), BF16), gate=v((rows, local), F32), heads=v((rows, local), F32),
        mid=v((block, wide), F32), n2=v((rows, wide), BF16), left=v((rows, ff), BF16), right=v((rows, ff), BF16),
        hid=v((rows, ff), BF16), ss=v((8, 128), F32), ss_mine=v((8, 128), F32), dh=v((rows, local), BF16),
        stat_wide=v((8, wide), F32), scale=v((rows, 128), F32), ss_land=v((cfg.layers, 3, 8, 128), F32),
        ss_send=dma((cfg.layers, 3)), ss_recv=dma((cfg.layers, 3)),
    )


def gather_sems():
    sems = pltpu.SemaphoreType.DMA((SUPER, 6))
    return dict(ag3_send=sems, ag3_recv=sems)


SAVED = ("ss", "mid", "n1", "ql", "kl", "q", "k", "v", "gate", "heads", "n2", "left", "right", "hid")


def run_layers(cfg, tokens, upstream, tables, weights):
    v, dma, s = pltpu.VMEM, pltpu.SemaphoreType.DMA, jax.ShapeDtypeStruct
    rows, wide, local, ff, block = cfg.length, cfg.width, cfg.local, cfg.ff, cfg.block
    inputs = dict(
        up=(upstream, True), x0=(tokens, True), **{k: (a, True) for k, a in tables.items()},
        **{k + "_h": (a, False) for k, a in weights.items()},
    )
    total_rows = cfg.chunks * CHUNK
    outputs = dict(
        xo=(s((block, wide), BF16), True), go=(s((block, wide), BF16), True), stat_total=(s((8, 128), F32), True),
        out_h=(s((cfg.layers * total_rows, wide), BF16), False),
    )
    small, ring, ring_sem = v((8, 128), F32), v((SLOTS, CHUNK // 2, wide), BF16), dma((SLOTS,))
    scratch = dict(
        **weight_scratch(cfg), **collective_scratch(cfg, ("1", "2"), (cfg.layers,)), **table_scratch(cfg), **forward_scratch(cfg),
        **gather_sems(),
        gd=v((rows, wide), BF16), ga=v((rows, wide), BF16),
        g=v((block, wide), F32), gm=v((block, wide), F32),
        branch=v((rows, local), BF16), dx=v((rows, 4 * local), BF16),
        dq=v((rows, 2 * HDIM), F32), dk=v((rows, 2 * HDIM), F32),
        grads=v((total_rows, wide), BF16),
        inner=small, intot=small,
        inner_land=v((cfg.layers, 3, 8, 128), F32), in_send=dma((cfg.layers, 3)), in_recv=dma((cfg.layers, 3)),
        pair_land=ring, right_land=ring, left_land=ring,
        pair_send=ring_sem, pair_recv=ring_sem, right_send=ring_sem, right_recv=ring_sem, left_send=ring_sem,
        left_recv=ring_sem, give_send=ring_sem, give_recv=ring_sem, keep_sem=ring_sem,
        stat_mine=small, stat_square=small, stat_pair=small, stat_right=small, stat_left=small,
        stat_land=v((3, 8, 128), F32), st_send=dma((3,)), st_recv=dma((3,)),
        line_land=v((3, 8, 128), F32), line_send=dma((3,)), line_recv=dma((3,)),
    )
    for layer in range(1, cfg.layers):
        scratch["x%d" % layer] = v((block, wide), F32)
    for layer in range(cfg.layers - 1):
        for key in SAVED:
            outputs["%s%d_h" % (key, layer)] = (s(scratch[key].shape, scratch[key].dtype), False)
    return call_kernel(layers_kernel, cfg, inputs, outputs, scratch, 0, "layers")


def widen_kernel(cfg, names, *refs):
    r = namespace(names, refs)
    tasks = []
    for layer in range(cfg.layers):
        for number, target in enumerate((r.down, r.left, r.right, r.out)):
            start, stop = cfg.bases[number], cfg.bases[number + 1]
            rows = (stop - start) // 2 if stop - start > 512 else stop - start
            for first in range(start, stop, rows):
                tasks.append((layer, first, rows, [(target.at[layer, pl.ds(first - start, rows), :], slice(None))]))
        for number, target in enumerate((r.gate, r.query, r.key, r.value)):
            pieces = [
                (target.at[layer, pl.ds(n * cfg.local, cfg.local), :], slice(n * cfg.local, (n + 1) * cfg.local))
                for n in range(cfg.width // cfg.local)
            ]
            start = cfg.bases[6] + (number - 1) * cfg.local if number > 0 else cfg.bases[4]
            tasks.append((layer, start, cfg.local, pieces))
    depth = WIDEN_DEPTH
    whole = [pltpu.make_async_copy(r.xo_in, r.xo, r.whole_sem.at[0]), pltpu.make_async_copy(r.go_in, r.go, r.whole_sem.at[1])]
    for copy in whole:
        copy.start()
    means = jnp.sum(r.stat[...], axis=1, keepdims=True) / cfg.entries
    roots = jnp.sqrt(means)
    for layer in range(cfg.layers):
        for number in range(3):
            row = 3 * layer + number
            r.rms[layer : layer + 1, number : number + 1] = roots[row : row + 1, :]

    def fetch(task):
        layer, first, rows, _ = tasks[task]
        start = layer * cfg.chunks * CHUNK + first
        slot = task % depth
        return pltpu.make_async_copy(r.grads.at[pl.ds(start, rows), :], r.narrow.at[slot, pl.ds(0, rows), :], r.in_sem.at[slot])

    def store(task):
        _, _, rows, pieces = tasks[task]
        slot = task % depth
        return [
            pltpu.make_async_copy(r.wide.at[slot, pl.ds(0, rows), lanes], target, r.out_sem.at[slot, n])
            for n, (target, lanes) in enumerate(pieces)
        ]

    for task in range(min(depth, len(tasks))):
        fetch(task).start()
    for task in range(len(tasks)):
        slot, rows = task % depth, tasks[task][2]
        fetch(task).wait()
        if task >= depth:
            for copy in store(task - depth):
                copy.wait()

        @pl.loop(0, rows // 32)
        def _(i):
            part = aligned(i * 32, 32)
            r.wide[slot, part, :] = r.narrow[slot, part, :].astype(F32)

        for copy in store(task):
            copy.start()
        if task + depth < len(tasks):
            fetch(task + depth).start()
    for task in range(max(len(tasks) - depth, 0), len(tasks)):
        for copy in store(task):
            copy.wait()
    for copy in whole:
        copy.wait()


def run_widen(cfg, back):
    v, dma, s = pltpu.VMEM, pltpu.SemaphoreType.DMA, jax.ShapeDtypeStruct
    thin, flat = s((cfg.layers, cfg.width, cfg.local), F32), s((cfg.layers, cfg.ff, cfg.width), F32)
    outputs = dict(
        down=(flat, False), left=(flat, False), right=(flat, False), out=(s((cfg.layers, cfg.local, cfg.width), F32), False),
        gate=(thin, False), query=(thin, False), key=(thin, False), value=(thin, False),
        xo=(s((cfg.block, cfg.width), BF16), False), go=(s((cfg.block, cfg.width), BF16), False),
        rms=(s((cfg.layers, 3), F32), True),
    )
    inputs = dict(grads=(back["out_h"], False), xo_in=(back["xo"], False), go_in=(back["go"], False), stat=(back["stat_total"], True))
    rows = max(cfg.ff // 2, cfg.local, 512)
    scratch = dict(
        narrow=v((WIDEN_DEPTH, rows, cfg.width), BF16), wide=v((WIDEN_DEPTH, rows, cfg.width), F32),
        whole_sem=dma((2,)), in_sem=dma((WIDEN_DEPTH,)), out_sem=dma((WIDEN_DEPTH, cfg.width // cfg.local)),
    )
    return call_kernel(widen_kernel, cfg, inputs, outputs, scratch, None, "widen_gradients")


def per_device_square(
    tokens, upstream, segment_ids, query_proj, key_proj, value_proj, gate_proj, output_proj, left_proj, right_proj, down_proj
):
    layers = query_proj.shape[0]
    block, width = tokens.shape
    length = segment_ids.shape[0]
    local, ff = query_proj.shape[2], left_proj.shape[2]
    heads_here = local // HDIM
    positions = np.arange(length, dtype=np.float32)
    frequency = np.exp(np.float32(-math.log(10000.0)) * np.arange(HDIM, dtype=np.float32) / np.float32(HDIM))
    angles = positions[:, None] * frequency[None, :]
    slopes = np.exp2(-8.0 * (np.arange(HEADS) + 1.0) / HEADS)
    decays = np.concatenate([-slopes * (1.0 - depth_start - depth_step * layer) for layer in range(layers)])
    tables = dict(
        cos=jnp.asarray(np.cos(angles)), sin=jnp.asarray(np.sin(angles)),
        dec=jnp.asarray(np.broadcast_to(decays[:, None], (layers * HEADS, 128)).astype(np.float32)),
        seg=segment_ids.reshape(8, length // 8),
    )
    weights = dict(
        wq=query_proj, wk=key_proj, wv=value_proj, wg=gate_proj, wo=output_proj,
        wl=jnp.swapaxes(left_proj, 1, 2), wr=jnp.swapaxes(right_proj, 1, 2), wd=down_proj,
    )
    ends = np.cumsum([0, ff, ff, ff, local, local]).tolist()
    ends += [-(-ends[-1] // CHUNK) * CHUNK]
    ends += [-(-(ends[-1] + 3 * local) // CHUNK) * CHUNK]
    common = dict(
        layers=layers, block=block, length=length, width=width, local=local, ff=ff, heads_here=heads_here,
        pairs=lax.axis_size("dp") // 2, bases=ends, chunks=ends[-1] // CHUNK,
    )
    back = run_layers(types.SimpleNamespace(**common), tokens, upstream, tables, weights)
    entries = float(length * lax.axis_size("dp") * width)
    wide = run_widen(types.SimpleNamespace(entries=entries, **common), back)
    return (
        wide["xo"], wide["go"], wide["query"], wide["key"], wide["value"], wide["gate"], wide["out"],
        jnp.swapaxes(wide["left"], 1, 2), jnp.swapaxes(wide["right"], 1, 2), wide["down"], wide["rms"],
    )


def solution(mesh):
    square = dict(mesh.shape) == SQUARE_MESH
    body = per_device_square if square else per_device
    return jax.shard_map(
        body,
        mesh=mesh,
        in_specs=(
            P(("dp", "tensor"), None),
            P(("dp", "tensor"), None),
            P("dp"),
            P(None, None, "tensor"),
            P(None, None, "tensor"),
            P(None, None, "tensor"),
            P(None, None, "tensor"),
            P(None, "tensor", None),
            P(None, None, "tensor"),
            P(None, None, "tensor"),
            P(None, "tensor", None),
        ),
        out_specs=(
            P(("dp", "tensor"), None),
            P(("dp", "tensor"), None),
            P(None, None, "tensor"),
            P(None, None, "tensor"),
            P(None, None, "tensor"),
            P(None, None, "tensor"),
            P(None, "tensor", None),
            P(None, None, "tensor"),
            P(None, None, "tensor"),
            P(None, "tensor", None),
            P(),
        ),
        check_vma=False,
    )
```

```python
import functools
import math
import types

import jax
import jax.numpy as jnp
import numpy as np
from jax import lax
from jax.experimental import pallas as pl
from jax.experimental.pallas import tpu as pltpu
from jax.sharding import PartitionSpec as P

HEADS = 8
HDIM = 128
BLK = 512


epsilon = 1e-06
depth_start = 0.5
depth_step = 1.0 / 24.0
highest = lax.Precision.HIGHEST


def rms_rows(values):
    return values * lax.rsqrt(jnp.mean(values * values, axis=1, keepdims=True) + epsilon)


def rms_back(values, gradient):
    scaling = lax.rsqrt(jnp.mean(values * values, axis=1, keepdims=True) + epsilon)
    normed = values * scaling
    return scaling * (gradient - normed * jnp.mean(gradient * normed, axis=1, keepdims=True))


def contract_last(left_part, right_part):
    return lax.dot_general(
        left_part, right_part, (((1,), (1,)), ((), ())), preferred_element_type=jnp.float32
    )


def contract_first(left_part, right_part):
    return lax.dot_general(
        left_part, right_part, (((0,), (0,)), ((), ())), preferred_element_type=jnp.float32
    )


def rotate(values, cosine, sine_table):
    return jnp.concatenate([values * cosine[:, None, :], values * sine_table[:, None, :]], axis=2)


def unrotate(gradient, cosine, sine_table):
    half_width = gradient.shape[2] // 2
    return (
        gradient[:, :, :half_width] * cosine[:, None, :]
        + gradient[:, :, half_width:] * sine_table[:, None, :]
    )


def split_blocks(array, block_count):
    return array.reshape((block_count, BLK) + array.shape[1:])


def block_weights(seg_block, next_seg, decay_log):
    block_width = seg_block.shape[0]
    places = jnp.arange(block_width, dtype=jnp.float32)
    distance = places[:, None] - places[None, :]
    allowed = (distance >= 0) & (seg_block[:, None] == seg_block[None, :])
    decay_grid = jnp.where(
        allowed[None], jnp.exp(decay_log[:, None, None] * jnp.maximum(distance, 0.0)[None]), 0.0
    )
    first_seg = seg_block[0]
    query_gain = jnp.where(
        (seg_block == first_seg)[:, None], jnp.exp(places[:, None] * decay_log[None, :]), 0.0
    )
    key_gain = jnp.where(
        (seg_block == next_seg)[:, None],
        jnp.exp((block_width - places)[:, None] * decay_log[None, :]),
        0.0,
    )
    carry_gain = jnp.where(first_seg == next_seg, jnp.exp(decay_log * block_width), 0.0)
    return (decay_grid, query_gain, key_gain, carry_gain)


def next_segments(segments, block_count):
    seg_blocks = segments.reshape(block_count, BLK)
    return (seg_blocks, jnp.concatenate([seg_blocks[1:, 0], jnp.full((1,), -1, jnp.int32)]))


def attend_forward(queries, keys_rot, values, segments, decay_log):
    length, heads_here, pair_width = queries.shape
    block_count = length // BLK
    seg_blocks, next_segs = next_segments(segments, block_count)

    def advance(state_now, block_items):
        query_block, key_block, value_block, seg_block, next_seg = block_items
        query_float = query_block.astype(jnp.float32)
        key_float = key_block.astype(jnp.float32)
        value_float = value_block.astype(jnp.float32)
        decay_grid, query_gain, key_gain, carry_gain = block_weights(seg_block, next_seg, decay_log)
        scores = (
            jnp.einsum("rhd,shd->hrs", query_block, key_block, preferred_element_type=jnp.float32)
            * decay_grid
        )
        block_out = jnp.einsum("hrs,she->rhe", scores, value_float, precision=highest)
        block_out = (
            block_out
            + jnp.einsum("rhd,hde->rhe", query_float, state_now, precision=highest)
            * query_gain[:, :, None]
        )
        new_state = carry_gain[:, None, None] * state_now + jnp.einsum(
            "shd,she->hde", key_float * key_gain[:, :, None], value_float, precision=highest
        )
        return (new_state, (block_out, state_now))

    zero_state = jnp.zeros((heads_here, pair_width, pair_width // 2), jnp.float32)
    _, (block_outs, states) = lax.scan(
        advance,
        zero_state,
        (
            split_blocks(queries, block_count),
            split_blocks(keys_rot, block_count),
            split_blocks(values, block_count),
            seg_blocks,
            next_segs,
        ),
    )
    return (block_outs.reshape(length, heads_here * (pair_width // 2)), states)


def attend_backward(queries, keys_rot, values, segments, decay_log, states, grad_heads):
    length, heads_here, pair_width = queries.shape
    block_count = length // BLK
    seg_blocks, next_segs = next_segments(segments, block_count)

    def retreat(later_grad, block_items):
        query_block, key_block, value_block, seg_block, next_seg, state_now, grad_block = (
            block_items
        )
        query_float = query_block.astype(jnp.float32)
        key_float = key_block.astype(jnp.float32)
        value_float = value_block.astype(jnp.float32)
        decay_grid, query_gain, key_gain, carry_gain = block_weights(seg_block, next_seg, decay_log)
        scores = (
            jnp.einsum("rhd,shd->hrs", query_block, key_block, preferred_element_type=jnp.float32)
            * decay_grid
        )
        pulled = jnp.einsum("rhe,she->hrs", grad_block, value_float, precision=highest) * decay_grid
        grad_query = jnp.einsum("hrs,shd->rhd", pulled, key_float, precision=highest)
        grad_query = (
            grad_query
            + jnp.einsum("rhe,hde->rhd", grad_block, state_now, precision=highest)
            * query_gain[:, :, None]
        )
        grad_key = jnp.einsum("hrs,rhd->shd", pulled, query_float, precision=highest)
        grad_key = (
            grad_key
            + jnp.einsum("she,hde->shd", value_float, later_grad, precision=highest)
            * key_gain[:, :, None]
        )
        grad_value = jnp.einsum("hrs,rhe->she", scores, grad_block, precision=highest)
        grad_value = (
            grad_value
            + jnp.einsum("shd,hde->she", key_float, later_grad, precision=highest)
            * key_gain[:, :, None]
        )
        earlier_grad = carry_gain[:, None, None] * later_grad + jnp.einsum(
            "rhd,rhe->hde", query_float * query_gain[:, :, None], grad_block, precision=highest
        )
        return (earlier_grad, (grad_query, grad_key, grad_value))

    zero_state = jnp.zeros((heads_here, pair_width, pair_width // 2), jnp.float32)
    _, (grad_query, grad_key, grad_value) = lax.scan(
        retreat,
        zero_state,
        (
            split_blocks(queries, block_count),
            split_blocks(keys_rot, block_count),
            split_blocks(values, block_count),
            seg_blocks,
            next_segs,
            states,
            split_blocks(grad_heads, block_count),
        ),
        reverse=True,
    )
    return (
        grad_query.reshape(length, heads_here, pair_width),
        grad_key.reshape(length, heads_here, pair_width),
        grad_value.reshape(length, heads_here, pair_width // 2),
    )


def per_device(
    tokens,
    upstream,
    segment_ids,
    query_proj,
    key_proj,
    value_proj,
    gate_proj,
    output_proj,
    left_proj,
    right_proj,
    down_proj,
):
    layers = query_proj.shape[0]
    row_count, model_width = tokens.shape
    length = segment_ids.shape[0]
    local_width = query_proj.shape[2]
    ff_local = left_proj.shape[2]
    heads_here = local_width // HDIM
    positions = jnp.arange(length, dtype=jnp.float32)
    frequency = jnp.exp(-math.log(10000.0) * jnp.arange(HDIM, dtype=jnp.float32) / HDIM)
    angles = positions[:, None] * frequency[None, :]
    cosine = jnp.cos(angles)
    sine_table = jnp.sin(angles)
    head_index = (lax.axis_index("tensor") * heads_here + jnp.arange(heads_here)).astype(
        jnp.float32
    )
    slopes = jnp.exp2(-8.0 * (head_index + 1.0) / HEADS)

    def gather_normed(normed):
        return lax.all_gather(normed, "tensor", axis=0, tiled=True)

    def gather_again(normed):
        return lax.all_gather(normed, "tensor", axis=0, tiled=True)

    def gather_grads(gradient):
        return lax.all_gather(gradient, "tensor", axis=0, tiled=True)

    def branch_sum(operand, matrix):
        return lax.psum_scatter(
            jnp.dot(operand, matrix, preferred_element_type=jnp.float32).astype(jnp.bfloat16),
            "tensor",
            scatter_dimension=0,
            tiled=True,
        ).astype(jnp.float32)

    def input_sum(pieces, matrix):
        operand = jnp.concatenate(pieces, axis=1)
        return lax.psum_scatter(
            contract_last(operand, matrix).astype(jnp.bfloat16),
            "tensor",
            scatter_dimension=0,
            tiled=True,
        ).astype(jnp.float32)

    current = tokens.astype(jnp.float32)
    saved_layers = []
    stat_terms = []
    for layer_index in range(layers):
        residual = current
        normed = rms_rows(residual).astype(jnp.bfloat16)
        full_normed = gather_normed(normed)
        attn_weight = jnp.concatenate(
            [
                query_proj[layer_index],
                key_proj[layer_index],
                value_proj[layer_index],
                gate_proj[layer_index],
            ],
            axis=1,
        )
        projected = jnp.dot(full_normed, attn_weight, preferred_element_type=jnp.float32)
        query_lin = projected[:, :local_width]
        key_lin = projected[:, local_width : 2 * local_width]
        values = (
            projected[:, 2 * local_width : 3 * local_width]
            .astype(jnp.bfloat16)
            .reshape(length, heads_here, HDIM)
        )
        gate_lin = projected[:, 3 * local_width :]
        queries = rotate(
            jax.nn.silu(query_lin).reshape(length, heads_here, HDIM), cosine, sine_table
        ).astype(jnp.bfloat16)
        keys_rot = rotate(
            jax.nn.silu(key_lin).reshape(length, heads_here, HDIM), cosine, sine_table
        ).astype(jnp.bfloat16)
        decay_log = -slopes * (1.0 - depth_start - depth_step * layer_index)
        heads_out, states = attend_forward(queries, keys_rot, values, segment_ids, decay_log)
        squares = lax.psum(jnp.sum(heads_out * heads_out, axis=1), "tensor")
        scaling = lax.rsqrt(squares / model_width + epsilon)[:, None]
        normed_heads = heads_out * scaling
        branch = (normed_heads * gate_lin).astype(jnp.bfloat16)
        attn_rows = branch_sum(branch, output_proj[layer_index])
        middle = residual + attn_rows
        normed_mid = rms_rows(middle).astype(jnp.bfloat16)
        full_mid = gather_normed(normed_mid)
        glu_weight = jnp.concatenate([left_proj[layer_index], right_proj[layer_index]], axis=1)
        gates_both = jnp.dot(full_mid, glu_weight, preferred_element_type=jnp.float32)
        left_lin = gates_both[:, :ff_local]
        right_lin = gates_both[:, ff_local:]
        hidden = (left_lin * right_lin).astype(jnp.bfloat16)
        glu_rows = branch_sum(hidden, down_proj[layer_index])
        current = middle + glu_rows
        stat_terms.append(
            jnp.stack(
                [
                    jnp.sum(attn_rows * attn_rows),
                    jnp.sum(glu_rows * glu_rows),
                    jnp.sum(current * current),
                ]
            )
        )
        saved_layers.append(
            (
                residual,
                middle,
                normed,
                normed_mid,
                full_normed,
                full_mid,
                attn_weight,
                glu_weight,
                query_lin,
                key_lin,
                gate_lin,
                queries,
                keys_rot,
                values,
                decay_log,
                states,
                normed_heads,
                scaling,
                branch,
                left_lin,
                right_lin,
                hidden,
            )
        )
    stat_sums = lax.psum(jnp.stack(stat_terms), ("dp", "tensor"))
    rms_stats = jnp.sqrt(stat_sums / (length * lax.axis_size("dp") * model_width))
    final_rows = current.astype(jnp.bfloat16)
    gradient = upstream.astype(jnp.float32)
    layer_results = [None] * layers
    for layer_index in reversed(range(layers)):
        (
            residual,
            middle,
            normed,
            normed_mid,
            full_normed,
            full_mid,
            attn_weight,
            glu_weight,
            query_lin,
            key_lin,
            gate_lin,
            queries,
            keys_rot,
            values,
            decay_log,
            states,
            normed_heads,
            scaling,
            branch,
            left_lin,
            right_lin,
            hidden,
        ) = saved_layers[layer_index]
        glu_grad = gather_grads(gradient.astype(jnp.bfloat16))
        grad_hidden = contract_last(glu_grad, down_proj[layer_index])
        down_part = contract_first(hidden, glu_grad)
        grad_left = (grad_hidden * right_lin).astype(jnp.bfloat16)
        grad_right = (grad_hidden * left_lin).astype(jnp.bfloat16)
        grad_gates = jnp.concatenate([grad_left, grad_right], axis=1)
        mid_rows = input_sum((grad_left, grad_right), glu_weight)
        source_mid = gather_again(normed_mid)
        glu_part = contract_first(source_mid, grad_gates)
        gradient = gradient + rms_back(middle, mid_rows)
        attn_grad = gather_grads(gradient.astype(jnp.bfloat16))
        output_part = contract_first(branch, attn_grad)
        grad_branch = contract_last(attn_grad, output_proj[layer_index])
        grad_normed = grad_branch * gate_lin
        grad_gate = (grad_branch * normed_heads).astype(jnp.bfloat16)
        inner_sum = lax.psum(jnp.sum(grad_normed * normed_heads, axis=1), "tensor")
        grad_heads = scaling * (grad_normed - normed_heads * (inner_sum / model_width)[:, None])
        grad_query, grad_key, grad_value = attend_backward(
            queries,
            keys_rot,
            values,
            segment_ids,
            decay_log,
            states,
            grad_heads.reshape(length, heads_here, HDIM),
        )
        sigmoid_query = jax.nn.sigmoid(query_lin)
        sigmoid_key = jax.nn.sigmoid(key_lin)
        query_back = unrotate(grad_query, cosine, sine_table).reshape(length, local_width)
        key_back = unrotate(grad_key, cosine, sine_table).reshape(length, local_width)
        grad_query_lin = (
            query_back * (sigmoid_query + query_lin * sigmoid_query * (1.0 - sigmoid_query))
        ).astype(jnp.bfloat16)
        grad_key_lin = (
            key_back * (sigmoid_key + key_lin * sigmoid_key * (1.0 - sigmoid_key))
        ).astype(jnp.bfloat16)
        grad_value_lin = grad_value.reshape(length, local_width).astype(jnp.bfloat16)
        grad_projected = jnp.concatenate(
            [grad_query_lin, grad_key_lin, grad_value_lin, grad_gate], axis=1
        )
        in_rows = input_sum((grad_query_lin, grad_key_lin, grad_value_lin, grad_gate), attn_weight)
        source_normed = gather_again(normed)
        attn_part = contract_first(source_normed, grad_projected)
        gradient = gradient + rms_back(residual, in_rows)
        query_part = attn_part[:, :local_width]
        key_part = attn_part[:, local_width : 2 * local_width]
        value_part = attn_part[:, 2 * local_width : 3 * local_width]
        gate_part = attn_part[:, 3 * local_width :]
        left_part = glu_part[:, :ff_local]
        right_part = glu_part[:, ff_local:]
        layer_results[layer_index] = (
            query_part,
            key_part,
            value_part,
            gate_part,
            output_part,
            left_part,
            right_part,
            down_part,
        )
    stacked = [
        jnp.stack([layer_results[index][member] for index in range(layers)]) for member in range(8)
    ]
    totals = (
        lax.psum(stacked[0].astype(jnp.bfloat16), "dp").astype(jnp.float32),
        lax.psum(stacked[1].astype(jnp.bfloat16), "dp").astype(jnp.float32),
        lax.psum(stacked[2].astype(jnp.bfloat16), "dp").astype(jnp.float32),
        lax.psum(stacked[3].astype(jnp.bfloat16), "dp").astype(jnp.float32),
        lax.psum(stacked[4].astype(jnp.bfloat16), "dp").astype(jnp.float32),
        lax.psum(stacked[5].astype(jnp.bfloat16), "dp").astype(jnp.float32),
        lax.psum(stacked[6].astype(jnp.bfloat16), "dp").astype(jnp.float32),
        lax.psum(stacked[7].astype(jnp.bfloat16), "dp").astype(jnp.float32),
    )
    input_grad = gradient.astype(jnp.bfloat16)
    return (
        final_rows,
        input_grad,
        totals[0],
        totals[1],
        totals[2],
        totals[3],
        totals[4],
        totals[5],
        totals[6],
        totals[7],
        rms_stats,
    )


SQUARE_MESH = {"dp": 8, "tensor": 4}


F32 = jnp.float32
BF16 = jnp.bfloat16
MESH = pl.DeviceIdType.MESH
VMEM_LIMIT = 62 * 2**20
SUPER = 2
EARLY = (0,)
WIDEN_DEPTH = 6
CHUNK = 128
HOP = 3
SLOTS = 16


def nn(a, b):
    return lax.dot_general(a, b, (((1,), (0,)), ((), ())), preferred_element_type=F32)


def nt(a, b):
    return lax.dot_general(a, b, (((1,), (1,)), ((), ())), preferred_element_type=F32)


def tn(a, b):
    return lax.dot_general(a, b, (((0,), (0,)), ((), ())), preferred_element_type=F32)


def exact(a, b, dims):
    return lax.dot_general(a, b, (dims, ((), ())), precision=highest, preferred_element_type=F32)


def aligned(index, size):
    return pl.ds(pl.multiple_of(index, size), size)


class Place:
    def __init__(self, pairs):
        self.dp = lax.axis_index("dp")
        self.me = lax.axis_index("tensor")
        self.low = lax.rem(self.me, 2)
        self.high = self.me // 2
        self.core = lax.rem(self.dp, 2)
        self.at = self.dp // 2
        self.last = pairs - 1

    def member(self, step):
        low = lax.rem(self.low + lax.rem(step, 2), 2)
        high = lax.rem(self.high + step // 2, 2)
        return 2 * high + low

    def device(self, step):
        return (self.dp, self.member(step))

    def partner(self):
        return (self.dp + 1 - 2 * self.core, self.me)

    def right(self):
        return (self.dp + 2, self.me)

    def left(self):
        return (self.dp - 2, self.me)

    def greet(self, line):
        barrier = pltpu.get_barrier_semaphore()

        def signal(device):
            pl.semaphore_signal(barrier, inc=1, device_id=device, device_id_type=MESH)

        for step in (1, 2, 3):
            signal(self.device(step))
        if not line:
            pl.semaphore_wait(barrier, 3)
            return
        signal(self.partner())

        @pl.when(self.at < self.last)
        def _():
            signal(self.right())

        @pl.when(self.at > 0)
        def _():
            signal(self.left())

        pl.semaphore_wait(barrier, 4 + jnp.minimum(self.at, 1) + jnp.minimum(self.last - self.at, 1))


class Wire:
    def __init__(self, device, send_sem, recv_sem, source, target, landing):
        self.source, self.target, self.landing = source, target, landing
        self.common = dict(send_sem=send_sem, recv_sem=recv_sem, device_id=device, device_id_type=MESH)

    def out(self):
        return pltpu.make_async_remote_copy(src_ref=self.source, dst_ref=self.target, **self.common)

    def start(self):
        self.out().start()

    def wait_recv(self):
        pltpu.make_async_remote_copy(src_ref=self.landing, dst_ref=self.landing, **self.common).wait_recv()

    def wait_send(self):
        self.out().wait_send()


class Gather:
    def __init__(self, place, buf, send, recv, block):
        self.place, self.buf, self.block = place, buf, block
        self.send, self.recv = send, recv
        self.half = block // (2 * SUPER)

    def rows(self, step, part, half):
        start = self.place.member(step) * self.block + (2 * part + half) * self.half
        return self.buf.at[aligned(start, self.half)]

    def wire(self, part, number):
        step, owner, half = ((1, 0, 0), (2, 0, 1), (1, 0, 1), (2, 0, 0), (2, 1, 0), (1, 2, 1))[number]
        source = self.rows(owner, part, half)
        landing = self.rows((0, 1, 2, 3)[owner ^ step], part, half)
        return Wire(self.place.device(step), self.send.at[part, number], self.recv.at[part, number], source, source, landing)

    def start(self, part):
        for number in range(4):
            self.wire(part, number).start()

    def forward(self, part):
        self.wire(part, 0).wait_recv()
        self.wire(part, 4).start()
        self.wire(part, 1).wait_recv()
        self.wire(part, 5).start()

    def finish(self, part, step):
        for number in {0: (), 1: (2,), 2: (3,), 3: (4, 5)}[step]:
            self.wire(part, number).wait_recv()

    def drain(self, parts=range(SUPER)):
        for part in parts:
            for number in range(6):
                self.wire(part, number).wait_send()


def gather_stage(gather, block_fn, beside):
    @pl.loop(0, 4 * SUPER)
    def _(i):
        mixed = i - SUPER
        part = jnp.where(i < SUPER, i, jnp.where(i < 3 * SUPER, mixed // 2, i - 3 * SUPER))
        step = jnp.where(i < SUPER, 0, jnp.where(i < 3 * SUPER, 1 + lax.rem(mixed, 2), 3))

        @pl.when(i == SUPER)
        def _():
            for one in range(SUPER):
                beside(one)
                gather.forward(one)

        @pl.when(i == 3 * SUPER)
        def _():
            beside(SUPER)

        for which in (1, 2, 3):
            @pl.when(step == which)
            def _():
                gather.finish(part, which)
        block_fn(part, step)


class Scatter:
    def __init__(self, place, buf, land, send, recv, block):
        self.place, self.buf, self.land, self.block = place, buf, land, block
        self.send, self.recv = send, recv
        self.half = block // (2 * SUPER)

    def rows(self, step, part, half):
        start = self.place.member(step) * self.block + (2 * part + half) * self.half
        return aligned(start, self.half)

    def wire(self, part, number):
        step, owner, half = ((1, 3, 0), (1, 1, 0), (2, 3, 1), (2, 2, 1), (2, 2, 0), (1, 1, 1))[number]
        target = self.land.at[part, number]
        return Wire(
            self.place.device(step), self.send.at[part, number], self.recv.at[part, number],
            self.buf.at[self.rows(owner, part, half)], target, target,
        )

    def send_block(self, part, step):
        for number in {0: (), 1: (1,), 2: (3,), 3: (0, 2)}[step]:
            self.wire(part, number).start()

    def middle(self, part):
        for first, second, owner, half in ((0, 4, 2, 0), (2, 5, 1, 1)):
            self.wire(part, first).wait_recv()
            rows = self.rows(owner, part, half)
            self.buf[rows, :] = self.buf[rows, :] + self.land[part, first]
            self.wire(part, second).start()

    def finish(self, part, half):
        first, second = ((1, 4), (3, 5))[half]
        self.wire(part, first).wait_recv()
        self.wire(part, second).wait_recv()

    def total(self, part, half, start, count):
        first, second = ((1, 4), (3, 5))[half]
        own = self.place.me * self.block + (2 * part + half) * self.half + start
        rows = pl.ds(start, count)
        return (
            self.buf[aligned(own, count), :].astype(F32)
            + self.land[part, first, rows, :].astype(F32)
            + self.land[part, second, rows, :].astype(F32)
        )

    def drain(self):
        for part in range(SUPER):
            for number in range(6):
                self.wire(part, number).wait_send()


class Share:
    def __init__(self, place, mine, land, send, recv):
        self.wires = [
            Wire(place.device(step), send.at[step - 1], recv.at[step - 1], mine, land.at[step - 1], land.at[step - 1])
            for step in (1, 2, 3)
        ]
        self.mine, self.land = mine, land

    def start(self):
        for wire in self.wires:
            wire.start()

    def total(self):
        for wire in self.wires:
            wire.wait_recv()
        return self.mine[...] + self.land[0] + self.land[1] + self.land[2]

    def drain(self):
        for wire in self.wires:
            wire.wait_send()


class Local:
    def __init__(self, sems):
        self.sems, self.used = sems, 0

    def start(self, source, target):
        copy = pltpu.make_async_copy(source, target, self.sems.at[self.used])
        self.used += 1
        copy.start()
        return copy


def row_sums(values, target, chunk):
    sums = exact(jnp.ones((8, values.shape[1]), F32), values, ((1,), (1,)))
    target[pl.ds(chunk, 1), :] = sums[0:1, :]


def spread(sums, chunk):
    picked = (lax.broadcasted_iota(jnp.int32, (8, 128), 0) == chunk).astype(F32)
    return exact(sums, picked, ((0,), (0,)))


def widen(columns, times):
    return jnp.concatenate([columns] * times, axis=1)


def decay_tiles(dec_ref, first_head, tiles, heads_here, size):
    rows = lax.broadcasted_iota(jnp.int32, (size, size), 0)
    cols = lax.broadcasted_iota(jnp.int32, (size, size), 1)
    distance = (rows - cols).astype(F32)
    for head in range(heads_here):
        decay = dec_ref[pl.ds(first_head + head, 1), 0:1]
        tiles[head, 0] = jnp.where(rows >= cols, jnp.exp(decay * jnp.maximum(distance, 0.0)), 0.0)
        tiles[head, 1] = jnp.exp(decay * (distance + float(size)))


def spread_segments(r, length):
    r.segf[...] = r.seg[...].astype(F32)
    for chunk in range(length // 128):
        r.segc[chunk * 128 : (chunk + 1) * 128, :] = spread(r.segf[...], chunk)


def tile_weight(r, first_head, head, row_tile, col_tile, size):
    gap = row_tile - col_tile
    if gap == 0:
        weight = r.tiles[head, 0]
    else:
        weight = r.tiles[head, 1]
        if gap > 1:
            decay = r.dec[pl.ds(first_head + head, 1), 0:1]
            weight = weight * jnp.exp(decay * float(size * (gap - 1)))
    row_seg = widen(r.segc[row_tile * size : (row_tile + 1) * size, :], size // 128)
    per = size // 128
    col_seg = jnp.concatenate([r.segf[per * col_tile + i : per * col_tile + i + 1, :] for i in range(per)], axis=1)
    return jnp.where(row_seg == col_seg, weight, 0.0)


def namespace(names, refs):
    return types.SimpleNamespace(**dict(zip(names, refs)))


def forward_front(cfg, r, place, copies, layer, x, save, third, third_parts, back_block):
    block, length, width = cfg.block, cfg.length, cfg.width
    heads_here, size = cfg.heads_here, cfg.block
    first_head = layer * HEADS + place.me * heads_here
    w_in = [copies.start(h.at[layer], v) for h, v in (
        (r.wq_h, r.wq), (r.wk_h, r.wk), (r.wv_h, r.wv), (r.wg_h, r.wg))]
    w_out = copies.start(r.wo_h.at[layer], r.wo)
    w_glu = [copies.start(h.at[layer], v) for h, v in ((r.wl_h, r.wl), (r.wr_h, r.wr), (r.wd_h, r.wd))]
    first = Gather(place, r.n1, r.fag1_send.at[layer], r.fag1_recv.at[layer], block)
    mid_sum = Scatter(place, r.part1, r.land1, r.frs1_send.at[layer], r.frs1_recv.at[layer], block)
    second = Gather(place, r.n2, r.fag2_send.at[layer], r.fag2_recv.at[layer], block)
    out_sum = Scatter(place, r.part2, r.land2, r.frs2_send.at[layer], r.frs2_recv.at[layer], block)
    share = Share(place, r.ss_mine, r.ss_land.at[layer], r.ss_send.at[layer], r.ss_recv.at[layer])
    half, step_rows = first.half, 32
    own_start = place.me * block

    if layer == 0:
        @pl.loop(0, block // step_rows)
        def _(i):
            rows = aligned(i * step_rows, step_rows)
            v = x[rows, :].astype(F32)
            scale = lax.rsqrt(jnp.mean(v * v, axis=1, keepdims=True) + epsilon)
            r.n1[aligned(own_start + i * step_rows, step_rows), :] = (v * scale).astype(BF16)

        place.greet(True)
        for part in range(SUPER):
            first.start(part)
        spread_segments(r, length)
    decay_tiles(r.dec, first_head, r.tiles, heads_here, size)
    for copy in w_in:
        copy.wait()

    @pl.loop(0, 4)
    def _(step):
        @pl.when(step == 1)
        def _():
            for part in range(SUPER):
                first.forward(part)
        for which in (1, 2, 3):
            @pl.when(step == which)
            def _():
                for part in range(SUPER):
                    first.finish(part, which)
        rows = aligned(place.member(step) * block, block)
        a = r.n1[rows, :]
        cosine, sine = r.cos[rows, :], r.sin[rows, :]
        for w, lin, rot in ((r.wq, r.ql, r.q), (r.wk, r.kl, r.k)):
            v = nn(a, w[...])
            lin[rows, :] = v.astype(BF16)
            v = v / (1.0 + jnp.exp(-v))
            for head in range(heads_here):
                one = v[:, head * HDIM : (head + 1) * HDIM]
                rot[rows, 2 * head * HDIM : (2 * head + 1) * HDIM] = (one * cosine).astype(BF16)
                rot[rows, (2 * head + 1) * HDIM : (2 * head + 2) * HDIM] = (one * sine).astype(BF16)
        r.v[rows, :] = nn(a, r.wv[...]).astype(BF16)
        r.gate[rows, :] = nn(a, r.wg[...])

    save("n1", "ql", "kl", "q", "k", "v", "gate")
    if third_parts:
        for part in third_parts:
            third.start(part)
    w_out.wait()
    part_rows, per = 2 * half, size // 128
    heads = range(heads_here)
    wide = [slice(head * 2 * HDIM, (head + 1) * 2 * HDIM) for head in heads]
    thin = [slice(head * HDIM, (head + 1) * HDIM) for head in heads]
    decay = [r.dec[pl.ds(first_head + head, 1), 0:1] for head in heads]

    @pl.loop(0, 4)
    def _(i):
        step = jnp.where(i == 0, 3, jnp.where(i == 3, 0, i))
        row_tile = place.member(step)
        rows = aligned(row_tile * size, size)
        row_seg = widen(r.segc[rows, :], per)
        queries = [r.q[rows, wide[head]] for head in heads]

        def terms(col_tile, weights):
            cols = aligned(col_tile * size, size)
            col_seg = jnp.concatenate([r.segf[pl.ds(per * col_tile + n, 1), :] for n in range(per)], axis=1)
            same = row_seg == col_seg
            out = []
            for head in heads:
                scores = nt(queries[head], r.k[cols, wide[head]]) * jnp.where(same, weights[head], 0.0)
                out.append(nn(scores.astype(BF16), r.v[cols, thin[head]]))
            return tuple(out)

        def add(col_tile, sums):
            gap = (size * (row_tile - col_tile - 1)).astype(F32)
            more = terms(col_tile, [r.tiles[head, 1] * jnp.exp(decay[head] * gap) for head in heads])
            return tuple(one + other for one, other in zip(sums, more))

        sums = lax.fori_loop(0, row_tile, add, terms(row_tile, [r.tiles[head, 0] for head in heads]))
        for head in heads:
            r.heads[rows, thin[head]] = sums[head]
            r.dh[rows, thin[head]] = (sums[head] * r.gate[rows, thin[head]]).astype(BF16)
        for part in range(SUPER):
            some = aligned(row_tile * block + part * part_rows, part_rows)
            r.part1[some, :] = nn(r.dh[some, :], r.wo[...]).astype(BF16)
            for which in (1, 2, 3):
                @pl.when(step == which)
                def _():
                    mid_sum.send_block(part, which)
        for n in range(per):
            v = r.heads[aligned(row_tile * size + n * 128, 128), :]
            row_sums(v * v, r.ss_mine, row_tile * per + n)

    share.start()
    save("heads")
    if third_parts:
        for part in third_parts:
            third.forward(part)
    for part in range(SUPER):
        mid_sum.middle(part)
    r.ss[...] = share.total()
    save("ss")
    scaling = lax.rsqrt(r.ss[...] / width + epsilon)
    per_block = block // 128
    for chunk in range(per_block):
        r.scale[aligned(own_start + chunk * 128, 128), :] = spread(scaling, place.me * per_block + chunk)
    r.stat_wide[...] = jnp.zeros_like(r.stat_wide)

    def add_stat(row, v):
        sums = jnp.sum(v * v, axis=0, keepdims=True)
        r.stat_wide[row : row + 1, :] += sums

    step_rows = min(32, half)
    for part in range(SUPER):
        for h in range(2):
            mid_sum.finish(part, h)
            for i in range(half // step_rows):
                offset = (2 * part + h) * half + i * step_rows
                scale = widen(r.scale[aligned(own_start + offset, step_rows), :], width // 128)
                attn = mid_sum.total(part, h, i * step_rows, step_rows) * scale
                middle = x[offset : offset + step_rows, :].astype(F32) + attn
                r.mid[offset : offset + step_rows, :] = middle
                add_stat(0, attn)
                norm = lax.rsqrt(jnp.mean(middle * middle, axis=1, keepdims=True) + epsilon)
                r.n2[aligned(own_start + offset, step_rows), :] = (middle * norm).astype(BF16)
        second.start(part)
    save("mid")
    for copy in w_glu:
        copy.wait()
    if third_parts:
        for part in third_parts:
            for which in (1, 2, 3):
                third.finish(part, which)
    if back_block is not None:
        mid_sum.drain()

    def glu(part, step):
        rows = aligned(place.member(step) * block + part * part_rows, part_rows)
        a = r.n2[rows, :]
        left = nt(a, r.wl[...])
        right = nt(a, r.wr[...])
        hidden = (left * right).astype(BF16)
        r.hid[rows, :] = hidden
        if back_block is not None:
            back_block(rows, left, right, part, step)
        else:
            r.left[rows, :] = left.astype(BF16)
            r.right[rows, :] = right.astype(BF16)
        r.part2[rows, :] = nn(hidden, r.wd[...]).astype(BF16)
        if back_block is None:
            for which in (1, 2, 3):
                @pl.when(step == which)
                def _():
                    out_sum.send_block(part, which)

    gather_stage(second, glu, lambda i: None)

    def finish(target, following):
        for part in range(SUPER):
            for h in range(2):
                out_sum.finish(part, h)
                for i in range(half // step_rows):
                    offset = (2 * part + h) * half + i * step_rows
                    glu_rows = out_sum.total(part, h, i * step_rows, step_rows)
                    after = r.mid[offset : offset + step_rows, :] + glu_rows
                    target[offset : offset + step_rows, :] = after.astype(target.dtype)
                    add_stat(1, glu_rows)
                    add_stat(2, after)
                    if following is not None:
                        norm = lax.rsqrt(jnp.mean(after * after, axis=1, keepdims=True) + epsilon)
                        r.n1[aligned(own_start + offset, step_rows), :] = (after * norm).astype(BF16)
            if following is not None:
                following.start(part)
        folded = r.stat_wide[:, :128]
        for n in range(1, width // 128):
            folded = folded + r.stat_wide[:, n * 128 : (n + 1) * 128]
        return folded

    groups = [first, second, share] + ([mid_sum] if back_block is None else [])
    return out_sum, finish, groups


def turns_of(k, size, count):
    return sum(((k >= size * n).astype(jnp.int32) for n in range(1, -(-count // size))), jnp.int32(0))


class Line:
    def __init__(self, cfg, place, r):
        self.place, self.r = place, r
        self.per, self.count = cfg.chunks, cfg.chunks * cfg.layers
        self.layers, self.rows_each = cfg.layers, cfg.chunks * CHUNK
        self.half = CHUNK // 2
        self.ticks = self.count + 3 + HOP * place.last
        self.done = 0

    def slot(self, k):
        return k - SLOTS * turns_of(k, SLOTS, self.count)

    def rows(self, k, core):
        place = k - self.per * turns_of(k, self.per, self.count)
        return aligned(place * CHUNK + core * self.half, self.half)

    def own(self, k):
        return self.rows(k, self.place.core)

    def out_rows(self, k, core):
        turn = turns_of(k, self.per, self.count)
        place = (self.layers - 1 - turn) * self.per + k - turn * self.per
        start = place * CHUNK + core * self.half
        return aligned(start, self.half)

    def pair(self, k):
        slot = self.slot(k)
        r = self.r
        return Wire(self.place.partner(), r.pair_send.at[slot], r.pair_recv.at[slot],
                    r.grads.at[self.rows(k, 1 - self.place.core)], r.pair_land.at[slot], r.pair_land.at[slot])

    def hop(self, k, land, send, recv, device):
        slot = self.slot(k)
        return Wire(device, send.at[slot], recv.at[slot], land.at[slot], land.at[slot], land.at[slot])

    def going_right(self, k):
        return self.hop(k, self.r.right_land, self.r.right_send, self.r.right_recv, self.place.right())

    def going_left(self, k):
        return self.hop(k, self.r.left_land, self.r.left_send, self.r.left_recv, self.place.left())

    def coming_right(self, k):
        return self.hop(k, self.r.right_land, self.r.right_send, self.r.right_recv, self.place.left())

    def coming_left(self, k):
        return self.hop(k, self.r.left_land, self.r.left_send, self.r.left_recv, self.place.right())

    def result(self, k):
        slot, r = self.slot(k), self.r
        return Wire(self.place.partner(), r.give_send.at[slot], r.give_recv.at[slot],
                    r.grads.at[self.own(k)], r.out_h.at[self.out_rows(k, self.place.core)],
                    r.out_h.at[self.out_rows(k, 1 - self.place.core)])

    def keep(self, k):
        slot, r = self.slot(k), self.r
        return pltpu.make_async_copy(
            r.grads.at[self.own(k)], r.out_h.at[self.out_rows(k, self.place.core)], r.keep_sem.at[slot]
        )

    def one_way(self, k, land, start_here, coming, ends_here, going):
        slot = self.slot(k)

        @pl.when(start_here)
        def _():
            land[slot] = self.r.grads[self.own(k), :]

        @pl.when(jnp.logical_not(start_here))
        def _():
            coming(k).wait_recv()
            land[slot] = land[slot] + self.r.grads[self.own(k), :]

        @pl.when(jnp.logical_not(ends_here))
        def _():
            going(k).start()

    def tick(self, n):
        place, r, last = self.place, self.r, self.place.last
        at_left, at_right = place.at == 0, place.at == last

        @pl.when(n < self.count)
        def _():
            self.pair(n).start()

        k = n - 1

        @pl.when(jnp.logical_and(k >= 0, k < self.count))
        def _():
            wire = self.pair(k)
            wire.wait_recv()
            wire.wait_send()
            slot = self.slot(k)
            r.grads[self.own(k), :] = r.grads[self.own(k), :] + r.pair_land[slot]

        left_k = n - 1 - HOP * (last - place.at)

        @pl.when(jnp.logical_and(left_k >= 0, left_k < self.count))
        def _():
            self.one_way(left_k, r.left_land, at_right, self.coming_left, at_left, self.going_left)

        right_k = n - 1 - HOP * place.at

        @pl.when(jnp.logical_and(right_k >= 0, right_k < self.count))
        def _():
            self.one_way(right_k, r.right_land, at_left, self.coming_right, at_right, self.going_right)

        full_k = n - 1 - HOP * last

        @pl.when(jnp.logical_and(full_k >= 0, full_k < self.count))
        def _():
            @pl.when(jnp.logical_not(at_right))
            def _():
                self.going_right(full_k).wait_send()

            @pl.when(jnp.logical_not(at_left))
            def _():
                self.going_left(full_k).wait_send()

            slot = self.slot(full_k)
            own = self.own(full_k)
            total = r.right_land[slot].astype(F32) + r.left_land[slot].astype(F32) - r.grads[own, :].astype(F32)
            r.grads[own, :] = total.astype(BF16)
            self.result(full_k).start()
            self.keep(full_k).start()

        old_k = full_k - 2

        @pl.when(jnp.logical_and(old_k >= 0, old_k < self.count))
        def _():
            wire = self.result(old_k)
            wire.wait_recv()
            wire.wait_send()
            self.keep(old_k).wait()

    def pump(self, ready, most):
        stop = min(self.done + most, ready)
        if stop > self.done:
            start, self.done = self.done, stop

            @pl.loop(start, stop)
            def _(n):
                self.tick(n)

    def release(self, turn, rows):
        needed = (turn - 1) * self.per + -(-rows // CHUNK) + 3 + HOP * self.place.last
        if turn > 0 and needed > self.done:
            self.pump(turn * self.per, needed - self.done)
            assert self.done >= needed

    def more(self, most):
        self.pump(self.ticks, most)


class StatLine:
    def __init__(self, place, r):
        self.place, self.r = place, r
        self.share = Share(place, r.stat_mine, r.stat_land, r.st_send, r.st_recv)

    def square(self):
        self.share.start()

    def pair(self):
        r = self.r
        r.stat_square[...] = self.share.total()
        self.wire(0, self.place.partner(), r.stat_square).start()

    def wire(self, number, device, source):
        r = self.r
        return Wire(device, r.line_send.at[number], r.line_recv.at[number], source, r.line_land.at[number], r.line_land.at[number])

    def stage(self, number):
        place, r = self.place, self.r
        if number == 0:
            self.wire(0, place.partner(), r.stat_square).wait_recv()
            r.stat_pair[...] = r.stat_square[...] + r.line_land[0]
            r.stat_right[...] = r.stat_pair[...]
            r.stat_left[...] = r.stat_pair[...]
        else:
            @pl.when(place.at == number)
            def _():
                self.wire(1, place.left(), r.stat_right).wait_recv()
                r.stat_right[...] = r.stat_pair[...] + r.line_land[1]

            @pl.when(place.last - place.at == number)
            def _():
                self.wire(2, place.right(), r.stat_left).wait_recv()
                r.stat_left[...] = r.stat_pair[...] + r.line_land[2]
        if number < place.last:
            @pl.when(place.at == number)
            def _():
                self.wire(1, place.right(), r.stat_right).start()

            @pl.when(place.last - place.at == number)
            def _():
                self.wire(2, place.left(), r.stat_left).start()

    def finish(self):
        place, r = self.place, self.r
        r.stat_total[...] = r.stat_right[...] + r.stat_left[...] - r.stat_pair[...]
        self.share.drain()
        self.wire(0, place.partner(), r.stat_square).wait_send()

        @pl.when(place.at < place.last)
        def _():
            self.wire(1, place.right(), r.stat_right).wait_send()

        @pl.when(place.at > 0)
        def _():
            self.wire(2, place.left(), r.stat_left).wait_send()


def layers_kernel(cfg, names, *refs):
    r = namespace(names, refs)
    block, length, width, local, ff = cfg.block, cfg.length, cfg.width, cfg.local, cfg.ff
    heads_here, size, layers = cfg.heads_here, cfg.block, cfg.layers
    place = Place(cfg.pairs)
    copies = Local(r.local_sem)
    line = Line(cfg, place, r)
    stats = StatLine(place, r)
    loads = {}
    base_down, base_left, base_right, base_out, base_gate, gate_end, base_qkv, _ = cfg.bases
    half = block // (2 * SUPER)
    part_rows = 2 * half
    own_start = place.me * block
    step_rows = min(32, half)
    per_block = block // 128
    tiles_here = length // size

    def load(layer, *keys):
        for key in keys:
            if key in SAVED:
                source = getattr(r, key + str(layer) + "_h")
            else:
                source = getattr(r, key + "_h").at[layer]
            loads[key] = copies.start(source, getattr(r, key))

    def await_loads(*keys):
        for key in keys:
            loads[key].wait()

    glu_in = ("wd", "left", "right", "wl", "wr")
    glu_grad = ("hid", "n2")
    out_in = ("ss", "wo", "gate", "heads")
    attn_in = ("q", "k", "v", "ql", "kl")
    in_in = ("wq", "wk", "wv", "wg")

    def gather_one(layer):
        return Gather(place, r.gd, r.ag1_send.at[layer], r.ag1_recv.at[layer], block)

    firsts = [gather_one(layer) for layer in range(layers)]

    @pl.loop(0, block // 32)
    def _(i):
        rows = aligned(i * 32, 32)
        r.g[rows, :] = r.up[rows, :].astype(F32)


        r.gd[aligned(own_start + i * 32, 32), :] = r.up[rows, :]
    for start, stop in ((gate_end, base_qkv), (base_qkv + 3 * local, cfg.chunks * CHUNK)):
        if stop > start:
            r.grads[start:stop, :] = jnp.zeros((stop - start, width), BF16)
    top = layers - 1
    third = Gather(place, r.gd, r.ag3_send, r.ag3_recv, block)
    top_sum = Scatter(place, r.part1, r.land1, r.rs1_send.at[top], r.rs1_recv.at[top], block)

    def back_block(rows, left, right, part, step):
        grad_hidden = nt(r.gd[rows, :], r.wd[...])
        grad_left = (grad_hidden * right).astype(BF16)
        grad_right = (grad_hidden * left).astype(BF16)
        r.right[rows, :] = grad_left
        r.left[rows, :] = grad_right
        r.part1[rows, :] = (nn(grad_left, r.wl[...]) + nn(grad_right, r.wr[...])).astype(BF16)
        for which in (1, 2, 3):
            @pl.when(step == which)
            def _():
                top_sum.send_block(part, which)

    r.stat_mine[...] = jnp.zeros_like(r.stat_mine)
    late = [part for part in range(SUPER) if part not in EARLY]
    for layer in range(top):
        saves = []

        def save(*keys):
            for key in keys:
                saves.append(copies.start(getattr(r, key), getattr(r, key + str(layer) + "_h")))

        out_sum, finish_forward, groups = forward_front(
            cfg, r, place, copies, layer, getattr(r, "x%d" % layer), save, third, EARLY if layer == top - 1 else (), None
        )
        for copy in saves:
            copy.wait()
        saves.clear()
        save("n2", "left", "right", "hid")
        for group in groups:
            group.drain()
        for part in range(SUPER):
            out_sum.middle(part)
        following = Gather(place, r.n1, r.fag1_send.at[layer + 1], r.fag1_recv.at[layer + 1], block)
        folded = finish_forward(getattr(r, "x%d" % (layer + 1)), following)
        r.stat_mine[3 * layer : 3 * layer + 3, :] = folded[0:3, :]
        for copy in saves:
            copy.wait()
        out_sum.drain()
    out_sum, finish_forward, groups = forward_front(
        cfg, r, place, copies, top, getattr(r, "x%d" % top), lambda *keys: None, third, late, back_block
    )
    for group in groups:
        group.drain()
    third.drain()

    def back_rows(total, values, grad):
        norm = lax.rsqrt(jnp.mean(values * values, axis=1, keepdims=True) + epsilon)
        m = values * norm
        inner = jnp.mean(total * m, axis=1, keepdims=True)
        return grad + norm * (total - m * inner)

    for turn, layer in enumerate(reversed(range(layers))):
        first = firsts[layer]
        mid_sum = top_sum if turn == 0 else Scatter(place, r.part1, r.land1, r.rs1_send.at[layer], r.rs1_recv.at[layer], block)
        second = Gather(place, r.ga, r.ag2_send.at[layer], r.ag2_recv.at[layer], block)
        in_sum = Scatter(place, r.part1, r.land1, r.rs2_send.at[layer], r.rs2_recv.at[layer], block)
        share = Share(place, r.inner, r.inner_land.at[layer], r.in_send.at[layer], r.in_recv.at[layer])
        first_head = layer * HEADS + place.me * heads_here

        def ready(rows):
            return turn * cfg.chunks + rows // CHUNK

        if turn > 0:
            decay_tiles(r.dec, first_head, r.tiles, heads_here, size)
            await_loads(*glu_in)
            await_loads(*out_in)
        scaling = lax.rsqrt(r.ss[...] / width + epsilon)
        for chunk in range(length // 128):
            r.scale[chunk * 128 : (chunk + 1) * 128, :] = spread(scaling, chunk)
        def glu_back(part, step):
            rows = aligned(place.member(step) * block + part * part_rows, part_rows)
            grad_hidden = nt(r.gd[rows, :], r.wd[...])
            grad_left = (grad_hidden * r.right[rows, :].astype(F32)).astype(BF16)
            grad_right = (grad_hidden * r.left[rows, :].astype(F32)).astype(BF16)
            r.right[rows, :] = grad_left
            r.left[rows, :] = grad_right
            r.part1[rows, :] = (nn(grad_left, r.wl[...]) + nn(grad_right, r.wr[...])).astype(BF16)
            for which in (1, 2, 3):
                @pl.when(step == which)
                def _():
                    mid_sum.send_block(part, which)

        if turn > 0:
            gather_stage(first, glu_back, lambda i: line.pump(ready(0), 2))
            first.drain()
        grad_left_ref, grad_right_ref = r.right, r.left

        def glu_grad_rows(base, a_ref, b_ref):
            line.release(turn, base + ff)
            for n in range(width // 256):
                cols = slice(n * 256, (n + 1) * 256)
                r.grads[base : base + ff, cols] = tn(a_ref[...], b_ref[:, cols]).astype(BF16)

        if turn > 0:
            await_loads(*glu_grad)
            for copy in mid_pieces:
                copy.wait()
        glu_grad_rows(base_down, r.hid, r.gd)
        line.pump(ready(base_left), 1 + turn)
        mid_sum.middle(0)
        glu_grad_rows(base_left, grad_left_ref, r.n2)
        line.pump(ready(base_right), 1 + turn)
        for part in range(1, SUPER):
            mid_sum.middle(part)
        glu_grad_rows(base_right, grad_right_ref, r.n2)
        for part in range(SUPER):
            line.pump(ready(base_out), 2 if part == 0 else 1)
            for h in range(2):
                mid_sum.finish(part, h)
                for i in range(half // step_rows):
                    offset = (2 * part + h) * half + i * step_rows
                    rows = slice(offset, offset + step_rows)
                    total = mid_sum.total(part, h, i * step_rows, step_rows)
                    if turn == 0:
                        values = r.mid[rows, :]
                    else:
                        pieces = range(width // (2 * HDIM))
                        values = jnp.concatenate([r.dq[n * block + offset : n * block + offset + step_rows, :] for n in pieces], axis=1)
                    new = back_rows(total, values, r.g[rows, :])
                    r.gm[rows, :] = new
                    r.ga[aligned(own_start + offset, step_rows), :] = new.astype(BF16)
            second.start(part)
        mid_sum.drain()
        if turn + 1 < layers:
            load(layer - 1, *glu_in, *glu_grad)

        def out_back(part, step):
            member = place.member(step)
            for chunk in range(part_rows // 128):
                number = part * (part_rows // 128) + chunk
                rows = aligned(member * block + number * 128, 128)
                grad_branch = nt(r.ga[rows, :], r.wo[...])
                gate = r.gate[rows, :]
                normed = r.heads[rows, :] * widen(r.scale[rows, :], local // 128)
                grad_normed = grad_branch * gate
                r.dx[rows, 3 * local : 4 * local] = (grad_branch * normed).astype(BF16)
                r.branch[rows, :] = (normed * gate).astype(BF16)
                r.gate[rows, :] = grad_normed
                row_sums(grad_normed * normed, r.inner, member * per_block + number)

        gather_stage(second, out_back, lambda i: line.pump(ready(base_out), 3 if i == SUPER else 2))
        share.start()
        line.release(turn, base_gate)
        r.grads[base_out : base_out + local, :] = tn(r.branch[...], r.ga[...]).astype(BF16)
        line.pump(ready(base_gate), 1)

        def in_grad_rows(number, base):
            cols = slice(number * local, (number + 1) * local)
            line.release(turn, base + local)
            for n in range(width // local):
                part_grad = tn(r.n1[:, n * local : (n + 1) * local], r.dx[:, cols])
                r.grads[base : base + local, n * local : (n + 1) * local] = part_grad.astype(BF16)

        if turn > 0:
            await_loads("n1")
        in_grad_rows(3, base_gate)
        line.pump(ready(base_qkv), 1)
        if turn > 0:
            await_loads(*attn_in)
        r.intot[...] = share.total() / width
        for chunk in range(length // 128):
            rows = slice(chunk * 128, (chunk + 1) * 128)
            scale = widen(r.scale[rows, :], local // 128)
            inner = widen(spread(r.intot[...], chunk), local // 128)
            normed = r.heads[rows, :] * scale
            r.dh[rows, :] = (scale * (r.gate[rows, :] - normed * inner)).astype(BF16)
        share.drain()
        second.drain()
        if turn + 1 < layers:
            load(layer - 1, *out_in)
        between = None
        if turn > 0:
            line.pump(ready(base_qkv), 1)
            between = line.done
            line.done += 1
            assert line.done <= ready(base_qkv)

        @pl.loop(0, heads_here)
        def _(head):
            if between is not None:
                @pl.when(head == 1)
                def _():
                    line.tick(between + head - 1)

            wide = aligned(head * 2 * HDIM, 2 * HDIM)
            thin = aligned(head * HDIM, HDIM)
            for col_tile in range(tiles_here):
                cols = slice(col_tile * size, (col_tile + 1) * size)
                keys = r.k[cols, wide]
                values = r.v[cols, thin]
                acc_key, acc_value = None, None
                for row_tile in range(col_tile, tiles_here):
                    rows = slice(row_tile * size, (row_tile + 1) * size)
                    queries = r.q[rows, wide]
                    grads = r.dh[rows, thin]
                    weight = tile_weight(r, first_head, head, row_tile, col_tile, size)
                    scores = (nt(queries, keys) * weight).astype(BF16)
                    pulled = (nt(grads, values) * weight).astype(BF16)
                    term = nn(pulled, keys)
                    if col_tile == 0:
                        r.dq[rows, :] = term
                    else:
                        r.dq[rows, :] += term
                    key_term = tn(pulled, queries)
                    value_term = tn(scores, grads)
                    acc_key = key_term if acc_key is None else acc_key + key_term
                    acc_value = value_term if acc_value is None else acc_value + value_term
                r.dk[cols, :] = acc_key
                r.dx[cols, aligned(2 * local + head * HDIM, HDIM)] = acc_value.astype(BF16)
            for row_tile in range(tiles_here):
                rows = slice(row_tile * size, (row_tile + 1) * size)
                cosine, sine = r.cos[rows, :], r.sin[rows, :]
                for grad, lin, base in ((r.dq, r.ql, 0), (r.dk, r.kl, local)):
                    v = lin[rows, thin].astype(F32)
                    gate = 1.0 / (1.0 + jnp.exp(-v))
                    back = grad[rows, :HDIM] * cosine + grad[rows, HDIM:] * sine
                    back = back * (gate + v * gate * (1.0 - gate))
                    r.dx[rows, aligned(base + head * HDIM, HDIM)] = back.astype(BF16)

        if turn + 1 < layers:
            load(layer - 1, *attn_in)
            source = getattr(r, "mid%d_h" % (layer - 1))
            mid_pieces = [
                copies.start(source.at[:, pl.ds(n * 2 * HDIM, 2 * HDIM)], r.dq.at[pl.ds(n * block, block), :])
                for n in range(width // (2 * HDIM))
            ]
        if turn > 0:
            await_loads(*in_in)
        last = turn == layers - 1
        if last:
            for number in range(3):
                in_grad_rows(number, base_qkv + number * local)
        for part in range(SUPER):
            for step in (3, 1, 2, 0):
                rows = aligned(place.member(step) * block + part * part_rows, part_rows)
                total = None
                for n, w in enumerate((r.wq, r.wk, r.wv, r.wg)):
                    term = nt(r.dx[rows, n * local : (n + 1) * local], w[...])
                    total = term if total is None else total + term
                r.part1[rows, :] = total.astype(BF16)
                in_sum.send_block(part, step)
            line.pump(ready(cfg.chunks * CHUNK if last else base_qkv), 2 if last else 1)
        for number in range(3):
            if not last:
                in_grad_rows(number, base_qkv + number * local)
            line.pump(ready(base_qkv + (number + 1) * local), 2 if last else 1)
            if number < SUPER:
                in_sum.middle(number)
        if last:
            for part in range(SUPER):
                for which in (1, 2, 3):
                    out_sum.send_block(part, which)
        if turn + 1 < layers:
            load(layer - 1, *in_in, "n1")
        for part in range(SUPER):
            line.pump(ready(cfg.chunks * CHUNK), 2 if last else 1)
            for h in range(2):
                in_sum.finish(part, h)
                for i in range(half // step_rows):
                    offset = (2 * part + h) * half + i * step_rows
                    rows = slice(offset, offset + step_rows)
                    total = in_sum.total(part, h, i * step_rows, step_rows)
                    values = getattr(r, "x%d" % layer)[rows, :].astype(F32)
                    new = back_rows(total, values, r.gm[rows, :])
                    if layer > 0:
                        r.g[rows, :] = new
                        r.gd[aligned(own_start + offset, step_rows), :] = new.astype(BF16)
                    else:
                        r.go[rows, :] = new.astype(BF16)
            if layer > 0:
                firsts[layer - 1].start(part)
        in_sum.drain()
    line.more(2)
    for part in range(SUPER):
        out_sum.middle(part)
        line.more(2)
    folded = finish_forward(r.xo, None)
    r.stat_mine[3 * top : 3 * top + 3, :] = folded[0:3, :]
    stats.square()
    line.more(1)
    stats.pair()
    for number in range(cfg.pairs):
        line.more(1)
        stats.stage(number)
    out_sum.drain()
    stats.finish()
    line.more(line.ticks)


def call_kernel(body, cfg, inputs, outputs, scratch, collective_id, name):
    vmem, anywhere = pl.BlockSpec(memory_space=pltpu.VMEM), pl.BlockSpec(memory_space=pl.ANY)
    names = list(inputs) + list(outputs) + list(scratch)
    result = pl.pallas_call(
        functools.partial(body, cfg, names),
        out_shape=[shape for shape, _ in outputs.values()],
        in_specs=[vmem if placed else anywhere for _, placed in inputs.values()],
        out_specs=[vmem if placed else anywhere for _, placed in outputs.values()],
        scratch_shapes=list(scratch.values()),
        compiler_params=pltpu.CompilerParams(
            collective_id=collective_id, has_side_effects=collective_id is not None, vmem_limit_bytes=VMEM_LIMIT
        ),
        name=name,
    )(*[array for array, _ in inputs.values()])
    return dict(zip(outputs, result))


def collective_scratch(cfg, copies, lead):
    dma = pltpu.SemaphoreType.DMA
    half = cfg.block // (2 * SUPER)
    out = {}
    for name in ("ag1", "ag2", "rs1", "rs2"):
        for key in (name, "f" + name):
            out[key + "_send"] = out[key + "_recv"] = dma((*lead, SUPER, 6))
    for name in copies:
        out["land" + name] = pltpu.VMEM((SUPER, 6, half, cfg.width), BF16)
        out["part" + name] = pltpu.VMEM((cfg.length, cfg.width), BF16)
    out["local_sem"] = dma((96,))
    return out


def weight_scratch(cfg):
    v = pltpu.VMEM
    return dict(
        wq=v((cfg.width, cfg.local), BF16), wk=v((cfg.width, cfg.local), BF16),
        wv=v((cfg.width, cfg.local), BF16), wg=v((cfg.width, cfg.local), BF16),
        wo=v((cfg.local, cfg.width), BF16), wl=v((cfg.ff, cfg.width), BF16),
        wr=v((cfg.ff, cfg.width), BF16), wd=v((cfg.ff, cfg.width), BF16),
    )


def table_scratch(cfg):
    v = pltpu.VMEM
    return dict(
        segc=v((cfg.length, 128), F32), segf=v((8, 128), F32),
        tiles=v((cfg.heads_here, 2, cfg.block, cfg.block), F32),
    )


def forward_scratch(cfg):
    v, dma = pltpu.VMEM, pltpu.SemaphoreType.DMA
    rows, wide, local, ff, block = cfg.length, cfg.width, cfg.local, cfg.ff, cfg.block
    return dict(
        n1=v((rows, wide), BF16), ql=v((rows, local), BF16), kl=v((rows, local), BF16), q=v((rows, 2 * local), BF16),
        k=v((rows, 2 * local), BF16), v=v((rows, local), BF16), gate=v((rows, local), F32), heads=v((rows, local), F32),
        mid=v((block, wide), F32), n2=v((rows, wide), BF16), left=v((rows, ff), BF16), right=v((rows, ff), BF16),
        hid=v((rows, ff), BF16), ss=v((8, 128), F32), ss_mine=v((8, 128), F32), dh=v((rows, local), BF16),
        stat_wide=v((8, wide), F32), scale=v((rows, 128), F32), ss_land=v((cfg.layers, 3, 8, 128), F32),
        ss_send=dma((cfg.layers, 3)), ss_recv=dma((cfg.layers, 3)),
    )


def gather_sems():
    sems = pltpu.SemaphoreType.DMA((SUPER, 6))
    return dict(ag3_send=sems, ag3_recv=sems)


SAVED = ("ss", "mid", "n1", "ql", "kl", "q", "k", "v", "gate", "heads", "n2", "left", "right", "hid")


def run_layers(cfg, tokens, upstream, tables, weights):
    v, dma, s = pltpu.VMEM, pltpu.SemaphoreType.DMA, jax.ShapeDtypeStruct
    rows, wide, local, ff, block = cfg.length, cfg.width, cfg.local, cfg.ff, cfg.block
    inputs = dict(
        up=(upstream, True), x0=(tokens, True), **{k: (a, True) for k, a in tables.items()},
        **{k + "_h": (a, False) for k, a in weights.items()},
    )
    total_rows = cfg.chunks * CHUNK
    outputs = dict(
        xo=(s((block, wide), BF16), True), go=(s((block, wide), BF16), True), stat_total=(s((8, 128), F32), True),
        out_h=(s((cfg.layers * total_rows, wide), BF16), False),
    )
    small, ring, ring_sem = v((8, 128), F32), v((SLOTS, CHUNK // 2, wide), BF16), dma((SLOTS,))
    scratch = dict(
        **weight_scratch(cfg), **collective_scratch(cfg, ("1", "2"), (cfg.layers,)), **table_scratch(cfg), **forward_scratch(cfg),
        **gather_sems(),
        gd=v((rows, wide), BF16), ga=v((rows, wide), BF16),
        g=v((block, wide), F32), gm=v((block, wide), F32),
        branch=v((rows, local), BF16), dx=v((rows, 4 * local), BF16),
        dq=v((rows, 2 * HDIM), F32), dk=v((rows, 2 * HDIM), F32),
        grads=v((total_rows, wide), BF16),
        inner=small, intot=small,
        inner_land=v((cfg.layers, 3, 8, 128), F32), in_send=dma((cfg.layers, 3)), in_recv=dma((cfg.layers, 3)),
        pair_land=ring, right_land=ring, left_land=ring,
        pair_send=ring_sem, pair_recv=ring_sem, right_send=ring_sem, right_recv=ring_sem, left_send=ring_sem,
        left_recv=ring_sem, give_send=ring_sem, give_recv=ring_sem, keep_sem=ring_sem,
        stat_mine=small, stat_square=small, stat_pair=small, stat_right=small, stat_left=small,
        stat_land=v((3, 8, 128), F32), st_send=dma((3,)), st_recv=dma((3,)),
        line_land=v((3, 8, 128), F32), line_send=dma((3,)), line_recv=dma((3,)),
    )
    for layer in range(1, cfg.layers):
        scratch["x%d" % layer] = v((block, wide), F32)
    for layer in range(cfg.layers - 1):
        for key in SAVED:
            outputs["%s%d_h" % (key, layer)] = (s(scratch[key].shape, scratch[key].dtype), False)
    return call_kernel(layers_kernel, cfg, inputs, outputs, scratch, 0, "layers")


def widen_kernel(cfg, names, *refs):
    r = namespace(names, refs)
    tasks = []
    for layer in range(cfg.layers):
        for number, target in enumerate((r.down, r.left, r.right, r.out)):
            start, stop = cfg.bases[number], cfg.bases[number + 1]
            rows = (stop - start) // 2 if stop - start > 512 else stop - start
            for first in range(start, stop, rows):
                tasks.append((layer, first, rows, [(target.at[layer, pl.ds(first - start, rows), :], slice(None))]))
        for number, target in enumerate((r.gate, r.query, r.key, r.value)):
            pieces = [
                (target.at[layer, pl.ds(n * cfg.local, cfg.local), :], slice(n * cfg.local, (n + 1) * cfg.local))
                for n in range(cfg.width // cfg.local)
            ]
            start = cfg.bases[6] + (number - 1) * cfg.local if number > 0 else cfg.bases[4]
            tasks.append((layer, start, cfg.local, pieces))
    depth = WIDEN_DEPTH
    whole_in = [
        pltpu.make_async_copy(r.xo_in, r.whole.at[0], r.whole_sem.at[0]),
        pltpu.make_async_copy(r.go_in, r.whole.at[1], r.whole_sem.at[1]),
    ]
    whole_out = [
        pltpu.make_async_copy(r.whole.at[0], r.xo, r.whole_sem.at[2]),
        pltpu.make_async_copy(r.whole.at[1], r.go, r.whole_sem.at[3]),
    ]
    for copy in whole_in:
        copy.start()
    means = jnp.sum(r.stat[...], axis=1, keepdims=True) / cfg.entries
    roots = jnp.sqrt(means)
    for layer in range(cfg.layers):
        for number in range(3):
            row = 3 * layer + number
            r.rms[layer : layer + 1, number : number + 1] = roots[row : row + 1, :]

    def fetch(task):
        layer, first, rows, _ = tasks[task]
        start = layer * cfg.chunks * CHUNK + first
        slot = task % depth
        return pltpu.make_async_copy(r.grads.at[pl.ds(start, rows), :], r.narrow.at[slot, pl.ds(0, rows), :], r.in_sem.at[slot])

    def store(task):
        _, _, rows, pieces = tasks[task]
        slot = task % depth
        return [
            pltpu.make_async_copy(r.wide.at[slot, pl.ds(0, rows), lanes], target, r.out_sem.at[slot, n])
            for n, (target, lanes) in enumerate(pieces)
        ]

    for task in range(min(depth, len(tasks))):
        fetch(task).start()
    for task in range(len(tasks)):
        if task == 2:
            for one, other in zip(whole_in, whole_out):
                one.wait()
                other.start()
        slot, rows = task % depth, tasks[task][2]
        fetch(task).wait()
        if task >= depth:
            for copy in store(task - depth):
                copy.wait()

        @pl.loop(0, rows // 32)
        def _(i):
            part = aligned(i * 32, 32)
            r.wide[slot, part, :] = r.narrow[slot, part, :].astype(F32)

        for copy in store(task):
            copy.start()
        if task + depth < len(tasks):
            fetch(task + depth).start()
    for task in range(max(len(tasks) - depth, 0), len(tasks)):
        for copy in store(task):
            copy.wait()
    for copy in whole_out:
        copy.wait()


def run_widen(cfg, back):
    v, dma, s = pltpu.VMEM, pltpu.SemaphoreType.DMA, jax.ShapeDtypeStruct
    thin, flat = s((cfg.layers, cfg.width, cfg.local), F32), s((cfg.layers, cfg.ff, cfg.width), F32)
    outputs = dict(
        down=(flat, False), left=(flat, False), right=(flat, False), out=(s((cfg.layers, cfg.local, cfg.width), F32), False),
        gate=(thin, False), query=(thin, False), key=(thin, False), value=(thin, False),
        xo=(s((cfg.block, cfg.width), BF16), False), go=(s((cfg.block, cfg.width), BF16), False),
        rms=(s((cfg.layers, 3), F32), True),
    )
    inputs = dict(grads=(back["out_h"], False), xo_in=(back["xo"], False), go_in=(back["go"], False), stat=(back["stat_total"], True))
    rows = max(cfg.ff // 2, cfg.local, 512)
    scratch = dict(
        narrow=v((WIDEN_DEPTH, rows, cfg.width), BF16), wide=v((WIDEN_DEPTH, rows, cfg.width), F32),
        whole=v((2, cfg.block, cfg.width), BF16), whole_sem=dma((4,)), in_sem=dma((WIDEN_DEPTH,)), out_sem=dma((WIDEN_DEPTH, cfg.width // cfg.local)),
    )
    return call_kernel(widen_kernel, cfg, inputs, outputs, scratch, None, "widen_gradients")


def per_device_square(
    tokens, upstream, segment_ids, query_proj, key_proj, value_proj, gate_proj, output_proj, left_proj, right_proj, down_proj
):
    layers = query_proj.shape[0]
    block, width = tokens.shape
    length = segment_ids.shape[0]
    local, ff = query_proj.shape[2], left_proj.shape[2]
    heads_here = local // HDIM
    positions = np.arange(length, dtype=np.float32)
    frequency = np.exp(np.float32(-math.log(10000.0)) * np.arange(HDIM, dtype=np.float32) / np.float32(HDIM))
    angles = positions[:, None] * frequency[None, :]
    slopes = np.exp2(-8.0 * (np.arange(HEADS) + 1.0) / HEADS)
    decays = np.concatenate([-slopes * (1.0 - depth_start - depth_step * layer) for layer in range(layers)])
    tables = dict(
        cos=jnp.asarray(np.cos(angles)), sin=jnp.asarray(np.sin(angles)),
        dec=jnp.asarray(np.broadcast_to(decays[:, None], (layers * HEADS, 128)).astype(np.float32)),
        seg=segment_ids.reshape(8, length // 8),
    )
    weights = dict(
        wq=query_proj, wk=key_proj, wv=value_proj, wg=gate_proj, wo=output_proj,
        wl=jnp.swapaxes(left_proj, 1, 2), wr=jnp.swapaxes(right_proj, 1, 2), wd=down_proj,
    )
    ends = np.cumsum([0, ff, ff, ff, local, local]).tolist()
    ends += [-(-ends[-1] // CHUNK) * CHUNK]
    ends += [-(-(ends[-1] + 3 * local) // CHUNK) * CHUNK]
    common = dict(
        layers=layers, block=block, length=length, width=width, local=local, ff=ff, heads_here=heads_here,
        pairs=lax.axis_size("dp") // 2, bases=ends, chunks=ends[-1] // CHUNK,
    )
    back = run_layers(types.SimpleNamespace(**common), tokens, upstream, tables, weights)
    entries = float(length * lax.axis_size("dp") * width)
    wide = run_widen(types.SimpleNamespace(entries=entries, **common), back)
    return (
        wide["xo"], wide["go"], wide["query"], wide["key"], wide["value"], wide["gate"], wide["out"],
        jnp.swapaxes(wide["left"], 1, 2), jnp.swapaxes(wide["right"], 1, 2), wide["down"], wide["rms"],
    )


def solution(mesh):
    square = dict(mesh.shape) == SQUARE_MESH
    body = per_device_square if square else per_device
    return jax.shard_map(
        body,
        mesh=mesh,
        in_specs=(
            P(("dp", "tensor"), None),
            P(("dp", "tensor"), None),
            P("dp"),
            P(None, None, "tensor"),
            P(None, None, "tensor"),
            P(None, None, "tensor"),
            P(None, None, "tensor"),
            P(None, "tensor", None),
            P(None, None, "tensor"),
            P(None, None, "tensor"),
            P(None, "tensor", None),
        ),
        out_specs=(
            P(("dp", "tensor"), None),
            P(("dp", "tensor"), None),
            P(None, None, "tensor"),
            P(None, None, "tensor"),
            P(None, None, "tensor"),
            P(None, None, "tensor"),
            P(None, "tensor", None),
            P(None, None, "tensor"),
            P(None, None, "tensor"),
            P(None, "tensor", None),
            P(),
        ),
        check_vma=False,
    )
```

```python
import functools
import math
import types

import jax
import jax.numpy as jnp
import numpy as np
from jax import lax
from jax.experimental import pallas as pl
from jax.experimental.pallas import tpu as pltpu
from jax.sharding import PartitionSpec as P

HEADS = 8
HDIM = 128
BLK = 512


epsilon = 1e-06
depth_start = 0.5
depth_step = 1.0 / 24.0
highest = lax.Precision.HIGHEST


def rms_rows(values):
    return values * lax.rsqrt(jnp.mean(values * values, axis=1, keepdims=True) + epsilon)


def rms_back(values, gradient):
    scaling = lax.rsqrt(jnp.mean(values * values, axis=1, keepdims=True) + epsilon)
    normed = values * scaling
    return scaling * (gradient - normed * jnp.mean(gradient * normed, axis=1, keepdims=True))


def contract_last(left_part, right_part):
    return lax.dot_general(
        left_part, right_part, (((1,), (1,)), ((), ())), preferred_element_type=jnp.float32
    )


def contract_first(left_part, right_part):
    return lax.dot_general(
        left_part, right_part, (((0,), (0,)), ((), ())), preferred_element_type=jnp.float32
    )


def rotate(values, cosine, sine_table):
    return jnp.concatenate([values * cosine[:, None, :], values * sine_table[:, None, :]], axis=2)


def unrotate(gradient, cosine, sine_table):
    half_width = gradient.shape[2] // 2
    return (
        gradient[:, :, :half_width] * cosine[:, None, :]
        + gradient[:, :, half_width:] * sine_table[:, None, :]
    )


def split_blocks(array, block_count):
    return array.reshape((block_count, BLK) + array.shape[1:])


def block_weights(seg_block, next_seg, decay_log):
    block_width = seg_block.shape[0]
    places = jnp.arange(block_width, dtype=jnp.float32)
    distance = places[:, None] - places[None, :]
    allowed = (distance >= 0) & (seg_block[:, None] == seg_block[None, :])
    decay_grid = jnp.where(
        allowed[None], jnp.exp(decay_log[:, None, None] * jnp.maximum(distance, 0.0)[None]), 0.0
    )
    first_seg = seg_block[0]
    query_gain = jnp.where(
        (seg_block == first_seg)[:, None], jnp.exp(places[:, None] * decay_log[None, :]), 0.0
    )
    key_gain = jnp.where(
        (seg_block == next_seg)[:, None],
        jnp.exp((block_width - places)[:, None] * decay_log[None, :]),
        0.0,
    )
    carry_gain = jnp.where(first_seg == next_seg, jnp.exp(decay_log * block_width), 0.0)
    return (decay_grid, query_gain, key_gain, carry_gain)


def next_segments(segments, block_count):
    seg_blocks = segments.reshape(block_count, BLK)
    return (seg_blocks, jnp.concatenate([seg_blocks[1:, 0], jnp.full((1,), -1, jnp.int32)]))


def attend_forward(queries, keys_rot, values, segments, decay_log):
    length, heads_here, pair_width = queries.shape
    block_count = length // BLK
    seg_blocks, next_segs = next_segments(segments, block_count)

    def advance(state_now, block_items):
        query_block, key_block, value_block, seg_block, next_seg = block_items
        query_float = query_block.astype(jnp.float32)
        key_float = key_block.astype(jnp.float32)
        value_float = value_block.astype(jnp.float32)
        decay_grid, query_gain, key_gain, carry_gain = block_weights(seg_block, next_seg, decay_log)
        scores = (
            jnp.einsum("rhd,shd->hrs", query_block, key_block, preferred_element_type=jnp.float32)
            * decay_grid
        )
        block_out = jnp.einsum("hrs,she->rhe", scores, value_float, precision=highest)
        block_out = (
            block_out
            + jnp.einsum("rhd,hde->rhe", query_float, state_now, precision=highest)
            * query_gain[:, :, None]
        )
        new_state = carry_gain[:, None, None] * state_now + jnp.einsum(
            "shd,she->hde", key_float * key_gain[:, :, None], value_float, precision=highest
        )
        return (new_state, (block_out, state_now))

    zero_state = jnp.zeros((heads_here, pair_width, pair_width // 2), jnp.float32)
    _, (block_outs, states) = lax.scan(
        advance,
        zero_state,
        (
            split_blocks(queries, block_count),
            split_blocks(keys_rot, block_count),
            split_blocks(values, block_count),
            seg_blocks,
            next_segs,
        ),
    )
    return (block_outs.reshape(length, heads_here * (pair_width // 2)), states)


def attend_backward(queries, keys_rot, values, segments, decay_log, states, grad_heads):
    length, heads_here, pair_width = queries.shape
    block_count = length // BLK
    seg_blocks, next_segs = next_segments(segments, block_count)

    def retreat(later_grad, block_items):
        query_block, key_block, value_block, seg_block, next_seg, state_now, grad_block = (
            block_items
        )
        query_float = query_block.astype(jnp.float32)
        key_float = key_block.astype(jnp.float32)
        value_float = value_block.astype(jnp.float32)
        decay_grid, query_gain, key_gain, carry_gain = block_weights(seg_block, next_seg, decay_log)
        scores = (
            jnp.einsum("rhd,shd->hrs", query_block, key_block, preferred_element_type=jnp.float32)
            * decay_grid
        )
        pulled = jnp.einsum("rhe,she->hrs", grad_block, value_float, precision=highest) * decay_grid
        grad_query = jnp.einsum("hrs,shd->rhd", pulled, key_float, precision=highest)
        grad_query = (
            grad_query
            + jnp.einsum("rhe,hde->rhd", grad_block, state_now, precision=highest)
            * query_gain[:, :, None]
        )
        grad_key = jnp.einsum("hrs,rhd->shd", pulled, query_float, precision=highest)
        grad_key = (
            grad_key
            + jnp.einsum("she,hde->shd", value_float, later_grad, precision=highest)
            * key_gain[:, :, None]
        )
        grad_value = jnp.einsum("hrs,rhe->she", scores, grad_block, precision=highest)
        grad_value = (
            grad_value
            + jnp.einsum("shd,hde->she", key_float, later_grad, precision=highest)
            * key_gain[:, :, None]
        )
        earlier_grad = carry_gain[:, None, None] * later_grad + jnp.einsum(
            "rhd,rhe->hde", query_float * query_gain[:, :, None], grad_block, precision=highest
        )
        return (earlier_grad, (grad_query, grad_key, grad_value))

    zero_state = jnp.zeros((heads_here, pair_width, pair_width // 2), jnp.float32)
    _, (grad_query, grad_key, grad_value) = lax.scan(
        retreat,
        zero_state,
        (
            split_blocks(queries, block_count),
            split_blocks(keys_rot, block_count),
            split_blocks(values, block_count),
            seg_blocks,
            next_segs,
            states,
            split_blocks(grad_heads, block_count),
        ),
        reverse=True,
    )
    return (
        grad_query.reshape(length, heads_here, pair_width),
        grad_key.reshape(length, heads_here, pair_width),
        grad_value.reshape(length, heads_here, pair_width // 2),
    )


def per_device(
    tokens,
    upstream,
    segment_ids,
    query_proj,
    key_proj,
    value_proj,
    gate_proj,
    output_proj,
    left_proj,
    right_proj,
    down_proj,
):
    layers = query_proj.shape[0]
    row_count, model_width = tokens.shape
    length = segment_ids.shape[0]
    local_width = query_proj.shape[2]
    ff_local = left_proj.shape[2]
    heads_here = local_width // HDIM
    positions = jnp.arange(length, dtype=jnp.float32)
    frequency = jnp.exp(-math.log(10000.0) * jnp.arange(HDIM, dtype=jnp.float32) / HDIM)
    angles = positions[:, None] * frequency[None, :]
    cosine = jnp.cos(angles)
    sine_table = jnp.sin(angles)
    head_index = (lax.axis_index("tensor") * heads_here + jnp.arange(heads_here)).astype(
        jnp.float32
    )
    slopes = jnp.exp2(-8.0 * (head_index + 1.0) / HEADS)

    def gather_normed(normed):
        return lax.all_gather(normed, "tensor", axis=0, tiled=True)

    def gather_again(normed):
        return lax.all_gather(normed, "tensor", axis=0, tiled=True)

    def gather_grads(gradient):
        return lax.all_gather(gradient, "tensor", axis=0, tiled=True)

    def branch_sum(operand, matrix):
        return lax.psum_scatter(
            jnp.dot(operand, matrix, preferred_element_type=jnp.float32).astype(jnp.bfloat16),
            "tensor",
            scatter_dimension=0,
            tiled=True,
        ).astype(jnp.float32)

    def input_sum(pieces, matrix):
        operand = jnp.concatenate(pieces, axis=1)
        return lax.psum_scatter(
            contract_last(operand, matrix).astype(jnp.bfloat16),
            "tensor",
            scatter_dimension=0,
            tiled=True,
        ).astype(jnp.float32)

    current = tokens.astype(jnp.float32)
    saved_layers = []
    stat_terms = []
    for layer_index in range(layers):
        residual = current
        normed = rms_rows(residual).astype(jnp.bfloat16)
        full_normed = gather_normed(normed)
        attn_weight = jnp.concatenate(
            [
                query_proj[layer_index],
                key_proj[layer_index],
                value_proj[layer_index],
                gate_proj[layer_index],
            ],
            axis=1,
        )
        projected = jnp.dot(full_normed, attn_weight, preferred_element_type=jnp.float32)
        query_lin = projected[:, :local_width]
        key_lin = projected[:, local_width : 2 * local_width]
        values = (
            projected[:, 2 * local_width : 3 * local_width]
            .astype(jnp.bfloat16)
            .reshape(length, heads_here, HDIM)
        )
        gate_lin = projected[:, 3 * local_width :]
        queries = rotate(
            jax.nn.silu(query_lin).reshape(length, heads_here, HDIM), cosine, sine_table
        ).astype(jnp.bfloat16)
        keys_rot = rotate(
            jax.nn.silu(key_lin).reshape(length, heads_here, HDIM), cosine, sine_table
        ).astype(jnp.bfloat16)
        decay_log = -slopes * (1.0 - depth_start - depth_step * layer_index)
        heads_out, states = attend_forward(queries, keys_rot, values, segment_ids, decay_log)
        squares = lax.psum(jnp.sum(heads_out * heads_out, axis=1), "tensor")
        scaling = lax.rsqrt(squares / model_width + epsilon)[:, None]
        normed_heads = heads_out * scaling
        branch = (normed_heads * gate_lin).astype(jnp.bfloat16)
        attn_rows = branch_sum(branch, output_proj[layer_index])
        middle = residual + attn_rows
        normed_mid = rms_rows(middle).astype(jnp.bfloat16)
        full_mid = gather_normed(normed_mid)
        glu_weight = jnp.concatenate([left_proj[layer_index], right_proj[layer_index]], axis=1)
        gates_both = jnp.dot(full_mid, glu_weight, preferred_element_type=jnp.float32)
        left_lin = gates_both[:, :ff_local]
        right_lin = gates_both[:, ff_local:]
        hidden = (left_lin * right_lin).astype(jnp.bfloat16)
        glu_rows = branch_sum(hidden, down_proj[layer_index])
        current = middle + glu_rows
        stat_terms.append(
            jnp.stack(
                [
                    jnp.sum(attn_rows * attn_rows),
                    jnp.sum(glu_rows * glu_rows),
                    jnp.sum(current * current),
                ]
            )
        )
        saved_layers.append(
            (
                residual,
                middle,
                normed,
                normed_mid,
                full_normed,
                full_mid,
                attn_weight,
                glu_weight,
                query_lin,
                key_lin,
                gate_lin,
                queries,
                keys_rot,
                values,
                decay_log,
                states,
                normed_heads,
                scaling,
                branch,
                left_lin,
                right_lin,
                hidden,
            )
        )
    stat_sums = lax.psum(jnp.stack(stat_terms), ("dp", "tensor"))
    rms_stats = jnp.sqrt(stat_sums / (length * lax.axis_size("dp") * model_width))
    final_rows = current.astype(jnp.bfloat16)
    gradient = upstream.astype(jnp.float32)
    layer_results = [None] * layers
    for layer_index in reversed(range(layers)):
        (
            residual,
            middle,
            normed,
            normed_mid,
            full_normed,
            full_mid,
            attn_weight,
            glu_weight,
            query_lin,
            key_lin,
            gate_lin,
            queries,
            keys_rot,
            values,
            decay_log,
            states,
            normed_heads,
            scaling,
            branch,
            left_lin,
            right_lin,
            hidden,
        ) = saved_layers[layer_index]
        glu_grad = gather_grads(gradient.astype(jnp.bfloat16))
        grad_hidden = contract_last(glu_grad, down_proj[layer_index])
        down_part = contract_first(hidden, glu_grad)
        grad_left = (grad_hidden * right_lin).astype(jnp.bfloat16)
        grad_right = (grad_hidden * left_lin).astype(jnp.bfloat16)
        grad_gates = jnp.concatenate([grad_left, grad_right], axis=1)
        mid_rows = input_sum((grad_left, grad_right), glu_weight)
        source_mid = gather_again(normed_mid)
        glu_part = contract_first(source_mid, grad_gates)
        gradient = gradient + rms_back(middle, mid_rows)
        attn_grad = gather_grads(gradient.astype(jnp.bfloat16))
        output_part = contract_first(branch, attn_grad)
        grad_branch = contract_last(attn_grad, output_proj[layer_index])
        grad_normed = grad_branch * gate_lin
        grad_gate = (grad_branch * normed_heads).astype(jnp.bfloat16)
        inner_sum = lax.psum(jnp.sum(grad_normed * normed_heads, axis=1), "tensor")
        grad_heads = scaling * (grad_normed - normed_heads * (inner_sum / model_width)[:, None])
        grad_query, grad_key, grad_value = attend_backward(
            queries,
            keys_rot,
            values,
            segment_ids,
            decay_log,
            states,
            grad_heads.reshape(length, heads_here, HDIM),
        )
        sigmoid_query = jax.nn.sigmoid(query_lin)
        sigmoid_key = jax.nn.sigmoid(key_lin)
        query_back = unrotate(grad_query, cosine, sine_table).reshape(length, local_width)
        key_back = unrotate(grad_key, cosine, sine_table).reshape(length, local_width)
        grad_query_lin = (
            query_back * (sigmoid_query + query_lin * sigmoid_query * (1.0 - sigmoid_query))
        ).astype(jnp.bfloat16)
        grad_key_lin = (
            key_back * (sigmoid_key + key_lin * sigmoid_key * (1.0 - sigmoid_key))
        ).astype(jnp.bfloat16)
        grad_value_lin = grad_value.reshape(length, local_width).astype(jnp.bfloat16)
        grad_projected = jnp.concatenate(
            [grad_query_lin, grad_key_lin, grad_value_lin, grad_gate], axis=1
        )
        in_rows = input_sum((grad_query_lin, grad_key_lin, grad_value_lin, grad_gate), attn_weight)
        source_normed = gather_again(normed)
        attn_part = contract_first(source_normed, grad_projected)
        gradient = gradient + rms_back(residual, in_rows)
        query_part = attn_part[:, :local_width]
        key_part = attn_part[:, local_width : 2 * local_width]
        value_part = attn_part[:, 2 * local_width : 3 * local_width]
        gate_part = attn_part[:, 3 * local_width :]
        left_part = glu_part[:, :ff_local]
        right_part = glu_part[:, ff_local:]
        layer_results[layer_index] = (
            query_part,
            key_part,
            value_part,
            gate_part,
            output_part,
            left_part,
            right_part,
            down_part,
        )
    stacked = [
        jnp.stack([layer_results[index][member] for index in range(layers)]) for member in range(8)
    ]
    totals = (
        lax.psum(stacked[0].astype(jnp.bfloat16), "dp").astype(jnp.float32),
        lax.psum(stacked[1].astype(jnp.bfloat16), "dp").astype(jnp.float32),
        lax.psum(stacked[2].astype(jnp.bfloat16), "dp").astype(jnp.float32),
        lax.psum(stacked[3].astype(jnp.bfloat16), "dp").astype(jnp.float32),
        lax.psum(stacked[4].astype(jnp.bfloat16), "dp").astype(jnp.float32),
        lax.psum(stacked[5].astype(jnp.bfloat16), "dp").astype(jnp.float32),
        lax.psum(stacked[6].astype(jnp.bfloat16), "dp").astype(jnp.float32),
        lax.psum(stacked[7].astype(jnp.bfloat16), "dp").astype(jnp.float32),
    )
    input_grad = gradient.astype(jnp.bfloat16)
    return (
        final_rows,
        input_grad,
        totals[0],
        totals[1],
        totals[2],
        totals[3],
        totals[4],
        totals[5],
        totals[6],
        totals[7],
        rms_stats,
    )


SQUARE_MESH = {"dp": 8, "tensor": 4}


F32 = jnp.float32
BF16 = jnp.bfloat16
MESH = pl.DeviceIdType.MESH
VMEM_LIMIT = 62 * 2**20
SUPER = 2
EARLY = (0,)
WIDEN_DEPTH = 6
CHUNK = 128
HOP = 3
SLOTS = 16


def nn(a, b):
    return lax.dot_general(a, b, (((1,), (0,)), ((), ())), preferred_element_type=F32)


def nt(a, b):
    return lax.dot_general(a, b, (((1,), (1,)), ((), ())), preferred_element_type=F32)


def tn(a, b):
    return lax.dot_general(a, b, (((0,), (0,)), ((), ())), preferred_element_type=F32)


def exact(a, b, dims):
    return lax.dot_general(a, b, (dims, ((), ())), precision=highest, preferred_element_type=F32)


def aligned(index, size):
    return pl.ds(pl.multiple_of(index, size), size)


class Place:
    def __init__(self, pairs):
        self.dp = lax.axis_index("dp")
        self.me = lax.axis_index("tensor")
        self.low = lax.rem(self.me, 2)
        self.high = self.me // 2
        self.core = lax.rem(self.dp, 2)
        self.at = self.dp // 2
        self.last = pairs - 1

    def member(self, step):
        low = lax.rem(self.low + lax.rem(step, 2), 2)
        high = lax.rem(self.high + step // 2, 2)
        return 2 * high + low

    def device(self, step):
        return (self.dp, self.member(step))

    def partner(self):
        return (self.dp + 1 - 2 * self.core, self.me)

    def right(self):
        return (self.dp + 2, self.me)

    def left(self):
        return (self.dp - 2, self.me)

    def greet(self, line):
        barrier = pltpu.get_barrier_semaphore()

        def signal(device):
            pl.semaphore_signal(barrier, inc=1, device_id=device, device_id_type=MESH)

        for step in (1, 2, 3):
            signal(self.device(step))
        if not line:
            pl.semaphore_wait(barrier, 3)
            return
        signal(self.partner())

        @pl.when(self.at < self.last)
        def _():
            signal(self.right())

        @pl.when(self.at > 0)
        def _():
            signal(self.left())

        pl.semaphore_wait(barrier, 4 + jnp.minimum(self.at, 1) + jnp.minimum(self.last - self.at, 1))


class Wire:
    def __init__(self, device, send_sem, recv_sem, source, target, landing):
        self.source, self.target, self.landing = source, target, landing
        self.common = dict(send_sem=send_sem, recv_sem=recv_sem, device_id=device, device_id_type=MESH)

    def out(self):
        return pltpu.make_async_remote_copy(src_ref=self.source, dst_ref=self.target, **self.common)

    def start(self):
        self.out().start()

    def wait_recv(self):
        pltpu.make_async_remote_copy(src_ref=self.landing, dst_ref=self.landing, **self.common).wait_recv()

    def wait_send(self):
        self.out().wait_send()


class Gather:
    def __init__(self, place, buf, send, recv, block):
        self.place, self.buf, self.block = place, buf, block
        self.send, self.recv = send, recv
        self.half = block // (2 * SUPER)

    def rows(self, step, part, half):
        start = self.place.member(step) * self.block + (2 * part + half) * self.half
        return self.buf.at[aligned(start, self.half)]

    def wire(self, part, number):
        step, owner, half = ((1, 0, 0), (2, 0, 1), (1, 0, 1), (2, 0, 0), (2, 1, 0), (1, 2, 1))[number]
        source = self.rows(owner, part, half)
        landing = self.rows((0, 1, 2, 3)[owner ^ step], part, half)
        return Wire(self.place.device(step), self.send.at[part, number], self.recv.at[part, number], source, source, landing)

    def start(self, part):
        for number in range(4):
            self.wire(part, number).start()

    def forward(self, part):
        self.wire(part, 0).wait_recv()
        self.wire(part, 4).start()
        self.wire(part, 1).wait_recv()
        self.wire(part, 5).start()

    def finish(self, part, step):
        for number in {0: (), 1: (2,), 2: (3,), 3: (4, 5)}[step]:
            self.wire(part, number).wait_recv()

    def drain(self, parts=range(SUPER)):
        for part in parts:
            for number in range(6):
                self.wire(part, number).wait_send()


def gather_stage(gather, block_fn, beside):
    @pl.loop(0, 4 * SUPER)
    def _(i):
        mixed = i - SUPER
        part = jnp.where(i < SUPER, i, jnp.where(i < 3 * SUPER, mixed // 2, i - 3 * SUPER))
        step = jnp.where(i < SUPER, 0, jnp.where(i < 3 * SUPER, 1 + lax.rem(mixed, 2), 3))

        @pl.when(i == SUPER)
        def _():
            for one in range(SUPER):
                beside(one)
                gather.forward(one)

        @pl.when(i == 3 * SUPER)
        def _():
            beside(SUPER)

        for which in (1, 2, 3):
            @pl.when(step == which)
            def _():
                gather.finish(part, which)
        block_fn(part, step)


class Scatter:
    def __init__(self, place, buf, land, send, recv, block):
        self.place, self.buf, self.land, self.block = place, buf, land, block
        self.send, self.recv = send, recv
        self.half = block // (2 * SUPER)

    def rows(self, step, part, half):
        start = self.place.member(step) * self.block + (2 * part + half) * self.half
        return aligned(start, self.half)

    def wire(self, part, number):
        step, owner, half = ((1, 3, 0), (1, 1, 0), (2, 3, 1), (2, 2, 1), (2, 2, 0), (1, 1, 1))[number]
        target = self.land.at[part, number]
        return Wire(
            self.place.device(step), self.send.at[part, number], self.recv.at[part, number],
            self.buf.at[self.rows(owner, part, half)], target, target,
        )

    def send_block(self, part, step):
        for number in {0: (), 1: (1,), 2: (3,), 3: (0, 2)}[step]:
            self.wire(part, number).start()

    def middle(self, part):
        for first, second, owner, half in ((0, 4, 2, 0), (2, 5, 1, 1)):
            self.wire(part, first).wait_recv()
            rows = self.rows(owner, part, half)
            self.buf[rows, :] = self.buf[rows, :] + self.land[part, first]
            self.wire(part, second).start()

    def finish(self, part, half):
        first, second = ((1, 4), (3, 5))[half]
        self.wire(part, first).wait_recv()
        self.wire(part, second).wait_recv()

    def total(self, part, half, start, count):
        first, second = ((1, 4), (3, 5))[half]
        own = self.place.me * self.block + (2 * part + half) * self.half + start
        rows = pl.ds(start, count)
        return (
            self.buf[aligned(own, count), :].astype(F32)
            + self.land[part, first, rows, :].astype(F32)
            + self.land[part, second, rows, :].astype(F32)
        )

    def drain(self):
        for part in range(SUPER):
            for number in range(6):
                self.wire(part, number).wait_send()


class Share:
    def __init__(self, place, mine, land, send, recv):
        self.wires = [
            Wire(place.device(step), send.at[step - 1], recv.at[step - 1], mine, land.at[step - 1], land.at[step - 1])
            for step in (1, 2, 3)
        ]
        self.mine, self.land = mine, land

    def start(self):
        for wire in self.wires:
            wire.start()

    def total(self):
        for wire in self.wires:
            wire.wait_recv()
        return self.mine[...] + self.land[0] + self.land[1] + self.land[2]

    def drain(self):
        for wire in self.wires:
            wire.wait_send()


class Local:
    def __init__(self, sems):
        self.sems, self.used = sems, 0

    def start(self, source, target):
        copy = pltpu.make_async_copy(source, target, self.sems.at[self.used])
        self.used += 1
        copy.start()
        return copy


def row_sums(values, target, chunk):
    sums = exact(jnp.ones((8, values.shape[1]), F32), values, ((1,), (1,)))
    target[pl.ds(chunk, 1), :] = sums[0:1, :]


def spread(sums, chunk):
    picked = (lax.broadcasted_iota(jnp.int32, (8, 128), 0) == chunk).astype(F32)
    return exact(sums, picked, ((0,), (0,)))


def widen(columns, times):
    return jnp.concatenate([columns] * times, axis=1)


def decay_tiles(dec_ref, first_head, tiles, heads_here, size):
    rows = lax.broadcasted_iota(jnp.int32, (size, size), 0)
    cols = lax.broadcasted_iota(jnp.int32, (size, size), 1)
    distance = (rows - cols).astype(F32)
    for head in range(heads_here):
        decay = dec_ref[pl.ds(first_head + head, 1), 0:1]
        tiles[head, 0] = jnp.where(rows >= cols, jnp.exp(decay * jnp.maximum(distance, 0.0)), 0.0)
        tiles[head, 1] = jnp.exp(decay * (distance + float(size)))


def spread_segments(r, length):
    r.segf[...] = r.seg[...].astype(F32)
    for chunk in range(length // 128):
        r.segc[chunk * 128 : (chunk + 1) * 128, :] = spread(r.segf[...], chunk)


def tile_weight(r, first_head, head, row_tile, col_tile, size):
    gap = row_tile - col_tile
    if gap == 0:
        weight = r.tiles[head, 0]
    else:
        weight = r.tiles[head, 1]
        if gap > 1:
            decay = r.dec[pl.ds(first_head + head, 1), 0:1]
            weight = weight * jnp.exp(decay * float(size * (gap - 1)))
    row_seg = widen(r.segc[row_tile * size : (row_tile + 1) * size, :], size // 128)
    per = size // 128
    col_seg = jnp.concatenate([r.segf[per * col_tile + i : per * col_tile + i + 1, :] for i in range(per)], axis=1)
    return jnp.where(row_seg == col_seg, weight, 0.0)


def namespace(names, refs):
    return types.SimpleNamespace(**dict(zip(names, refs)))


def forward_front(cfg, r, place, copies, layer, x, save, third, third_parts, back_block):
    block, length, width = cfg.block, cfg.length, cfg.width
    heads_here, size = cfg.heads_here, cfg.block
    first_head = layer * HEADS + place.me * heads_here
    w_in = [copies.start(h.at[layer], v) for h, v in (
        (r.wq_h, r.wq), (r.wk_h, r.wk), (r.wv_h, r.wv), (r.wg_h, r.wg))]
    w_out = copies.start(r.wo_h.at[layer], r.wo)
    w_glu = [copies.start(h.at[layer], v) for h, v in ((r.wl_h, r.wl), (r.wr_h, r.wr), (r.wd_h, r.wd))]
    first = Gather(place, r.n1, r.fag1_send.at[layer], r.fag1_recv.at[layer], block)
    mid_sum = Scatter(place, r.part1, r.land1, r.frs1_send.at[layer], r.frs1_recv.at[layer], block)
    second = Gather(place, r.n2, r.fag2_send.at[layer], r.fag2_recv.at[layer], block)
    out_sum = Scatter(place, r.part2, r.land2, r.frs2_send.at[layer], r.frs2_recv.at[layer], block)
    share = Share(place, r.ss_mine, r.ss_land.at[layer], r.ss_send.at[layer], r.ss_recv.at[layer])
    half, step_rows = first.half, 32
    own_start = place.me * block

    if layer == 0:
        @pl.loop(0, block // step_rows)
        def _(i):
            rows = aligned(i * step_rows, step_rows)
            v = x[rows, :].astype(F32)
            scale = lax.rsqrt(jnp.mean(v * v, axis=1, keepdims=True) + epsilon)
            r.n1[aligned(own_start + i * step_rows, step_rows), :] = (v * scale).astype(BF16)

        place.greet(True)
        for part in range(SUPER):
            first.start(part)
        spread_segments(r, length)
    decay_tiles(r.dec, first_head, r.tiles, heads_here, size)
    for copy in w_in:
        copy.wait()

    @pl.loop(0, 4)
    def _(step):
        @pl.when(step == 1)
        def _():
            for part in range(SUPER):
                first.forward(part)
        for which in (1, 2, 3):
            @pl.when(step == which)
            def _():
                for part in range(SUPER):
                    first.finish(part, which)
        rows = aligned(place.member(step) * block, block)
        a = r.n1[rows, :]
        cosine, sine = r.cos[rows, :], r.sin[rows, :]
        for w, lin, rot in ((r.wq, r.ql, r.q), (r.wk, r.kl, r.k)):
            v = nn(a, w[...])
            lin[rows, :] = v.astype(BF16)
            v = v / (1.0 + jnp.exp(-v))
            for head in range(heads_here):
                one = v[:, head * HDIM : (head + 1) * HDIM]
                rot[rows, 2 * head * HDIM : (2 * head + 1) * HDIM] = (one * cosine).astype(BF16)
                rot[rows, (2 * head + 1) * HDIM : (2 * head + 2) * HDIM] = (one * sine).astype(BF16)
        r.v[rows, :] = nn(a, r.wv[...]).astype(BF16)
        r.gate[rows, :] = nn(a, r.wg[...])

    save("n1", "ql", "kl", "q", "k", "v", "gate")
    if third_parts:
        for part in third_parts:
            third.start(part)
    w_out.wait()
    part_rows, per = 2 * half, size // 128
    heads = range(heads_here)
    wide = [slice(head * 2 * HDIM, (head + 1) * 2 * HDIM) for head in heads]
    thin = [slice(head * HDIM, (head + 1) * HDIM) for head in heads]
    decay = [r.dec[pl.ds(first_head + head, 1), 0:1] for head in heads]

    @pl.loop(0, 4)
    def _(i):
        step = jnp.where(i == 0, 3, jnp.where(i == 3, 0, i))
        row_tile = place.member(step)
        rows = aligned(row_tile * size, size)
        row_seg = widen(r.segc[rows, :], per)
        queries = [r.q[rows, wide[head]] for head in heads]

        def terms(col_tile, weights):
            cols = aligned(col_tile * size, size)
            col_seg = jnp.concatenate([r.segf[pl.ds(per * col_tile + n, 1), :] for n in range(per)], axis=1)
            same = row_seg == col_seg
            out = []
            for head in heads:
                scores = nt(queries[head], r.k[cols, wide[head]]) * jnp.where(same, weights[head], 0.0)
                out.append(nn(scores.astype(BF16), r.v[cols, thin[head]]))
            return tuple(out)

        def add(col_tile, sums):
            gap = (size * (row_tile - col_tile - 1)).astype(F32)
            more = terms(col_tile, [r.tiles[head, 1] * jnp.exp(decay[head] * gap) for head in heads])
            return tuple(one + other for one, other in zip(sums, more))

        sums = lax.fori_loop(0, row_tile, add, terms(row_tile, [r.tiles[head, 0] for head in heads]))
        for head in heads:
            r.heads[rows, thin[head]] = sums[head]
            r.dh[rows, thin[head]] = (sums[head] * r.gate[rows, thin[head]]).astype(BF16)
        for part in range(SUPER):
            some = aligned(row_tile * block + part * part_rows, part_rows)
            r.part1[some, :] = nn(r.dh[some, :], r.wo[...]).astype(BF16)
            for which in (1, 2, 3):
                @pl.when(step == which)
                def _():
                    mid_sum.send_block(part, which)
        for n in range(per):
            v = r.heads[aligned(row_tile * size + n * 128, 128), :]
            row_sums(v * v, r.ss_mine, row_tile * per + n)

    share.start()
    save("heads")
    if third_parts:
        for part in third_parts:
            third.forward(part)
    for part in range(SUPER):
        mid_sum.middle(part)
    r.ss[...] = share.total()
    save("ss")
    scaling = lax.rsqrt(r.ss[...] / width + epsilon)
    per_block = block // 128
    for chunk in range(per_block):
        r.scale[aligned(own_start + chunk * 128, 128), :] = spread(scaling, place.me * per_block + chunk)
    r.stat_wide[...] = jnp.zeros_like(r.stat_wide)

    def add_stat(row, v):
        sums = jnp.sum(v * v, axis=0, keepdims=True)
        r.stat_wide[row : row + 1, :] += sums

    step_rows = min(32, half)
    for part in range(SUPER):
        for h in range(2):
            mid_sum.finish(part, h)
            for i in range(half // step_rows):
                offset = (2 * part + h) * half + i * step_rows
                scale = widen(r.scale[aligned(own_start + offset, step_rows), :], width // 128)
                attn = mid_sum.total(part, h, i * step_rows, step_rows) * scale
                middle = x[offset : offset + step_rows, :].astype(F32) + attn
                r.mid[offset : offset + step_rows, :] = middle
                add_stat(0, attn)
                norm = lax.rsqrt(jnp.mean(middle * middle, axis=1, keepdims=True) + epsilon)
                r.n2[aligned(own_start + offset, step_rows), :] = (middle * norm).astype(BF16)
        second.start(part)
    save("mid")
    for copy in w_glu:
        copy.wait()
    if third_parts:
        for part in third_parts:
            for which in (1, 2, 3):
                third.finish(part, which)
    if back_block is not None:
        mid_sum.drain()

    def glu(part, step):
        rows = aligned(place.member(step) * block + part * part_rows, part_rows)
        a = r.n2[rows, :]
        left = nt(a, r.wl[...])
        right = nt(a, r.wr[...])
        hidden = (left * right).astype(BF16)
        r.hid[rows, :] = hidden
        if back_block is not None:
            back_block(rows, left, right, part, step)
        else:
            r.left[rows, :] = left.astype(BF16)
            r.right[rows, :] = right.astype(BF16)
        r.part2[rows, :] = nn(hidden, r.wd[...]).astype(BF16)
        if back_block is None:
            for which in (1, 2, 3):
                @pl.when(step == which)
                def _():
                    out_sum.send_block(part, which)

    gather_stage(second, glu, lambda i: None)

    def finish(target, following):
        for part in range(SUPER):
            for h in range(2):
                out_sum.finish(part, h)
                for i in range(half // step_rows):
                    offset = (2 * part + h) * half + i * step_rows
                    glu_rows = out_sum.total(part, h, i * step_rows, step_rows)
                    after = r.mid[offset : offset + step_rows, :] + glu_rows
                    target[offset : offset + step_rows, :] = after.astype(target.dtype)
                    add_stat(1, glu_rows)
                    add_stat(2, after)
                    if following is not None:
                        norm = lax.rsqrt(jnp.mean(after * after, axis=1, keepdims=True) + epsilon)
                        r.n1[aligned(own_start + offset, step_rows), :] = (after * norm).astype(BF16)
            if following is not None:
                following.start(part)
        folded = r.stat_wide[:, :128]
        for n in range(1, width // 128):
            folded = folded + r.stat_wide[:, n * 128 : (n + 1) * 128]
        return folded

    groups = [first, second, share] + ([mid_sum] if back_block is None else [])
    return out_sum, finish, groups


def turns_of(k, size, count):
    return sum(((k >= size * n).astype(jnp.int32) for n in range(1, -(-count // size))), jnp.int32(0))


class Line:
    def __init__(self, cfg, place, r):
        self.place, self.r = place, r
        self.per, self.count = cfg.chunks, cfg.chunks * cfg.layers
        self.layers, self.rows_each = cfg.layers, cfg.chunks * CHUNK
        self.half = CHUNK // 2
        self.ticks = self.count + 3 + HOP * place.last
        self.done = 0

    def slot(self, k):
        return k - SLOTS * turns_of(k, SLOTS, self.count)

    def rows(self, k, core):
        place = k - self.per * turns_of(k, self.per, self.count)
        return aligned(place * CHUNK + core * self.half, self.half)

    def own(self, k):
        return self.rows(k, self.place.core)

    def out_rows(self, k, core):
        turn = turns_of(k, self.per, self.count)
        place = (self.layers - 1 - turn) * self.per + k - turn * self.per
        start = place * CHUNK + core * self.half
        return aligned(start, self.half)

    def pair(self, k):
        slot = self.slot(k)
        r = self.r
        return Wire(self.place.partner(), r.pair_send.at[slot], r.pair_recv.at[slot],
                    r.grads.at[self.rows(k, 1 - self.place.core)], r.pair_land.at[slot], r.pair_land.at[slot])

    def hop(self, k, land, send, recv, device):
        slot = self.slot(k)
        return Wire(device, send.at[slot], recv.at[slot], land.at[slot], land.at[slot], land.at[slot])

    def going_right(self, k):
        return self.hop(k, self.r.right_land, self.r.right_send, self.r.right_recv, self.place.right())

    def going_left(self, k):
        return self.hop(k, self.r.left_land, self.r.left_send, self.r.left_recv, self.place.left())

    def coming_right(self, k):
        return self.hop(k, self.r.right_land, self.r.right_send, self.r.right_recv, self.place.left())

    def coming_left(self, k):
        return self.hop(k, self.r.left_land, self.r.left_send, self.r.left_recv, self.place.right())

    def result(self, k):
        slot, r = self.slot(k), self.r
        return Wire(self.place.partner(), r.give_send.at[slot], r.give_recv.at[slot],
                    r.grads.at[self.own(k)], r.out_h.at[self.out_rows(k, self.place.core)],
                    r.out_h.at[self.out_rows(k, 1 - self.place.core)])

    def keep(self, k):
        slot, r = self.slot(k), self.r
        return pltpu.make_async_copy(
            r.grads.at[self.own(k)], r.out_h.at[self.out_rows(k, self.place.core)], r.keep_sem.at[slot]
        )

    def one_way(self, k, land, start_here, coming, ends_here, going):
        slot = self.slot(k)

        @pl.when(start_here)
        def _():
            land[slot] = self.r.grads[self.own(k), :]

        @pl.when(jnp.logical_not(start_here))
        def _():
            coming(k).wait_recv()
            land[slot] = land[slot] + self.r.grads[self.own(k), :]

        @pl.when(jnp.logical_not(ends_here))
        def _():
            going(k).start()

    def tick(self, n):
        place, r, last = self.place, self.r, self.place.last
        at_left, at_right = place.at == 0, place.at == last

        @pl.when(n < self.count)
        def _():
            self.pair(n).start()

        k = n - 1

        @pl.when(jnp.logical_and(k >= 0, k < self.count))
        def _():
            wire = self.pair(k)
            wire.wait_recv()
            wire.wait_send()
            slot = self.slot(k)
            r.grads[self.own(k), :] = r.grads[self.own(k), :] + r.pair_land[slot]

        left_k = n - 1 - HOP * (last - place.at)

        @pl.when(jnp.logical_and(left_k >= 0, left_k < self.count))
        def _():
            self.one_way(left_k, r.left_land, at_right, self.coming_left, at_left, self.going_left)

        right_k = n - 1 - HOP * place.at

        @pl.when(jnp.logical_and(right_k >= 0, right_k < self.count))
        def _():
            self.one_way(right_k, r.right_land, at_left, self.coming_right, at_right, self.going_right)

        full_k = n - 1 - HOP * last

        @pl.when(jnp.logical_and(full_k >= 0, full_k < self.count))
        def _():
            @pl.when(jnp.logical_not(at_right))
            def _():
                self.going_right(full_k).wait_send()

            @pl.when(jnp.logical_not(at_left))
            def _():
                self.going_left(full_k).wait_send()

            slot = self.slot(full_k)
            own = self.own(full_k)
            total = r.right_land[slot].astype(F32) + r.left_land[slot].astype(F32) - r.grads[own, :].astype(F32)
            r.grads[own, :] = total.astype(BF16)
            self.result(full_k).start()
            self.keep(full_k).start()

        old_k = full_k - 2

        @pl.when(jnp.logical_and(old_k >= 0, old_k < self.count))
        def _():
            wire = self.result(old_k)
            wire.wait_recv()
            wire.wait_send()
            self.keep(old_k).wait()

    def pump(self, ready, most):
        stop = min(self.done + most, ready)
        if stop > self.done:
            start, self.done = self.done, stop

            @pl.loop(start, stop)
            def _(n):
                self.tick(n)

    def release(self, turn, rows):
        needed = (turn - 1) * self.per + -(-rows // CHUNK) + 3 + HOP * self.place.last
        if turn > 0 and needed > self.done:
            self.pump(turn * self.per, needed - self.done)
            assert self.done >= needed

    def more(self, most):
        self.pump(self.ticks, most)


class StatLine:
    def __init__(self, place, r):
        self.place, self.r = place, r
        self.share = Share(place, r.stat_mine, r.stat_land, r.st_send, r.st_recv)

    def square(self):
        self.share.start()

    def pair(self):
        r = self.r
        r.stat_square[...] = self.share.total()
        self.wire(0, self.place.partner(), r.stat_square).start()

    def wire(self, number, device, source):
        r = self.r
        return Wire(device, r.line_send.at[number], r.line_recv.at[number], source, r.line_land.at[number], r.line_land.at[number])

    def stage(self, number):
        place, r = self.place, self.r
        if number == 0:
            self.wire(0, place.partner(), r.stat_square).wait_recv()
            r.stat_pair[...] = r.stat_square[...] + r.line_land[0]
            r.stat_right[...] = r.stat_pair[...]
            r.stat_left[...] = r.stat_pair[...]
        else:
            @pl.when(place.at == number)
            def _():
                self.wire(1, place.left(), r.stat_right).wait_recv()
                r.stat_right[...] = r.stat_pair[...] + r.line_land[1]

            @pl.when(place.last - place.at == number)
            def _():
                self.wire(2, place.right(), r.stat_left).wait_recv()
                r.stat_left[...] = r.stat_pair[...] + r.line_land[2]
        if number < place.last:
            @pl.when(place.at == number)
            def _():
                self.wire(1, place.right(), r.stat_right).start()

            @pl.when(place.last - place.at == number)
            def _():
                self.wire(2, place.left(), r.stat_left).start()

    def finish(self):
        place, r = self.place, self.r
        r.stat_total[...] = r.stat_right[...] + r.stat_left[...] - r.stat_pair[...]
        self.share.drain()
        self.wire(0, place.partner(), r.stat_square).wait_send()

        @pl.when(place.at < place.last)
        def _():
            self.wire(1, place.right(), r.stat_right).wait_send()

        @pl.when(place.at > 0)
        def _():
            self.wire(2, place.left(), r.stat_left).wait_send()


def layers_kernel(cfg, names, *refs):
    r = namespace(names, refs)
    block, length, width, local, ff = cfg.block, cfg.length, cfg.width, cfg.local, cfg.ff
    heads_here, size, layers = cfg.heads_here, cfg.block, cfg.layers
    place = Place(cfg.pairs)
    copies = Local(r.local_sem)
    line = Line(cfg, place, r)
    stats = StatLine(place, r)
    loads = {}
    base_down, base_left, base_right, base_out, base_gate, gate_end, base_qkv, _ = cfg.bases
    half = block // (2 * SUPER)
    part_rows = 2 * half
    own_start = place.me * block
    step_rows = min(32, half)
    per_block = block // 128
    tiles_here = length // size

    def load(layer, *keys):
        for key in keys:
            if key in SAVED:
                source = getattr(r, key + str(layer) + "_h")
            else:
                source = getattr(r, key + "_h").at[layer]
            loads[key] = copies.start(source, getattr(r, key))

    def await_loads(*keys):
        for key in keys:
            loads[key].wait()

    glu_in = ("wd", "left", "right", "wl", "wr")
    glu_grad = ("hid", "n2")
    out_in = ("ss", "wo", "gate", "heads")
    attn_in = ("q", "k", "v", "ql", "kl")
    in_in = ("wq", "wk", "wv", "wg")

    def gather_one(layer):
        return Gather(place, r.gd, r.ag1_send.at[layer], r.ag1_recv.at[layer], block)

    firsts = [gather_one(layer) for layer in range(layers)]

    @pl.loop(0, block // 32)
    def _(i):
        rows = aligned(i * 32, 32)
        r.g[rows, :] = r.up[rows, :].astype(F32)


        r.gd[aligned(own_start + i * 32, 32), :] = r.up[rows, :]
    for start, stop in ((gate_end, base_qkv), (base_qkv + 3 * local, cfg.chunks * CHUNK)):
        if stop > start:
            r.grads[start:stop, :] = jnp.zeros((stop - start, width), BF16)
    top = layers - 1
    third = Gather(place, r.gd, r.ag3_send, r.ag3_recv, block)
    top_sum = Scatter(place, r.part1, r.land1, r.rs1_send.at[top], r.rs1_recv.at[top], block)

    def back_block(rows, left, right, part, step):
        grad_hidden = nt(r.gd[rows, :], r.wd[...])
        grad_left = (grad_hidden * right).astype(BF16)
        grad_right = (grad_hidden * left).astype(BF16)
        r.right[rows, :] = grad_left
        r.left[rows, :] = grad_right
        r.part1[rows, :] = (nn(grad_left, r.wl[...]) + nn(grad_right, r.wr[...])).astype(BF16)
        for which in (1, 2, 3):
            @pl.when(step == which)
            def _():
                top_sum.send_block(part, which)

    r.stat_mine[...] = jnp.zeros_like(r.stat_mine)
    late = [part for part in range(SUPER) if part not in EARLY]
    for layer in range(top):
        saves = []

        def save(*keys):
            for key in keys:
                saves.append(copies.start(getattr(r, key), getattr(r, key + str(layer) + "_h")))

        out_sum, finish_forward, groups = forward_front(
            cfg, r, place, copies, layer, getattr(r, "x%d" % layer), save, third, EARLY if layer == top - 1 else (), None
        )
        for copy in saves:
            copy.wait()
        saves.clear()
        save("n2", "left", "right", "hid")
        for group in groups:
            group.drain()
        for part in range(SUPER):
            out_sum.middle(part)
        following = Gather(place, r.n1, r.fag1_send.at[layer + 1], r.fag1_recv.at[layer + 1], block)
        folded = finish_forward(getattr(r, "x%d" % (layer + 1)), following)
        r.stat_mine[3 * layer : 3 * layer + 3, :] = folded[0:3, :]
        for copy in saves:
            copy.wait()
        out_sum.drain()
    out_sum, finish_forward, groups = forward_front(
        cfg, r, place, copies, top, getattr(r, "x%d" % top), lambda *keys: None, third, late, back_block
    )
    for group in groups:
        group.drain()
    third.drain()

    def back_rows(total, values, grad):
        norm = lax.rsqrt(jnp.mean(values * values, axis=1, keepdims=True) + epsilon)
        m = values * norm
        inner = jnp.mean(total * m, axis=1, keepdims=True)
        return grad + norm * (total - m * inner)

    for turn, layer in enumerate(reversed(range(layers))):
        first = firsts[layer]
        mid_sum = top_sum if turn == 0 else Scatter(place, r.part1, r.land1, r.rs1_send.at[layer], r.rs1_recv.at[layer], block)
        second = Gather(place, r.ga, r.ag2_send.at[layer], r.ag2_recv.at[layer], block)
        in_sum = Scatter(place, r.part1, r.land1, r.rs2_send.at[layer], r.rs2_recv.at[layer], block)
        share = Share(place, r.inner, r.inner_land.at[layer], r.in_send.at[layer], r.in_recv.at[layer])
        first_head = layer * HEADS + place.me * heads_here

        def ready(rows):
            return turn * cfg.chunks + rows // CHUNK

        if turn > 0:
            decay_tiles(r.dec, first_head, r.tiles, heads_here, size)
            await_loads(*glu_in)
            await_loads(*out_in)
        scaling = lax.rsqrt(r.ss[...] / width + epsilon)
        for chunk in range(length // 128):
            r.scale[chunk * 128 : (chunk + 1) * 128, :] = spread(scaling, chunk)
        def glu_back(part, step):
            rows = aligned(place.member(step) * block + part * part_rows, part_rows)
            grad_hidden = nt(r.gd[rows, :], r.wd[...])
            grad_left = (grad_hidden * r.right[rows, :].astype(F32)).astype(BF16)
            grad_right = (grad_hidden * r.left[rows, :].astype(F32)).astype(BF16)
            r.right[rows, :] = grad_left
            r.left[rows, :] = grad_right
            r.part1[rows, :] = (nn(grad_left, r.wl[...]) + nn(grad_right, r.wr[...])).astype(BF16)
            for which in (1, 2, 3):
                @pl.when(step == which)
                def _():
                    mid_sum.send_block(part, which)

        if turn > 0:
            gather_stage(first, glu_back, lambda i: line.pump(ready(0), 2))
            first.drain()
        grad_left_ref, grad_right_ref = r.right, r.left

        def glu_grad_rows(base, a_ref, b_ref):
            line.release(turn, base + ff)
            for n in range(width // 256):
                cols = slice(n * 256, (n + 1) * 256)
                r.grads[base : base + ff, cols] = tn(a_ref[...], b_ref[:, cols]).astype(BF16)

        if turn > 0:
            await_loads(*glu_grad)
            for copy in mid_pieces:
                copy.wait()
        glu_grad_rows(base_down, r.hid, r.gd)
        line.pump(ready(base_left), 1 + turn)
        mid_sum.middle(0)
        glu_grad_rows(base_left, grad_left_ref, r.n2)
        line.pump(ready(base_right), 1 + turn)
        for part in range(1, SUPER):
            mid_sum.middle(part)
        glu_grad_rows(base_right, grad_right_ref, r.n2)
        for part in range(SUPER):
            line.pump(ready(base_out), 2 if part == 0 else 1)
            for h in range(2):
                mid_sum.finish(part, h)
                for i in range(half // step_rows):
                    offset = (2 * part + h) * half + i * step_rows
                    rows = slice(offset, offset + step_rows)
                    total = mid_sum.total(part, h, i * step_rows, step_rows)
                    if turn == 0:
                        values = r.mid[rows, :]
                    else:
                        pieces = range(width // (2 * HDIM))
                        values = jnp.concatenate([r.dq[n * block + offset : n * block + offset + step_rows, :] for n in pieces], axis=1)
                    new = back_rows(total, values, r.g[rows, :])
                    r.gm[rows, :] = new
                    r.ga[aligned(own_start + offset, step_rows), :] = new.astype(BF16)
            second.start(part)
        mid_sum.drain()
        if turn + 1 < layers:
            load(layer - 1, *glu_in, *glu_grad)

        def out_back(part, step):
            member = place.member(step)
            for chunk in range(part_rows // 128):
                number = part * (part_rows // 128) + chunk
                rows = aligned(member * block + number * 128, 128)
                grad_branch = nt(r.ga[rows, :], r.wo[...])
                gate = r.gate[rows, :]
                normed = r.heads[rows, :] * widen(r.scale[rows, :], local // 128)
                grad_normed = grad_branch * gate
                r.dx[rows, 3 * local : 4 * local] = (grad_branch * normed).astype(BF16)
                r.branch[rows, :] = (normed * gate).astype(BF16)
                r.gate[rows, :] = grad_normed
                row_sums(grad_normed * normed, r.inner, member * per_block + number)

        gather_stage(second, out_back, lambda i: line.pump(ready(base_out), 3 if i == SUPER else 2))
        share.start()
        line.release(turn, base_gate)
        r.grads[base_out : base_out + local, :] = tn(r.branch[...], r.ga[...]).astype(BF16)
        line.pump(ready(base_gate), 1)

        def in_grad_rows(number, base):
            cols = slice(number * local, (number + 1) * local)
            line.release(turn, base + local)
            for n in range(width // local):
                part_grad = tn(r.n1[:, n * local : (n + 1) * local], r.dx[:, cols])
                r.grads[base : base + local, n * local : (n + 1) * local] = part_grad.astype(BF16)

        if turn > 0:
            await_loads("n1")
        in_grad_rows(3, base_gate)
        line.pump(ready(base_qkv), 1)
        if turn > 0:
            await_loads(*attn_in)
        r.intot[...] = share.total() / width
        for chunk in range(length // 128):
            rows = slice(chunk * 128, (chunk + 1) * 128)
            scale = widen(r.scale[rows, :], local // 128)
            inner = widen(spread(r.intot[...], chunk), local // 128)
            normed = r.heads[rows, :] * scale
            r.dh[rows, :] = (scale * (r.gate[rows, :] - normed * inner)).astype(BF16)
        share.drain()
        second.drain()
        if turn + 1 < layers:
            load(layer - 1, *out_in)
        between = None
        if turn > 0:
            line.pump(ready(base_qkv), 1)
            between = line.done
            line.done += 1
            assert line.done <= ready(base_qkv)

        @pl.loop(0, heads_here)
        def _(head):
            if between is not None:
                @pl.when(head == 1)
                def _():
                    line.tick(between + head - 1)

            wide = aligned(head * 2 * HDIM, 2 * HDIM)
            thin = aligned(head * HDIM, HDIM)
            for col_tile in range(tiles_here):
                cols = slice(col_tile * size, (col_tile + 1) * size)
                keys = r.k[cols, wide]
                values = r.v[cols, thin]
                acc_key, acc_value = None, None
                for row_tile in range(col_tile, tiles_here):
                    rows = slice(row_tile * size, (row_tile + 1) * size)
                    queries = r.q[rows, wide]
                    grads = r.dh[rows, thin]
                    weight = tile_weight(r, first_head, head, row_tile, col_tile, size)
                    scores = (nt(queries, keys) * weight).astype(BF16)
                    pulled = (nt(grads, values) * weight).astype(BF16)
                    term = nn(pulled, keys)
                    if col_tile == 0:
                        r.dq[rows, :] = term
                    else:
                        r.dq[rows, :] += term
                    key_term = tn(pulled, queries)
                    value_term = tn(scores, grads)
                    acc_key = key_term if acc_key is None else acc_key + key_term
                    acc_value = value_term if acc_value is None else acc_value + value_term
                r.dk[cols, :] = acc_key
                r.dx[cols, aligned(2 * local + head * HDIM, HDIM)] = acc_value.astype(BF16)
            for row_tile in range(tiles_here):
                rows = slice(row_tile * size, (row_tile + 1) * size)
                cosine, sine = r.cos[rows, :], r.sin[rows, :]
                for grad, lin, base in ((r.dq, r.ql, 0), (r.dk, r.kl, local)):
                    v = lin[rows, thin].astype(F32)
                    gate = 1.0 / (1.0 + jnp.exp(-v))
                    back = grad[rows, :HDIM] * cosine + grad[rows, HDIM:] * sine
                    back = back * (gate + v * gate * (1.0 - gate))
                    r.dx[rows, aligned(base + head * HDIM, HDIM)] = back.astype(BF16)

        if turn + 1 < layers:
            load(layer - 1, *attn_in)
            source = getattr(r, "mid%d_h" % (layer - 1))
            mid_pieces = [
                copies.start(source.at[:, pl.ds(n * 2 * HDIM, 2 * HDIM)], r.dq.at[pl.ds(n * block, block), :])
                for n in range(width // (2 * HDIM))
            ]
        if turn > 0:
            await_loads(*in_in)
        last = turn == layers - 1
        for part in range(SUPER):
            for step in (3, 1, 2, 0):
                rows = aligned(place.member(step) * block + part * part_rows, part_rows)
                total = None
                for n, w in enumerate((r.wq, r.wk, r.wv, r.wg)):
                    term = nt(r.dx[rows, n * local : (n + 1) * local], w[...])
                    total = term if total is None else total + term
                r.part1[rows, :] = total.astype(BF16)
                in_sum.send_block(part, step)
            line.pump(ready(base_qkv), 1)
        for number in range(3):
            in_grad_rows(number, base_qkv + number * local)
            line.pump(ready(base_qkv + (number + 1) * local), 2 if last else 1)
            if number < SUPER:
                in_sum.middle(number)
        if last:
            for part in range(SUPER):
                for which in (1, 2, 3):
                    out_sum.send_block(part, which)
        if turn + 1 < layers:
            load(layer - 1, *in_in, "n1")
        for part in range(SUPER):
            line.pump(ready(cfg.chunks * CHUNK), 2 if last else 1)
            for h in range(2):
                in_sum.finish(part, h)
                for i in range(half // step_rows):
                    offset = (2 * part + h) * half + i * step_rows
                    rows = slice(offset, offset + step_rows)
                    total = in_sum.total(part, h, i * step_rows, step_rows)
                    values = getattr(r, "x%d" % layer)[rows, :].astype(F32)
                    new = back_rows(total, values, r.gm[rows, :])
                    if layer > 0:
                        r.g[rows, :] = new
                        r.gd[aligned(own_start + offset, step_rows), :] = new.astype(BF16)
                    else:
                        r.go[rows, :] = new.astype(BF16)
            if layer > 0:
                firsts[layer - 1].start(part)
        in_sum.drain()
    line.more(2)
    for part in range(SUPER):
        out_sum.middle(part)
        line.more(2)
    folded = finish_forward(r.xo, None)
    r.stat_mine[3 * top : 3 * top + 3, :] = folded[0:3, :]
    stats.square()
    line.more(1)
    stats.pair()
    for number in range(cfg.pairs):
        line.more(1)
        stats.stage(number)
    out_sum.drain()
    stats.finish()
    line.more(line.ticks)


def call_kernel(body, cfg, inputs, outputs, scratch, collective_id, name):
    vmem, anywhere = pl.BlockSpec(memory_space=pltpu.VMEM), pl.BlockSpec(memory_space=pl.ANY)
    names = list(inputs) + list(outputs) + list(scratch)
    result = pl.pallas_call(
        functools.partial(body, cfg, names),
        out_shape=[shape for shape, _ in outputs.values()],
        in_specs=[vmem if placed else anywhere for _, placed in inputs.values()],
        out_specs=[vmem if placed else anywhere for _, placed in outputs.values()],
        scratch_shapes=list(scratch.values()),
        compiler_params=pltpu.CompilerParams(
            collective_id=collective_id, has_side_effects=collective_id is not None, vmem_limit_bytes=VMEM_LIMIT
        ),
        name=name,
    )(*[array for array, _ in inputs.values()])
    return dict(zip(outputs, result))


def collective_scratch(cfg, copies, lead):
    dma = pltpu.SemaphoreType.DMA
    half = cfg.block // (2 * SUPER)
    out = {}
    for name in ("ag1", "ag2", "rs1", "rs2"):
        for key in (name, "f" + name):
            out[key + "_send"] = out[key + "_recv"] = dma((*lead, SUPER, 6))
    for name in copies:
        out["land" + name] = pltpu.VMEM((SUPER, 6, half, cfg.width), BF16)
        out["part" + name] = pltpu.VMEM((cfg.length, cfg.width), BF16)
    out["local_sem"] = dma((96,))
    return out


def weight_scratch(cfg):
    v = pltpu.VMEM
    return dict(
        wq=v((cfg.width, cfg.local), BF16), wk=v((cfg.width, cfg.local), BF16),
        wv=v((cfg.width, cfg.local), BF16), wg=v((cfg.width, cfg.local), BF16),
        wo=v((cfg.local, cfg.width), BF16), wl=v((cfg.ff, cfg.width), BF16),
        wr=v((cfg.ff, cfg.width), BF16), wd=v((cfg.ff, cfg.width), BF16),
    )


def table_scratch(cfg):
    v = pltpu.VMEM
    return dict(
        segc=v((cfg.length, 128), F32), segf=v((8, 128), F32),
        tiles=v((cfg.heads_here, 2, cfg.block, cfg.block), F32),
    )


def forward_scratch(cfg):
    v, dma = pltpu.VMEM, pltpu.SemaphoreType.DMA
    rows, wide, local, ff, block = cfg.length, cfg.width, cfg.local, cfg.ff, cfg.block
    return dict(
        n1=v((rows, wide), BF16), ql=v((rows, local), BF16), kl=v((rows, local), BF16), q=v((rows, 2 * local), BF16),
        k=v((rows, 2 * local), BF16), v=v((rows, local), BF16), gate=v((rows, local), F32), heads=v((rows, local), F32),
        mid=v((block, wide), F32), n2=v((rows, wide), BF16), left=v((rows, ff), BF16), right=v((rows, ff), BF16),
        hid=v((rows, ff), BF16), ss=v((8, 128), F32), ss_mine=v((8, 128), F32), dh=v((rows, local), BF16),
        stat_wide=v((8, wide), F32), scale=v((rows, 128), F32), ss_land=v((cfg.layers, 3, 8, 128), F32),
        ss_send=dma((cfg.layers, 3)), ss_recv=dma((cfg.layers, 3)),
    )


def gather_sems():
    sems = pltpu.SemaphoreType.DMA((SUPER, 6))
    return dict(ag3_send=sems, ag3_recv=sems)


SAVED = ("ss", "mid", "n1", "ql", "kl", "q", "k", "v", "gate", "heads", "n2", "left", "right", "hid")


def run_layers(cfg, tokens, upstream, tables, weights):
    v, dma, s = pltpu.VMEM, pltpu.SemaphoreType.DMA, jax.ShapeDtypeStruct
    rows, wide, local, ff, block = cfg.length, cfg.width, cfg.local, cfg.ff, cfg.block
    inputs = dict(
        up=(upstream, True), x0=(tokens, True), **{k: (a, True) for k, a in tables.items()},
        **{k + "_h": (a, False) for k, a in weights.items()},
    )
    total_rows = cfg.chunks * CHUNK
    outputs = dict(
        xo=(s((block, wide), BF16), True), go=(s((block, wide), BF16), True), stat_total=(s((8, 128), F32), True),
        out_h=(s((cfg.layers * total_rows, wide), BF16), False),
    )
    small, ring, ring_sem = v((8, 128), F32), v((SLOTS, CHUNK // 2, wide), BF16), dma((SLOTS,))
    scratch = dict(
        **weight_scratch(cfg), **collective_scratch(cfg, ("1", "2"), (cfg.layers,)), **table_scratch(cfg), **forward_scratch(cfg),
        **gather_sems(),
        gd=v((rows, wide), BF16), ga=v((rows, wide), BF16),
        g=v((block, wide), F32), gm=v((block, wide), F32),
        branch=v((rows, local), BF16), dx=v((rows, 4 * local), BF16),
        dq=v((rows, 2 * HDIM), F32), dk=v((rows, 2 * HDIM), F32),
        grads=v((total_rows, wide), BF16),
        inner=small, intot=small,
        inner_land=v((cfg.layers, 3, 8, 128), F32), in_send=dma((cfg.layers, 3)), in_recv=dma((cfg.layers, 3)),
        pair_land=ring, right_land=ring, left_land=ring,
        pair_send=ring_sem, pair_recv=ring_sem, right_send=ring_sem, right_recv=ring_sem, left_send=ring_sem,
        left_recv=ring_sem, give_send=ring_sem, give_recv=ring_sem, keep_sem=ring_sem,
        stat_mine=small, stat_square=small, stat_pair=small, stat_right=small, stat_left=small,
        stat_land=v((3, 8, 128), F32), st_send=dma((3,)), st_recv=dma((3,)),
        line_land=v((3, 8, 128), F32), line_send=dma((3,)), line_recv=dma((3,)),
    )
    for layer in range(1, cfg.layers):
        scratch["x%d" % layer] = v((block, wide), F32)
    for layer in range(cfg.layers - 1):
        for key in SAVED:
            outputs["%s%d_h" % (key, layer)] = (s(scratch[key].shape, scratch[key].dtype), False)
    return call_kernel(layers_kernel, cfg, inputs, outputs, scratch, 0, "layers")


def widen_kernel(cfg, names, *refs):
    r = namespace(names, refs)
    tasks = []
    for layer in range(cfg.layers):
        for number, target in enumerate((r.down, r.left, r.right, r.out)):
            start, stop = cfg.bases[number], cfg.bases[number + 1]
            rows = (stop - start) // 2 if stop - start > 512 else stop - start
            for first in range(start, stop, rows):
                tasks.append((layer, first, rows, [(target.at[layer, pl.ds(first - start, rows), :], slice(None))]))
        for number, target in enumerate((r.gate, r.query, r.key, r.value)):
            pieces = [
                (target.at[layer, pl.ds(n * cfg.local, cfg.local), :], slice(n * cfg.local, (n + 1) * cfg.local))
                for n in range(cfg.width // cfg.local)
            ]
            start = cfg.bases[6] + (number - 1) * cfg.local if number > 0 else cfg.bases[4]
            tasks.append((layer, start, cfg.local, pieces))
    depth = WIDEN_DEPTH
    whole_in = [
        pltpu.make_async_copy(r.xo_in, r.whole.at[0], r.whole_sem.at[0]),
        pltpu.make_async_copy(r.go_in, r.whole.at[1], r.whole_sem.at[1]),
    ]
    whole_out = [
        pltpu.make_async_copy(r.whole.at[0], r.xo, r.whole_sem.at[2]),
        pltpu.make_async_copy(r.whole.at[1], r.go, r.whole_sem.at[3]),
    ]
    for copy in whole_in:
        copy.start()
    means = jnp.sum(r.stat[...], axis=1, keepdims=True) / cfg.entries
    roots = jnp.sqrt(means)
    for layer in range(cfg.layers):
        for number in range(3):
            row = 3 * layer + number
            r.rms[layer : layer + 1, number : number + 1] = roots[row : row + 1, :]

    def fetch(task):
        layer, first, rows, _ = tasks[task]
        start = layer * cfg.chunks * CHUNK + first
        slot = task % depth
        return pltpu.make_async_copy(r.grads.at[pl.ds(start, rows), :], r.narrow.at[slot, pl.ds(0, rows), :], r.in_sem.at[slot])

    def store(task):
        _, _, rows, pieces = tasks[task]
        slot = task % depth
        return [
            pltpu.make_async_copy(r.wide.at[slot, pl.ds(0, rows), lanes], target, r.out_sem.at[slot, n])
            for n, (target, lanes) in enumerate(pieces)
        ]

    for task in range(min(depth, len(tasks))):
        fetch(task).start()
    for task in range(len(tasks)):
        if task == 2:
            for one, other in zip(whole_in, whole_out):
                one.wait()
                other.start()
        slot, rows = task % depth, tasks[task][2]
        fetch(task).wait()
        if task >= depth:
            for copy in store(task - depth):
                copy.wait()

        @pl.loop(0, rows // 32)
        def _(i):
            part = aligned(i * 32, 32)
            r.wide[slot, part, :] = r.narrow[slot, part, :].astype(F32)

        for copy in store(task):
            copy.start()
        if task + depth < len(tasks):
            fetch(task + depth).start()
    for task in range(max(len(tasks) - depth, 0), len(tasks)):
        for copy in store(task):
            copy.wait()
    for copy in whole_out:
        copy.wait()


def run_widen(cfg, back):
    v, dma, s = pltpu.VMEM, pltpu.SemaphoreType.DMA, jax.ShapeDtypeStruct
    thin, flat = s((cfg.layers, cfg.width, cfg.local), F32), s((cfg.layers, cfg.ff, cfg.width), F32)
    outputs = dict(
        down=(flat, False), left=(flat, False), right=(flat, False), out=(s((cfg.layers, cfg.local, cfg.width), F32), False),
        gate=(thin, False), query=(thin, False), key=(thin, False), value=(thin, False),
        xo=(s((cfg.block, cfg.width), BF16), False), go=(s((cfg.block, cfg.width), BF16), False),
        rms=(s((cfg.layers, 3), F32), True),
    )
    inputs = dict(grads=(back["out_h"], False), xo_in=(back["xo"], False), go_in=(back["go"], False), stat=(back["stat_total"], True))
    rows = max(cfg.ff // 2, cfg.local, 512)
    scratch = dict(
        narrow=v((WIDEN_DEPTH, rows, cfg.width), BF16), wide=v((WIDEN_DEPTH, rows, cfg.width), F32),
        whole=v((2, cfg.block, cfg.width), BF16), whole_sem=dma((4,)), in_sem=dma((WIDEN_DEPTH,)), out_sem=dma((WIDEN_DEPTH, cfg.width // cfg.local)),
    )
    return call_kernel(widen_kernel, cfg, inputs, outputs, scratch, None, "widen_gradients")


def per_device_square(
    tokens, upstream, segment_ids, query_proj, key_proj, value_proj, gate_proj, output_proj, left_proj, right_proj, down_proj
):
    layers = query_proj.shape[0]
    block, width = tokens.shape
    length = segment_ids.shape[0]
    local, ff = query_proj.shape[2], left_proj.shape[2]
    heads_here = local // HDIM
    positions = np.arange(length, dtype=np.float32)
    frequency = np.exp(np.float32(-math.log(10000.0)) * np.arange(HDIM, dtype=np.float32) / np.float32(HDIM))
    angles = positions[:, None] * frequency[None, :]
    slopes = np.exp2(-8.0 * (np.arange(HEADS) + 1.0) / HEADS)
    decays = np.concatenate([-slopes * (1.0 - depth_start - depth_step * layer) for layer in range(layers)])
    tables = dict(
        cos=jnp.asarray(np.cos(angles)), sin=jnp.asarray(np.sin(angles)),
        dec=jnp.asarray(np.broadcast_to(decays[:, None], (layers * HEADS, 128)).astype(np.float32)),
        seg=segment_ids.reshape(8, length // 8),
    )
    weights = dict(
        wq=query_proj, wk=key_proj, wv=value_proj, wg=gate_proj, wo=output_proj,
        wl=jnp.swapaxes(left_proj, 1, 2), wr=jnp.swapaxes(right_proj, 1, 2), wd=down_proj,
    )
    ends = np.cumsum([0, ff, ff, ff, local, local]).tolist()
    ends += [-(-ends[-1] // CHUNK) * CHUNK]
    ends += [-(-(ends[-1] + 3 * local) // CHUNK) * CHUNK]
    common = dict(
        layers=layers, block=block, length=length, width=width, local=local, ff=ff, heads_here=heads_here,
        pairs=lax.axis_size("dp") // 2, bases=ends, chunks=ends[-1] // CHUNK,
    )
    back = run_layers(types.SimpleNamespace(**common), tokens, upstream, tables, weights)
    entries = float(length * lax.axis_size("dp") * width)
    wide = run_widen(types.SimpleNamespace(entries=entries, **common), back)
    return (
        wide["xo"], wide["go"], wide["query"], wide["key"], wide["value"], wide["gate"], wide["out"],
        jnp.swapaxes(wide["left"], 1, 2), jnp.swapaxes(wide["right"], 1, 2), wide["down"], wide["rms"],
    )


def solution(mesh):
    square = dict(mesh.shape) == SQUARE_MESH
    body = per_device_square if square else per_device
    return jax.shard_map(
        body,
        mesh=mesh,
        in_specs=(
            P(("dp", "tensor"), None),
            P(("dp", "tensor"), None),
            P("dp"),
            P(None, None, "tensor"),
            P(None, None, "tensor"),
            P(None, None, "tensor"),
            P(None, None, "tensor"),
            P(None, "tensor", None),
            P(None, None, "tensor"),
            P(None, None, "tensor"),
            P(None, "tensor", None),
        ),
        out_specs=(
            P(("dp", "tensor"), None),
            P(("dp", "tensor"), None),
            P(None, None, "tensor"),
            P(None, None, "tensor"),
            P(None, None, "tensor"),
            P(None, None, "tensor"),
            P(None, "tensor", None),
            P(None, None, "tensor"),
            P(None, None, "tensor"),
            P(None, "tensor", None),
            P(),
        ),
        check_vma=False,
    )
```
